32 devices in a mesh: row: 4 (over x, core), col: 8 (over z, y).
Axes of the slice: x: 2, y: 2, z: 4, core: 2. Of those that a mesh axis runs over, the one named last changes fastest.
Arguments:
- tokens: bfloat16 [24576, 768], P(('row', 'col')), may hold values from -6 to 6
- w_qkv: bfloat16 [3, 768, 768], replicated, may hold values from -0.21875 to 0.21875
- w_attn_out: bfloat16 [768, 768], replicated, may hold values from -0.875 to 0.875
- w_in: bfloat16 [768, 3072], replicated, may hold values from -0.21875 to 0.21875
- w_out: bfloat16 [3072, 768], replicated, may hold values from -0.109375 to 0.109375
- vectors: float32 [9216], replicated
- out_grad: bfloat16 [24576, 768], P(('row', 'col')), may hold values from -6 to 6
- span_count: int32 [32], replicated, may hold values from 1 to 6, as said below
- pair_index: int32 [192], replicated, may hold values from 0 to 191, as said below
- owner_list: int32 [48], replicated, may hold values from 0 to 47, each once
- master: float32 [48, 768, 192], P('col'), may hold values from -0.21875 to 0.21875
- first_moment: float32 [48, 768, 192], P('col'), may hold values from -56 to 56
- second_moment: float32 [48, 768, 192], P('col'), may hold values from 6.144 to 24.576
- left_basis: float32 [48, 768, 768], P('col'), as said below
- right_basis: float32 [48, 192, 192], P('col'), as said below
- vec_first: float32 [9216], replicated, may hold values from -112 to 112
- vec_second: float32 [9216], replicated, may hold values from 24.576 to 98.304
Outputs:
- encoded: bfloat16 [24576, 768], P(('row', 'col'))
- input_grad: float32 [24576, 768], P(('row', 'col'))
- loss: float32 [], replicated
- new_master: float32 [48, 768, 192], P('col')
- new_first: float32 [48, 768, 192], P('col')
- new_second: float32 [48, 768, 192], P('col')
- master_copy: bfloat16 [48, 768, 192], P('col')
- vec_new: float32 [9216], replicated
- vec_first_new: float32 [9216], replicated
- vec_second_new: float32 [9216], replicated
The draws below stay inside these ranges and needn't reach their ends.
Inputs may be any that keep to these rules, and one draw needn't show every extreme that they name: `span_count`: the live spans of a device fill its first slots; the last device has 6 live spans. pair_index[i] = i for padding slots and for live spans without a partner; otherwise j = pair_index[i] is another live span, on any device, with pair_index[j] = i. `owner_list`: each block number once. `left_basis`: each [s] is orthogonal: the columns are orthonormal DCT-II basis vectors, permuted and signed. `right_basis`: each [s] is orthogonal: the columns are orthonormal DCT-II basis vectors, permuted and signed.
All inputs are finite; a program needn't handle non-finite values.
Results may differ from the reference program's by a relative error of at most 0.01.
Values may be sent and summed in bfloat16 or wider, within the bound.
No kernel may reach another device: no remote copies, remote signals or barrier semaphores. Data moves between devices by JAX's collectives and lax.ppermute only.
A program may use at most 192 MiB of HBM per device.

```python
import math
import jax
import jax.numpy as jnp
from jax import lax

D = 768
HEADS = 12
HEAD = 64
FF = 3072
SPAN = 128
SLOTS = 6
STEP = 10
BW = 192
NBLK = 48
NSPAN = 192
TOKENS = 24576
NVEC = 9216
N_ROW = 4
N_COL = 8
DEVICES = 32


def live_counts(key):
    device = jnp.arange(DEVICES, dtype=jnp.int32)
    row_pos = device // N_COL
    col_pos = device % N_COL
    rising = (SLOTS - 1) * (row_pos * (N_COL - 1) + col_pos * (N_ROW - 1)) // (2 * (N_ROW - 1) * (N_COL - 1))
    extra = jax.random.randint(jax.random.fold_in(key, 11), (DEVICES,), 0, 2)
    return jnp.minimum(SLOTS, 1 + rising + extra).astype(jnp.int32)


def pairing(key):
    counts = live_counts(key)
    span_ids = jnp.arange(NSPAN, dtype=jnp.int32)
    live = span_ids % SLOTS < jnp.repeat(counts, SLOTS)
    random_rank = jax.random.randint(jax.random.fold_in(key, 12), (NSPAN,), 0, 4 * NSPAN)
    ranking = jnp.where(live, random_rank, 8 * NSPAN)
    order = jnp.argsort(ranking, stable=True).astype(jnp.int32)
    live_total = jnp.sum(live.astype(jnp.int32))
    paired_total = 2 * (live_total * 4 // 10)
    places = jnp.arange(NSPAN, dtype=jnp.int32)
    partner_sorted = jnp.where(places < paired_total, order[places ^ 1], order)
    return jnp.zeros((NSPAN,), jnp.int32).at[order].set(partner_sorted)


def orthogonal_blocks(key, width):
    signs = (jax.random.randint(jax.random.fold_in(key, 1), (NBLK, width), 0, 2) * 2 - 1).astype(jnp.float32)
    block_keys = jax.random.split(jax.random.fold_in(key, 2), NBLK)
    shuffled = jax.vmap(lambda single: jax.random.permutation(single, width))(block_keys).astype(jnp.int32)
    rows_idx = jnp.arange(width, dtype=jnp.int32)
    phase = (2 * rows_idx[None, :, None] + 1) * shuffled[:, None, :] % (4 * width)
    amplitude = jnp.where(shuffled == 0, math.sqrt(1.0 / width), math.sqrt(2.0 / width)).astype(jnp.float32)
    angles = phase.astype(jnp.float32) * (math.pi / (2.0 * width))
    return (signs * amplitude)[:, None, :] * jnp.cos(angles)


def draw_span_count(key, part):
    return live_counts(key)


def draw_pair_index(key, part):
    return pairing(key)


def draw_left_basis(key, part):
    key = jax.random.fold_in(key, 21)
    return orthogonal_blocks(key, D)


def draw_right_basis(key, part):
    key = jax.random.fold_in(key, 22)
    return orthogonal_blocks(key, D // 4)


def draw_vectors(key, part):
    key = jax.random.fold_in(key, 31)
    gains = 1.0 + 0.15 * jax.random.uniform(jax.random.fold_in(key, 1), (2 * D,), jnp.float32, -1.0, 1.0)
    biases = 0.2 * jax.random.normal(jax.random.fold_in(key, 2), (6 * D + FF,), jnp.float32)
    return jnp.concatenate([gains, biases])


def levels(own_key, shape, cuts, least, high):
    level, own = 1.0, jax.random.fold_in(own_key, 6)
    for dim, shards_of in cuts:
        heights = jnp.exp(jax.random.uniform(jax.random.fold_in(own, dim), (shards_of,), jnp.float32, least / len(cuts), high / len(cuts)))
        level = level * jnp.repeat(heights, shape[dim] // shards_of).reshape([-1 if axis == dim else 1 for axis in range(len(shape))])
    return level


def normal_values(key, shape, scale, bound, cuts=(), kind=jnp.bfloat16):
    factor_of = levels(key, shape, cuts, -0.22, 0.18) if cuts else 1.0
    array = jax.random.normal(key, shape, jnp.float32) * scale * factor_of
    return jnp.minimum(jnp.maximum(array, -bound), bound).astype(kind)


def setup_inputs(seed: int = 0) -> dict:
    splits = jax.random.split(jax.random.key(seed), 18)
    tokens = normal_values(splits[0], (TOKENS, D), 1.0, 6.0, ((0, 32),))
    w_qkv = normal_values(splits[1], (3, D, D), D ** -0.5, 0.21875)
    w_attn_out = normal_values(splits[2], (D, D), (D // 16) ** -0.5, 0.875)
    w_in = normal_values(splits[3], (D, FF), D ** -0.5, 0.21875)
    w_out = normal_values(splits[4], (FF, D), FF ** -0.5, 0.109375)
    vectors = draw_vectors(jax.random.fold_in(splits[17], 71), 0)
    out_grad = normal_values(splits[6], (TOKENS, D), 1.0, 6.0, ((0, 32),))
    span_count = draw_span_count(jax.random.fold_in(splits[17], 71), 0)
    pair_index = draw_pair_index(jax.random.fold_in(splits[17], 71), 0)
    owner_list = jax.random.permutation(splits[9], NBLK).astype(jnp.int32)
    master = normal_values(splits[10], (NBLK, D, BW), D ** -0.5, 0.21875, ((0, 8),), jnp.float32)
    first_moment = normal_values(splits[11], (NBLK, D, BW), (0.055 * TOKENS ** 0.5), 56.0, ((0, 8),), jnp.float32)
    second_moment = jnp.clip(jnp.exp(math.log(24.576) - 1.3862944 * jax.random.uniform(splits[12], (NBLK, D, BW), jnp.float32) ** levels(splits[12], (NBLK, D, BW), ((0, 8),), -0.2, 0.2)), 6.144, 24.576)
    left_basis = draw_left_basis(jax.random.fold_in(splits[17], 71), 0)
    right_basis = draw_right_basis(jax.random.fold_in(splits[17], 71), 0)
    vec_first = normal_values(splits[15], (NVEC,), (0.11 * TOKENS ** 0.5), 112.0, (), jnp.float32)
    vec_second = jnp.clip(jnp.exp(jax.random.uniform(splits[16], (NVEC,), jnp.float32, math.log(24.576), math.log(98.304))), 24.576, 98.304)
    return {"tokens": tokens, "w_qkv": w_qkv, "w_attn_out": w_attn_out, "w_in": w_in, "w_out": w_out, "vectors": vectors, "out_grad": out_grad, "span_count": span_count, "pair_index": pair_index, "owner_list": owner_list, "master": master, "first_moment": first_moment, "second_moment": second_moment, "left_basis": left_basis, "right_basis": right_basis, "vec_first": vec_first, "vec_second": vec_second}


@jax.custom_vjp
def low(v):
    return lax.optimization_barrier(v.astype(jnp.bfloat16)).astype(jnp.float32)

@jax.custom_vjp
def low_back(v):
    return v

def low_keep(v):
    return (low(v), None)

def low_pass(kept, grad):
    return (grad,)

def back_keep(v):
    return (v, None)

def back_low(kept, grad):
    return (low(grad),)
low.defvjp(low_keep, low_pass)
low_back.defvjp(back_keep, back_low)
HIGH = lax.Precision.HIGHEST
RATE = 0.01
DECAY = 0.01
VECTOR_RATE = 0.3

def product(left_side, right_side):
    return jnp.dot(left_side, right_side, precision=HIGH)

def layer_norm(resid, gain, shift):
    average = lax.optimization_barrier(jnp.mean(resid, axis=-1, keepdims=True))
    centred = resid - average
    variance = lax.optimization_barrier(jnp.mean(centred * centred, axis=-1, keepdims=True))
    return centred * lax.rsqrt(variance + 1e-06) * gain + shift

def unpack(vectors):
    pieces = [vectors[index * D:(index + 1) * D] for index in range(8)]
    return pieces + [vectors[8 * D:]]

def layer(span_block, w_qkv, w_attn_out, w_in, w_out, vectors):
    gain_one, gain_two, shift_one, shift_two, bias_query, bias_value, bias_mixed, bias_outer, bias_inner = unpack(vectors)
    span_num = span_block.shape[0] // SPAN
    head_shape = (span_num, SPAN, HEADS, HEAD)
    queries = low(low_back(product(span_block, w_qkv[0])) + bias_query)
    key_rows = low(low_back(product(span_block, w_qkv[1])))
    value_rows = low(low_back(product(span_block, w_qkv[2])) + bias_value)
    scores = low_back(jnp.einsum('sqhd,skhd->shqk', queries.reshape(head_shape), key_rows.reshape(head_shape), precision=HIGH) * HEAD ** (-0.5))
    weights = low(jax.nn.softmax(scores, axis=-1))
    attended = jnp.einsum('shqk,skhd->sqhd', weights, value_rows.reshape(head_shape), precision=HIGH).reshape(span_block.shape)
    attended = low(low_back(attended))
    normed = layer_norm(span_block + low_back(product(attended, w_attn_out)) + bias_mixed, gain_one, shift_one)
    pre_act = low_back(product(low(normed), w_in)) + bias_inner
    hidden = low(jax.nn.gelu(pre_act, approximate=False))
    return layer_norm(normed + low_back(product(hidden, w_out)) + bias_outer, gain_two, shift_two)

def to_blocks(grad_project, grad_mixing, grad_inner, grad_outer):
    quarter = D // 4
    attention = jnp.concatenate([grad_project, grad_mixing[None]], axis=0)
    attention = attention.reshape(4, D, 4, quarter).transpose(0, 2, 1, 3).reshape(16, D, quarter)
    inner_part = grad_inner.reshape(D, FF // quarter, quarter).transpose(1, 0, 2)
    outer_part = grad_outer.reshape(FF // D, D, 4, quarter).transpose(0, 2, 1, 3).reshape(4 * (FF // D), D, quarter)
    return jnp.concatenate([attention, inner_part, outer_part], axis=0)

def rotated_adam(gradient, master, first_moment, second_moment, left_basis, right_basis):
    turned = jnp.einsum('kda,kdb->kab', left_basis, gradient, precision=HIGH)
    turned = jnp.einsum('kab,kbc->kac', turned, right_basis, precision=HIGH)
    new_first = 0.9 * first_moment + 0.1 * turned
    new_second = 0.999 * second_moment + 0.001 * turned * turned
    update = new_first / (1.0 - 0.9 ** STEP) / (jnp.sqrt(new_second / (1.0 - 0.999 ** STEP)) + 1e-08)
    update = jnp.einsum('kda,kab->kdb', left_basis, update, precision=HIGH)
    update = jnp.einsum('kdb,kcb->kdc', update, right_basis, precision=HIGH)
    new_master = master - RATE * (update + DECAY * master)
    return (new_master, new_first, new_second)

def reference(tokens, w_qkv, w_attn_out, w_in, w_out, vectors, out_grad, span_count, pair_index, owner_list, master, first_moment, second_moment, left_basis, right_basis, vec_first, vec_second):
    span_ids = jnp.arange(NSPAN, dtype=jnp.int32)
    live = span_ids % SLOTS < jnp.repeat(span_count, SLOTS)
    token_live = jnp.repeat(live.astype(jnp.float32), SPAN)[:, None]
    cotangent = out_grad.astype(jnp.float32) * token_live
    valid = live[None, :] & (span_ids[:, None] != span_ids[None, :])
    anchor = (live & (pair_index != span_ids)).astype(jnp.float32)
    partner = (pair_index[:, None] == span_ids[None, :]).astype(jnp.float32)
    groups = DEVICES // 4

    def objective(inputs, project, mixing, inner_w, outer_w, vector_all):

        def one_group(span_block):
            return layer(span_block, project, mixing, inner_w, outer_w, vector_all)
        stacked = inputs.reshape(groups, TOKENS // groups, D)
        layer_out = lax.map(jax.checkpoint(one_group), stacked).reshape(TOKENS, D) * token_live
        heads_cls = low(layer_out.reshape(NSPAN, SPAN, D)[:, 0])
        similar = low_back(product(heads_cls, heads_cls.T) * (2.0 * D ** (-0.5)))
        masked = jnp.where(valid, similar, -1e+30)
        highest = lax.optimization_barrier(jnp.max(masked, axis=1, keepdims=True))
        totals = lax.optimization_barrier(jnp.sum(jnp.where(valid, jnp.exp(masked - highest), 0.0), axis=1))
        lse = jnp.log(totals) + highest[:, 0]
        positive = lax.optimization_barrier(jnp.sum(partner * similar, axis=1))
        loss = jnp.sum(anchor * (lse - positive))
        return (jnp.sum(layer_out * cotangent) + loss, (layer_out, loss))
    floats = (tokens.astype(jnp.float32), w_qkv.astype(jnp.float32), w_attn_out.astype(jnp.float32), w_in.astype(jnp.float32), w_out.astype(jnp.float32), vectors)
    total_value, pullback, extras = jax.vjp(objective, *floats, has_aux=True)
    layer_out, loss = extras
    grads = pullback(jnp.ones((), jnp.float32))
    input_grad = grads[0]
    blocks = to_blocks(grads[1], grads[2], grads[3], grads[4])
    slot_grad = jnp.take(blocks, owner_list, axis=0)
    new_master, new_first, new_second = rotated_adam(slot_grad, master, first_moment, second_moment, left_basis, right_basis)
    grad_vec = grads[5]
    vec_first_new = 0.9 * vec_first + 0.1 * grad_vec
    vec_second_new = 0.999 * vec_second + 0.001 * grad_vec * grad_vec
    vec_step = vec_first_new / (1.0 - 0.9 ** STEP) / (jnp.sqrt(vec_second_new / (1.0 - 0.999 ** STEP)) + 1e-08)
    vec_new = vectors - VECTOR_RATE * vec_step
    return (layer_out.astype(jnp.bfloat16), input_grad, loss, new_master, new_first, new_second, new_master.astype(jnp.bfloat16), vec_new, vec_first_new, vec_second_new)
```

```python
from functools import partial

import jax
import jax.numpy as jnp
from jax import lax
from jax.sharding import PartitionSpec as P

D = 768
HEADS = 12
HEAD = 64
FF = 3072
SPAN = 128
STEP = 10


RATE = 0.01
DECAY = 0.01
VECTOR_RATE = 0.3


def layer_norm(resid, gain, shift):
    average = jnp.mean(resid, axis=-1, keepdims=True)
    centred = resid - average
    variance = jnp.mean(centred * centred, axis=-1, keepdims=True)
    inverse = lax.rsqrt(variance + 1e-06)
    unit_rows = centred * inverse
    return (unit_rows * gain + shift, unit_rows, inverse)


def norm_backward(grad_out, unit_rows, inverse, gain):
    grad_gain = jnp.sum(grad_out * unit_rows, axis=0)
    grad_shift = jnp.sum(grad_out, axis=0)
    scaled_grad = grad_out * gain
    grad_resid = inverse * (
        scaled_grad
        - jnp.mean(scaled_grad, axis=-1, keepdims=True)
        - unit_rows * jnp.mean(scaled_grad * unit_rows, axis=-1, keepdims=True)
    )
    return (grad_resid, grad_gain, grad_shift)


def unpack(vectors):
    pieces = [vectors[index * D : (index + 1) * D] for index in range(8)]
    return pieces + [vectors[8 * D :]]


def encode(tokens, w_qkv, w_attn_out, w_in, w_out, vectors):
    (
        gain_one,
        gain_two,
        shift_one,
        shift_two,
        bias_query,
        bias_value,
        bias_mixed,
        bias_outer,
        bias_inner,
    ) = unpack(vectors)
    rows_total = tokens.shape[0]
    head_shape = (rows_total // SPAN, SPAN, HEADS, HEAD)
    scaling = HEAD ** (-0.5)
    projected = jnp.einsum("td,kde->kte", tokens, w_qkv, preferred_element_type=jnp.float32)
    queries = (projected[0] + bias_query).astype(jnp.bfloat16).reshape(head_shape)
    key_rows = projected[1].astype(jnp.bfloat16).reshape(head_shape)
    value_rows = (projected[2] + bias_value).astype(jnp.bfloat16).reshape(head_shape)
    scores = (
        jnp.einsum("sqhd,skhd->shqk", queries, key_rows, preferred_element_type=jnp.float32)
        * scaling
    )
    weights = jax.nn.softmax(scores, axis=-1)
    weights_low = weights.astype(jnp.bfloat16)
    attended = jnp.einsum(
        "shqk,skhd->sqhd", weights_low, value_rows, preferred_element_type=jnp.float32
    )
    attended = attended.reshape(rows_total, D).astype(jnp.bfloat16)
    mixed_out = jnp.dot(attended, w_attn_out, preferred_element_type=jnp.float32) + bias_mixed
    normed, unit_one, inverse_one = layer_norm(
        tokens.astype(jnp.float32) + mixed_out, gain_one, shift_one
    )
    normed_low = normed.astype(jnp.bfloat16)
    pre_act = jnp.dot(normed_low, w_in, preferred_element_type=jnp.float32) + bias_inner
    hidden = jax.nn.gelu(pre_act, approximate=False).astype(jnp.bfloat16)
    outer_out = jnp.dot(hidden, w_out, preferred_element_type=jnp.float32) + bias_outer
    result, unit_two, inverse_two = layer_norm(normed + outer_out, gain_two, shift_two)
    saved = (
        queries,
        key_rows,
        value_rows,
        weights,
        weights_low,
        attended,
        unit_one,
        inverse_one,
        normed_low,
        pre_act,
        hidden,
        unit_two,
        inverse_two,
    )
    return (result, saved)


def backward(saved, grad_y, tokens, w_qkv, w_attn_out, w_in, w_out, vectors):
    (
        queries,
        key_rows,
        value_rows,
        weights,
        weights_low,
        attended,
        unit_one,
        inverse_one,
        normed_low,
        pre_act,
        hidden,
        unit_two,
        inverse_two,
    ) = saved
    gain_one = vectors[0:D]
    gain_two = vectors[D : 2 * D]
    rows_total = tokens.shape[0]
    head_shape = (rows_total // SPAN, SPAN, HEADS, HEAD)
    scaling = HEAD ** (-0.5)
    grad_two, grad_gain_two, grad_shift_two = norm_backward(grad_y, unit_two, inverse_two, gain_two)
    outer_low = grad_two.astype(jnp.bfloat16)
    grad_bias_outer = jnp.sum(grad_two, axis=0)
    grad_w_out = jnp.einsum("tf,td->fd", hidden, outer_low, preferred_element_type=jnp.float32)
    grad_hidden = jnp.einsum("td,fd->tf", outer_low, w_out, preferred_element_type=jnp.float32)
    gelu_pull = jax.vjp(partial(jax.nn.gelu, approximate=False), pre_act)[1]
    grad_pre = gelu_pull(grad_hidden)[0]
    grad_bias_inner = jnp.sum(grad_pre, axis=0)
    pre_low = grad_pre.astype(jnp.bfloat16)
    grad_w_in = jnp.einsum("td,tf->df", normed_low, pre_low, preferred_element_type=jnp.float32)
    grad_normed = grad_two + jnp.einsum(
        "tf,df->td", pre_low, w_in, preferred_element_type=jnp.float32
    )
    grad_one, grad_gain_one, grad_shift_one = norm_backward(
        grad_normed, unit_one, inverse_one, gain_one
    )
    grad_bias_mixed = jnp.sum(grad_one, axis=0)
    mixed_low = grad_one.astype(jnp.bfloat16)
    grad_w_mixing = jnp.einsum("td,te->de", attended, mixed_low, preferred_element_type=jnp.float32)
    grad_attended = jnp.einsum(
        "te,de->td", mixed_low, w_attn_out, preferred_element_type=jnp.float32
    )
    grad_attended = grad_attended.astype(jnp.bfloat16).reshape(head_shape)
    grad_values = jnp.einsum(
        "shqk,sqhd->skhd", weights_low, grad_attended, preferred_element_type=jnp.float32
    )
    grad_weights = jnp.einsum(
        "sqhd,skhd->shqk", grad_attended, value_rows, preferred_element_type=jnp.float32
    )
    grad_scores = weights * (grad_weights - jnp.sum(grad_weights * weights, axis=-1, keepdims=True))
    grad_scores = grad_scores.astype(jnp.bfloat16)
    grad_queries = (
        jnp.einsum("shqk,skhd->sqhd", grad_scores, key_rows, preferred_element_type=jnp.float32)
        * scaling
    )
    grad_keys = (
        jnp.einsum("shqk,sqhd->skhd", grad_scores, queries, preferred_element_type=jnp.float32)
        * scaling
    )
    grad_stack = jnp.stack([grad_queries, grad_keys, grad_values]).reshape(3, rows_total, D)
    grad_bias_query = jnp.sum(grad_stack[0], axis=0)
    grad_bias_value = jnp.sum(grad_stack[2], axis=0)
    stack_low = grad_stack.astype(jnp.bfloat16)
    grad_project = jnp.einsum("td,kte->kde", tokens, stack_low, preferred_element_type=jnp.float32)
    grad_tokens = grad_one + jnp.einsum(
        "kte,kde->td", stack_low, w_qkv, preferred_element_type=jnp.float32
    )
    grad_vector = jnp.concatenate(
        [
            grad_gain_one,
            grad_gain_two,
            grad_shift_one,
            grad_shift_two,
            grad_bias_query,
            grad_bias_value,
            grad_bias_mixed,
            grad_bias_outer,
            grad_bias_inner,
        ]
    )
    return (grad_tokens, grad_project, grad_w_mixing, grad_w_in, grad_w_out, grad_vector)


def axis_bits(name):
    size = lax.axis_size(name)
    return [(name, 1 << k) for k in range(size.bit_length() - 1)]


def bit_of(step):
    return jnp.where((lax.axis_index(step[0]) & step[1]) != 0, 1, 0)


def swap(send, step):
    size = lax.axis_size(step[0])
    return lax.ppermute(send, step[0], [(i, i ^ step[1]) for i in range(size)])


def pick(array, index, dim):
    return lax.dynamic_index_in_dim(array, index, dim, False)


def ordered(own, other, bit):
    first = jnp.where(bit == 0, own, other)
    second = jnp.where(bit == 0, other, own)
    return jnp.stack([first, second])


def gather_all(rows):
    shape = rows.shape
    for step in axis_bits("col") + axis_bits("row"):
        pair = ordered(rows, swap(rows, step), bit_of(step))
        rows = pair.reshape((-1,) + shape[1:])
    return rows


def row_steps():
    row_bits, col_bits = axis_bits("row"), axis_bits("col")
    core, across = row_bits[:1], row_bits[1:][::-1]
    y_bits, z_bits = col_bits[:-2][::-1], col_bits[-2:]
    return core, across, y_bits, z_bits


def reduce_panels(panels, order):
    core, across, y_bits, z_bits = row_steps()
    left = core + across + y_bits + z_bits
    width = panels.shape[1] >> len(left)
    part = panels.reshape((panels.shape[0],) + (2,) * len(left) + (width, panels.shape[2]))
    for step in order:
        dim = 1 + left.index(step)
        bit = bit_of(step)
        other = swap(pick(part, 1 - bit, dim), step)
        part = pick(part, bit, dim).astype(jnp.float32) + other.astype(jnp.float32)
        left = left[: dim - 1] + left[dim:]
        if left:
            part = part.astype(jnp.bfloat16)
    return part


def to_slots(shares, owner_list):
    quarter = D // 4
    panels, rows, _ = shares.shape
    blocks = shares.reshape(panels, rows, 4, quarter).transpose(0, 2, 1, 3)
    blocks = blocks.reshape(panels * 4, rows, quarter)
    slots = jnp.take(blocks, owner_list, axis=0)
    cols = lax.axis_size("col")
    flat = slots.reshape(cols, slots.shape[0] // cols * rows, quarter)
    half = flat.shape[1] // 2
    return jnp.concatenate([flat[:, :half], flat[:, half:]], axis=-1)


def spread(slots):
    core, across, y_bits, z_bits = row_steps()
    part = slots.reshape((2,) * len(axis_bits("col")) + slots.shape[1:])
    left = axis_bits("col")[::-1]
    gathered = 0
    tail = slots.shape[1:]
    for step in (y_bits + z_bits)[::-1]:
        dim = gathered + left.index(step)
        bit = bit_of(step)
        other = swap(pick(part, 1 - bit, dim), step)
        part = ordered(pick(part, bit, dim), other, bit)
        left.remove(step)
        gathered += 1
    part = part.reshape((-1,) + tail)
    for step in (core + across)[::-1]:
        part = ordered(part, swap(part, step), bit_of(step)).reshape((-1,) + tail)
    return part


def to_owned(gathered, per_owner):
    quarter = D // 4
    flat = jnp.concatenate([gathered[..., :quarter], gathered[..., quarter:]], axis=1)
    rows = flat.shape[1] // per_owner
    flat = flat.reshape(flat.shape[0], per_owner, rows, quarter).transpose(1, 0, 2, 3)
    return flat.reshape(per_owner, D, quarter)


def rotated_adam(gradient, master, first_moment, second_moment, left_basis, right_basis):
    low = jnp.bfloat16
    dot = partial(jnp.einsum, preferred_element_type=jnp.float32)
    left, right = left_basis.astype(low), right_basis.astype(low)
    turned = dot("kda,kdb->kab", left, gradient.astype(low))
    turned = dot("kab,kbc->kac", turned.astype(low), right)
    new_first = 0.9 * first_moment + 0.1 * turned
    new_second = 0.999 * second_moment + 0.001 * turned * turned
    update = new_first / (1.0 - 0.9**STEP) / (jnp.sqrt(new_second / (1.0 - 0.999**STEP)) + 1e-08)
    update = dot("kda,kab->kdb", left, update.astype(low))
    update = dot("kdb,kcb->kdc", update.astype(low), right)
    new_master = master - RATE * (update + DECAY * master)
    return (new_master, new_first, new_second)


def contrast(cls_rows, span_count, pair_index, device, slots):
    total_spans = pair_index.shape[0]
    span_ids = jnp.arange(total_spans, dtype=jnp.int32)
    live = span_ids % slots < jnp.repeat(span_count, slots)
    scale = 2.0 * D ** (-0.5)
    valid = live[None, :] & (span_ids[:, None] != span_ids[None, :])
    matched = (pair_index[:, None] == span_ids[None, :]).astype(jnp.float32)
    anchor = (live & (pair_index != span_ids)).astype(jnp.float32)
    similar = jnp.einsum("rd,cd->rc", cls_rows, cls_rows, preferred_element_type=jnp.float32) * scale
    masked = jnp.where(valid, similar, -1e30)
    peak = jnp.max(masked, axis=1)
    total = jnp.sum(jnp.where(valid, jnp.exp(masked - peak[:, None]), 0.0), axis=1)
    log_total = jnp.log(total) + peak
    loss = jnp.sum(anchor * (log_total - jnp.sum(matched * similar, axis=1)))
    grad_similar = anchor[:, None] * (
        jnp.where(valid, jnp.exp(masked - log_total[:, None]), 0.0) - matched
    )
    grad_similar = grad_similar.astype(jnp.bfloat16)
    own_rows = lax.dynamic_slice_in_dim(grad_similar, device * slots, slots, axis=0)
    own_cols = lax.dynamic_slice_in_dim(grad_similar, device * slots, slots, axis=1)
    grad_cls = jnp.einsum("rc,cd->rd", own_rows, cls_rows, preferred_element_type=jnp.float32)
    grad_cls += jnp.einsum("cr,cd->rd", own_cols, cls_rows, preferred_element_type=jnp.float32)
    return loss, grad_cls * scale


def shards(
    tokens,
    w_qkv,
    w_attn_out,
    w_in,
    w_out,
    vectors,
    out_grad,
    span_count,
    pair_index,
    owner_list,
    master,
    first_moment,
    second_moment,
    left_basis,
    right_basis,
    vec_first,
    vec_second,
):
    slots = tokens.shape[0] // SPAN
    device = lax.axis_index("row") * lax.axis_size("col") + lax.axis_index("col")
    own_count = lax.dynamic_index_in_dim(span_count, device, 0, False)
    own_live = (jnp.arange(slots) < own_count).astype(jnp.float32)
    token_live = jnp.repeat(own_live, SPAN)[:, None]
    result, saved = encode(tokens, w_qkv, w_attn_out, w_in, w_out, vectors)
    layer_out = result * token_live
    cls_rows = layer_out.reshape(slots, SPAN, D)[:, 0].astype(jnp.bfloat16)
    loss, grad_cls = contrast(gather_all(cls_rows), span_count, pair_index, device, slots)
    grad_y = (
        out_grad.astype(jnp.float32)
        .reshape(slots, SPAN, D)
        .at[:, 0]
        .add(grad_cls)
        .reshape(slots * SPAN, D)
        * token_live
    )
    grad_tokens, grad_project, grad_mixing, grad_inner, grad_outer, grad_vector = backward(
        saved, grad_y, tokens, w_qkv, w_attn_out, w_in, w_out, vectors
    )
    low = jnp.bfloat16
    core, across, y_bits, z_bits = row_steps()
    orders = (core + across + y_bits + z_bits, core + y_bits + across + z_bits[::-1])
    groups = (
        grad_outer.astype(low).reshape(FF // D, D, D),
        grad_inner.astype(low).reshape(D, FF // D, D).transpose(1, 0, 2),
        jnp.concatenate([grad_project.astype(low), grad_mixing.astype(low)[None]]),
    )
    sums = []
    for group in groups:
        half = group.shape[0] // 2
        sums.append([reduce_panels(group[:half], orders[0]), reduce_panels(group[half:], orders[1])])
    shares = jnp.concatenate(sums[2] + sums[1] + sums[0])
    owned = to_owned(spread(to_slots(shares.astype(low), owner_list)), master.shape[0])
    vec_grad = grad_vector.reshape(-1, 128)
    for step in core + across + y_bits + z_bits:
        vec_grad += swap(vec_grad, step)
    vec_grad = vec_grad.reshape(-1)
    new_master, new_first, new_second = rotated_adam(
        owned, master, first_moment, second_moment, left_basis, right_basis
    )
    vec_first_new = 0.9 * vec_first + 0.1 * vec_grad
    vec_second_new = 0.999 * vec_second + 0.001 * vec_grad * vec_grad
    vec_step = (
        vec_first_new / (1.0 - 0.9**STEP) / (jnp.sqrt(vec_second_new / (1.0 - 0.999**STEP)) + 1e-08)
    )
    vec_new = vectors - VECTOR_RATE * vec_step
    return (
        layer_out.astype(jnp.bfloat16),
        grad_tokens,
        loss,
        new_master,
        new_first,
        new_second,
        new_master.astype(jnp.bfloat16),
        vec_new,
        vec_first_new,
        vec_second_new,
    )


def solution(mesh):
    in_specs = (
        P(("row", "col"), None),
        P(),
        P(),
        P(),
        P(),
        P(),
        P(("row", "col"), None),
        P(),
        P(),
        P(),
        P("col", None, None),
        P("col", None, None),
        P("col", None, None),
        P("col", None, None),
        P("col", None, None),
        P(),
        P(),
    )
    out_specs = (
        P(("row", "col"), None),
        P(("row", "col"), None),
        P(),
        P("col", None, None),
        P("col", None, None),
        P("col", None, None),
        P("col", None, None),
        P(),
        P(),
        P(),
    )
    return jax.shard_map(shards, mesh=mesh, in_specs=in_specs, out_specs=out_specs, check_vma=False)
```

```python
from functools import partial

import jax
import jax.numpy as jnp
from jax import lax
from jax.experimental import pallas as pl
from jax.experimental.pallas import tpu as pltpu
from jax.sharding import PartitionSpec as P

D = 768
HEADS = 12
HEAD = 64
FF = 3072
SPAN = 128
STEP = 10
GROUP = 8

RATE = 0.01
DECAY = 0.01
VECTOR_RATE = 0.3

LOW = jnp.bfloat16
F32 = jnp.float32
TALL = 2 * SPAN
VMEM_LIMIT = 56 * 1024 * 1024


def dot(left_side, right_side, contract=(1, 0)):
    dims = (((contract[0],), (contract[1],)), ((), ()))
    return lax.dot_general(left_side, right_side, dims, preferred_element_type=F32)


def whole(shape):
    return pl.BlockSpec(shape, lambda *ids: (0,) * len(shape))


def params():
    return pltpu.CompilerParams(vmem_limit_bytes=VMEM_LIMIT)


def split_heads(pair):
    lane = lax.broadcasted_iota(jnp.int32, pair.shape, 1)
    zero = jnp.zeros_like(pair)
    return jnp.concatenate([jnp.where(lane < HEAD, pair, zero), jnp.where(lane < HEAD, zero, pair)])


def normalise(scores):
    peak = jnp.max(scores, axis=-1, keepdims=True)
    raised = jnp.exp(scores - peak)
    return raised * (1.0 / jnp.sum(raised, axis=-1, keepdims=True))


def attend_kernel(tokens, w_qkv, rows, q_out, k_out, v_out, p_out, a_out):
    block = tokens[...]
    scaling = HEAD ** (-0.5)
    q_out[...] = ((dot(block, w_qkv[0]) + rows[4:5]).astype(LOW) * scaling).astype(LOW)
    k_out[...] = dot(block, w_qkv[1]).astype(LOW)
    v_out[...] = (dot(block, w_qkv[2]) + rows[5:6]).astype(LOW)
    for span in range(TALL // SPAN):
        at = slice(span * SPAN, (span + 1) * SPAN)
        for pair in range(HEADS // 2):
            lanes = slice(pair * 2 * HEAD, (pair + 1) * 2 * HEAD)
            scores = dot(q_out[at, lanes], split_heads(k_out[at, lanes]), (1, 1))
            weights = jnp.concatenate(
                [normalise(scores[:, :SPAN]), normalise(scores[:, SPAN:])], axis=1
            ).astype(LOW)
            p_out[span, pair] = weights
            a_out[at, lanes] = dot(weights, split_heads(v_out[at, lanes])).astype(LOW)


def attend(tokens, w_qkv, rows):
    total = tokens.shape[0]
    tall = pl.BlockSpec((TALL, D), lambda i: (i, 0))
    like = jax.ShapeDtypeStruct((total, D), LOW)
    spans = TALL // SPAN
    return pl.pallas_call(
        attend_kernel,
        grid=(total // TALL,),
        in_specs=[tall, whole(w_qkv.shape), whole(rows.shape)],
        out_specs=[
            tall,
            tall,
            tall,
            pl.BlockSpec((spans, HEADS // 2, SPAN, 2 * SPAN), lambda i: (i, 0, 0, 0)),
            tall,
        ],
        out_shape=[
            like,
            like,
            like,
            jax.ShapeDtypeStruct((total // SPAN, HEADS // 2, SPAN, 2 * SPAN), LOW),
            like,
        ],
        compiler_params=params(),
        cost_estimate=pl.CostEstimate(
            flops=2 * total * D * (3 * D + 2 * SPAN),
            bytes_accessed=14 * total * D + 6 * D * D,
            transcendentals=total * HEADS * SPAN,
        ),
        name="attend",
    )(tokens, w_qkv, rows)


def unit_norm(resid):
    centred = resid - jnp.mean(resid, axis=-1, keepdims=True)
    inverse = lax.rsqrt(jnp.mean(centred * centred, axis=-1, keepdims=True) + 1e-06)
    return centred * inverse, inverse


def gelu_pair(x):
    z = jnp.abs(x) * 0.7071067811865476
    base = 1.0 + 0.3275911 * z
    t = pltpu.reciprocal(base, approx=True)
    t = t * (2.0 - base * t)
    poly = 0.5 * 1.061405429
    for term in (-1.453152027, 1.421413741, -0.284496736, 0.254829592):
        poly = poly * t + 0.5 * term
    gauss = jnp.exp(-(z * z))
    tail = poly * t * gauss
    cdf = jnp.where(x < 0, tail, 1.0 - tail)
    return x * cdf, cdf + x * gauss * 0.3989422804014327


def feed_kernel(
    tokens, attended, live, w_attn, w_in, w_out, rows,
    enc_out, hid_out, slope_out, norm_out, u1_out, i1_out, u2_out, i2_out,
):
    resid = tokens[...].astype(F32) + dot(attended[...], w_attn[...]) + rows[6:7]
    unit_one, inverse_one = unit_norm(resid)
    normed = unit_one * rows[0:1] + rows[2:3]
    u1_out[...] = unit_one.astype(LOW)
    i1_out[...] = inverse_one
    norm_out[...] = normed.astype(LOW)
    step = 256
    for at in range(0, FF, step):
        bias = rows[8 + at // D : 9 + at // D, at % D : at % D + step]
        pre_act = dot(norm_out[...], w_in[:, at : at + step]) + bias
        hidden, slope = gelu_pair(pre_act)
        hid_out[:, at : at + step] = hidden.astype(LOW)
        slope_out[:, at : at + step] = slope.astype(LOW)
    resid = normed + dot(hid_out[...], w_out[...]) + rows[7:8]
    unit_two, inverse_two = unit_norm(resid)
    u2_out[...] = unit_two.astype(LOW)
    i2_out[...] = inverse_two
    enc_out[...] = (live[...] * (unit_two * rows[1:2] + rows[3:4])).astype(LOW)


def feed(tokens, attended, live, w_attn, w_in, w_out, rows):
    total = tokens.shape[0]
    tall = lambda width: pl.BlockSpec((TALL, width), lambda i: (i, 0))
    like = lambda width, kind: jax.ShapeDtypeStruct((total, width), kind)
    return pl.pallas_call(
        feed_kernel,
        grid=(total // TALL,),
        in_specs=[tall(D), tall(D), tall(1)] + [whole(a.shape) for a in (w_attn, w_in, w_out, rows)],
        out_specs=[tall(D), tall(FF), tall(FF), tall(D), tall(D), tall(1), tall(D), tall(1)],
        out_shape=[
            like(D, LOW), like(FF, LOW), like(FF, LOW), like(D, LOW),
            like(D, LOW), like(1, F32), like(D, LOW), like(1, F32),
        ],
        compiler_params=params(),
        cost_estimate=pl.CostEstimate(
            flops=2 * total * D * (D + 2 * FF),
            bytes_accessed=total * (12 * D + 4 * FF) + 4 * D * FF,
            transcendentals=total * FF * 2,
        ),
        name="feed",
    )(tokens, attended, live, w_attn, w_in, w_out, rows)


def norm_back(grad_out, unit_rows, inverse, gain):
    scaled = grad_out * gain
    along = jnp.mean(scaled * unit_rows, axis=-1, keepdims=True)
    return inverse * (scaled - jnp.mean(scaled, axis=-1, keepdims=True) - unit_rows * along)


def column_sums(*arrays):
    return [jnp.sum(a, axis=0, keepdims=True) for a in arrays]


def outer_kernel(out_grad, grad_cls, live, unit_two, inverse_two, rows, two_out, low_out, vec_out):
    spot = lax.broadcasted_iota(jnp.int32, (SPAN, 1), 0) == 0
    sums = None
    for span in range(out_grad.shape[0] // SPAN):
        at = slice(span * SPAN, (span + 1) * SPAN)
        added = jnp.where(spot, grad_cls[span : span + 1], 0.0)
        grad_y = live[at] * (out_grad[at].astype(F32) + added)
        unit_rows = unit_two[at].astype(F32)
        grad_two = norm_back(grad_y, unit_rows, inverse_two[at], rows[1:2])
        two_out[at] = grad_two
        low_out[at] = grad_two.astype(LOW)
        here = column_sums(grad_y * unit_rows, grad_y, grad_two)
        sums = here if sums is None else [a + b for a, b in zip(sums, here)]
    for index, total in enumerate(sums):
        vec_out[index : index + 1] = total


def outer_grad(out_grad, grad_cls, live, unit_two, inverse_two, rows):
    total = out_grad.shape[0]
    return pl.pallas_call(
        outer_kernel,
        out_shape=[
            jax.ShapeDtypeStruct((total, D), F32),
            jax.ShapeDtypeStruct((total, D), LOW),
            jax.ShapeDtypeStruct((3, D), F32),
        ],
        compiler_params=params(),
        cost_estimate=pl.CostEstimate(
            flops=20 * total * D, bytes_accessed=10 * total * D, transcendentals=0
        ),
        name="outer",
    )(out_grad, grad_cls, live, unit_two, inverse_two, rows)


def weight_kernel(panels, bit, left_side, right_side, *rest):
    extra_left, extra_right = rest[:-2] or (None, None)
    send_out, keep_out = rest[-2:]

    def store(left_from, right_from):
        value = dot(left_from[...], right_from[...], (0, 0)).astype(LOW)

        @pl.when(pl.program_id(0) == 0)
        def _():
            send_out[0] = value

        @pl.when(pl.program_id(0) == 1)
        def _():
            keep_out[0] = value

    if extra_left is None:
        store(left_side, right_side)
        return

    @pl.when(pl.program_id(1) < panels)
    def _():
        store(left_side, right_side)

    @pl.when(pl.program_id(1) == panels)
    def _():
        store(extra_left, extra_right)


def weight_grad(bit, left_side, right_side, panels, banded, extra=()):
    total = left_side.shape[0]
    half = D // 2
    every = panels + len(extra) // 2

    def side_of(phase, bit):
        return jnp.where(phase == 0, 1 - bit[0], bit[0])

    def left_at(phase, panel, bit):
        side = side_of(phase, bit)
        return (0, jnp.minimum(panel, panels - 1) * 2 + side if banded else side)

    def right_at(phase, panel, bit):
        return (0, 0 if banded else jnp.minimum(panel, panels - 1))

    like = jax.ShapeDtypeStruct((every, half, D), LOW)
    tall = lambda width, at: pl.BlockSpec((total, width), at)
    more = [tall(half, lambda f, p, b: (0, side_of(f, b))), tall(D, lambda f, p, b: (0, 0))]
    return pl.pallas_call(
        partial(weight_kernel, panels),
        grid_spec=pltpu.PrefetchScalarGridSpec(
            num_scalar_prefetch=1,
            grid=(2, every),
            in_specs=[tall(half, left_at), tall(D, right_at)] + more[: len(extra)],
            out_specs=[
                pl.BlockSpec((1, half, D), lambda f, p, b: (jnp.where(f == 0, p, every - 1), 0, 0)),
                pl.BlockSpec((1, half, D), lambda f, p, b: (jnp.where(f == 0, 0, p), 0, 0)),
            ],
        ),
        out_shape=[like, like],
        compiler_params=params(),
        cost_estimate=pl.CostEstimate(
            flops=2 * total * D * D * every,
            bytes_accessed=2 * (total + D) * D * every,
            transcendentals=0,
        ),
        name="weight",
    )(bit.reshape(1), left_side, right_side, *extra)


def inner_kernel(
    low, grad_two, slope, unit_one, inverse_one, w_attn, w_in, w_out, rows,
    pre_out, one_out, mixed_out, ga_out, vec_out,
):
    first = pl.program_id(0) == 0

    @pl.when(first)
    def _():
        vec_out[...] = jnp.zeros_like(vec_out)

    step = 256
    for at in range(0, FF, step):
        grad_pre = dot(low[...], w_out[at : at + step], (1, 1)) * slope[:, at : at + step].astype(F32)
        pre_out[:, at : at + step] = grad_pre.astype(LOW)
        spot = (slice(3 + at // D, 4 + at // D), slice(at % D, at % D + step))
        vec_out[spot] += jnp.sum(grad_pre, axis=0, keepdims=True)
    grad_normed = grad_two[...] + dot(pre_out[...], w_in[...], (1, 1))
    unit_rows = unit_one[...].astype(F32)
    grad_one = norm_back(grad_normed, unit_rows, inverse_one[...], rows[0:1])
    one_out[...] = grad_one
    mixed = grad_one.astype(LOW)
    mixed_out[...] = mixed
    ga_out[...] = dot(mixed, w_attn[...], (1, 1)).astype(LOW)
    for index, total in enumerate(column_sums(grad_normed * unit_rows, grad_normed, grad_one)):
        vec_out[index : index + 1] += total


def inner_grad(low, grad_two, slope, unit_one, inverse_one, w_attn, w_in, w_out, rows):
    total = low.shape[0]
    tall = lambda width: pl.BlockSpec((TALL, width), lambda i: (i, 0))
    like = lambda width, kind: jax.ShapeDtypeStruct((total, width), kind)
    return pl.pallas_call(
        inner_kernel,
        grid=(total // TALL,),
        in_specs=[tall(D), tall(D), tall(FF), tall(D), tall(1)]
        + [whole(a.shape) for a in (w_attn, w_in, w_out, rows)],
        out_specs=[tall(FF), tall(D), tall(D), tall(D), whole((7, D))],
        out_shape=[
            like(FF, LOW), like(D, F32), like(D, LOW), like(D, LOW),
            jax.ShapeDtypeStruct((7, D), F32),
        ],
        compiler_params=params(),
        cost_estimate=pl.CostEstimate(
            flops=2 * total * D * (D + 2 * FF),
            bytes_accessed=total * (14 * D + 4 * FF) + 4 * D * FF,
            transcendentals=0,
        ),
        name="inner",
    )(low, grad_two, slope, unit_one, inverse_one, w_attn, w_in, w_out, rows)


def unattend_kernel(q, k, v, p, ga, stack_out, vec_out):
    scaling = HEAD ** (-0.5)
    first = pl.program_id(0) == 0

    @pl.when(first)
    def _():
        vec_out[...] = jnp.zeros_like(vec_out)

    lane = lax.broadcasted_iota(jnp.int32, (SPAN, 2 * HEAD), 1)
    for span in range(TALL // SPAN):
        at = slice(span * SPAN, (span + 1) * SPAN)
        for pair in range(HEADS // 2):
            lo = pair * 2 * HEAD
            lanes = slice(lo, lo + 2 * HEAD)
            weights = p[span, pair]
            grad = ga[at, lanes]
            spread_out = dot(grad, split_heads(v[at, lanes]), (1, 1))
            wide = weights.astype(F32)
            parts = []
            for half in range(2):
                cols = slice(half * SPAN, (half + 1) * SPAN)
                wgt, gw = wide[:, cols], spread_out[:, cols]
                parts.append((wgt * (gw - jnp.sum(gw * wgt, axis=-1, keepdims=True))).astype(LOW))
            grad_scores = jnp.concatenate(parts, axis=1)
            grad_q = dot(grad_scores, split_heads(k[at, lanes])) * scaling
            tall_scores = jnp.concatenate(parts, axis=0)
            tall_weights = jnp.concatenate([weights[:, :SPAN], weights[:, SPAN:]], axis=0)
            grad_k = dot(tall_scores, split_heads(q[at, lanes]), (0, 0))
            grad_v = dot(tall_weights, split_heads(grad), (0, 0))
            stack_out[at, lo : lo + 2 * HEAD] = grad_q.astype(LOW)
            stack_out[at, D + lo : D + lo + 2 * HEAD] = grad_k.astype(LOW)
            stack_out[at, 2 * D + lo : 2 * D + lo + 2 * HEAD] = grad_v.astype(LOW)
            vec_out[0:1, lanes] += jnp.sum(grad_q, axis=0, keepdims=True)
            vec_out[1:2, lanes] += jnp.sum(grad_v, axis=0, keepdims=True)


def unattend(q, k, v, p, ga):
    total = q.shape[0]
    spans = TALL // SPAN
    tall = lambda width: pl.BlockSpec((TALL, width), lambda i: (i, 0))
    return pl.pallas_call(
        unattend_kernel,
        grid=(total // TALL,),
        in_specs=[
            tall(D),
            tall(D),
            tall(D),
            pl.BlockSpec((spans, HEADS // 2, SPAN, 2 * SPAN), lambda i: (i, 0, 0, 0)),
            tall(D),
        ],
        out_specs=[tall(3 * D), whole((2, D))],
        out_shape=[jax.ShapeDtypeStruct((total, 3 * D), LOW), jax.ShapeDtypeStruct((2, D), F32)],
        compiler_params=params(),
        cost_estimate=pl.CostEstimate(
            flops=2 * total * D * 4 * SPAN, bytes_accessed=20 * total * D, transcendentals=0
        ),
        name="unattend",
    )(q, k, v, p, ga)


def contrast_kernel(slots, place, rows, counts, partners, loss_out, grad_out):
    total, scale = rows.shape[0], 2.0 * D ** (-0.5)

    def number(shape, axis):
        at = lax.broadcasted_iota(jnp.int32, shape, axis)
        return (at // GROUP) ^ place[0], at % GROUP

    device, slot = number((counts.shape[1], total), 1)
    hit = lax.broadcasted_iota(jnp.int32, device.shape, 0) == device
    count = dot(counts[...].astype(LOW), jnp.where(hit, 1.0, 0.0).astype(LOW))
    live_across = (slot[:1].astype(F32) < count) & (slot[:1] < slots)
    device, slot = number((total, counts.shape[1]), 0)
    hit = lax.broadcasted_iota(jnp.int32, device.shape, 1) == device
    count = jnp.sum(jnp.where(hit, counts[...], 0.0), axis=1, keepdims=True)
    live_down = (slot[:, :1].astype(F32) < count) & (slot[:, :1] < slots)
    device, slot = number((total, partners.shape[1]), 0)
    own_id = device * slots + slot
    hit = lax.broadcasted_iota(jnp.int32, own_id.shape, 1) == own_id
    pair = jnp.sum(jnp.where(hit, partners[...], 0.0), axis=1, keepdims=True)
    device, slot = number((total, total), 0)
    down = (device * slots + slot).astype(F32)
    device, slot = number((total, total), 1)
    across = (device * slots + slot).astype(F32)
    valid = live_across & (down != across)
    matched = jnp.where((slot < slots) & (pair == across), 1.0, 0.0)
    anchor = jnp.where(live_down & (pair != down[:, :1]), 1.0, 0.0)
    similar = dot(rows[...], rows[...], (1, 1)) * scale
    masked = jnp.where(valid, similar, -1e30)
    peak = jnp.max(masked, axis=1, keepdims=True)
    summed = jnp.sum(jnp.where(valid, jnp.exp(masked - peak), 0.0), axis=1, keepdims=True)
    log_total = jnp.log(summed) + peak
    positive = jnp.sum(matched * similar, axis=1, keepdims=True)
    loss_out[...] = jnp.sum(anchor * (log_total - positive), axis=0, keepdims=True)
    grad = (anchor * (jnp.where(valid, jnp.exp(masked - log_total), 0.0) - matched)).astype(LOW)
    own = lax.broadcasted_iota(jnp.int32, (GROUP, total), 0)
    own = jnp.where(own == lax.broadcasted_iota(jnp.int32, (GROUP, total), 1), 1.0, 0.0)
    down_part = dot(dot(own.astype(LOW), grad, (1, 1)).astype(LOW), rows[...])
    grad_out[...] = (dot(grad[: 2 * GROUP], rows[...])[:GROUP] + down_part) * scale


def contrast(cls_rows, span_count, pair_index, device, slots):
    total = cls_rows.shape[0]
    return pl.pallas_call(
        partial(contrast_kernel, slots),
        in_specs=[pl.BlockSpec(memory_space=pltpu.SMEM)]
        + [pl.BlockSpec(memory_space=pltpu.VMEM)] * 3,
        out_shape=[
            jax.ShapeDtypeStruct((1, 1), F32),
            jax.ShapeDtypeStruct((GROUP, D), F32),
        ],
        compiler_params=params(),
        cost_estimate=pl.CostEstimate(
            flops=2 * total * total * D, bytes_accessed=2 * total * D, transcendentals=2 * total**2
        ),
        name="contrast",
    )(
        device.reshape(1),
        cls_rows,
        span_count.astype(F32).reshape(1, -1),
        pair_index.astype(F32).reshape(1, -1),
    )


def adam_kernel(
    packed, position, gathered, master, first, second, left, right,
    master_out, first_out, second_out, low_out, *scratch,
):
    quarter = D // 4
    slot = pl.program_id(0)
    if packed:
        owned = scratch[0]
        shares, tall, _ = gathered.shape
        rows = D // shares

        @pl.when(slot == 0)
        def _():
            def place(share, carry):
                block = gathered[share].astype(F32)
                at = pl.multiple_of((share ^ position[0]) * rows, rows)
                for index in range(owned.shape[0]):
                    lo = index * rows % tall
                    side = index * rows // tall
                    piece = block[lo : lo + rows, side * quarter : (side + 1) * quarter]
                    owned[index, pl.ds(at, rows), :] = piece
                return carry

            lax.fori_loop(0, shares, place, 0)

        gradient = owned[slot].astype(LOW)
    else:
        gradient = gathered[0]
    low_left, low_right = left[0].astype(LOW), right[0].astype(LOW)
    turned = dot(gradient, low_left, (0, 0))
    turned = dot(turned.astype(LOW), low_right, (0, 0))
    new_first = 0.9 * first[0] + 0.1 * turned
    new_second = 0.999 * second[0] + 0.001 * turned * turned
    first_out[0] = new_first
    second_out[0] = new_second
    spread_by = jnp.sqrt(new_second * (1.0 / (1.0 - 0.999**STEP))) + 1e-08
    update = new_first * (1.0 / (1.0 - 0.9**STEP)) / spread_by
    update = dot(low_left, update.astype(LOW))
    update = dot(update.astype(LOW), low_right, (1, 1))
    new_master = master[0] - RATE * (update + DECAY * master[0])
    master_out[0] = new_master
    low_out[0] = new_master.astype(LOW)


def to_owned(gathered, position, per_owner):
    quarter = D // 4
    gathered = jnp.take(gathered, jnp.arange(gathered.shape[0]) ^ position, axis=0)
    flat = jnp.concatenate([gathered[..., :quarter], gathered[..., quarter:]], axis=1)
    rows = flat.shape[1] // per_owner
    flat = flat.reshape(flat.shape[0], per_owner, rows, quarter).transpose(1, 0, 2, 3)
    return flat.reshape(per_owner, D, quarter)


def rotated_adam(position, gathered, master, first_moment, second_moment, left_basis, right_basis):
    per_owner, _, quarter = master.shape
    rows = D // gathered.shape[0]
    packed = rows % 8 == 0 and per_owner % 2 == 0
    if not packed:
        gathered = to_owned(gathered, position, per_owner)
    block = lambda a: pl.BlockSpec((1,) + a.shape[1:], lambda s, p: (s, 0, 0))
    like = jax.ShapeDtypeStruct(master.shape, F32)
    operands = (master, first_moment, second_moment, left_basis, right_basis)
    fixed = pl.BlockSpec(gathered.shape, lambda s, p: (0, 0, 0))
    return pl.pallas_call(
        partial(adam_kernel, packed),
        grid_spec=pltpu.PrefetchScalarGridSpec(
            num_scalar_prefetch=1,
            grid=(per_owner,),
            in_specs=[fixed if packed else block(gathered)] + [block(a) for a in operands],
            out_specs=[block(master)] * 4,
            scratch_shapes=[pltpu.VMEM((per_owner, D, quarter), F32)] if packed else [],
        ),
        out_shape=[like, like, like, jax.ShapeDtypeStruct(master.shape, LOW)],
        compiler_params=params(),
        cost_estimate=pl.CostEstimate(
            flops=4 * per_owner * D * quarter * (D + quarter),
            bytes_accessed=per_owner * (D * D + 7 * D * quarter) * 4,
            transcendentals=2 * per_owner * D * quarter,
        ),
        name="adam",
    )(position.reshape(1), gathered, *operands)


def axis_bits(name):
    size = lax.axis_size(name)
    return [(name, 1 << k) for k in range(size.bit_length() - 1)]


def bit_of(step):
    return jnp.where((lax.axis_index(step[0]) & step[1]) != 0, 1, 0)


def swap(send, step):
    size = lax.axis_size(step[0])
    return lax.ppermute(send, step[0], [(i, i ^ step[1]) for i in range(size)])


def pick(array, index, dim):
    return lax.dynamic_index_in_dim(array, index, dim, False)


def gather_all(rows):
    for step in axis_bits("col") + axis_bits("row"):
        rows = jnp.concatenate([rows, swap(rows, step)])
    return rows


def row_steps():
    row_bits, col_bits = axis_bits("row"), axis_bits("col")
    core, across = row_bits[:1], row_bits[1:][::-1]
    y_bits, z_bits = col_bits[:-2][::-1], col_bits[-2:]
    return core, across, y_bits, z_bits


def halve(part, step, left):
    dim = 1 + left.index(step)
    bit = bit_of(step)
    other = swap(pick(part, 1 - bit, dim), step)
    part = pick(part, bit, dim).astype(F32) + other.astype(F32)
    left.remove(step)
    return part.astype(LOW)


def reduce_panels(send, keep):
    core, across, y_bits, z_bits = row_steps()
    left = across + y_bits + z_bits
    part = keep.astype(F32) + swap(send, core[0]).astype(F32)
    width = part.shape[1] >> len(left)
    part = part.astype(LOW).reshape(part.shape[:1] + (2,) * len(left) + (width, D))
    halves = []
    for side, order in enumerate((across + y_bits, y_bits + across)):
        here, rest = part[..., side * D // 2 : (side + 1) * D // 2], list(left)
        for step in order:
            here = halve(here, step, rest)
        halves.append(here)
    part, rest = jnp.concatenate(halves, axis=-1), list(z_bits)
    for step in z_bits:
        part = halve(part, step, rest)
    return part


def to_slots(shares, owner_list):
    quarter = D // 4
    panels, rows, _ = shares.shape
    blocks = shares.reshape(panels, rows, 4, quarter).transpose(0, 2, 1, 3)
    blocks = blocks.reshape(panels * 4, rows, quarter)
    slots = jnp.take(blocks, owner_list, axis=0)
    cols = lax.axis_size("col")
    flat = slots.reshape(cols, slots.shape[0] // cols * rows, quarter)
    half = flat.shape[1] // 2
    return jnp.concatenate([flat[:, :half], flat[:, half:]], axis=-1)


def spread(slots):
    core, across, y_bits, z_bits = row_steps()
    tail = slots.shape[1:]
    left = axis_bits("col")[::-1]
    part = slots.reshape((1,) + (2,) * len(left) + tail)
    for step in (y_bits + z_bits)[::-1]:
        dim = 1 + left.index(step)
        bit = bit_of(step)
        other = swap(pick(part, 1 - bit, dim), step)
        part = jnp.concatenate([pick(part, bit, dim), other])
        left.remove(step)
    for step in (core + across)[::-1]:
        part = jnp.concatenate([part, swap(part, step)])
    return part


def row_place():
    place = 0
    for group in row_steps():
        for step in group:
            place = place * 2 + bit_of(step)
    return place


def shards(
    tokens,
    w_qkv,
    w_attn_out,
    w_in,
    w_out,
    vectors,
    out_grad,
    span_count,
    pair_index,
    owner_list,
    master,
    first_moment,
    second_moment,
    left_basis,
    right_basis,
    vec_first,
    vec_second,
):
    slots = tokens.shape[0] // SPAN
    device = lax.axis_index("row") * lax.axis_size("col") + lax.axis_index("col")
    own_count = lax.dynamic_index_in_dim(span_count, device, 0, False)
    own_live = (jnp.arange(slots) < own_count).astype(F32)
    token_live = jnp.repeat(own_live, SPAN)[:, None]
    core, across, y_bits, z_bits = row_steps()
    core_bit = bit_of(core[0])
    rows = vectors.reshape(-1, D)
    q, k, v, p, attended = attend(tokens, w_qkv, rows)
    encoded, hidden, slope, normed_low, unit_one, inverse_one, unit_two, inverse_two = feed(
        tokens, attended, token_live, w_attn_out, w_in, w_out, rows
    )
    cls_rows = jnp.pad(encoded.reshape(slots, SPAN, D)[:, 0], ((0, GROUP - slots), (0, 0)))
    loss, grad_cls = contrast(gather_all(cls_rows), span_count, pair_index, device, slots)
    grad_two, outer_low, vec_two = outer_grad(
        out_grad, grad_cls, token_live, unit_two, inverse_two, rows
    )
    outer_sum = reduce_panels(*weight_grad(core_bit, hidden, outer_low, FF // D, True))
    pre_low, grad_one, mixed_low, grad_attended, vec_one = inner_grad(
        outer_low, grad_two, slope, unit_one, inverse_one, w_attn_out, w_in, w_out, rows
    )
    inner_sum = reduce_panels(
        *weight_grad(core_bit, normed_low, pre_low, FF // D, False, (attended, mixed_low))
    )
    stack_low, vec_heads = unattend(q, k, v, p, grad_attended)
    project_sum = reduce_panels(*weight_grad(core_bit, tokens, stack_low, 3, False))
    grad_tokens = grad_one + dot(stack_low, w_qkv.transpose(1, 0, 2).reshape(D, 3 * D), (1, 1))
    shares = jnp.concatenate([project_sum, inner_sum[-1:], inner_sum[:-1], outer_sum])
    gathered = spread(to_slots(shares, owner_list))
    grad_vector = jnp.concatenate(
        [
            vec_one[0],
            vec_two[0],
            vec_one[1],
            vec_two[1],
            vec_heads[0],
            vec_heads[1],
            vec_one[2],
            vec_two[2],
            vec_one[3:].reshape(-1),
        ]
    )
    vec_grad = grad_vector.reshape(-1, 128)
    for step in core + across + y_bits + z_bits:
        vec_grad += swap(vec_grad, step)
    vec_grad = vec_grad.reshape(-1)
    new_master, new_first, new_second, master_copy = rotated_adam(
        row_place(), gathered, master, first_moment, second_moment, left_basis, right_basis
    )
    vec_first_new = 0.9 * vec_first + 0.1 * vec_grad
    vec_second_new = 0.999 * vec_second + 0.001 * vec_grad * vec_grad
    vec_step = (
        vec_first_new / (1.0 - 0.9**STEP) / (jnp.sqrt(vec_second_new / (1.0 - 0.999**STEP)) + 1e-08)
    )
    vec_new = vectors - VECTOR_RATE * vec_step
    return (
        encoded,
        grad_tokens,
        loss[0, 0],
        new_master,
        new_first,
        new_second,
        master_copy,
        vec_new,
        vec_first_new,
        vec_second_new,
    )


def solution(mesh):
    in_specs = (
        P(("row", "col"), None),
        P(),
        P(),
        P(),
        P(),
        P(),
        P(("row", "col"), None),
        P(),
        P(),
        P(),
        P("col", None, None),
        P("col", None, None),
        P("col", None, None),
        P("col", None, None),
        P("col", None, None),
        P(),
        P(),
    )
    out_specs = (
        P(("row", "col"), None),
        P(("row", "col"), None),
        P(),
        P("col", None, None),
        P("col", None, None),
        P("col", None, None),
        P("col", None, None),
        P(),
        P(),
        P(),
    )
    return jax.shard_map(shards, mesh=mesh, in_specs=in_specs, out_specs=out_specs, check_vma=False)
```

```python
from functools import partial

import jax
import jax.numpy as jnp
from jax import lax
from jax.experimental import pallas as pl
from jax.experimental.pallas import tpu as pltpu
from jax.sharding import PartitionSpec as P

D = 768
HEADS = 12
HEAD = 64
FF = 3072
SPAN = 128
STEP = 10
GROUP = 8

RATE = 0.01
DECAY = 0.01
VECTOR_RATE = 0.3

LOW = jnp.bfloat16
F32 = jnp.float32
TALL = 2 * SPAN
VMEM_LIMIT = 56 * 1024 * 1024


def dot(left_side, right_side, contract=(1, 0)):
    dims = (((contract[0],), (contract[1],)), ((), ()))
    return lax.dot_general(left_side, right_side, dims, preferred_element_type=F32)


def whole(shape):
    return pl.BlockSpec(shape, lambda *ids: (0,) * len(shape))


def params():
    return pltpu.CompilerParams(vmem_limit_bytes=VMEM_LIMIT)


def row_of(rows, index):
    return rows[:, index * D : (index + 1) * D]


def live_rows(place, counts, first_row, height):
    at = first_row + lax.broadcasted_iota(jnp.int32, (height, 1), 0)
    return jnp.where(at < counts[place[0]] * SPAN, 1.0, 0.0)


ANY = pl.BlockSpec(memory_space=pl.ANY)
SMEM = pl.BlockSpec(memory_space=pltpu.SMEM)


def split_heads(pair):
    lane = lax.broadcasted_iota(jnp.int32, pair.shape, 1)
    zero = jnp.zeros_like(pair)
    return jnp.concatenate([jnp.where(lane < HEAD, pair, zero), jnp.where(lane < HEAD, zero, pair)])


def normalise(scores):
    peak = jnp.max(scores, axis=-1, keepdims=True)
    raised = jnp.exp(scores - peak)
    return raised * (1.0 / jnp.sum(raised, axis=-1, keepdims=True))


def attend_kernel(tokens, w_qkv, rows, q_out, k_out, v_out, p_out, a_out):
    block = tokens[...]
    scaling = HEAD ** (-0.5)
    q_out[...] = ((dot(block, w_qkv[0]) + row_of(rows, 4)).astype(LOW) * scaling).astype(LOW)
    k_out[...] = dot(block, w_qkv[1]).astype(LOW)
    v_out[...] = (dot(block, w_qkv[2]) + row_of(rows, 5)).astype(LOW)
    for span in range(TALL // SPAN):
        at = slice(span * SPAN, (span + 1) * SPAN)
        for pair in range(HEADS // 2):
            lanes = slice(pair * 2 * HEAD, (pair + 1) * 2 * HEAD)
            scores = dot(q_out[at, lanes], split_heads(k_out[at, lanes]), (1, 1))
            weights = jnp.concatenate(
                [normalise(scores[:, :SPAN]), normalise(scores[:, SPAN:])], axis=1
            ).astype(LOW)
            p_out[span, pair] = weights
            a_out[at, lanes] = dot(weights, split_heads(v_out[at, lanes])).astype(LOW)


def attend(tokens, w_qkv, rows):
    total = tokens.shape[0]
    tall = pl.BlockSpec((TALL, D), lambda i: (i, 0))
    like = jax.ShapeDtypeStruct((total, D), LOW)
    spans = TALL // SPAN
    return pl.pallas_call(
        attend_kernel,
        grid=(total // TALL,),
        in_specs=[tall, whole(w_qkv.shape), whole(rows.shape)],
        out_specs=[
            tall,
            tall,
            tall,
            pl.BlockSpec((spans, HEADS // 2, SPAN, 2 * SPAN), lambda i: (i, 0, 0, 0)),
            tall,
        ],
        out_shape=[
            like,
            like,
            like,
            jax.ShapeDtypeStruct((total // SPAN, HEADS // 2, SPAN, 2 * SPAN), LOW),
            like,
        ],
        compiler_params=params(),
        cost_estimate=pl.CostEstimate(
            flops=2 * total * D * (3 * D + 2 * SPAN),
            bytes_accessed=14 * total * D + 6 * D * D,
            transcendentals=total * HEADS * SPAN,
        ),
        name="attend",
    )(tokens, w_qkv, rows)


def unit_norm(resid):
    centred = resid - jnp.mean(resid, axis=-1, keepdims=True)
    inverse = lax.rsqrt(jnp.mean(centred * centred, axis=-1, keepdims=True) + 1e-06)
    return centred * inverse, inverse


def gelu_pair(x):
    z = jnp.abs(x) * 0.7071067811865476
    base = 1.0 + 0.3275911 * z
    t = pltpu.reciprocal(base, approx=True)
    t = t * (2.0 - base * t)
    poly = 0.5 * 1.061405429
    for term in (-1.453152027, 1.421413741, -0.284496736, 0.254829592):
        poly = poly * t + 0.5 * term
    gauss = jnp.exp(-(z * z))
    tail = poly * t * gauss
    cdf = jnp.where(x < 0, tail, 1.0 - tail)
    return x * cdf, cdf + x * gauss * 0.3989422804014327


def feed_kernel(
    place, counts, tokens, attended, w_attn, w_in, w_out, rows,
    enc_out, hid_out, slope_out, norm_out, u1_out, i1_out, u2_out, i2_out,
):
    resid = tokens[...].astype(F32) + dot(attended[...], w_attn[...]) + row_of(rows, 6)
    unit_one, inverse_one = unit_norm(resid)
    normed = unit_one * row_of(rows, 0) + row_of(rows, 2)
    u1_out[...] = unit_one.astype(LOW)
    i1_out[...] = inverse_one
    norm_out[...] = normed.astype(LOW)
    step = 256
    for at in range(0, FF, step):
        bias = rows[:, 8 * D + at : 8 * D + at + step]
        pre_act = dot(norm_out[...], w_in[:, at : at + step]) + bias
        hidden, slope = gelu_pair(pre_act)
        hid_out[:, at : at + step] = hidden.astype(LOW)
        slope_out[:, at : at + step] = slope.astype(LOW)
    resid = normed + dot(hid_out[...], w_out[...]) + row_of(rows, 7)
    unit_two, inverse_two = unit_norm(resid)
    u2_out[...] = unit_two.astype(LOW)
    i2_out[...] = inverse_two
    live = live_rows(place, counts, pl.program_id(0) * TALL, TALL)
    enc_out[...] = (live * (unit_two * row_of(rows, 1) + row_of(rows, 3))).astype(LOW)


def feed(place, counts, tokens, attended, w_attn, w_in, w_out, rows):
    total = tokens.shape[0]
    tall = lambda width: pl.BlockSpec((TALL, width), lambda i: (i, 0))
    like = lambda width, kind: jax.ShapeDtypeStruct((total, width), kind)
    return pl.pallas_call(
        feed_kernel,
        grid=(total // TALL,),
        in_specs=[SMEM, SMEM, tall(D), tall(D)]
        + [whole(a.shape) for a in (w_attn, w_in, w_out, rows)],
        out_specs=[tall(D), tall(FF), tall(FF), tall(D), tall(D), tall(1), tall(D), tall(1)],
        out_shape=[
            like(D, LOW), like(FF, LOW), like(FF, LOW), like(D, LOW),
            like(D, LOW), like(1, F32), like(D, LOW), like(1, F32),
        ],
        compiler_params=params(),
        cost_estimate=pl.CostEstimate(
            flops=2 * total * D * (D + 2 * FF),
            bytes_accessed=total * (12 * D + 4 * FF) + 4 * D * FF,
            transcendentals=total * FF * 2,
        ),
        name="feed",
    )(place, counts, tokens, attended, w_attn, w_in, w_out, rows)


def norm_back(grad_out, unit_rows, inverse, gain):
    scaled = grad_out * gain
    along = jnp.mean(scaled * unit_rows, axis=-1, keepdims=True)
    return inverse * (scaled - jnp.mean(scaled, axis=-1, keepdims=True) - unit_rows * along)


def column_sums(*arrays):
    return [jnp.sum(a, axis=0, keepdims=True) for a in arrays]


def outer_kernel(place, counts, out_grad, grad_cls, unit_two, inverse_two, rows, two_out, low_out, vec_out):
    spot = lax.broadcasted_iota(jnp.int32, (SPAN, 1), 0) == 0
    sums = None
    for span in range(out_grad.shape[0] // SPAN):
        at = slice(span * SPAN, (span + 1) * SPAN)
        added = jnp.where(spot, grad_cls[span : span + 1], 0.0)
        live = live_rows(place, counts, span * SPAN, SPAN)
        grad_y = live * (out_grad[at].astype(F32) + added)
        unit_rows = unit_two[at].astype(F32)
        grad_two = norm_back(grad_y, unit_rows, inverse_two[at], row_of(rows, 1))
        two_out[at] = grad_two
        low_out[at] = grad_two.astype(LOW)
        here = column_sums(grad_y * unit_rows, grad_y, grad_two)
        sums = here if sums is None else [a + b for a, b in zip(sums, here)]
    for index, total in enumerate(sums):
        vec_out[index : index + 1] = total


def outer_grad(place, counts, out_grad, grad_cls, unit_two, inverse_two, rows):
    total = out_grad.shape[0]
    return pl.pallas_call(
        outer_kernel,
        in_specs=[SMEM, SMEM] + [pl.BlockSpec(memory_space=pltpu.VMEM)] * 5,
        out_shape=[
            jax.ShapeDtypeStruct((total, D), F32),
            jax.ShapeDtypeStruct((total, D), LOW),
            jax.ShapeDtypeStruct((3, D), F32),
        ],
        compiler_params=params(),
        cost_estimate=pl.CostEstimate(
            flops=20 * total * D, bytes_accessed=10 * total * D, transcendentals=0
        ),
        name="outer",
    )(place, counts, out_grad, grad_cls, unit_two, inverse_two, rows)


def weight_kernel(panels, ordered_after, bit, *refs):
    left_side, right_side, *rest = refs[ordered_after:]
    extra_left, extra_right = rest[:-2] or (None, None)
    send_out, keep_out = rest[-2:]

    def store(left_from, right_from):
        value = dot(left_from[...], right_from[...], (0, 0)).astype(LOW)

        @pl.when(pl.program_id(0) == 0)
        def _():
            send_out[0] = value

        @pl.when(pl.program_id(0) == 1)
        def _():
            keep_out[0] = value

    if extra_left is None:
        store(left_side, right_side)
        return

    @pl.when(pl.program_id(1) < panels)
    def _():
        store(left_side, right_side)

    @pl.when(pl.program_id(1) == panels)
    def _():
        store(extra_left, extra_right)


def weight_grad(after, bit, left_side, right_side, panels, banded, extra=()):
    total = left_side.shape[0]
    half = D // 2
    every = panels + len(extra) // 2

    def side_of(phase, bit):
        return jnp.where(phase == 0, 1 - bit[0], bit[0])

    def left_at(phase, panel, bit):
        side = side_of(phase, bit)
        return (0, jnp.minimum(panel, panels - 1) * 2 + side if banded else side)

    def right_at(phase, panel, bit):
        return (0, 0 if banded else jnp.minimum(panel, panels - 1))

    like = jax.ShapeDtypeStruct((every, half, D), LOW)
    tall = lambda width, at: pl.BlockSpec((total, width), at)
    more = [tall(half, lambda f, p, b: (0, side_of(f, b))), tall(D, lambda f, p, b: (0, 0))]
    return pl.pallas_call(
        partial(weight_kernel, panels, len(after)),
        grid_spec=pltpu.PrefetchScalarGridSpec(
            num_scalar_prefetch=1,
            grid=(2, every),
            in_specs=[ANY] * len(after)
            + [tall(half, left_at), tall(D, right_at)]
            + more[: len(extra)],
            out_specs=[
                pl.BlockSpec((1, half, D), lambda f, p, b: (jnp.where(f == 0, p, every - 1), 0, 0)),
                pl.BlockSpec((1, half, D), lambda f, p, b: (jnp.where(f == 0, 0, p), 0, 0)),
            ],
        ),
        out_shape=[like, like],
        compiler_params=params(),
        cost_estimate=pl.CostEstimate(
            flops=2 * total * D * D * every,
            bytes_accessed=2 * (total + D) * D * every,
            transcendentals=0,
        ),
        name="weight",
    )(bit.reshape(1), *after, left_side, right_side, *extra)


def slope_kernel(*refs):
    low, slope, w_out, pre_out, vec_out = refs[-5:]
    step = 256
    for at in range(0, pre_out.shape[1], step):
        here = slice(at, at + step)
        grad_pre = dot(low[...], w_out[here], (1, 1)) * slope[:, here].astype(F32)
        pre_out[:, here] = grad_pre.astype(LOW)
        vec_out[0, :, here] = jnp.sum(grad_pre, axis=0, keepdims=True)


def slope_grad(after, low, slope, w_out):
    total = low.shape[0]
    band = pl.BlockSpec((total, D), lambda i: (0, i))
    return pl.pallas_call(
        slope_kernel,
        grid=(FF // D,),
        in_specs=[ANY] * len(after)
        + [whole(low.shape), band, pl.BlockSpec((D, D), lambda i: (i, 0))],
        out_specs=[band, pl.BlockSpec((1, 1, D), lambda i: (i, 0, 0))],
        out_shape=[
            jax.ShapeDtypeStruct((total, FF), LOW),
            jax.ShapeDtypeStruct((FF // D, 1, D), F32),
        ],
        compiler_params=params(),
        cost_estimate=pl.CostEstimate(
            flops=2 * total * D * FF, bytes_accessed=4 * total * FF + 2 * D * FF, transcendentals=0
        ),
        name="slope",
    )(*after, low, slope, w_out)


def inner_kernel(*refs):
    pre_low, grad_two, unit_one, inverse_one, w_attn, w_in, rows = refs[-11:-4]
    one_out, mixed_out, ga_out, vec_out = refs[-4:]
    first = pl.program_id(0) == 0

    @pl.when(first)
    def _():
        vec_out[...] = jnp.zeros_like(vec_out)

    grad_normed = grad_two[...] + dot(pre_low[...], w_in[...], (1, 1))
    unit_rows = unit_one[...].astype(F32)
    grad_one = norm_back(grad_normed, unit_rows, inverse_one[...], row_of(rows, 0))
    one_out[...] = grad_one
    mixed = grad_one.astype(LOW)
    mixed_out[...] = mixed
    ga_out[...] = dot(mixed, w_attn[...], (1, 1)).astype(LOW)
    for index, total in enumerate(column_sums(grad_normed * unit_rows, grad_normed, grad_one)):
        vec_out[index : index + 1] += total


def inner_grad(after, pre_low, grad_two, unit_one, inverse_one, w_attn, w_in, rows):
    total = pre_low.shape[0]
    tall = lambda width: pl.BlockSpec((TALL, width), lambda i: (i, 0))
    like = lambda width, kind: jax.ShapeDtypeStruct((total, width), kind)
    return pl.pallas_call(
        inner_kernel,
        grid=(total // TALL,),
        in_specs=[ANY] * len(after)
        + [tall(FF), tall(D), tall(D), tall(1)]
        + [whole(a.shape) for a in (w_attn, w_in, rows)],
        out_specs=[tall(D), tall(D), tall(D), whole((3, D))],
        out_shape=[
            like(D, F32), like(D, LOW), like(D, LOW), jax.ShapeDtypeStruct((3, D), F32),
        ],
        compiler_params=params(),
        cost_estimate=pl.CostEstimate(
            flops=2 * total * D * (D + FF),
            bytes_accessed=total * (14 * D + 2 * FF) + 2 * D * FF,
            transcendentals=0,
        ),
        name="inner",
    )(*after, pre_low, grad_two, unit_one, inverse_one, w_attn, w_in, rows)


def unattend_kernel(*refs):
    q, k, v, p, ga, stack_out, vec_out = refs[-7:]
    scaling = HEAD ** (-0.5)
    first = pl.program_id(0) == 0

    @pl.when(first)
    def _():
        vec_out[...] = jnp.zeros_like(vec_out)

    for span in range(p.shape[0]):
        at = slice(span * SPAN, (span + 1) * SPAN)
        for pair in range(HEADS // 2):
            lo = pair * 2 * HEAD
            lanes = slice(lo, lo + 2 * HEAD)
            weights = p[span, pair]
            grad = ga[at, lanes]
            spread_out = dot(grad, split_heads(v[at, lanes]), (1, 1))
            wide = weights.astype(F32)
            parts = []
            for half in range(2):
                cols = slice(half * SPAN, (half + 1) * SPAN)
                wgt, gw = wide[:, cols], spread_out[:, cols]
                parts.append((wgt * (gw - jnp.sum(gw * wgt, axis=-1, keepdims=True))).astype(LOW))
            grad_scores = jnp.concatenate(parts, axis=1)
            grad_q = dot(grad_scores, split_heads(k[at, lanes])) * scaling
            tall_scores = jnp.concatenate(parts, axis=0)
            tall_weights = jnp.concatenate([weights[:, :SPAN], weights[:, SPAN:]], axis=0)
            grad_k = dot(tall_scores, split_heads(q[at, lanes]), (0, 0))
            grad_v = dot(tall_weights, split_heads(grad), (0, 0))
            stack_out[at, lo : lo + 2 * HEAD] = grad_q.astype(LOW)
            stack_out[at, D + lo : D + lo + 2 * HEAD] = grad_k.astype(LOW)
            stack_out[at, 2 * D + lo : 2 * D + lo + 2 * HEAD] = grad_v.astype(LOW)
            vec_out[0:1, lanes] += jnp.sum(grad_q, axis=0, keepdims=True)
            vec_out[1:2, lanes] += jnp.sum(grad_v, axis=0, keepdims=True)


def unattend(after, part, parts, q, k, v, p, ga):
    spans = 1
    tall_rows = spans * SPAN
    total = q.shape[0] // parts
    first = part * (total // tall_rows)
    tall = lambda width: pl.BlockSpec((tall_rows, width), lambda i: (first + i, 0))
    return pl.pallas_call(
        unattend_kernel,
        grid=(total // tall_rows,),
        in_specs=[ANY] * len(after)
        + [tall(D)] * 3
        + [
            pl.BlockSpec((spans, HEADS // 2, SPAN, 2 * SPAN), lambda i: (first + i, 0, 0, 0)),
            tall(D),
        ],
        out_specs=[pl.BlockSpec((tall_rows, 3 * D), lambda i: (i, 0)), whole((2, D))],
        out_shape=[
            jax.ShapeDtypeStruct((total, 3 * D), LOW),
            jax.ShapeDtypeStruct((2, D), F32),
        ],
        compiler_params=params(),
        cost_estimate=pl.CostEstimate(
            flops=2 * total * D * 4 * SPAN, bytes_accessed=20 * total * D, transcendentals=0
        ),
        name="unattend",
    )(*after, q, k, v, p, ga)


def input_kernel(*refs):
    grad_one, stack, w_qkv, out = refs[-4:]
    total = grad_one[...]
    for index in range(3):
        total += dot(stack[:, index * D : (index + 1) * D], w_qkv[index], (1, 1))
    out[...] = total


def input_grad(after, grad_one, stack, w_qkv):
    total = grad_one.shape[0]
    tall = lambda width: pl.BlockSpec((TALL, width), lambda i: (i, 0))
    return pl.pallas_call(
        input_kernel,
        grid=(total // TALL,),
        in_specs=[ANY] * len(after) + [tall(D), tall(3 * D), whole(w_qkv.shape)],
        out_specs=tall(D),
        out_shape=jax.ShapeDtypeStruct((total, D), F32),
        compiler_params=params(),
        cost_estimate=pl.CostEstimate(
            flops=6 * total * D * D, bytes_accessed=14 * total * D + 6 * D * D, transcendentals=0
        ),
        name="input",
    )(*after, grad_one, stack, w_qkv)


def contrast_kernel(slots, place, rows, counts, partners, loss_out, grad_out):
    total, scale = rows.shape[0], 2.0 * D ** (-0.5)

    def number(shape, axis):
        at = lax.broadcasted_iota(jnp.int32, shape, axis)
        return (at // GROUP) ^ place[0], at % GROUP

    device, slot = number((counts.shape[1], total), 1)
    hit = lax.broadcasted_iota(jnp.int32, device.shape, 0) == device
    count = dot(counts[...].astype(LOW), jnp.where(hit, 1.0, 0.0).astype(LOW))
    live_across = (slot[:1].astype(F32) < count) & (slot[:1] < slots)
    device, slot = number((total, counts.shape[1]), 0)
    hit = lax.broadcasted_iota(jnp.int32, device.shape, 1) == device
    count = jnp.sum(jnp.where(hit, counts[...], 0.0), axis=1, keepdims=True)
    live_down = (slot[:, :1].astype(F32) < count) & (slot[:, :1] < slots)
    device, slot = number((total, partners.shape[1]), 0)
    own_id = device * slots + slot
    hit = lax.broadcasted_iota(jnp.int32, own_id.shape, 1) == own_id
    pair = jnp.sum(jnp.where(hit, partners[...], 0.0), axis=1, keepdims=True)
    device, slot = number((total, total), 0)
    down = (device * slots + slot).astype(F32)
    device, slot = number((total, total), 1)
    across = (device * slots + slot).astype(F32)
    valid = live_across & (down != across)
    matched = jnp.where((slot < slots) & (pair == across), 1.0, 0.0)
    anchor = jnp.where(live_down & (pair != down[:, :1]), 1.0, 0.0)
    similar = dot(rows[...], rows[...], (1, 1)) * scale
    masked = jnp.where(valid, similar, -1e30)
    peak = jnp.max(masked, axis=1, keepdims=True)
    summed = jnp.sum(jnp.where(valid, jnp.exp(masked - peak), 0.0), axis=1, keepdims=True)
    log_total = jnp.log(summed) + peak
    positive = jnp.sum(matched * similar, axis=1, keepdims=True)
    loss_out[...] = jnp.sum(anchor * (log_total - positive), axis=0, keepdims=True)
    grad = (anchor * (jnp.where(valid, jnp.exp(masked - log_total), 0.0) - matched)).astype(LOW)
    own = lax.broadcasted_iota(jnp.int32, (GROUP, total), 0)
    own = jnp.where(own == lax.broadcasted_iota(jnp.int32, (GROUP, total), 1), 1.0, 0.0)
    down_part = dot(dot(own.astype(LOW), grad, (1, 1)).astype(LOW), rows[...])
    grad_out[...] = (dot(grad[: 2 * GROUP], rows[...])[:GROUP] + down_part) * scale


def contrast(cls_rows, span_count, pair_index, device, slots):
    total = cls_rows.shape[0]
    return pl.pallas_call(
        partial(contrast_kernel, slots),
        in_specs=[pl.BlockSpec(memory_space=pltpu.SMEM)]
        + [pl.BlockSpec(memory_space=pltpu.VMEM)] * 3,
        out_shape=[
            jax.ShapeDtypeStruct((1, 1), F32),
            jax.ShapeDtypeStruct((GROUP, D), F32),
        ],
        compiler_params=params(),
        cost_estimate=pl.CostEstimate(
            flops=2 * total * total * D, bytes_accessed=2 * total * D, transcendentals=2 * total**2
        ),
        name="contrast",
    )(
        device,
        cls_rows,
        span_count.astype(F32).reshape(1, -1),
        pair_index.astype(F32).reshape(1, -1),
    )


def adam_kernel(
    packed, position, gathered, master, first, second, left, right,
    master_out, first_out, second_out, low_out, *scratch,
):
    quarter = D // 4
    slot = pl.program_id(0)
    if packed:
        owned = scratch[0]
        shares, tall, _ = gathered.shape
        rows = D // shares

        @pl.when(slot == 0)
        def _():
            def place(share, carry):
                block = gathered[share].astype(F32)
                at = pl.multiple_of((share ^ position[0]) * rows, rows)
                for index in range(owned.shape[0]):
                    lo = index * rows % tall
                    side = index * rows // tall
                    piece = block[lo : lo + rows, side * quarter : (side + 1) * quarter]
                    owned[index, pl.ds(at, rows), :] = piece
                return carry

            lax.fori_loop(0, shares, place, 0)

        gradient = owned[slot].astype(LOW)
    else:
        gradient = gathered[0]
    low_left, low_right = left[0].astype(LOW), right[0].astype(LOW)
    turned = dot(gradient, low_left, (0, 0))
    turned = dot(low_right, turned.astype(LOW), (0, 0))
    new_first = 0.9 * first[0] + 0.1 * turned
    new_second = 0.999 * second[0] + 0.001 * turned * turned
    first_out[0] = new_first
    second_out[0] = new_second
    spread_by = jnp.sqrt(new_second * (1.0 / (1.0 - 0.999**STEP))) + 1e-08
    update = new_first * (1.0 / (1.0 - 0.9**STEP)) / spread_by
    update = dot(update.astype(LOW), low_left, (1, 1))
    update = dot(low_right, update.astype(LOW))
    new_master = master[0] - RATE * (update + DECAY * master[0])
    master_out[0] = new_master
    low_out[0] = new_master.astype(LOW)


def to_owned(gathered, position, per_owner):
    quarter = D // 4
    gathered = jnp.take(gathered, jnp.arange(gathered.shape[0]) ^ position, axis=0)
    flat = jnp.concatenate([gathered[..., :quarter], gathered[..., quarter:]], axis=1)
    rows = flat.shape[1] // per_owner
    flat = flat.reshape(flat.shape[0], per_owner, rows, quarter).transpose(1, 0, 2, 3)
    return flat.reshape(per_owner, D, quarter)


def rotated_adam(position, gathered, master, first_moment, second_moment, left_basis, right_basis):
    per_owner, _, quarter = master.shape
    turn = lambda a: a.transpose(0, 2, 1)
    rows = D // gathered.shape[0]
    packed = rows % 8 == 0 and per_owner % 2 == 0
    if not packed:
        gathered = to_owned(gathered, position, per_owner)
    block = lambda a: pl.BlockSpec((1,) + a.shape[1:], lambda s, p: (s, 0, 0))
    operands = (turn(master), turn(first_moment), turn(second_moment), left_basis, right_basis)
    like = jax.ShapeDtypeStruct(operands[0].shape, F32)
    fixed = pl.BlockSpec(gathered.shape, lambda s, p: (0, 0, 0))
    outputs = pl.pallas_call(
        partial(adam_kernel, packed),
        grid_spec=pltpu.PrefetchScalarGridSpec(
            num_scalar_prefetch=1,
            grid=(per_owner,),
            in_specs=[fixed if packed else block(gathered)] + [block(a) for a in operands],
            out_specs=[block(operands[0])] * 4,
            scratch_shapes=[pltpu.VMEM((per_owner, D, quarter), F32)] if packed else [],
        ),
        out_shape=[like, like, like, jax.ShapeDtypeStruct(like.shape, LOW)],
        compiler_params=params(),
        cost_estimate=pl.CostEstimate(
            flops=4 * per_owner * D * quarter * (D + quarter),
            bytes_accessed=per_owner * (D * D + 7 * D * quarter) * 4,
            transcendentals=2 * per_owner * D * quarter,
        ),
        name="adam",
    )(position.reshape(1), gathered, *operands)
    return [turn(a) for a in outputs]


def axis_bits(name):
    size = lax.axis_size(name)
    return [(name, 1 << k) for k in range(size.bit_length() - 1)]


def bit_of(step):
    return jnp.where((lax.axis_index(step[0]) & step[1]) != 0, 1, 0)


def swap(send, step):
    size = lax.axis_size(step[0])
    return lax.ppermute(send, step[0], [(i, i ^ step[1]) for i in range(size)])


def pick(array, index, dim):
    return lax.dynamic_index_in_dim(array, index, dim, False)


def gather_all(rows):
    for step in axis_bits("col") + axis_bits("row"):
        rows = jnp.concatenate([rows, swap(rows, step)])
    return rows


def row_steps():
    row_bits, col_bits = axis_bits("row"), axis_bits("col")
    core, across = row_bits[:1], row_bits[1:][::-1]
    y_bits, z_bits = col_bits[:-2][::-1], col_bits[-2:]
    return core, across, y_bits, z_bits


def launch(part, step, left):
    dim = 1 + left.index(step)
    bit = bit_of(step)
    left.remove(step)
    send = pick(part, 1 - bit, dim)
    return send, pick(part, bit, dim), swap(send, step)


def landed(keep, other):
    return (keep.astype(F32) + other.astype(F32)).astype(LOW)


def reduce_panels(send, keep):
    core, across, y_bits, z_bits = row_steps()
    left = across + y_bits + z_bits
    sends = []
    part = landed(keep, swap(send, core[0]))
    width = part.shape[1] >> len(left)
    part = part.reshape(part.shape[:1] + (2,) * len(left) + (width, D))
    sides = [part[..., : D // 2], part[..., D // 2 :]]
    rest = [list(left), list(left)]
    for steps in zip(across + y_bits, y_bits + across):
        moves = [launch(sides[i], steps[i], rest[i]) for i in range(2)]
        sends.append([move[0] for move in moves])
        sides = [landed(move[1], move[2]) for move in moves]
    part, left = jnp.concatenate(sides, axis=-1), list(z_bits)
    for step in z_bits:
        sent, stays, other = launch(part, step, left)
        sends.append([sent])
        part = landed(stays, other)
    return part, sends


def slots_kernel(cols, after, owners, *refs):
    parts, out, shares, packed = refs[after:-3], refs[-3], refs[-2], refs[-1]
    quarter = D // 4
    at = 0
    for part in parts:
        shares[at : at + part.shape[0]] = part[...].astype(F32)
        at += part.shape[0]
    rows, half = shares.shape[1], packed.shape[1]
    slots = at * 4
    for slot in range(slots):
        col, place = divmod(slot, slots // cols)
        owner = owners[slot]
        block = shares[owner // 4]
        which = owner % 4
        value = block[:, :quarter]
        for index in range(1, 4):
            other = block[:, index * quarter : (index + 1) * quarter]
            value = jnp.where(which == index, other, value)
        first = place * rows
        for side in range(2):
            lo, hi = max(first, side * half), min(first + rows, (side + 1) * half)
            if lo < hi:
                lanes = slice(side * quarter, (side + 1) * quarter)
                packed[col, lo - side * half : hi - side * half, lanes] = value[lo - first : hi - first]
    out[...] = packed[...].astype(LOW)


def to_slots(after, parts, owner_list):
    quarter, cols = D // 4, lax.axis_size("col")
    panels, rows = sum(part.shape[0] for part in parts), parts[0].shape[1]
    shape = (cols, panels * 4 // cols * rows // 2, 2 * quarter)
    return pl.pallas_call(
        partial(slots_kernel, cols, len(after)),
        in_specs=[SMEM] + [ANY] * len(after) + [pl.BlockSpec(memory_space=pltpu.VMEM)] * len(parts),
        out_shape=jax.ShapeDtypeStruct(shape, LOW),
        scratch_shapes=[pltpu.VMEM((panels, rows, D), F32), pltpu.VMEM(shape, F32)],
        compiler_params=params(),
        name="slots",
    )(owner_list, *after, *parts)


def spread(slots):
    core, across, y_bits, z_bits = row_steps()
    tail = slots.shape[1:]
    left = axis_bits("col")[::-1]
    part = slots.reshape((1,) + (2,) * len(left) + tail)
    for step in (y_bits + z_bits)[::-1]:
        dim = 1 + left.index(step)
        bit = bit_of(step)
        other = swap(pick(part, 1 - bit, dim), step)
        part = jnp.concatenate([pick(part, bit, dim), other])
        left.remove(step)
    for step in (core + across)[::-1]:
        part = jnp.concatenate([part, swap(part, step)])
    return part


def row_place():
    place = 0
    for group in row_steps():
        for step in group:
            place = place * 2 + bit_of(step)
    return place


def shards(
    tokens,
    w_qkv,
    w_attn_out,
    w_in,
    w_out,
    vectors,
    out_grad,
    span_count,
    pair_index,
    owner_list,
    master,
    first_moment,
    second_moment,
    left_basis,
    right_basis,
    vec_first,
    vec_second,
):
    slots = tokens.shape[0] // SPAN
    device = (lax.axis_index("row") * lax.axis_size("col") + lax.axis_index("col")).reshape(1)
    core, across, y_bits, z_bits = row_steps()
    core_bit = bit_of(core[0])
    rows = vectors.reshape(1, -1)
    q, k, v, p, attended = attend(tokens, w_qkv, rows)
    encoded, hidden, slope, normed_low, unit_one, inverse_one, unit_two, inverse_two = feed(
        device, span_count, tokens, attended, w_attn_out, w_in, w_out, rows
    )
    cls_rows = jnp.pad(encoded.reshape(slots, SPAN, D)[:, 0], ((0, GROUP - slots), (0, 0)))
    loss, grad_cls = contrast(gather_all(cls_rows), span_count, pair_index, device, slots)
    grad_two, outer_low, vec_two = outer_grad(
        device, span_count, out_grad, grad_cls, unit_two, inverse_two, rows
    )
    outer_parts = weight_grad([], core_bit, hidden, outer_low, FF // D, True)
    outer_sum, outer_sent = reduce_panels(*outer_parts)
    pre_low, vec_inner = slope_grad([outer_parts[0]], outer_low, slope, w_out)
    grad_one, mixed_low, grad_attended, vec_one = inner_grad(
        outer_sent[0], pre_low, grad_two, unit_one, inverse_one, w_attn_out, w_in, rows
    )
    inner_parts = weight_grad(
        outer_sent[1], core_bit, normed_low, pre_low, FF // D, False, (attended, mixed_low)
    )
    inner_sum, inner_sent = reduce_panels(*inner_parts)
    early, vec_early = unattend(
        [inner_parts[0]] + outer_sent[2], 0, 2, q, k, v, p, grad_attended
    )
    late, vec_late = unattend(
        [early] + outer_sent[3] + inner_sent[0], 1, 2, q, k, v, p, grad_attended
    )
    stack_low = jnp.concatenate([early, late])
    vec_heads = vec_early + vec_late
    project_parts = weight_grad(
        [outer_sum] + inner_sent[1], core_bit, tokens, stack_low, 3, False
    )
    project_sum, project_sent = reduce_panels(*project_parts)
    grad_tokens = input_grad(
        [project_parts[0]] + inner_sent[2], grad_one, stack_low, w_qkv
    )
    grad_vector = jnp.concatenate(
        [
            jnp.stack([vec_one[0], vec_two[0], vec_one[1], vec_two[1]]),
            vec_heads,
            jnp.stack([vec_one[2], vec_two[2]]),
            vec_inner[:, 0],
        ]
    )
    vec_grad = grad_vector
    for step in core + across + y_bits + z_bits:
        vec_grad += swap(vec_grad, step)
    parts = (project_sum, inner_sum[-1:], inner_sum[:-1], outer_sum)
    gathered = spread(to_slots([grad_tokens, vec_grad], parts, owner_list))
    vec_grad = vec_grad.reshape(-1)
    new_master, new_first, new_second, master_copy = rotated_adam(
        row_place(), gathered, master, first_moment, second_moment, left_basis, right_basis
    )
    vec_first_new = 0.9 * vec_first + 0.1 * vec_grad
    vec_second_new = 0.999 * vec_second + 0.001 * vec_grad * vec_grad
    vec_step = (
        vec_first_new / (1.0 - 0.9**STEP) / (jnp.sqrt(vec_second_new / (1.0 - 0.999**STEP)) + 1e-08)
    )
    vec_new = vectors - VECTOR_RATE * vec_step
    return (
        encoded,
        grad_tokens,
        loss[0, 0],
        new_master,
        new_first,
        new_second,
        master_copy,
        vec_new,
        vec_first_new,
        vec_second_new,
    )


def solution(mesh):
    in_specs = (
        P(("row", "col"), None),
        P(),
        P(),
        P(),
        P(),
        P(),
        P(("row", "col"), None),
        P(),
        P(),
        P(),
        P("col", None, None),
        P("col", None, None),
        P("col", None, None),
        P("col", None, None),
        P("col", None, None),
        P(),
        P(),
    )
    out_specs = (
        P(("row", "col"), None),
        P(("row", "col"), None),
        P(),
        P("col", None, None),
        P("col", None, None),
        P("col", None, None),
        P("col", None, None),
        P(),
        P(),
        P(),
    )
    return jax.shard_map(shards, mesh=mesh, in_specs=in_specs, out_specs=out_specs, check_vma=False)
```

```python
from functools import partial

import jax
import jax.numpy as jnp
from jax import lax
from jax.experimental import pallas as pl
from jax.experimental.pallas import tpu as pltpu
from jax.sharding import PartitionSpec as P

D = 768
HEADS = 12
HEAD = 64
FF = 3072
SPAN = 128
STEP = 10
GROUP = 8

RATE = 0.01
DECAY = 0.01
VECTOR_RATE = 0.3

LOW = jnp.bfloat16
F32 = jnp.float32
TALL = 2 * SPAN
VMEM_LIMIT = 56 * 1024 * 1024


def dot(left_side, right_side, contract=(1, 0)):
    dims = (((contract[0],), (contract[1],)), ((), ()))
    return lax.dot_general(left_side, right_side, dims, preferred_element_type=F32)


def whole(shape):
    return pl.BlockSpec(shape, lambda *ids: (0,) * len(shape))


def cost(microseconds, transcendentals=0):
    return pl.CostEstimate(
        flops=int(microseconds * 1.1e9), bytes_accessed=0, transcendentals=transcendentals
    )


def params():
    return pltpu.CompilerParams(vmem_limit_bytes=VMEM_LIMIT)


def row_of(rows, index):
    return rows[:, index * D : (index + 1) * D]


def live_rows(place, counts, first_row, height):
    at = first_row + lax.broadcasted_iota(jnp.int32, (height, 1), 0)
    return jnp.where(at < counts[place[0]] * SPAN, 1.0, 0.0)


ANY = pl.BlockSpec(memory_space=pl.ANY)
SMEM = pl.BlockSpec(memory_space=pltpu.SMEM)


def split_heads(pair):
    lane = lax.broadcasted_iota(jnp.int32, pair.shape, 1)
    zero = jnp.zeros_like(pair)
    return jnp.concatenate([jnp.where(lane < HEAD, pair, zero), jnp.where(lane < HEAD, zero, pair)])


def normalise(scores):
    peak = jnp.max(scores, axis=-1, keepdims=True)
    raised = jnp.exp(scores - peak)
    return raised * (1.0 / jnp.sum(raised, axis=-1, keepdims=True))


def attend_kernel(tokens, w_qkv, rows, q_out, k_out, v_out, p_out, a_out):
    block = tokens[...]
    scaling = HEAD ** (-0.5)
    q_out[...] = ((dot(block, w_qkv[0]) + row_of(rows, 4)).astype(LOW) * scaling).astype(LOW)
    k_out[...] = dot(block, w_qkv[1]).astype(LOW)
    v_out[...] = (dot(block, w_qkv[2]) + row_of(rows, 5)).astype(LOW)
    for span in range(TALL // SPAN):
        at = slice(span * SPAN, (span + 1) * SPAN)
        for pair in range(HEADS // 2):
            lanes = slice(pair * 2 * HEAD, (pair + 1) * 2 * HEAD)
            scores = dot(q_out[at, lanes], split_heads(k_out[at, lanes]), (1, 1))
            weights = jnp.concatenate(
                [normalise(scores[:, :SPAN]), normalise(scores[:, SPAN:])], axis=1
            ).astype(LOW)
            p_out[span, pair] = weights
            a_out[at, lanes] = dot(weights, split_heads(v_out[at, lanes])).astype(LOW)


def attend(tokens, w_qkv, rows):
    total = tokens.shape[0]
    tall = pl.BlockSpec((TALL, D), lambda i: (i, 0))
    like = jax.ShapeDtypeStruct((total, D), LOW)
    spans = TALL // SPAN
    return pl.pallas_call(
        attend_kernel,
        grid=(total // TALL,),
        in_specs=[tall, whole(w_qkv.shape), whole(rows.shape)],
        out_specs=[
            tall,
            tall,
            tall,
            pl.BlockSpec((spans, HEADS // 2, SPAN, 2 * SPAN), lambda i: (i, 0, 0, 0)),
            tall,
        ],
        out_shape=[
            like,
            like,
            like,
            jax.ShapeDtypeStruct((total // SPAN, HEADS // 2, SPAN, 2 * SPAN), LOW),
            like,
        ],
        compiler_params=params(),
        cost_estimate=cost(10),
        name="attend",
    )(tokens, w_qkv, rows)


def unit_norm(resid):
    centred = resid - jnp.mean(resid, axis=-1, keepdims=True)
    inverse = lax.rsqrt(jnp.mean(centred * centred, axis=-1, keepdims=True) + 1e-06)
    return centred * inverse, inverse


def gelu_pair(x):
    z = jnp.abs(x) * 0.7071067811865476
    base = 1.0 + 0.3275911 * z
    t = pltpu.reciprocal(base, approx=True)
    t = t * (2.0 - base * t)
    poly = 0.5 * 1.061405429
    for term in (-1.453152027, 1.421413741, -0.284496736, 0.254829592):
        poly = poly * t + 0.5 * term
    gauss = jnp.exp(-(z * z))
    tail = poly * t * gauss
    cdf = jnp.where(x < 0, tail, 1.0 - tail)
    return x * cdf, cdf + x * gauss * 0.3989422804014327


def feed_kernel(
    place, counts, tokens, attended, w_attn, w_in, w_out, rows,
    enc_out, hid_out, slope_out, norm_out, u1_out, i1_out, u2_out, i2_out,
):
    resid = tokens[...].astype(F32) + dot(attended[...], w_attn[...]) + row_of(rows, 6)
    unit_one, inverse_one = unit_norm(resid)
    normed = unit_one * row_of(rows, 0) + row_of(rows, 2)
    u1_out[...] = unit_one.astype(LOW)
    i1_out[...] = inverse_one
    norm_out[...] = normed.astype(LOW)
    step = 256
    for at in range(0, FF, step):
        bias = rows[:, 8 * D + at : 8 * D + at + step]
        pre_act = dot(norm_out[...], w_in[:, at : at + step]) + bias
        hidden, slope = gelu_pair(pre_act)
        hid_out[:, at : at + step] = hidden.astype(LOW)
        slope_out[:, at : at + step] = slope.astype(LOW)
    resid = normed + dot(hid_out[...], w_out[...]) + row_of(rows, 7)
    unit_two, inverse_two = unit_norm(resid)
    u2_out[...] = unit_two.astype(LOW)
    i2_out[...] = inverse_two
    live = live_rows(place, counts, pl.program_id(0) * TALL, TALL)
    enc_out[...] = (live * (unit_two * row_of(rows, 1) + row_of(rows, 3))).astype(LOW)


def feed(place, counts, tokens, attended, w_attn, w_in, w_out, rows):
    total = tokens.shape[0]
    tall = lambda width: pl.BlockSpec((TALL, width), lambda i: (i, 0))
    like = lambda width, kind: jax.ShapeDtypeStruct((total, width), kind)
    return pl.pallas_call(
        feed_kernel,
        grid=(total // TALL,),
        in_specs=[SMEM, SMEM, tall(D), tall(D)]
        + [whole(a.shape) for a in (w_attn, w_in, w_out, rows)],
        out_specs=[tall(D), tall(FF), tall(FF), tall(D), tall(D), tall(1), tall(D), tall(1)],
        out_shape=[
            like(D, LOW), like(FF, LOW), like(FF, LOW), like(D, LOW),
            like(D, LOW), like(1, F32), like(D, LOW), like(1, F32),
        ],
        compiler_params=params(),
        cost_estimate=cost(26),
        name="feed",
    )(place, counts, tokens, attended, w_attn, w_in, w_out, rows)


def norm_back(grad_out, unit_rows, inverse, gain):
    scaled = grad_out * gain
    along = jnp.mean(scaled * unit_rows, axis=-1, keepdims=True)
    return inverse * (scaled - jnp.mean(scaled, axis=-1, keepdims=True) - unit_rows * along)


def column_sums(*arrays):
    return [jnp.sum(a, axis=0, keepdims=True) for a in arrays]


def outer_kernel(place, counts, out_grad, grad_cls, unit_two, inverse_two, rows, two_out, low_out, vec_out):
    spot = lax.broadcasted_iota(jnp.int32, (SPAN, 1), 0) == 0
    sums = None
    for span in range(out_grad.shape[0] // SPAN):
        at = slice(span * SPAN, (span + 1) * SPAN)
        added = jnp.where(spot, grad_cls[span : span + 1], 0.0)
        live = live_rows(place, counts, span * SPAN, SPAN)
        grad_y = live * (out_grad[at].astype(F32) + added)
        unit_rows = unit_two[at].astype(F32)
        grad_two = norm_back(grad_y, unit_rows, inverse_two[at], row_of(rows, 1))
        two_out[at] = grad_two
        low_out[at] = grad_two.astype(LOW)
        here = column_sums(grad_y * unit_rows, grad_y, grad_two)
        sums = here if sums is None else [a + b for a, b in zip(sums, here)]
    for index, total in enumerate(sums):
        vec_out[index : index + 1] = total


def outer_grad(place, counts, out_grad, grad_cls, unit_two, inverse_two, rows):
    total = out_grad.shape[0]
    return pl.pallas_call(
        outer_kernel,
        in_specs=[SMEM, SMEM] + [pl.BlockSpec(memory_space=pltpu.VMEM)] * 5,
        out_shape=[
            jax.ShapeDtypeStruct((total, D), F32),
            jax.ShapeDtypeStruct((total, D), LOW),
            jax.ShapeDtypeStruct((3, D), F32),
        ],
        compiler_params=params(),
        cost_estimate=cost(5),
        name="outer",
    )(place, counts, out_grad, grad_cls, unit_two, inverse_two, rows)


def weight_kernel(panels, after, side, *refs):
    *sides, out = refs[after:]

    @pl.when(pl.program_id(0) < panels)
    def _():
        out[0] = dot(sides[0][...], sides[1][...], (0, 0)).astype(LOW)

    if len(sides) > 2:

        @pl.when(pl.program_id(0) == panels)
        def _():
            out[0] = dot(sides[2][...], sides[3][...], (0, 0)).astype(LOW)


def weight_half(hint, after, side, left_side, right_side, panels, banded, extra=()):
    total = left_side.shape[0]
    half = D // 2
    every = panels + len(extra) // 2
    tall = lambda width, at: pl.BlockSpec((total, width), at)
    last = lambda panel: jnp.minimum(panel, panels - 1)
    left_at = lambda panel, side: (0, last(panel) * 2 + side[0] if banded else side[0])
    right_at = lambda panel, side: (0, 0 if banded else last(panel))
    more = [tall(half, lambda p, s: (0, s[0])), tall(D, lambda p, s: (0, 0))]
    return pl.pallas_call(
        partial(weight_kernel, panels, len(after)),
        grid_spec=pltpu.PrefetchScalarGridSpec(
            num_scalar_prefetch=1,
            grid=(every,),
            in_specs=[ANY] * len(after)
            + [tall(half, left_at), tall(D, right_at)]
            + more[: len(extra)],
            out_specs=pl.BlockSpec((1, half, D), lambda p, s: (p, 0, 0)),
        ),
        out_shape=jax.ShapeDtypeStruct((every, half, D), LOW),
        compiler_params=params(),
        cost_estimate=cost(hint),
        name="weight",
    )(side.reshape(1), *after, left_side, right_side, *extra)


def slope_kernel(*refs):
    low, slope, w_out, pre_out, vec_out = refs[-5:]
    step = 256
    for at in range(0, pre_out.shape[1], step):
        here = slice(at, at + step)
        grad_pre = dot(low[...], w_out[here], (1, 1)) * slope[:, here].astype(F32)
        pre_out[:, here] = grad_pre.astype(LOW)
        vec_out[0, :, here] = jnp.sum(grad_pre, axis=0, keepdims=True)


def slope_grad(after, low, slope, w_out):
    total = low.shape[0]
    band = pl.BlockSpec((total, D), lambda i: (0, i))
    return pl.pallas_call(
        slope_kernel,
        grid=(FF // D,),
        in_specs=[ANY] * len(after)
        + [whole(low.shape), band, pl.BlockSpec((D, D), lambda i: (i, 0))],
        out_specs=[band, pl.BlockSpec((1, 1, D), lambda i: (i, 0, 0))],
        out_shape=[
            jax.ShapeDtypeStruct((total, FF), LOW),
            jax.ShapeDtypeStruct((FF // D, 1, D), F32),
        ],
        compiler_params=params(),
        cost_estimate=cost(9),
        name="slope",
    )(*after, low, slope, w_out)


def inner_kernel(*refs):
    pre_low, grad_two, unit_one, inverse_one, w_attn, w_in, rows = refs[-11:-4]
    one_out, mixed_out, ga_out, vec_out = refs[-4:]
    first = pl.program_id(0) == 0

    @pl.when(first)
    def _():
        vec_out[...] = jnp.zeros_like(vec_out)

    grad_normed = grad_two[...] + dot(pre_low[...], w_in[...], (1, 1))
    unit_rows = unit_one[...].astype(F32)
    grad_one = norm_back(grad_normed, unit_rows, inverse_one[...], row_of(rows, 0))
    one_out[...] = grad_one
    mixed = grad_one.astype(LOW)
    mixed_out[...] = mixed
    ga_out[...] = dot(mixed, w_attn[...], (1, 1)).astype(LOW)
    for index, total in enumerate(column_sums(grad_normed * unit_rows, grad_normed, grad_one)):
        vec_out[index : index + 1] += total


def inner_grad(after, pre_low, grad_two, unit_one, inverse_one, w_attn, w_in, rows):
    total = pre_low.shape[0]
    tall = lambda width: pl.BlockSpec((TALL, width), lambda i: (i, 0))
    like = lambda width, kind: jax.ShapeDtypeStruct((total, width), kind)
    return pl.pallas_call(
        inner_kernel,
        grid=(total // TALL,),
        in_specs=[ANY] * len(after)
        + [tall(FF), tall(D), tall(D), tall(1)]
        + [whole(a.shape) for a in (w_attn, w_in, rows)],
        out_specs=[tall(D), tall(D), tall(D), whole((3, D))],
        out_shape=[
            like(D, F32), like(D, LOW), like(D, LOW), jax.ShapeDtypeStruct((3, D), F32),
        ],
        compiler_params=params(),
        cost_estimate=cost(12),
        name="inner",
    )(*after, pre_low, grad_two, unit_one, inverse_one, w_attn, w_in, rows)


def unattend_kernel(*refs):
    q, k, v, p, ga, stack_out, vec_out = refs[-7:]
    scaling = HEAD ** (-0.5)
    first = pl.program_id(0) == 0

    @pl.when(first)
    def _():
        vec_out[...] = jnp.zeros_like(vec_out)

    for span in range(p.shape[0]):
        at = slice(span * SPAN, (span + 1) * SPAN)
        for pair in range(HEADS // 2):
            lo = pair * 2 * HEAD
            lanes = slice(lo, lo + 2 * HEAD)
            weights = p[span, pair]
            grad = ga[at, lanes]
            spread_out = dot(grad, split_heads(v[at, lanes]), (1, 1))
            wide = weights.astype(F32)
            parts = []
            for half in range(2):
                cols = slice(half * SPAN, (half + 1) * SPAN)
                wgt, gw = wide[:, cols], spread_out[:, cols]
                parts.append((wgt * (gw - jnp.sum(gw * wgt, axis=-1, keepdims=True))).astype(LOW))
            grad_scores = jnp.concatenate(parts, axis=1)
            grad_q = dot(grad_scores, split_heads(k[at, lanes])) * scaling
            tall_scores = jnp.concatenate(parts, axis=0)
            tall_weights = jnp.concatenate([weights[:, :SPAN], weights[:, SPAN:]], axis=0)
            grad_k = dot(tall_scores, split_heads(q[at, lanes]), (0, 0))
            grad_v = dot(tall_weights, split_heads(grad), (0, 0))
            stack_out[at, lo : lo + 2 * HEAD] = grad_q.astype(LOW)
            stack_out[at, D + lo : D + lo + 2 * HEAD] = grad_k.astype(LOW)
            stack_out[at, 2 * D + lo : 2 * D + lo + 2 * HEAD] = grad_v.astype(LOW)
            vec_out[0:1, lanes] += jnp.sum(grad_q, axis=0, keepdims=True)
            vec_out[1:2, lanes] += jnp.sum(grad_v, axis=0, keepdims=True)


def unattend(after, part, parts, q, k, v, p, ga, stack=None):
    total = q.shape[0]
    count = total // SPAN // parts
    first = part * count
    tall = lambda width: pl.BlockSpec((SPAN, width), lambda i: (first + i, 0))
    after = after if stack is None else [stack] + after
    return pl.pallas_call(
        unattend_kernel,
        grid=(count,),
        in_specs=[ANY] * len(after)
        + [tall(D)] * 3
        + [
            pl.BlockSpec((1, HEADS // 2, SPAN, 2 * SPAN), lambda i: (first + i, 0, 0, 0)),
            tall(D),
        ],
        out_specs=[tall(3 * D), whole((2, D))],
        out_shape=[
            jax.ShapeDtypeStruct((total, 3 * D), LOW),
            jax.ShapeDtypeStruct((2, D), F32),
        ],
        input_output_aliases={} if stack is None else {0: 0},
        compiler_params=params(),
        cost_estimate=cost(8),
        name="unattend",
    )(*after, q, k, v, p, ga)


def input_kernel(*refs):
    grad_one, stack, w_qkv, out = refs[-4:]
    total = grad_one[...]
    for index in range(3):
        total += dot(stack[:, index * D : (index + 1) * D], w_qkv[index], (1, 1))
    out[...] = total


def input_grad(after, grad_one, stack, w_qkv):
    total = grad_one.shape[0]
    tall = lambda width: pl.BlockSpec((TALL, width), lambda i: (i, 0))
    return pl.pallas_call(
        input_kernel,
        grid=(total // TALL,),
        in_specs=[ANY] * len(after) + [tall(D), tall(3 * D), whole(w_qkv.shape)],
        out_specs=tall(D),
        out_shape=jax.ShapeDtypeStruct((total, D), F32),
        compiler_params=params(),
        cost_estimate=cost(8),
        name="input",
    )(*after, grad_one, stack, w_qkv)


def contrast_kernel(slots, place, rows, counts, partners, loss_out, grad_out):
    total, scale = rows.shape[0], 2.0 * D ** (-0.5)

    def number(shape, axis):
        at = lax.broadcasted_iota(jnp.int32, shape, axis)
        return (at // GROUP) ^ place[0], at % GROUP

    device, slot = number((counts.shape[1], total), 1)
    hit = lax.broadcasted_iota(jnp.int32, device.shape, 0) == device
    count = dot(counts[...].astype(LOW), jnp.where(hit, 1.0, 0.0).astype(LOW))
    live_across = (slot[:1].astype(F32) < count) & (slot[:1] < slots)
    device, slot = number((total, counts.shape[1]), 0)
    hit = lax.broadcasted_iota(jnp.int32, device.shape, 1) == device
    count = jnp.sum(jnp.where(hit, counts[...], 0.0), axis=1, keepdims=True)
    live_down = (slot[:, :1].astype(F32) < count) & (slot[:, :1] < slots)
    device, slot = number((total, partners.shape[1]), 0)
    own_id = device * slots + slot
    hit = lax.broadcasted_iota(jnp.int32, own_id.shape, 1) == own_id
    pair = jnp.sum(jnp.where(hit, partners[...], 0.0), axis=1, keepdims=True)
    device, slot = number((total, total), 0)
    down = (device * slots + slot).astype(F32)
    device, slot = number((total, total), 1)
    across = (device * slots + slot).astype(F32)
    valid = live_across & (down != across)
    matched = jnp.where((slot < slots) & (pair == across), 1.0, 0.0)
    anchor = jnp.where(live_down & (pair != down[:, :1]), 1.0, 0.0)
    similar = dot(rows[...], rows[...], (1, 1)) * scale
    masked = jnp.where(valid, similar, -1e30)
    peak = jnp.max(masked, axis=1, keepdims=True)
    summed = jnp.sum(jnp.where(valid, jnp.exp(masked - peak), 0.0), axis=1, keepdims=True)
    log_total = jnp.log(summed) + peak
    positive = jnp.sum(matched * similar, axis=1, keepdims=True)
    loss_out[...] = jnp.sum(anchor * (log_total - positive), axis=0, keepdims=True)
    grad = (anchor * (jnp.where(valid, jnp.exp(masked - log_total), 0.0) - matched)).astype(LOW)
    own = lax.broadcasted_iota(jnp.int32, (GROUP, total), 0)
    own = jnp.where(own == lax.broadcasted_iota(jnp.int32, (GROUP, total), 1), 1.0, 0.0)
    down_part = dot(dot(own.astype(LOW), grad, (1, 1)).astype(LOW), rows[...])
    grad_out[...] = (dot(grad[: 2 * GROUP], rows[...])[:GROUP] + down_part) * scale


def contrast(cls_rows, span_count, pair_index, device, slots):
    total = cls_rows.shape[0]
    return pl.pallas_call(
        partial(contrast_kernel, slots),
        in_specs=[pl.BlockSpec(memory_space=pltpu.SMEM)]
        + [pl.BlockSpec(memory_space=pltpu.VMEM)] * 3,
        out_shape=[
            jax.ShapeDtypeStruct((1, 1), F32),
            jax.ShapeDtypeStruct((GROUP, D), F32),
        ],
        compiler_params=params(),
        cost_estimate=cost(3),
        name="contrast",
    )(
        device,
        cls_rows,
        span_count.astype(F32).reshape(1, -1),
        pair_index.astype(F32).reshape(1, -1),
    )


def adam_kernel(
    packed, position, gathered, master, first, second, left, right,
    master_out, first_out, second_out, low_out, *scratch,
):
    quarter = D // 4
    slot = pl.program_id(0)
    if packed:
        owned = scratch[0]
        shares, tall, _ = gathered.shape
        rows = D // shares

        @pl.when(slot == 0)
        def _():
            def place(share, carry):
                block = gathered[share].astype(F32)
                at = pl.multiple_of((share ^ position[0]) * rows, rows)
                for index in range(owned.shape[0]):
                    lo = index * rows % tall
                    side = index * rows // tall
                    piece = block[lo : lo + rows, side * quarter : (side + 1) * quarter]
                    owned[index, pl.ds(at, rows), :] = piece
                return carry

            lax.fori_loop(0, shares, place, 0)

        gradient = owned[slot].astype(LOW)
    else:
        gradient = gathered[0]
    low_left, low_right = left[0].astype(LOW), right[0].astype(LOW)
    turned = dot(gradient, low_left, (0, 0))
    turned = dot(low_right, turned.astype(LOW), (0, 0))
    new_first = 0.9 * first[0] + 0.1 * turned
    new_second = 0.999 * second[0] + 0.001 * turned * turned
    first_out[0] = new_first
    second_out[0] = new_second
    spread_by = jnp.sqrt(new_second * (1.0 / (1.0 - 0.999**STEP))) + 1e-08
    update = new_first * (1.0 / (1.0 - 0.9**STEP)) / spread_by
    update = dot(update.astype(LOW), low_left, (1, 1))
    update = dot(low_right, update.astype(LOW))
    new_master = master[0] - RATE * (update + DECAY * master[0])
    master_out[0] = new_master
    low_out[0] = new_master.astype(LOW)


def to_owned(gathered, position, per_owner):
    quarter = D // 4
    gathered = jnp.take(gathered, jnp.arange(gathered.shape[0]) ^ position, axis=0)
    flat = jnp.concatenate([gathered[..., :quarter], gathered[..., quarter:]], axis=1)
    rows = flat.shape[1] // per_owner
    flat = flat.reshape(flat.shape[0], per_owner, rows, quarter).transpose(1, 0, 2, 3)
    return flat.reshape(per_owner, D, quarter)


def rotated_adam(position, gathered, master, first_moment, second_moment, left_basis, right_basis):
    per_owner, _, quarter = master.shape
    turn = lambda a: a.transpose(0, 2, 1)
    rows = D // gathered.shape[0]
    packed = rows % 8 == 0 and per_owner % 2 == 0
    if not packed:
        gathered = to_owned(gathered, position, per_owner)
    block = lambda a: pl.BlockSpec((1,) + a.shape[1:], lambda s, p: (s, 0, 0))
    operands = (turn(master), turn(first_moment), turn(second_moment), left_basis, right_basis)
    like = jax.ShapeDtypeStruct(operands[0].shape, F32)
    fixed = pl.BlockSpec(gathered.shape, lambda s, p: (0, 0, 0))
    outputs = pl.pallas_call(
        partial(adam_kernel, packed),
        grid_spec=pltpu.PrefetchScalarGridSpec(
            num_scalar_prefetch=1,
            grid=(per_owner,),
            in_specs=[fixed if packed else block(gathered)] + [block(a) for a in operands],
            out_specs=[block(operands[0])] * 4,
            scratch_shapes=[pltpu.VMEM((per_owner, D, quarter), F32)] if packed else [],
        ),
        out_shape=[like, like, like, jax.ShapeDtypeStruct(like.shape, LOW)],
        compiler_params=params(),
        cost_estimate=cost(20),
        name="adam",
    )(position.reshape(1), gathered, *operands)
    return [turn(a) for a in outputs]


def axis_bits(name):
    size = lax.axis_size(name)
    return [(name, 1 << k) for k in range(size.bit_length() - 1)]


def bit_of(step):
    return jnp.where((lax.axis_index(step[0]) & step[1]) != 0, 1, 0)


def swap(send, step):
    size = lax.axis_size(step[0])
    return lax.ppermute(send, step[0], [(i, i ^ step[1]) for i in range(size)])


def pick(array, index, dim):
    return lax.dynamic_index_in_dim(array, index, dim, False)


def gather_all(rows):
    for step in axis_bits("col") + axis_bits("row"):
        rows = jnp.concatenate([rows, swap(rows, step)])
    return rows


def row_steps():
    row_bits, col_bits = axis_bits("row"), axis_bits("col")
    core, across = row_bits[:1], row_bits[1:][::-1]
    y_bits, z_bits = col_bits[:-2][::-1], col_bits[-2:]
    return core, across, y_bits, z_bits


def launch(part, step, left, rider=None):
    dim = 1 + left.index(step)
    bit = bit_of(step)
    left.remove(step)
    send, keep = pick(part, 1 - bit, dim), pick(part, bit, dim)
    shape, flat = send.shape, send.reshape(-1, send.shape[-1])
    message = flat
    if rider is not None:
        message = jnp.concatenate([flat, rider.astype(LOW).reshape(-1, flat.shape[1])])
    other = swap(message, step)
    total = landed(keep, other[: flat.shape[0]].reshape(shape))
    if rider is not None:
        rider = rider + other[flat.shape[0] :].reshape(rider.shape).astype(F32)
    return message, total, rider


def landed(keep, other):
    return (keep.astype(F32) + other.astype(F32)).astype(LOW)


def begin_sum(send):
    return swap(send, row_steps()[0][0])


def reduce_panels(other, keep, rider=None):
    core, across, y_bits, z_bits = row_steps()
    left = across + y_bits + z_bits
    sends = []
    part = landed(keep, other)
    if rider is not None:
        rider = rider + swap(rider, core[0])
    width = part.shape[1] >> len(left)
    part = part.reshape(part.shape[:1] + (2,) * len(left) + (width, D))
    sides = [part[..., : D // 2], part[..., D // 2 :]]
    rest = [list(left), list(left)]
    for first, second in zip(across + y_bits, y_bits + across):
        sent, one, rider = launch(sides[0], first, rest[0], rider)
        also, two, _ = launch(sides[1], second, rest[1])
        sends.append([sent, also])
        sides = [one, two]
    part, left = jnp.concatenate(sides, axis=-1), list(z_bits)
    for step in z_bits:
        sent, part, rider = launch(part, step, left, rider)
        sends.append([sent])
    return part, sends, rider


def slots_kernel(cols, after, owners, *refs):
    parts, out, blocks, packed = refs[after:-3], refs[-3], refs[-2], refs[-1]
    quarter = D // 4
    at = 0
    for part in parts:
        for panel in range(part.shape[0]):
            value = part[panel].astype(F32)
            for index in range(4):
                blocks[at] = value[:, index * quarter : (index + 1) * quarter]
                at += 1
    rows, half = blocks.shape[1], packed.shape[1]
    for slot in range(at):
        col, place = divmod(slot, at // cols)
        value = blocks[owners[slot]]
        first = place * rows
        for side in range(2):
            lo, hi = max(first, side * half), min(first + rows, (side + 1) * half)
            if lo < hi:
                lanes = slice(side * quarter, (side + 1) * quarter)
                packed[col, lo - side * half : hi - side * half, lanes] = value[lo - first : hi - first]
    out[...] = packed[...].astype(LOW)


def to_slots(after, parts, owner_list):
    quarter, cols = D // 4, lax.axis_size("col")
    panels, rows = sum(part.shape[0] for part in parts), parts[0].shape[1]
    shape = (cols, panels * 4 // cols * rows // 2, 2 * quarter)
    return pl.pallas_call(
        partial(slots_kernel, cols, len(after)),
        in_specs=[SMEM] + [ANY] * len(after) + [pl.BlockSpec(memory_space=pltpu.VMEM)] * len(parts),
        out_shape=jax.ShapeDtypeStruct(shape, LOW),
        scratch_shapes=[pltpu.VMEM((panels * 4, rows, quarter), F32), pltpu.VMEM(shape, F32)],
        compiler_params=params(),
        cost_estimate=cost(4),
        name="slots",
    )(owner_list, *after, *parts)


def spread(slots):
    core, across, y_bits, z_bits = row_steps()
    tail = slots.shape[1:]
    left = axis_bits("col")[::-1]
    part = slots.reshape((1,) + (2,) * len(left) + tail)
    for step in (y_bits + z_bits)[::-1]:
        dim = 1 + left.index(step)
        bit = bit_of(step)
        other = swap(pick(part, 1 - bit, dim), step)
        part = jnp.concatenate([pick(part, bit, dim), other])
        left.remove(step)
    for step in (core + across)[::-1]:
        part = jnp.concatenate([part, swap(part, step)])
    return part


def row_place():
    place = 0
    for group in row_steps():
        for step in group:
            place = place * 2 + bit_of(step)
    return place


def shards(
    tokens,
    w_qkv,
    w_attn_out,
    w_in,
    w_out,
    vectors,
    out_grad,
    span_count,
    pair_index,
    owner_list,
    master,
    first_moment,
    second_moment,
    left_basis,
    right_basis,
    vec_first,
    vec_second,
):
    slots = tokens.shape[0] // SPAN
    device = (lax.axis_index("row") * lax.axis_size("col") + lax.axis_index("col")).reshape(1)
    core, across, y_bits, z_bits = row_steps()
    core_bit = bit_of(core[0])
    rows = vectors.reshape(1, -1)
    q, k, v, p, attended = attend(tokens, w_qkv, rows)
    encoded, hidden, slope, normed_low, unit_one, inverse_one, unit_two, inverse_two = feed(
        device, span_count, tokens, attended, w_attn_out, w_in, w_out, rows
    )
    cls_rows = jnp.pad(encoded.reshape(slots, SPAN, D)[:, 0], ((0, GROUP - slots), (0, 0)))
    loss, grad_cls = contrast(gather_all(cls_rows), span_count, pair_index, device, slots)
    grad_two, outer_low, vec_two = outer_grad(
        device, span_count, out_grad, grad_cls, unit_two, inverse_two, rows
    )
    outer_args = (hidden, outer_low, FF // D, True)
    outer_away = weight_half(8, [], 1 - core_bit, *outer_args)
    outer_here = weight_half(60, [outer_away], core_bit, *outer_args)
    outer_sum, outer_sent, _ = reduce_panels(begin_sum(outer_away), outer_here)
    pre_low, vec_inner = slope_grad(outer_sent[0], outer_low, slope, w_out)
    grad_one, mixed_low, grad_attended, vec_one = inner_grad(
        [], pre_low, grad_two, unit_one, inverse_one, w_attn_out, w_in, rows
    )
    inner_args = (normed_low, pre_low, FF // D, False, (attended, mixed_low))
    inner_away = weight_half(8, outer_sent[1], 1 - core_bit, *inner_args)
    inner_here = weight_half(60, [inner_away] + outer_sent[2], core_bit, *inner_args)
    inner_sum, inner_sent, _ = reduce_panels(begin_sum(inner_away), inner_here)
    early, vec_early = unattend(
        outer_sent[3] + inner_sent[0], 0, 2, q, k, v, p, grad_attended
    )
    stack_low, vec_late = unattend([outer_sum], 1, 2, q, k, v, p, grad_attended, early)
    project_args = (tokens, stack_low, 3, False)
    project_away = weight_half(8, inner_sent[1], 1 - core_bit, *project_args)
    project_here = weight_half(60, [project_away] + inner_sent[2], core_bit, *project_args)
    vec_heads = vec_early + vec_late
    grad_vector = jnp.concatenate(
        [
            jnp.stack([vec_one[0], vec_two[0], vec_one[1], vec_two[1]]),
            vec_heads,
            jnp.stack([vec_one[2], vec_two[2]]),
            vec_inner[:, 0],
        ]
    )
    project_sum, project_sent, vec_grad = reduce_panels(
        begin_sum(project_away), project_here, grad_vector
    )
    grad_tokens = input_grad(
        inner_sent[3] + project_sent[0], grad_one, stack_low, w_qkv
    )
    parts = (project_sum, inner_sum[-1:], inner_sum[:-1], outer_sum)
    gathered = spread(to_slots([grad_tokens], parts, owner_list))
    vec_grad = vec_grad.reshape(-1)
    new_master, new_first, new_second, master_copy = rotated_adam(
        row_place(), gathered, master, first_moment, second_moment, left_basis, right_basis
    )
    vec_first_new = 0.9 * vec_first + 0.1 * vec_grad
    vec_second_new = 0.999 * vec_second + 0.001 * vec_grad * vec_grad
    vec_step = (
        vec_first_new / (1.0 - 0.9**STEP) / (jnp.sqrt(vec_second_new / (1.0 - 0.999**STEP)) + 1e-08)
    )
    vec_new = vectors - VECTOR_RATE * vec_step
    return (
        encoded,
        grad_tokens,
        loss[0, 0],
        new_master,
        new_first,
        new_second,
        master_copy,
        vec_new,
        vec_first_new,
        vec_second_new,
    )


def solution(mesh):
    in_specs = (
        P(("row", "col"), None),
        P(),
        P(),
        P(),
        P(),
        P(),
        P(("row", "col"), None),
        P(),
        P(),
        P(),
        P("col", None, None),
        P("col", None, None),
        P("col", None, None),
        P("col", None, None),
        P("col", None, None),
        P(),
        P(),
    )
    out_specs = (
        P(("row", "col"), None),
        P(("row", "col"), None),
        P(),
        P("col", None, None),
        P("col", None, None),
        P("col", None, None),
        P("col", None, None),
        P(),
        P(),
        P(),
    )
    return jax.shard_map(shards, mesh=mesh, in_specs=in_specs, out_specs=out_specs, check_vma=False)
```

```python
from functools import partial

import jax
import jax.numpy as jnp
from jax import lax
from jax.experimental import pallas as pl
from jax.experimental.pallas import tpu as pltpu
from jax.sharding import PartitionSpec as P

D = 768
HEADS = 12
HEAD = 64
FF = 3072
SPAN = 128
STEP = 10
GROUP = 8

RATE = 0.01
DECAY = 0.01
VECTOR_RATE = 0.3

LOW = jnp.bfloat16
F32 = jnp.float32
TALL = 2 * SPAN
VMEM_LIMIT = 36 * 1024 * 1024


def dot(left_side, right_side, contract=(1, 0)):
    dims = (((contract[0],), (contract[1],)), ((), ()))
    return lax.dot_general(left_side, right_side, dims, preferred_element_type=F32)


def whole(shape):
    return pl.BlockSpec(shape, lambda *ids: (0,) * len(shape))


def cost(microseconds, transcendentals=0):
    return pl.CostEstimate(
        flops=int(microseconds * 1.1e9), bytes_accessed=0, transcendentals=transcendentals
    )


def params():
    return pltpu.CompilerParams(vmem_limit_bytes=VMEM_LIMIT)


def row_of(rows, index):
    return rows[:, index * D : (index + 1) * D]


def live_rows(place, counts, first_row, height):
    at = first_row + lax.broadcasted_iota(jnp.int32, (height, 1), 0)
    return jnp.where(at < counts[place[0]] * SPAN, 1.0, 0.0)


ANY = pl.BlockSpec(memory_space=pl.ANY)
SMEM = pl.BlockSpec(memory_space=pltpu.SMEM)


def split_heads(pair):
    lane = lax.broadcasted_iota(jnp.int32, pair.shape, 1)
    zero = jnp.zeros_like(pair)
    return jnp.concatenate([jnp.where(lane < HEAD, pair, zero), jnp.where(lane < HEAD, zero, pair)])


def normalise(scores):
    peak = jnp.max(scores, axis=-1, keepdims=True)
    raised = jnp.exp(scores - peak)
    return raised * (1.0 / jnp.sum(raised, axis=-1, keepdims=True))


def attend_kernel(tokens, w_qkv, rows, q_out, k_out, v_out, p_out, a_out):
    block = tokens[...]
    scaling = HEAD ** (-0.5)
    q_out[...] = ((dot(block, w_qkv[0]) + row_of(rows, 4)).astype(LOW) * scaling).astype(LOW)
    k_out[...] = dot(block, w_qkv[1]).astype(LOW)
    v_out[...] = (dot(block, w_qkv[2]) + row_of(rows, 5)).astype(LOW)
    for span in range(TALL // SPAN):
        at = slice(span * SPAN, (span + 1) * SPAN)
        for pair in range(HEADS // 2):
            lanes = slice(pair * 2 * HEAD, (pair + 1) * 2 * HEAD)
            scores = dot(q_out[at, lanes], split_heads(k_out[at, lanes]), (1, 1))
            weights = jnp.concatenate(
                [normalise(scores[:, :SPAN]), normalise(scores[:, SPAN:])], axis=1
            ).astype(LOW)
            p_out[span, pair] = weights
            a_out[at, lanes] = dot(weights, split_heads(v_out[at, lanes])).astype(LOW)


def attend(tokens, w_qkv, rows):
    total = tokens.shape[0]
    tall = pl.BlockSpec((TALL, D), lambda i: (i, 0))
    like = jax.ShapeDtypeStruct((total, D), LOW)
    spans = TALL // SPAN
    return pl.pallas_call(
        attend_kernel,
        grid=(total // TALL,),
        in_specs=[tall, whole(w_qkv.shape), whole(rows.shape)],
        out_specs=[
            tall,
            tall,
            tall,
            pl.BlockSpec((spans, HEADS // 2, SPAN, 2 * SPAN), lambda i: (i, 0, 0, 0)),
            tall,
        ],
        out_shape=[
            like,
            like,
            like,
            jax.ShapeDtypeStruct((total // SPAN, HEADS // 2, SPAN, 2 * SPAN), LOW),
            like,
        ],
        compiler_params=params(),
        cost_estimate=cost(10),
        name="attend",
    )(tokens, w_qkv, rows)


def unit_norm(resid):
    centred = resid - jnp.mean(resid, axis=-1, keepdims=True)
    inverse = lax.rsqrt(jnp.mean(centred * centred, axis=-1, keepdims=True) + 1e-06)
    return centred * inverse, inverse


def gelu_pair(x):
    cdf = 0.5 + 0.5 * lax.erf(x * 0.7071067811865476)
    return x * cdf, cdf + x * jnp.exp(-0.5 * x * x) * 0.3989422804014327


def feed_kernel(
    place, counts, tokens, attended, w_attn, w_in, w_out, rows, bias,
    enc_out, hid_out, slope_out, norm_out, u1_out, i1_out, u2_out, i2_out, total,
):
    band = pl.program_id(0)
    chunks = [slice(at, at + TALL) for at in range(0, tokens.shape[0], TALL)]

    @pl.when(band == 0)
    def _():
        for at in chunks:
            resid = tokens[at].astype(F32) + dot(attended[at], w_attn[...]) + row_of(rows, 6)
            unit_one, inverse_one = unit_norm(resid)
            value = unit_one * row_of(rows, 0) + row_of(rows, 2)
            u1_out[at] = unit_one.astype(LOW)
            i1_out[at] = inverse_one
            norm_out[at] = value.astype(LOW)
            total[at] = value + row_of(rows, 7)

    step = 256
    for at in range(0, hid_out.shape[1], step):
        here = slice(at, at + step)
        pre_act = dot(norm_out[...], w_in[:, here]) + bias[:, here]
        hidden, slope = gelu_pair(pre_act)
        hid_out[:, here] = hidden.astype(LOW)
        slope_out[:, here] = slope.astype(LOW)

    @pl.when(band < pl.num_programs(0) - 1)
    def _():
        total[...] += dot(hid_out[...], w_out[...])

    @pl.when(band == pl.num_programs(0) - 1)
    def _():
        for at in chunks:
            resid = total[at] + dot(hid_out[at], w_out[...])
            unit_two, inverse_two = unit_norm(resid)
            u2_out[at] = unit_two.astype(LOW)
            i2_out[at] = inverse_two
            live = live_rows(place, counts, at.start, TALL)
            value = live * (unit_two * row_of(rows, 1) + row_of(rows, 3))
            enc_out[at] = value.astype(LOW)


def feed(place, counts, tokens, attended, w_attn, w_in, w_out, rows):
    total = tokens.shape[0]
    tall = lambda width: pl.BlockSpec((total, width), lambda j: (0, 0))
    band = lambda height: pl.BlockSpec((height, D), lambda j: (0, j))
    like = lambda width, kind: jax.ShapeDtypeStruct((total, width), kind)
    return pl.pallas_call(
        feed_kernel,
        grid=(FF // D,),
        in_specs=[
            SMEM, SMEM, tall(D), tall(D), whole(w_attn.shape), band(D),
            pl.BlockSpec((D, D), lambda j: (j, 0)),
            pl.BlockSpec((1, 8 * D), lambda j: (0, 0)),
            pl.BlockSpec((1, D), lambda j: (0, 8 + j)),
        ],
        out_specs=[
            tall(D), band(total), band(total), tall(D), tall(D), tall(1), tall(D), tall(1),
        ],
        out_shape=[
            like(D, LOW), like(FF, LOW), like(FF, LOW), like(D, LOW),
            like(D, LOW), like(1, F32), like(D, LOW), like(1, F32),
        ],
        scratch_shapes=[pltpu.VMEM((total, D), F32)],
        compiler_params=params(),
        cost_estimate=cost(20),
        name="feed",
    )(place, counts, tokens, attended, w_attn, w_in, w_out, rows, rows)


def norm_back(grad_out, unit_rows, inverse, gain):
    scaled = grad_out * gain
    along = jnp.mean(scaled * unit_rows, axis=-1, keepdims=True)
    return inverse * (scaled - jnp.mean(scaled, axis=-1, keepdims=True) - unit_rows * along)


def column_sums(*arrays):
    return [jnp.sum(a, axis=0, keepdims=True) for a in arrays]


def outer_kernel(place, counts, out_grad, grad_cls, unit_two, inverse_two, rows, two_out, low_out, vec_out):
    spot = lax.broadcasted_iota(jnp.int32, (SPAN, 1), 0) == 0
    sums = None
    for span in range(out_grad.shape[0] // SPAN):
        at = slice(span * SPAN, (span + 1) * SPAN)
        added = jnp.where(spot, grad_cls[span : span + 1], 0.0)
        live = live_rows(place, counts, span * SPAN, SPAN)
        grad_y = live * (out_grad[at].astype(F32) + added)
        unit_rows = unit_two[at].astype(F32)
        grad_two = norm_back(grad_y, unit_rows, inverse_two[at], row_of(rows, 1))
        two_out[at] = grad_two
        low_out[at] = grad_two.astype(LOW)
        here = column_sums(grad_y * unit_rows, grad_y, grad_two)
        sums = here if sums is None else [a + b for a, b in zip(sums, here)]
    for index, total in enumerate(sums):
        vec_out[index : index + 1] = total


def outer_grad(place, counts, out_grad, grad_cls, unit_two, inverse_two, rows):
    total = out_grad.shape[0]
    return pl.pallas_call(
        outer_kernel,
        in_specs=[SMEM, SMEM] + [pl.BlockSpec(memory_space=pltpu.VMEM)] * 5,
        out_shape=[
            jax.ShapeDtypeStruct((total, D), F32),
            jax.ShapeDtypeStruct((total, D), LOW),
            jax.ShapeDtypeStruct((3, D), F32),
        ],
        compiler_params=params(),
        cost_estimate=cost(5),
        name="outer",
    )(place, counts, out_grad, grad_cls, unit_two, inverse_two, rows)


def weight_kernel(panels, after, side, *refs):
    *sides, out = refs[after:]

    @pl.when(pl.program_id(0) < panels)
    def _():
        out[0] = dot(sides[0][...], sides[1][...], (0, 0)).astype(LOW)

    if len(sides) > 2:

        @pl.when(pl.program_id(0) == panels)
        def _():
            out[0] = dot(sides[2][...], sides[3][...], (0, 0)).astype(LOW)


def weight_half(hint, after, side, left_side, right_side, panels, banded, extra=()):
    total = left_side.shape[0]
    half = D // 2
    every = panels + len(extra) // 2
    tall = lambda width, at: pl.BlockSpec((total, width), at)
    last = lambda panel: jnp.minimum(panel, panels - 1)
    left_at = lambda panel, side: (0, last(panel) * 2 + side[0] if banded else side[0])
    right_at = lambda panel, side: (0, 0 if banded else last(panel))
    more = [tall(half, lambda p, s: (0, s[0])), tall(D, lambda p, s: (0, 0))]
    return pl.pallas_call(
        partial(weight_kernel, panels, len(after)),
        grid_spec=pltpu.PrefetchScalarGridSpec(
            num_scalar_prefetch=1,
            grid=(every,),
            in_specs=[ANY] * len(after)
            + [tall(half, left_at), tall(D, right_at)]
            + more[: len(extra)],
            out_specs=pl.BlockSpec((1, half, D), lambda p, s: (p, 0, 0)),
        ),
        out_shape=jax.ShapeDtypeStruct((every, half, D), LOW),
        compiler_params=params(),
        cost_estimate=cost(hint),
        name="weight",
    )(side.reshape(1), *after, left_side, right_side, *extra)


def inner_kernel(after, *refs):
    low, grad_two, slope, unit_one, inverse_one, w_attn, w_in, w_out, rows = refs[after:-6]
    pre_out, one_out, mixed_out, ga_out, vec_out, total = refs[-6:]
    band = pl.program_id(0)
    last = pl.num_programs(0) - 1
    step = 256
    for at in range(0, D, step):
        here = slice(at, at + step)
        grad_pre = dot(low[...], w_out[here], (1, 1)) * slope[:, here].astype(F32)
        pre_out[:, here] = grad_pre.astype(LOW)
        vec_out[pl.ds(3 + band, 1), here] = jnp.sum(grad_pre, axis=0, keepdims=True)

    @pl.when(band == 0)
    def _():
        total[...] = grad_two[...] + dot(pre_out[...], w_in[...], (1, 1))

    @pl.when((band > 0) & (band < last))
    def _():
        total[...] += dot(pre_out[...], w_in[...], (1, 1))

    @pl.when(band == last)
    def _():
        sums = None
        for first in range(0, low.shape[0], TALL):
            at = slice(first, first + TALL)
            grad_normed = total[at] + dot(pre_out[at], w_in[...], (1, 1))
            unit_rows = unit_one[at].astype(F32)
            grad_one = norm_back(grad_normed, unit_rows, inverse_one[at], row_of(rows, 0))
            one_out[at] = grad_one
            mixed = grad_one.astype(LOW)
            mixed_out[at] = mixed
            ga_out[at] = dot(mixed, w_attn[...], (1, 1)).astype(LOW)
            here = column_sums(grad_normed * unit_rows, grad_normed, grad_one)
            sums = here if sums is None else [a + b for a, b in zip(sums, here)]
        for index, value in enumerate(sums):
            vec_out[index : index + 1] = value


def inner_grad(after, low, grad_two, slope, unit_one, inverse_one, w_attn, w_in, w_out, rows):
    total = low.shape[0]
    bands = FF // D
    like = lambda width, kind: jax.ShapeDtypeStruct((total, width), kind)
    band = lambda height: pl.BlockSpec((height, D), lambda j: (0, j))
    return pl.pallas_call(
        partial(inner_kernel, len(after)),
        grid=(bands,),
        in_specs=[ANY] * len(after)
        + [
            whole(low.shape), whole(grad_two.shape), band(total), whole(unit_one.shape),
            whole(inverse_one.shape), whole(w_attn.shape), band(D),
            pl.BlockSpec((D, D), lambda j: (j, 0)), whole(rows.shape),
        ],
        out_specs=[band(total)] + [whole((total, D))] * 3 + [whole((3 + bands, D))],
        out_shape=[
            like(FF, LOW), like(D, F32), like(D, LOW), like(D, LOW),
            jax.ShapeDtypeStruct((3 + bands, D), F32),
        ],
        scratch_shapes=[pltpu.VMEM((total, D), F32)],
        compiler_params=params(),
        cost_estimate=cost(16),
        name="inner",
    )(*after, low, grad_two, slope, unit_one, inverse_one, w_attn, w_in, w_out, rows)


def unattend_kernel(*refs):
    q, k, v, p, ga, stack_out, vec_out = refs[-7:]
    scaling = HEAD ** (-0.5)
    first = pl.program_id(0) == 0

    @pl.when(first)
    def _():
        vec_out[...] = jnp.zeros_like(vec_out)

    for span in range(p.shape[0]):
        at = slice(span * SPAN, (span + 1) * SPAN)
        for pair in range(HEADS // 2):
            lo = pair * 2 * HEAD
            lanes = slice(lo, lo + 2 * HEAD)
            weights = p[span, pair]
            grad = ga[at, lanes]
            spread_out = dot(grad, split_heads(v[at, lanes]), (1, 1))
            wide = weights.astype(F32)
            parts = []
            for half in range(2):
                cols = slice(half * SPAN, (half + 1) * SPAN)
                wgt, gw = wide[:, cols], spread_out[:, cols]
                parts.append((wgt * (gw - jnp.sum(gw * wgt, axis=-1, keepdims=True))).astype(LOW))
            grad_scores = jnp.concatenate(parts, axis=1)
            grad_q = dot(grad_scores, split_heads(k[at, lanes])) * scaling
            tall_scores = jnp.concatenate(parts, axis=0)
            tall_weights = jnp.concatenate([weights[:, :SPAN], weights[:, SPAN:]], axis=0)
            grad_k = dot(tall_scores, split_heads(q[at, lanes]), (0, 0))
            grad_v = dot(tall_weights, split_heads(grad), (0, 0))
            stack_out[at, lo : lo + 2 * HEAD] = grad_q.astype(LOW)
            stack_out[at, D + lo : D + lo + 2 * HEAD] = grad_k.astype(LOW)
            stack_out[at, 2 * D + lo : 2 * D + lo + 2 * HEAD] = grad_v.astype(LOW)
            vec_out[0:1, lanes] += jnp.sum(grad_q, axis=0, keepdims=True)
            vec_out[1:2, lanes] += jnp.sum(grad_v, axis=0, keepdims=True)


def unattend(after, part, parts, q, k, v, p, ga, stack=None):
    total = q.shape[0]
    count = total // SPAN // parts
    first = part * count
    tall = lambda width: pl.BlockSpec((SPAN, width), lambda i: (first + i, 0))
    after = after if stack is None else [stack] + after
    return pl.pallas_call(
        unattend_kernel,
        grid=(count,),
        in_specs=[ANY] * len(after)
        + [tall(D)] * 3
        + [
            pl.BlockSpec((1, HEADS // 2, SPAN, 2 * SPAN), lambda i: (first + i, 0, 0, 0)),
            tall(D),
        ],
        out_specs=[tall(3 * D), whole((2, D))],
        out_shape=[
            jax.ShapeDtypeStruct((total, 3 * D), LOW),
            jax.ShapeDtypeStruct((2, D), F32),
        ],
        input_output_aliases={} if stack is None else {0: 0},
        compiler_params=params(),
        cost_estimate=cost(8),
        name="unattend",
    )(*after, q, k, v, p, ga)


def input_kernel(*refs):
    grad_one, stack, w_qkv, out = refs[-4:]
    total = grad_one[...]
    for index in range(3):
        total += dot(stack[:, index * D : (index + 1) * D], w_qkv[index], (1, 1))
    out[...] = total


def input_grad(after, grad_one, stack, w_qkv):
    total = grad_one.shape[0]
    tall = lambda width: pl.BlockSpec((TALL, width), lambda i: (i, 0))
    return pl.pallas_call(
        input_kernel,
        grid=(total // TALL,),
        in_specs=[ANY] * len(after) + [tall(D), tall(3 * D), whole(w_qkv.shape)],
        out_specs=tall(D),
        out_shape=jax.ShapeDtypeStruct((total, D), F32),
        compiler_params=params(),
        cost_estimate=cost(8),
        name="input",
    )(*after, grad_one, stack, w_qkv)


def contrast_kernel(slots, place, rows, counts, partners, loss_out, grad_out):
    total, scale = rows.shape[0], 2.0 * D ** (-0.5)

    def number(shape, axis):
        at = lax.broadcasted_iota(jnp.int32, shape, axis)
        return (at // GROUP) ^ place[0], at % GROUP

    device, slot = number((counts.shape[1], total), 1)
    hit = lax.broadcasted_iota(jnp.int32, device.shape, 0) == device
    count = dot(counts[...].astype(LOW), jnp.where(hit, 1.0, 0.0).astype(LOW))
    live_across = (slot[:1].astype(F32) < count) & (slot[:1] < slots)
    device, slot = number((total, counts.shape[1]), 0)
    hit = lax.broadcasted_iota(jnp.int32, device.shape, 1) == device
    count = jnp.sum(jnp.where(hit, counts[...], 0.0), axis=1, keepdims=True)
    live_down = (slot[:, :1].astype(F32) < count) & (slot[:, :1] < slots)
    device, slot = number((total, partners.shape[1]), 0)
    own_id = device * slots + slot
    hit = lax.broadcasted_iota(jnp.int32, own_id.shape, 1) == own_id
    pair = jnp.sum(jnp.where(hit, partners[...], 0.0), axis=1, keepdims=True)
    device, slot = number((total, total), 0)
    down = (device * slots + slot).astype(F32)
    device, slot = number((total, total), 1)
    across = (device * slots + slot).astype(F32)
    valid = live_across & (down != across)
    matched = jnp.where((slot < slots) & (pair == across), 1.0, 0.0)
    anchor = jnp.where(live_down & (pair != down[:, :1]), 1.0, 0.0)
    similar = dot(rows[...], rows[...], (1, 1)) * scale
    masked = jnp.where(valid, similar, -1e30)
    peak = jnp.max(masked, axis=1, keepdims=True)
    summed = jnp.sum(jnp.where(valid, jnp.exp(masked - peak), 0.0), axis=1, keepdims=True)
    log_total = jnp.log(summed) + peak
    positive = jnp.sum(matched * similar, axis=1, keepdims=True)
    loss_out[...] = jnp.sum(anchor * (log_total - positive), axis=0, keepdims=True)
    grad = (anchor * (jnp.where(valid, jnp.exp(masked - log_total), 0.0) - matched)).astype(LOW)
    own = lax.broadcasted_iota(jnp.int32, (GROUP, total), 0)
    own = jnp.where(own == lax.broadcasted_iota(jnp.int32, (GROUP, total), 1), 1.0, 0.0)
    down_part = dot(dot(own.astype(LOW), grad, (1, 1)).astype(LOW), rows[...])
    grad_out[...] = (dot(grad[: 2 * GROUP], rows[...])[:GROUP] + down_part) * scale


def contrast(cls_rows, span_count, pair_index, device, slots):
    total = cls_rows.shape[0]
    return pl.pallas_call(
        partial(contrast_kernel, slots),
        in_specs=[pl.BlockSpec(memory_space=pltpu.SMEM)]
        + [pl.BlockSpec(memory_space=pltpu.VMEM)] * 3,
        out_shape=[
            jax.ShapeDtypeStruct((1, 1), F32),
            jax.ShapeDtypeStruct((GROUP, D), F32),
        ],
        compiler_params=params(),
        cost_estimate=cost(3),
        name="contrast",
    )(
        device,
        cls_rows,
        span_count.astype(F32).reshape(1, -1),
        pair_index.astype(F32).reshape(1, -1),
    )


def adam_kernel(
    packed, position, gathered, master, first, second, left, right,
    master_out, first_out, second_out, low_out, *scratch,
):
    quarter = D // 4
    slot = pl.program_id(0)
    if packed:
        owned = scratch[0]
        shares, tall, _ = gathered.shape
        rows = D // shares

        @pl.when(slot == 0)
        def _():
            def place(share, carry):
                block = gathered[share].astype(F32)
                at = pl.multiple_of((share ^ position[0]) * rows, rows)
                for index in range(owned.shape[0]):
                    lo = index * rows % tall
                    side = index * rows // tall
                    piece = block[lo : lo + rows, side * quarter : (side + 1) * quarter]
                    owned[index, pl.ds(at, rows), :] = piece
                return carry

            lax.fori_loop(0, shares, place, 0)

        gradient = owned[slot].astype(LOW)
    else:
        gradient = gathered[0]
    low_left, low_right = left[0].astype(LOW), right[0].astype(LOW)
    turned = dot(gradient, low_left, (0, 0))
    turned = dot(low_right, turned.astype(LOW), (0, 0))
    new_first = 0.9 * first[0] + 0.1 * turned
    new_second = 0.999 * second[0] + 0.001 * turned * turned
    first_out[0] = new_first
    second_out[0] = new_second
    spread_by = jnp.sqrt(new_second * (1.0 / (1.0 - 0.999**STEP))) + 1e-08
    update = new_first * (1.0 / (1.0 - 0.9**STEP)) / spread_by
    update = dot(update.astype(LOW), low_left, (1, 1))
    update = dot(low_right, update.astype(LOW))
    new_master = master[0] - RATE * (update + DECAY * master[0])
    master_out[0] = new_master
    low_out[0] = new_master.astype(LOW)


def to_owned(gathered, position, per_owner):
    quarter = D // 4
    gathered = jnp.take(gathered, jnp.arange(gathered.shape[0]) ^ position, axis=0)
    flat = jnp.concatenate([gathered[..., :quarter], gathered[..., quarter:]], axis=1)
    rows = flat.shape[1] // per_owner
    flat = flat.reshape(flat.shape[0], per_owner, rows, quarter).transpose(1, 0, 2, 3)
    return flat.reshape(per_owner, D, quarter)


def rotated_adam(position, gathered, master, first_moment, second_moment, left_basis, right_basis):
    per_owner, _, quarter = master.shape
    turn = lambda a: a.transpose(0, 2, 1)
    rows = D // gathered.shape[0]
    packed = rows % 8 == 0 and per_owner % 2 == 0
    if not packed:
        gathered = to_owned(gathered, position, per_owner)
    block = lambda a: pl.BlockSpec((1,) + a.shape[1:], lambda s, p: (s, 0, 0))
    operands = (turn(master), turn(first_moment), turn(second_moment), left_basis, right_basis)
    like = jax.ShapeDtypeStruct(operands[0].shape, F32)
    fixed = pl.BlockSpec(gathered.shape, lambda s, p: (0, 0, 0))
    outputs = pl.pallas_call(
        partial(adam_kernel, packed),
        grid_spec=pltpu.PrefetchScalarGridSpec(
            num_scalar_prefetch=1,
            grid=(per_owner,),
            in_specs=[fixed if packed else block(gathered)] + [block(a) for a in operands],
            out_specs=[block(operands[0])] * 4,
            scratch_shapes=[pltpu.VMEM((per_owner, D, quarter), F32)] if packed else [],
        ),
        out_shape=[like, like, like, jax.ShapeDtypeStruct(like.shape, LOW)],
        compiler_params=params(),
        cost_estimate=cost(20),
        name="adam",
    )(position.reshape(1), gathered, *operands)
    return [turn(a) for a in outputs]


def axis_bits(name):
    size = lax.axis_size(name)
    return [(name, 1 << k) for k in range(size.bit_length() - 1)]


def bit_of(step):
    return jnp.where((lax.axis_index(step[0]) & step[1]) != 0, 1, 0)


def swap(send, step):
    size = lax.axis_size(step[0])
    return lax.ppermute(send, step[0], [(i, i ^ step[1]) for i in range(size)])


def pick(array, index, dim):
    return lax.dynamic_index_in_dim(array, index, dim, False)


def gather_all(rows):
    for step in axis_bits("col") + axis_bits("row"):
        rows = jnp.concatenate([rows, swap(rows, step)])
    return rows


def row_steps():
    row_bits, col_bits = axis_bits("row"), axis_bits("col")
    core, across = row_bits[:1], row_bits[1:][::-1]
    y_bits, z_bits = col_bits[:-2][::-1], col_bits[-2:]
    return core, across, y_bits, z_bits


def launch(part, step, left, rider=None):
    dim = 1 + left.index(step)
    bit = bit_of(step)
    left.remove(step)
    send, keep = pick(part, 1 - bit, dim), pick(part, bit, dim)
    shape, flat = send.shape, send.reshape(-1, send.shape[-1])
    message = flat
    if rider is not None:
        message = jnp.concatenate([flat, rider.astype(LOW).reshape(-1, flat.shape[1])])
    other = swap(message, step)
    arrived = other[: flat.shape[0]].reshape(shape)
    if rider is not None:
        rider = rider + other[flat.shape[0] :].reshape(rider.shape).astype(F32)
    return message, partial(landed, keep, arrived), rider


def landed(keep, other, tied=None):
    total = keep.astype(F32) + other.astype(F32)
    if tied is not None:
        total += 0.0 * tied[(0,) * tied.ndim].astype(F32)
    return total.astype(LOW)


def begin_sum(send):
    return swap(send, row_steps()[0][0])


class Reduction:
    def __init__(self, other, keep, rider=None):
        core, across, y_bits, z_bits = row_steps()
        left = across + y_bits + z_bits
        part = landed(keep, other)
        self.rider = rider if rider is None else rider + swap(rider, core[0])
        width = part.shape[1] >> len(left)
        part = part.reshape(part.shape[:1] + (2,) * len(left) + (width, D))
        self.steps = list(zip(across + y_bits, y_bits + across)) + [(step,) for step in z_bits]
        self.parts = [part[..., : D // 2], part[..., D // 2 :]]
        self.left = [list(left), list(left)]
        self.start()

    def start(self):
        if not self.steps:
            self.moves = None
            return
        steps = self.steps.pop(0)
        if len(steps) < len(self.parts):
            self.parts, self.left = [jnp.concatenate(self.parts, axis=-1)], self.left[:1]
        self.moves = []
        for side, step in enumerate(steps):
            rider = self.rider if side == 0 else None
            self.moves.append(launch(self.parts[side], step, self.left[side], rider))

    def sent(self):
        return [move[0] for move in self.moves or ()]

    def land(self, tied=None):
        self.parts = [land(tied) for _, land, _ in self.moves]
        self.rider = self.moves[0][2]
        self.start()

    def finish(self):
        while self.moves:
            self.land()
        return self.parts[0]


def slots_kernel(cols, after, owners, *refs):
    parts, out, blocks, packed = refs[after:-3], refs[-3], refs[-2], refs[-1]
    quarter = D // 4
    at = 0
    for part in parts:
        for panel in range(part.shape[0]):
            value = part[panel].astype(F32)
            for index in range(4):
                blocks[at] = value[:, index * quarter : (index + 1) * quarter]
                at += 1
    rows, half = blocks.shape[1], packed.shape[1]
    for slot in range(at):
        col, place = divmod(slot, at // cols)
        value = blocks[owners[slot]]
        first = place * rows
        for side in range(2):
            lo, hi = max(first, side * half), min(first + rows, (side + 1) * half)
            if lo < hi:
                lanes = slice(side * quarter, (side + 1) * quarter)
                packed[col, lo - side * half : hi - side * half, lanes] = value[lo - first : hi - first]
    out[...] = packed[...].astype(LOW)


def to_slots(after, parts, owner_list):
    quarter, cols = D // 4, lax.axis_size("col")
    panels, rows = sum(part.shape[0] for part in parts), parts[0].shape[1]
    shape = (cols, panels * 4 // cols * rows // 2, 2 * quarter)
    return pl.pallas_call(
        partial(slots_kernel, cols, len(after)),
        in_specs=[SMEM] + [ANY] * len(after) + [pl.BlockSpec(memory_space=pltpu.VMEM)] * len(parts),
        out_shape=jax.ShapeDtypeStruct(shape, LOW),
        scratch_shapes=[pltpu.VMEM((panels * 4, rows, quarter), F32), pltpu.VMEM(shape, F32)],
        compiler_params=params(),
        cost_estimate=cost(4),
        name="slots",
    )(owner_list, *after, *parts)


def spread(slots):
    core, across, y_bits, z_bits = row_steps()
    tail = slots.shape[1:]
    left = axis_bits("col")[::-1]
    part = slots.reshape((1,) + (2,) * len(left) + tail)
    for step in (y_bits + z_bits)[::-1]:
        dim = 1 + left.index(step)
        bit = bit_of(step)
        other = swap(pick(part, 1 - bit, dim), step)
        part = jnp.concatenate([pick(part, bit, dim), other])
        left.remove(step)
    for step in (core + across)[::-1]:
        part = jnp.concatenate([part, swap(part, step)])
    return part


def row_place():
    place = 0
    for group in row_steps():
        for step in group:
            place = place * 2 + bit_of(step)
    return place


def shards(
    tokens,
    w_qkv,
    w_attn_out,
    w_in,
    w_out,
    vectors,
    out_grad,
    span_count,
    pair_index,
    owner_list,
    master,
    first_moment,
    second_moment,
    left_basis,
    right_basis,
    vec_first,
    vec_second,
):
    slots = tokens.shape[0] // SPAN
    device = (lax.axis_index("row") * lax.axis_size("col") + lax.axis_index("col")).reshape(1)
    core, across, y_bits, z_bits = row_steps()
    core_bit = bit_of(core[0])
    rows = vectors.reshape(1, -1)
    q, k, v, p, attended = attend(tokens, w_qkv, rows)
    encoded, hidden, slope, normed_low, unit_one, inverse_one, unit_two, inverse_two = feed(
        device, span_count, tokens, attended, w_attn_out, w_in, w_out, rows
    )
    cls_rows = jnp.pad(encoded.reshape(slots, SPAN, D)[:, 0], ((0, GROUP - slots), (0, 0)))
    loss, grad_cls = contrast(gather_all(cls_rows), span_count, pair_index, device, slots)
    grad_two, outer_low, vec_two = outer_grad(
        device, span_count, out_grad, grad_cls, unit_two, inverse_two, rows
    )
    outer_args = (hidden, outer_low, FF // D, True)
    outer_away = weight_half(8, [], 1 - core_bit, *outer_args)
    outer_here = weight_half(60, [outer_away], core_bit, *outer_args)
    outer_run = Reduction(begin_sum(outer_away), outer_here)
    pre_low, grad_one, mixed_low, grad_attended, vec_one = inner_grad(
        outer_run.sent(), outer_low, grad_two, slope, unit_one, inverse_one,
        w_attn_out, w_in, w_out, rows,
    )
    outer_run.land(vec_one)
    inner_args = (normed_low, pre_low, FF // D, False, (attended, mixed_low))
    inner_away = weight_half(8, outer_run.sent(), 1 - core_bit, *inner_args)
    outer_run.land(inner_away)
    inner_here = weight_half(60, [inner_away] + outer_run.sent(), core_bit, *inner_args)
    outer_run.land(inner_here)
    inner_run = Reduction(begin_sum(inner_away), inner_here)
    early, vec_early = unattend(
        outer_run.sent() + inner_run.sent(), 0, 2, q, k, v, p, grad_attended
    )
    outer_run.land(vec_early)
    stack_low, vec_late = unattend([], 1, 2, q, k, v, p, grad_attended, early)
    inner_run.land(vec_late)
    project_args = (tokens, stack_low, 3, False)
    project_away = weight_half(8, inner_run.sent(), 1 - core_bit, *project_args)
    project_here = weight_half(60, [project_away], core_bit, *project_args)
    inner_run.land(project_here)
    vec_heads = vec_early + vec_late
    grad_vector = jnp.concatenate(
        [
            jnp.stack([vec_one[0], vec_two[0], vec_one[1], vec_two[1]]),
            vec_heads,
            jnp.stack([vec_one[2], vec_two[2]]),
            vec_one[3:],
        ]
    )
    project_run = Reduction(begin_sum(project_away), project_here, grad_vector)
    grad_tokens = input_grad(
        inner_run.sent() + project_run.sent(), grad_one, stack_low, w_qkv
    )
    project_run.land(grad_tokens)
    inner_run.land(grad_tokens)
    outer_sum, inner_sum, project_sum = (
        run.finish() for run in (outer_run, inner_run, project_run)
    )
    vec_grad = project_run.rider
    parts = (project_sum, inner_sum[-1:], inner_sum[:-1], outer_sum)
    gathered = spread(to_slots([], parts, owner_list))
    vec_grad = vec_grad.reshape(-1)
    new_master, new_first, new_second, master_copy = rotated_adam(
        row_place(), gathered, master, first_moment, second_moment, left_basis, right_basis
    )
    vec_first_new = 0.9 * vec_first + 0.1 * vec_grad
    vec_second_new = 0.999 * vec_second + 0.001 * vec_grad * vec_grad
    vec_step = (
        vec_first_new / (1.0 - 0.9**STEP) / (jnp.sqrt(vec_second_new / (1.0 - 0.999**STEP)) + 1e-08)
    )
    vec_new = vectors - VECTOR_RATE * vec_step
    return (
        encoded,
        grad_tokens,
        loss[0, 0],
        new_master,
        new_first,
        new_second,
        master_copy,
        vec_new,
        vec_first_new,
        vec_second_new,
    )


def solution(mesh):
    in_specs = (
        P(("row", "col"), None),
        P(),
        P(),
        P(),
        P(),
        P(),
        P(("row", "col"), None),
        P(),
        P(),
        P(),
        P("col", None, None),
        P("col", None, None),
        P("col", None, None),
        P("col", None, None),
        P("col", None, None),
        P(),
        P(),
    )
    out_specs = (
        P(("row", "col"), None),
        P(("row", "col"), None),
        P(),
        P("col", None, None),
        P("col", None, None),
        P("col", None, None),
        P("col", None, None),
        P(),
        P(),
        P(),
    )
    return jax.shard_map(shards, mesh=mesh, in_specs=in_specs, out_specs=out_specs, check_vma=False)
```

```python
from functools import partial

import jax
import jax.numpy as jnp
from jax import lax
from jax.experimental import pallas as pl
from jax.experimental.pallas import tpu as pltpu
from jax.sharding import PartitionSpec as P

D = 768
HEADS = 12
HEAD = 64
FF = 3072
SPAN = 128
STEP = 10
GROUP = 8

RATE = 0.01
DECAY = 0.01
VECTOR_RATE = 0.3

LOW = jnp.bfloat16
F32 = jnp.float32
TALL = 2 * SPAN


def dot(left_side, right_side, contract=(1, 0)):
    dims = (((contract[0],), (contract[1],)), ((), ()))
    return lax.dot_general(left_side, right_side, dims, preferred_element_type=F32)


def whole(shape):
    return pl.BlockSpec(shape, lambda *ids: (0,) * len(shape))


def cost(microseconds, transcendentals=0):
    return pl.CostEstimate(
        flops=int(microseconds * 1.1e9), bytes_accessed=0, transcendentals=transcendentals
    )


def params(mebibytes=36):
    return pltpu.CompilerParams(vmem_limit_bytes=mebibytes * 1024 * 1024)


def row_of(rows, index):
    return rows[:, index * D : (index + 1) * D]


def live_rows(place, counts, first_row, height):
    at = first_row + lax.broadcasted_iota(jnp.int32, (height, 1), 0)
    return jnp.where(at < counts[place[0]] * SPAN, 1.0, 0.0)


near = pltpu.VMEM
far = pltpu.HBM


def streamed(*arrays):
    return [pltpu.with_memory_space_constraint(a, pltpu.HBM) for a in arrays]


ANY = pl.BlockSpec(memory_space=pl.ANY)
SMEM = pl.BlockSpec(memory_space=pltpu.SMEM)


def split_heads(pair):
    lane = lax.broadcasted_iota(jnp.int32, pair.shape, 1)
    zero = jnp.zeros_like(pair)
    return jnp.concatenate([jnp.where(lane < HEAD, pair, zero), jnp.where(lane < HEAD, zero, pair)])


def normalise(scores):
    peak = jnp.max(scores, axis=-1, keepdims=True)
    raised = jnp.exp(scores - peak)
    return raised * (1.0 / jnp.sum(raised, axis=-1, keepdims=True))


def attend_kernel(tokens, w_qkv, rows, q_out, k_out, v_out, p_out, a_out):
    block = tokens[...]
    scaling = HEAD ** (-0.5)
    q_out[...] = ((dot(block, w_qkv[0]) + row_of(rows, 4)).astype(LOW) * scaling).astype(LOW)
    k_out[...] = dot(block, w_qkv[1]).astype(LOW)
    v_out[...] = (dot(block, w_qkv[2]) + row_of(rows, 5)).astype(LOW)
    for span in range(TALL // SPAN):
        at = slice(span * SPAN, (span + 1) * SPAN)
        for pair in range(HEADS // 2):
            lanes = slice(pair * 2 * HEAD, (pair + 1) * 2 * HEAD)
            scores = dot(q_out[at, lanes], split_heads(k_out[at, lanes]), (1, 1))
            weights = jnp.concatenate(
                [normalise(scores[:, :SPAN]), normalise(scores[:, SPAN:])], axis=1
            ).astype(LOW)
            p_out[span, pair] = weights
            a_out[at, lanes] = dot(weights, split_heads(v_out[at, lanes])).astype(LOW)


def attend(tokens, w_qkv, rows):
    total = tokens.shape[0]
    tall = pl.BlockSpec((TALL, D), lambda i: (i, 0))
    like = far((total, D), LOW)
    tokens, w_qkv, rows = streamed(tokens, w_qkv, rows)
    spans = TALL // SPAN
    return pl.pallas_call(
        attend_kernel,
        grid=(total // TALL,),
        in_specs=[tall, whole(w_qkv.shape), whole(rows.shape)],
        out_specs=[
            tall,
            tall,
            tall,
            pl.BlockSpec((spans, HEADS // 2, SPAN, 2 * SPAN), lambda i: (i, 0, 0, 0)),
            tall,
        ],
        out_shape=[
            like,
            like,
            like,
            far((total // SPAN, HEADS // 2, SPAN, 2 * SPAN), LOW),
            near((total, D), LOW),
        ],
        compiler_params=params(),
        cost_estimate=cost(10),
        name="attend",
    )(tokens, w_qkv, rows)


def unit_norm(resid):
    centred = resid - jnp.mean(resid, axis=-1, keepdims=True)
    inverse = lax.rsqrt(jnp.mean(centred * centred, axis=-1, keepdims=True) + 1e-06)
    return centred * inverse, inverse


def gelu_pair(x):
    cdf = 0.5 + 0.5 * lax.erf(x * 0.7071067811865476)
    return x * cdf, cdf + x * jnp.exp(-0.5 * x * x) * 0.3989422804014327


def feed_kernel(
    place, counts, tokens, attended, w_attn, w_in, w_out, rows, bias,
    enc_out, hid_out, slope_out, norm_out, u1_out, i1_out, u2_out, i2_out, total,
):
    band = pl.program_id(0)
    chunks = [slice(at, at + TALL) for at in range(0, tokens.shape[0], TALL)]

    @pl.when(band == 0)
    def _():
        for at in chunks:
            resid = tokens[at].astype(F32) + dot(attended[at], w_attn[...]) + row_of(rows, 6)
            unit_one, inverse_one = unit_norm(resid)
            value = unit_one * row_of(rows, 0) + row_of(rows, 2)
            u1_out[at] = unit_one.astype(LOW)
            i1_out[at] = inverse_one
            norm_out[at] = value.astype(LOW)
            total[at] = value + row_of(rows, 7)

    step = 256
    for at in range(0, hid_out.shape[1], step):
        here = slice(at, at + step)
        pre_act = dot(norm_out[...], w_in[:, here]) + bias[:, here]
        hidden, slope = gelu_pair(pre_act)
        hid_out[:, here] = hidden.astype(LOW)
        slope_out[:, here] = slope.astype(LOW)

    @pl.when(band < pl.num_programs(0) - 1)
    def _():
        total[...] += dot(hid_out[...], w_out[...])

    @pl.when(band == pl.num_programs(0) - 1)
    def _():
        for at in chunks:
            resid = total[at] + dot(hid_out[at], w_out[...])
            unit_two, inverse_two = unit_norm(resid)
            u2_out[at] = unit_two.astype(LOW)
            i2_out[at] = inverse_two
            live = live_rows(place, counts, at.start, TALL)
            value = live * (unit_two * row_of(rows, 1) + row_of(rows, 3))
            enc_out[at] = value.astype(LOW)


def feed(place, counts, tokens, attended, w_attn, w_in, w_out, rows):
    total = tokens.shape[0]
    tall = lambda width: pl.BlockSpec((total, width), lambda j: (0, 0))
    band = lambda height: pl.BlockSpec((height, D), lambda j: (0, j))
    tokens, w_attn, w_in, w_out, rows = streamed(tokens, w_attn, w_in, w_out, rows)
    return pl.pallas_call(
        feed_kernel,
        grid=(FF // D,),
        in_specs=[
            SMEM, SMEM, tall(D), tall(D), whole(w_attn.shape), band(D),
            pl.BlockSpec((D, D), lambda j: (j, 0)),
            pl.BlockSpec((1, 8 * D), lambda j: (0, 0)),
            pl.BlockSpec((1, D), lambda j: (0, 8 + j)),
        ],
        out_specs=[
            tall(D), band(total), band(total), tall(D), tall(D), tall(1), tall(D), tall(1),
        ],
        out_shape=[
            jax.ShapeDtypeStruct((total, D), LOW),
            far((total, FF), LOW),
            far((total, FF), LOW),
            far((total, D), LOW),
            far((total, D), LOW),
            far((total, 1), F32),
            near((total, D), LOW),
            near((total, 1), F32),
        ],
        scratch_shapes=[pltpu.VMEM((total, D), F32)],
        compiler_params=params(),
        cost_estimate=cost(20),
        name="feed",
    )(place, counts, tokens, attended, w_attn, w_in, w_out, rows, rows)


def norm_back(grad_out, unit_rows, inverse, gain):
    scaled = grad_out * gain
    along = jnp.mean(scaled * unit_rows, axis=-1, keepdims=True)
    return inverse * (scaled - jnp.mean(scaled, axis=-1, keepdims=True) - unit_rows * along)


def column_sums(*arrays):
    return [jnp.sum(a, axis=0, keepdims=True) for a in arrays]


def outer_kernel(place, counts, out_grad, grad_cls, unit_two, inverse_two, rows, two_out, low_out, vec_out):
    spot = lax.broadcasted_iota(jnp.int32, (SPAN, 1), 0) == 0
    sums = None
    for span in range(out_grad.shape[0] // SPAN):
        at = slice(span * SPAN, (span + 1) * SPAN)
        added = jnp.where(spot, grad_cls[span : span + 1], 0.0)
        live = live_rows(place, counts, span * SPAN, SPAN)
        grad_y = live * (out_grad[at].astype(F32) + added)
        unit_rows = unit_two[at].astype(F32)
        grad_two = norm_back(grad_y, unit_rows, inverse_two[at], row_of(rows, 1))
        two_out[at] = grad_two
        low_out[at] = grad_two.astype(LOW)
        here = column_sums(grad_y * unit_rows, grad_y, grad_two)
        sums = here if sums is None else [a + b for a, b in zip(sums, here)]
    for index, total in enumerate(sums):
        vec_out[index : index + 1] = total


def outer_grad(place, counts, out_grad, grad_cls, unit_two, inverse_two, rows):
    total = out_grad.shape[0]
    return pl.pallas_call(
        outer_kernel,
        in_specs=[SMEM, SMEM] + [pl.BlockSpec(memory_space=pltpu.VMEM)] * 5,
        out_shape=[
            jax.ShapeDtypeStruct((total, D), F32),
            jax.ShapeDtypeStruct((total, D), LOW),
            jax.ShapeDtypeStruct((3, D), F32),
        ],
        compiler_params=params(),
        cost_estimate=cost(5),
        name="outer",
    )(place, counts, out_grad, grad_cls, unit_two, inverse_two, rows)


def weight_kernel(panels, after, side, *refs):
    *sides, out = refs[after:]

    @pl.when(pl.program_id(0) < panels)
    def _():
        out[0] = dot(sides[0][...], sides[1][...], (0, 0)).astype(LOW)

    if len(sides) > 2:

        @pl.when(pl.program_id(0) == panels)
        def _():
            out[0] = dot(sides[2][...], sides[3][...], (0, 0)).astype(LOW)


def weight_half(hint, after, side, left_side, right_side, panels, banded, extra=()):
    total = left_side.shape[0]
    half = D // 2
    every = panels + len(extra) // 2
    tall = lambda width, at: pl.BlockSpec((total, width), at)
    last = lambda panel: jnp.minimum(panel, panels - 1)
    left_at = lambda panel, side: (0, last(panel) * 2 + side[0] if banded else side[0])
    right_at = lambda panel, side: (0, 0 if banded else last(panel))
    more = [tall(half, lambda p, s: (0, s[0])), tall(D, lambda p, s: (0, 0))]
    return pl.pallas_call(
        partial(weight_kernel, panels, len(after)),
        grid_spec=pltpu.PrefetchScalarGridSpec(
            num_scalar_prefetch=1,
            grid=(every,),
            in_specs=[ANY] * len(after)
            + [tall(half, left_at), tall(D, right_at)]
            + more[: len(extra)],
            out_specs=pl.BlockSpec((1, half, D), lambda p, s: (p, 0, 0)),
        ),
        out_shape=jax.ShapeDtypeStruct((every, half, D), LOW),
        compiler_params=params(),
        cost_estimate=cost(hint),
        name="weight",
    )(side.reshape(1), *after, left_side, right_side, *extra)


def inner_kernel(after, *refs):
    low, grad_two, slope, unit_one, inverse_one, w_attn, w_in, w_out, rows = refs[after:-6]
    pre_out, one_out, mixed_out, ga_out, vec_out, total = refs[-6:]
    band = pl.program_id(0)
    last = pl.num_programs(0) - 1
    step = 256
    for at in range(0, D, step):
        here = slice(at, at + step)
        grad_pre = dot(low[...], w_out[here], (1, 1)) * slope[:, here].astype(F32)
        pre_out[:, here] = grad_pre.astype(LOW)
        vec_out[pl.ds(3 + band, 1), here] = jnp.sum(grad_pre, axis=0, keepdims=True)

    @pl.when(band == 0)
    def _():
        total[...] = grad_two[...] + dot(pre_out[...], w_in[...], (1, 1))

    @pl.when((band > 0) & (band < last))
    def _():
        total[...] += dot(pre_out[...], w_in[...], (1, 1))

    @pl.when(band == last)
    def _():
        sums = None
        for first in range(0, low.shape[0], TALL):
            at = slice(first, first + TALL)
            grad_normed = total[at] + dot(pre_out[at], w_in[...], (1, 1))
            unit_rows = unit_one[at].astype(F32)
            grad_one = norm_back(grad_normed, unit_rows, inverse_one[at], row_of(rows, 0))
            one_out[at] = grad_one
            mixed = grad_one.astype(LOW)
            mixed_out[at] = mixed
            ga_out[at] = dot(mixed, w_attn[...], (1, 1)).astype(LOW)
            here = column_sums(grad_normed * unit_rows, grad_normed, grad_one)
            sums = here if sums is None else [a + b for a, b in zip(sums, here)]
        for index, value in enumerate(sums):
            vec_out[index : index + 1] = value


def inner_grad(after, low, grad_two, slope, unit_one, inverse_one, w_attn, w_in, w_out, rows):
    total = low.shape[0]
    bands = FF // D
    slope, w_attn, w_in, w_out, rows = streamed(slope, w_attn, w_in, w_out, rows)
    band = lambda height: pl.BlockSpec((height, D), lambda j: (0, j))
    return pl.pallas_call(
        partial(inner_kernel, len(after)),
        grid=(bands,),
        in_specs=[ANY] * len(after)
        + [
            whole(low.shape), whole(grad_two.shape), band(total), whole(unit_one.shape),
            whole(inverse_one.shape), whole(w_attn.shape), band(D),
            pl.BlockSpec((D, D), lambda j: (j, 0)), whole(rows.shape),
        ],
        out_specs=[band(total)] + [whole((total, D))] * 3 + [whole((3 + bands, D))],
        out_shape=[
            near((total, FF), LOW),
            far((total, D), F32),
            near((total, D), LOW),
            near((total, D), LOW),
            jax.ShapeDtypeStruct((3 + bands, D), F32),
        ],
        scratch_shapes=[pltpu.VMEM((total, D), F32)],
        compiler_params=params(),
        cost_estimate=cost(16),
        name="inner",
    )(*after, low, grad_two, slope, unit_one, inverse_one, w_attn, w_in, w_out, rows)


def unattend_kernel(*refs):
    q, k, v, p, ga, stack_out, vec_out = refs[-7:]
    scaling = HEAD ** (-0.5)
    first = pl.program_id(0) == 0

    @pl.when(first)
    def _():
        vec_out[...] = jnp.zeros_like(vec_out)

    for span in range(p.shape[0]):
        at = slice(span * SPAN, (span + 1) * SPAN)
        for pair in range(HEADS // 2):
            lo = pair * 2 * HEAD
            lanes = slice(lo, lo + 2 * HEAD)
            weights = p[span, pair]
            grad = ga[at, lanes]
            spread_out = dot(grad, split_heads(v[at, lanes]), (1, 1))
            wide = weights.astype(F32)
            parts = []
            for half in range(2):
                cols = slice(half * SPAN, (half + 1) * SPAN)
                wgt, gw = wide[:, cols], spread_out[:, cols]
                parts.append((wgt * (gw - jnp.sum(gw * wgt, axis=-1, keepdims=True))).astype(LOW))
            grad_scores = jnp.concatenate(parts, axis=1)
            grad_q = dot(grad_scores, split_heads(k[at, lanes])) * scaling
            tall_scores = jnp.concatenate(parts, axis=0)
            tall_weights = jnp.concatenate([weights[:, :SPAN], weights[:, SPAN:]], axis=0)
            grad_k = dot(tall_scores, split_heads(q[at, lanes]), (0, 0))
            grad_v = dot(tall_weights, split_heads(grad), (0, 0))
            stack_out[at, lo : lo + 2 * HEAD] = grad_q.astype(LOW)
            stack_out[at, D + lo : D + lo + 2 * HEAD] = grad_k.astype(LOW)
            stack_out[at, 2 * D + lo : 2 * D + lo + 2 * HEAD] = grad_v.astype(LOW)
            vec_out[0:1, lanes] += jnp.sum(grad_q, axis=0, keepdims=True)
            vec_out[1:2, lanes] += jnp.sum(grad_v, axis=0, keepdims=True)


def unattend(after, part, parts, q, k, v, p, ga, stack=None):
    total = q.shape[0]
    count = total // SPAN // parts
    first = part * count
    tall = lambda width: pl.BlockSpec((SPAN, width), lambda i: (first + i, 0))
    after = after if stack is None else [stack] + after
    return pl.pallas_call(
        unattend_kernel,
        grid=(count,),
        in_specs=[ANY] * len(after)
        + [tall(D)] * 3
        + [
            pl.BlockSpec((1, HEADS // 2, SPAN, 2 * SPAN), lambda i: (first + i, 0, 0, 0)),
            tall(D),
        ],
        out_specs=[tall(3 * D), whole((2, D))],
        out_shape=[
far((total, 3 * D), LOW),
            jax.ShapeDtypeStruct((2, D), F32),
        ],
        input_output_aliases={} if stack is None else {0: 0},
        compiler_params=params(),
        cost_estimate=cost(8),
        name="unattend",
    )(*after, q, k, v, p, ga)


def input_kernel(*refs):
    grad_one, stack, w_qkv, out = refs[-4:]
    total = grad_one[...]
    for index in range(3):
        total += dot(stack[:, index * D : (index + 1) * D], w_qkv[index], (1, 1))
    out[...] = total


def input_grad(after, grad_one, stack, w_qkv):
    total = grad_one.shape[0]
    tall = lambda width: pl.BlockSpec((TALL, width), lambda i: (i, 0))
    return pl.pallas_call(
        input_kernel,
        grid=(total // TALL,),
        in_specs=[ANY] * len(after) + [tall(D), tall(3 * D), whole(w_qkv.shape)],
        out_specs=tall(D),
        out_shape=jax.ShapeDtypeStruct((total, D), F32),
        compiler_params=params(),
        cost_estimate=cost(8),
        name="input",
    )(*after, grad_one, stack, w_qkv)


def contrast_kernel(slots, place, rows, counts, partners, loss_out, grad_out):
    total, scale = rows.shape[0], 2.0 * D ** (-0.5)

    def number(shape, axis):
        at = lax.broadcasted_iota(jnp.int32, shape, axis)
        return (at // GROUP) ^ place[0], at % GROUP

    device, slot = number((counts.shape[1], total), 1)
    hit = lax.broadcasted_iota(jnp.int32, device.shape, 0) == device
    count = dot(counts[...].astype(LOW), jnp.where(hit, 1.0, 0.0).astype(LOW))
    live_across = (slot[:1].astype(F32) < count) & (slot[:1] < slots)
    device, slot = number((total, counts.shape[1]), 0)
    hit = lax.broadcasted_iota(jnp.int32, device.shape, 1) == device
    count = jnp.sum(jnp.where(hit, counts[...], 0.0), axis=1, keepdims=True)
    live_down = (slot[:, :1].astype(F32) < count) & (slot[:, :1] < slots)
    device, slot = number((total, partners.shape[1]), 0)
    own_id = device * slots + slot
    hit = lax.broadcasted_iota(jnp.int32, own_id.shape, 1) == own_id
    pair = jnp.sum(jnp.where(hit, partners[...], 0.0), axis=1, keepdims=True)
    device, slot = number((total, total), 0)
    down = (device * slots + slot).astype(F32)
    device, slot = number((total, total), 1)
    across = (device * slots + slot).astype(F32)
    valid = live_across & (down != across)
    matched = jnp.where((slot < slots) & (pair == across), 1.0, 0.0)
    anchor = jnp.where(live_down & (pair != down[:, :1]), 1.0, 0.0)
    similar = dot(rows[...], rows[...], (1, 1)) * scale
    masked = jnp.where(valid, similar, -1e30)
    peak = jnp.max(masked, axis=1, keepdims=True)
    summed = jnp.sum(jnp.where(valid, jnp.exp(masked - peak), 0.0), axis=1, keepdims=True)
    log_total = jnp.log(summed) + peak
    positive = jnp.sum(matched * similar, axis=1, keepdims=True)
    loss_out[...] = jnp.sum(anchor * (log_total - positive), axis=0, keepdims=True)
    grad = (anchor * (jnp.where(valid, jnp.exp(masked - log_total), 0.0) - matched)).astype(LOW)
    own = lax.broadcasted_iota(jnp.int32, (GROUP, total), 0)
    own = jnp.where(own == lax.broadcasted_iota(jnp.int32, (GROUP, total), 1), 1.0, 0.0)
    down_part = dot(dot(own.astype(LOW), grad, (1, 1)).astype(LOW), rows[...])
    grad_out[...] = (dot(grad[: 2 * GROUP], rows[...])[:GROUP] + down_part) * scale


def contrast(cls_rows, span_count, pair_index, device, slots):
    total = cls_rows.shape[0]
    return pl.pallas_call(
        partial(contrast_kernel, slots),
        in_specs=[pl.BlockSpec(memory_space=pltpu.SMEM)]
        + [pl.BlockSpec(memory_space=pltpu.VMEM)] * 3,
        out_shape=[
            jax.ShapeDtypeStruct((1, 1), F32),
            jax.ShapeDtypeStruct((GROUP, D), F32),
        ],
        compiler_params=params(),
        cost_estimate=cost(3),
        name="contrast",
    )(
        device,
        cls_rows,
        span_count.astype(F32).reshape(1, -1),
        pair_index.astype(F32).reshape(1, -1),
    )


def adam_kernel(
    packed, position, gathered, master, first, second, left, right,
    master_out, first_out, second_out, low_out, *scratch,
):
    quarter = D // 4
    slot = pl.program_id(0)
    if packed:
        owned = scratch[0]
        shares, tall, _ = gathered.shape
        rows = D // shares

        @pl.when(slot == 0)
        def _():
            def place(share, carry):
                block = gathered[share].astype(F32)
                at = pl.multiple_of((share ^ position[0]) * rows, rows)
                for index in range(owned.shape[0]):
                    lo = index * rows % tall
                    side = index * rows // tall
                    piece = block[lo : lo + rows, side * quarter : (side + 1) * quarter]
                    owned[index, pl.ds(at, rows), :] = piece
                return carry

            lax.fori_loop(0, shares, place, 0)

        gradient = owned[slot].astype(LOW)
    else:
        gradient = gathered[0]
    low_left, low_right = left[0], right[0].astype(LOW)
    turned = dot(gradient, low_left, (0, 0))
    turned = dot(low_right, turned.astype(LOW), (0, 0))
    new_first = 0.9 * first[0] + 0.1 * turned
    new_second = 0.999 * second[0] + 0.001 * turned * turned
    first_out[0] = new_first
    second_out[0] = new_second
    spread_by = jnp.sqrt(new_second * (1.0 / (1.0 - 0.999**STEP))) + 1e-08
    update = new_first * (1.0 / (1.0 - 0.9**STEP)) / spread_by
    update = dot(update.astype(LOW), low_left, (1, 1))
    update = dot(low_right, update.astype(LOW))
    new_master = master[0] - RATE * (update + DECAY * master[0])
    master_out[0] = new_master
    low_out[0] = new_master.astype(LOW)


def ready_kernel(*refs):
    source, out = refs[-2:]
    out[...] = source[...].astype(out.dtype)


def ready(after, array, kind):
    block = pl.BlockSpec((1,) + array.shape[1:], lambda s: (s, 0, 0))
    return pl.pallas_call(
        ready_kernel,
        grid=(array.shape[0],),
        in_specs=[ANY] * len(after) + [block],
        out_specs=block,
        out_shape=far(array.shape, kind),
        compiler_params=params(16),
        cost_estimate=cost(4),
        name="ready",
    )(*after, *streamed(array))


def to_owned(gathered, position, per_owner):
    quarter = D // 4
    gathered = jnp.take(gathered, jnp.arange(gathered.shape[0]) ^ position, axis=0)
    flat = jnp.concatenate([gathered[..., :quarter], gathered[..., quarter:]], axis=1)
    rows = flat.shape[1] // per_owner
    flat = flat.reshape(flat.shape[0], per_owner, rows, quarter).transpose(1, 0, 2, 3)
    return flat.reshape(per_owner, D, quarter)


def turn(array):
    return array.transpose(0, 2, 1)


def rotated_adam(position, gathered, master, first_moment, second_moment, left_basis, right_basis):
    per_owner, quarter, _ = master.shape
    rows = D // gathered.shape[0]
    packed = rows % 8 == 0 and per_owner % 2 == 0
    if not packed:
        gathered = to_owned(gathered, position, per_owner)
    block = lambda a: pl.BlockSpec((1,) + a.shape[1:], lambda s, p: (s, 0, 0))
    operands = streamed(master, first_moment, second_moment, left_basis, right_basis)
    like = jax.ShapeDtypeStruct(operands[0].shape, F32)
    fixed = pl.BlockSpec(gathered.shape, lambda s, p: (0, 0, 0))
    outputs = pl.pallas_call(
        partial(adam_kernel, packed),
        grid_spec=pltpu.PrefetchScalarGridSpec(
            num_scalar_prefetch=1,
            grid=(per_owner,),
            in_specs=[fixed if packed else block(gathered)] + [block(a) for a in operands],
            out_specs=[block(operands[0])] * 4,
            scratch_shapes=[pltpu.VMEM((per_owner, D, quarter), F32)] if packed else [],
        ),
        out_shape=[like, like, like, jax.ShapeDtypeStruct(like.shape, LOW)],
        compiler_params=params(28),
        cost_estimate=cost(20),
        name="adam",
    )(position.reshape(1), gathered, *operands)
    return [turn(a) for a in outputs]


def axis_bits(name):
    size = lax.axis_size(name)
    return [(name, 1 << k) for k in range(size.bit_length() - 1)]


def bit_of(step):
    return jnp.where((lax.axis_index(step[0]) & step[1]) != 0, 1, 0)


def swap(send, step):
    size = lax.axis_size(step[0])
    return lax.ppermute(send, step[0], [(i, i ^ step[1]) for i in range(size)])


def pick(array, index, dim):
    return lax.dynamic_index_in_dim(array, index, dim, False)


def gather_all(rows):
    for step in axis_bits("col") + axis_bits("row"):
        rows = jnp.concatenate([rows, swap(rows, step)])
    return rows


def row_steps():
    row_bits, col_bits = axis_bits("row"), axis_bits("col")
    core, across = row_bits[:1], row_bits[1:][::-1]
    y_bits, z_bits = col_bits[:-2][::-1], col_bits[-2:]
    return core, across, y_bits, z_bits


def launch(part, step, left, rider=None):
    dim = 1 + left.index(step)
    bit = bit_of(step)
    left.remove(step)
    send, keep = pick(part, 1 - bit, dim), pick(part, bit, dim)
    shape, flat = send.shape, send.reshape(-1, send.shape[-1])
    message = flat
    if rider is not None:
        message = jnp.concatenate([flat, rider.astype(LOW).reshape(-1, flat.shape[1])])
    other = swap(message, step)
    arrived = other[: flat.shape[0]].reshape(shape)
    if rider is not None:
        rider = rider + other[flat.shape[0] :].reshape(rider.shape).astype(F32)
    return message, partial(landed, keep, arrived), rider


def landed(keep, other, tied=None):
    total = keep.astype(F32) + other.astype(F32)
    if tied is not None:
        total += 0.0 * tied[(0,) * tied.ndim].astype(F32)
    return total.astype(LOW)


def begin_sum(send):
    return swap(send, row_steps()[0][0])


class Reduction:
    def __init__(self, other, keep, rider=None):
        core, across, y_bits, z_bits = row_steps()
        left = across + y_bits + z_bits
        part = landed(keep, other)
        self.rider = rider if rider is None else rider + swap(rider, core[0])
        width = part.shape[1] >> len(left)
        part = part.reshape(part.shape[:1] + (2,) * len(left) + (width, D))
        self.steps = list(zip(across + y_bits, y_bits + across)) + [(step,) for step in z_bits]
        self.parts = [part[..., : D // 2], part[..., D // 2 :]]
        self.left = [list(left), list(left)]
        self.start()

    def start(self):
        if not self.steps:
            self.moves = None
            return
        steps = self.steps.pop(0)
        if len(steps) < len(self.parts):
            self.parts, self.left = [jnp.concatenate(self.parts, axis=-1)], self.left[:1]
        self.moves = []
        for side, step in enumerate(steps):
            rider = self.rider if side == 0 else None
            self.moves.append(launch(self.parts[side], step, self.left[side], rider))

    def sent(self):
        return [move[0] for move in self.moves or ()]

    def land(self, tied=None):
        self.parts = [land(tied) for _, land, _ in self.moves]
        self.rider = self.moves[0][2]
        self.start()

    def finish(self):
        while self.moves:
            self.land()
        return self.parts[0]


def slots_kernel(cols, after, owners, *refs):
    parts, out, blocks, packed = refs[after:-3], refs[-3], refs[-2], refs[-1]
    quarter = D // 4
    at = 0
    for part in parts:
        for panel in range(part.shape[0]):
            value = part[panel].astype(F32)
            for index in range(4):
                blocks[at] = value[:, index * quarter : (index + 1) * quarter]
                at += 1
    rows, half = blocks.shape[1], packed.shape[1]
    for slot in range(at):
        col, place = divmod(slot, at // cols)
        value = blocks[owners[slot]]
        first = place * rows
        for side in range(2):
            lo, hi = max(first, side * half), min(first + rows, (side + 1) * half)
            if lo < hi:
                lanes = slice(side * quarter, (side + 1) * quarter)
                packed[col, lo - side * half : hi - side * half, lanes] = value[lo - first : hi - first]
    out[...] = packed[...].astype(LOW)


def to_slots(after, parts, owner_list):
    quarter, cols = D // 4, lax.axis_size("col")
    panels, rows = sum(part.shape[0] for part in parts), parts[0].shape[1]
    shape = (cols, panels * 4 // cols * rows // 2, 2 * quarter)
    return pl.pallas_call(
        partial(slots_kernel, cols, len(after)),
        in_specs=[SMEM] + [ANY] * len(after) + [pl.BlockSpec(memory_space=pltpu.VMEM)] * len(parts),
        out_shape=jax.ShapeDtypeStruct(shape, LOW),
        scratch_shapes=[pltpu.VMEM((panels * 4, rows, quarter), F32), pltpu.VMEM(shape, F32)],
        compiler_params=params(),
        cost_estimate=cost(4),
        name="slots",
    )(owner_list, *after, *parts)


def spread(slots, beside):
    core, across, y_bits, z_bits = row_steps()
    tail = slots.shape[1:]
    left = axis_bits("col")[::-1]
    part = slots.reshape((1,) + (2,) * len(left) + tail)
    made = []
    for step in (y_bits + z_bits)[::-1]:
        dim = 1 + left.index(step)
        bit = bit_of(step)
        send, keep = pick(part, 1 - bit, dim), pick(part, bit, dim)
        other = swap(send, step)
        if len(made) < len(beside):
            made.append(beside[len(made)]([send] + made[-1:]))
            keep += (0.0 * made[-1][(0,) * made[-1].ndim]).astype(LOW)
        part = jnp.concatenate([keep, other])
        left.remove(step)
    for step in (core + across)[::-1]:
        part = jnp.concatenate([part, swap(part, step)])
    return part, made


def row_place():
    place = 0
    for group in row_steps():
        for step in group:
            place = place * 2 + bit_of(step)
    return place


def shards(
    tokens,
    w_qkv,
    w_attn_out,
    w_in,
    w_out,
    vectors,
    out_grad,
    span_count,
    pair_index,
    owner_list,
    master,
    first_moment,
    second_moment,
    left_basis,
    right_basis,
    vec_first,
    vec_second,
):
    slots = tokens.shape[0] // SPAN
    device = (lax.axis_index("row") * lax.axis_size("col") + lax.axis_index("col")).reshape(1)
    core, across, y_bits, z_bits = row_steps()
    core_bit = bit_of(core[0])
    rows = vectors.reshape(1, -1)
    q, k, v, p, attended = attend(tokens, w_qkv, rows)
    encoded, hidden, slope, normed_low, unit_one, inverse_one, unit_two, inverse_two = feed(
        device, span_count, tokens, attended, w_attn_out, w_in, w_out, rows
    )
    cls_rows = jnp.pad(encoded.reshape(slots, SPAN, D)[:, 0], ((0, GROUP - slots), (0, 0)))
    loss, grad_cls = contrast(gather_all(cls_rows), span_count, pair_index, device, slots)
    grad_two, outer_low, vec_two = outer_grad(
        device, span_count, out_grad, grad_cls, unit_two, inverse_two, rows
    )
    outer_args = (hidden, outer_low, FF // D, True)
    outer_away = weight_half(8, [], 1 - core_bit, *outer_args)
    outer_here = weight_half(60, [outer_away], core_bit, *outer_args)
    outer_run = Reduction(begin_sum(outer_away), outer_here)
    pre_low, grad_one, mixed_low, grad_attended, vec_one = inner_grad(
        outer_run.sent(), outer_low, grad_two, slope, unit_one, inverse_one,
        w_attn_out, w_in, w_out, rows,
    )
    outer_run.land(vec_one)
    inner_args = (normed_low, pre_low, FF // D, False, (attended, mixed_low))
    inner_away = weight_half(8, outer_run.sent(), 1 - core_bit, *inner_args)
    outer_run.land(inner_away)
    inner_here = weight_half(60, [inner_away] + outer_run.sent(), core_bit, *inner_args)
    outer_run.land(inner_here)
    inner_run = Reduction(begin_sum(inner_away), inner_here)
    early, vec_early = unattend(
        outer_run.sent() + inner_run.sent(), 0, 2, q, k, v, p, grad_attended
    )
    outer_run.land(vec_early)
    stack_low, vec_late = unattend([], 1, 2, q, k, v, p, grad_attended, early)
    inner_run.land(vec_late)
    project_args = (tokens, stack_low, 3, False)
    project_away = weight_half(8, inner_run.sent(), 1 - core_bit, *project_args)
    project_here = weight_half(60, [project_away], core_bit, *project_args)
    inner_run.land(project_here)
    vec_heads = vec_early + vec_late
    grad_vector = jnp.concatenate(
        [
            jnp.stack([vec_one[0], vec_two[0], vec_one[1], vec_two[1]]),
            vec_heads,
            jnp.stack([vec_one[2], vec_two[2]]),
            vec_one[3:],
        ]
    )
    project_run = Reduction(begin_sum(project_away), project_here, grad_vector)
    grad_tokens = input_grad(
        inner_run.sent() + project_run.sent(), grad_one, stack_low, w_qkv
    )
    project_run.land(grad_tokens)
    inner_run.land(grad_tokens)
    outer_sum, inner_sum, project_sum = (
        run.finish() for run in (outer_run, inner_run, project_run)
    )
    vec_grad = project_run.rider
    parts = (project_sum, inner_sum[-1:], inner_sum[:-1], outer_sum)
    gathered, (low_left,) = spread(
        to_slots([], parts, owner_list), [lambda after: ready(after, left_basis, LOW)]
    )
    vec_grad = vec_grad.reshape(-1)
    new_master, new_first, new_second, master_copy = rotated_adam(
        row_place(), gathered, turn(master), turn(first_moment), turn(second_moment),
        low_left, right_basis,
    )
    vec_first_new = 0.9 * vec_first + 0.1 * vec_grad
    vec_second_new = 0.999 * vec_second + 0.001 * vec_grad * vec_grad
    vec_step = (
        vec_first_new / (1.0 - 0.9**STEP) / (jnp.sqrt(vec_second_new / (1.0 - 0.999**STEP)) + 1e-08)
    )
    vec_new = vectors - VECTOR_RATE * vec_step
    return (
        encoded,
        grad_tokens,
        loss[0, 0],
        new_master,
        new_first,
        new_second,
        master_copy,
        vec_new,
        vec_first_new,
        vec_second_new,
    )


def solution(mesh):
    in_specs = (
        P(("row", "col"), None),
        P(),
        P(),
        P(),
        P(),
        P(),
        P(("row", "col"), None),
        P(),
        P(),
        P(),
        P("col", None, None),
        P("col", None, None),
        P("col", None, None),
        P("col", None, None),
        P("col", None, None),
        P(),
        P(),
    )
    out_specs = (
        P(("row", "col"), None),
        P(("row", "col"), None),
        P(),
        P("col", None, None),
        P("col", None, None),
        P("col", None, None),
        P("col", None, None),
        P(),
        P(),
        P(),
    )
    return jax.shard_map(shards, mesh=mesh, in_specs=in_specs, out_specs=out_specs, check_vma=False)
```

```python
from functools import partial

import jax
import jax.numpy as jnp
from jax import lax
from jax.experimental import pallas as pl
from jax.experimental.pallas import tpu as pltpu
from jax.sharding import PartitionSpec as P

D = 768
HEADS = 12
HEAD = 64
FF = 3072
SPAN = 128
STEP = 10
GROUP = 8

RATE = 0.01
DECAY = 0.01
VECTOR_RATE = 0.3

LOW = jnp.bfloat16
F32 = jnp.float32
TALL = 2 * SPAN


def dot(left_side, right_side, contract=(1, 0)):
    dims = (((contract[0],), (contract[1],)), ((), ()))
    return lax.dot_general(left_side, right_side, dims, preferred_element_type=F32)


def whole(shape):
    return pl.BlockSpec(shape, lambda *ids: (0,) * len(shape))


def cost(microseconds, transcendentals=0):
    return pl.CostEstimate(
        flops=int(microseconds * 1.1e9), bytes_accessed=0, transcendentals=transcendentals
    )


def params(mebibytes=36):
    return pltpu.CompilerParams(vmem_limit_bytes=mebibytes * 1024 * 1024)


def row_of(rows, index):
    return rows[:, index * D : (index + 1) * D]


def live_rows(place, counts, first_row, height):
    at = first_row + lax.broadcasted_iota(jnp.int32, (height, 1), 0)
    return jnp.where(at < counts[place[0]] * SPAN, 1.0, 0.0)


near = pltpu.VMEM
far = pltpu.HBM


def streamed(*arrays):
    return [pltpu.with_memory_space_constraint(a, pltpu.HBM) for a in arrays]


ANY = pl.BlockSpec(memory_space=pl.ANY)
SMEM = pl.BlockSpec(memory_space=pltpu.SMEM)


def split_heads(pair):
    lane = lax.broadcasted_iota(jnp.int32, pair.shape, 1)
    zero = jnp.zeros_like(pair)
    return jnp.concatenate([jnp.where(lane < HEAD, pair, zero), jnp.where(lane < HEAD, zero, pair)])


def normalise(scores):
    peak = jnp.max(scores, axis=-1, keepdims=True)
    raised = jnp.exp(scores - peak)
    return raised * (1.0 / jnp.sum(raised, axis=-1, keepdims=True))


def attend_kernel(tokens, w_qkv, rows, q_out, k_out, v_out, p_out, a_out):
    block = tokens[...]
    scaling = HEAD ** (-0.5)
    q_out[...] = ((dot(block, w_qkv[0]) + row_of(rows, 4)).astype(LOW) * scaling).astype(LOW)
    k_out[...] = dot(block, w_qkv[1]).astype(LOW)
    v_out[...] = (dot(block, w_qkv[2]) + row_of(rows, 5)).astype(LOW)
    for span in range(TALL // SPAN):
        at = slice(span * SPAN, (span + 1) * SPAN)
        for pair in range(HEADS // 2):
            lanes = slice(pair * 2 * HEAD, (pair + 1) * 2 * HEAD)
            scores = dot(q_out[at, lanes], split_heads(k_out[at, lanes]), (1, 1))
            weights = jnp.concatenate(
                [normalise(scores[:, :SPAN]), normalise(scores[:, SPAN:])], axis=1
            ).astype(LOW)
            p_out[span, pair] = weights
            a_out[at, lanes] = dot(weights, split_heads(v_out[at, lanes])).astype(LOW)


def attend(tokens, w_qkv, rows):
    total = tokens.shape[0]
    tall = pl.BlockSpec((TALL, D), lambda i: (i, 0))
    like = far((total, D), LOW)
    tokens, w_qkv, rows = streamed(tokens, w_qkv, rows)
    spans = TALL // SPAN
    return pl.pallas_call(
        attend_kernel,
        grid=(total // TALL,),
        in_specs=[tall, whole(w_qkv.shape), whole(rows.shape)],
        out_specs=[
            tall,
            tall,
            tall,
            pl.BlockSpec((spans, HEADS // 2, SPAN, 2 * SPAN), lambda i: (i, 0, 0, 0)),
            tall,
        ],
        out_shape=[
            like,
            like,
            like,
            far((total // SPAN, HEADS // 2, SPAN, 2 * SPAN), LOW),
            near((total, D), LOW),
        ],
        compiler_params=params(),
        cost_estimate=cost(10),
        name="attend",
    )(tokens, w_qkv, rows)


def unit_norm(resid):
    centred = resid - jnp.mean(resid, axis=-1, keepdims=True)
    inverse = lax.rsqrt(jnp.mean(centred * centred, axis=-1, keepdims=True) + 1e-06)
    return centred * inverse, inverse


def gelu_pair(x):
    cdf = 0.5 + 0.5 * lax.erf(x * 0.7071067811865476)
    return x * cdf, cdf + x * jnp.exp(-0.5 * x * x) * 0.3989422804014327


def feed_kernel(
    place, counts, tokens, attended, w_attn, w_in, w_out, rows, bias,
    enc_out, hid_out, slope_out, norm_out, u1_out, i1_out, u2_out, i2_out, cls_out, total, firsts,
):
    band = pl.program_id(0)
    chunks = [slice(at, at + TALL) for at in range(0, tokens.shape[0], TALL)]

    @pl.when(band == 0)
    def _():
        for at in chunks:
            resid = tokens[at].astype(F32) + dot(attended[at], w_attn[...]) + row_of(rows, 6)
            unit_one, inverse_one = unit_norm(resid)
            value = unit_one * row_of(rows, 0) + row_of(rows, 2)
            u1_out[at] = unit_one.astype(LOW)
            i1_out[at] = inverse_one
            norm_out[at] = value.astype(LOW)
            total[at] = value + row_of(rows, 7)

    step = 256
    for at in range(0, hid_out.shape[1], step):
        here = slice(at, at + step)
        pre_act = dot(norm_out[...], w_in[:, here]) + bias[:, here]
        hidden, slope = gelu_pair(pre_act)
        hid_out[:, here] = hidden.astype(LOW)
        slope_out[:, here] = slope.astype(LOW)

    @pl.when(band < pl.num_programs(0) - 1)
    def _():
        total[...] += dot(hid_out[...], w_out[...])

    @pl.when(band == pl.num_programs(0) - 1)
    def _():
        for at in chunks:
            resid = total[at] + dot(hid_out[at], w_out[...])
            unit_two, inverse_two = unit_norm(resid)
            u2_out[at] = unit_two.astype(LOW)
            i2_out[at] = inverse_two
            live = live_rows(place, counts, at.start, TALL)
            value = live * (unit_two * row_of(rows, 1) + row_of(rows, 3))
            enc_out[at] = value.astype(LOW)
            for first in range(at.start, at.stop, SPAN):
                row = first - at.start
                firsts[first // SPAN : first // SPAN + 1] = value[row : row + 1]
        firsts[tokens.shape[0] // SPAN :] = jnp.zeros((GROUP - tokens.shape[0] // SPAN, D), F32)
        cls_out[...] = firsts[...].astype(LOW)


def feed(place, counts, tokens, attended, w_attn, w_in, w_out, rows):
    total = tokens.shape[0]
    tall = lambda width: pl.BlockSpec((total, width), lambda j: (0, 0))
    band = lambda height: pl.BlockSpec((height, D), lambda j: (0, j))
    tokens, w_attn, w_in, w_out, rows = streamed(tokens, w_attn, w_in, w_out, rows)
    return pl.pallas_call(
        feed_kernel,
        grid=(FF // D,),
        in_specs=[
            SMEM, SMEM, tall(D), tall(D), whole(w_attn.shape), band(D),
            pl.BlockSpec((D, D), lambda j: (j, 0)),
            pl.BlockSpec((1, 8 * D), lambda j: (0, 0)),
            pl.BlockSpec((1, D), lambda j: (0, 8 + j)),
        ],
        out_specs=[
            tall(D), band(total), band(total), tall(D), tall(D), tall(1), tall(D), tall(1),
            whole((GROUP, D)),
        ],
        out_shape=[
            jax.ShapeDtypeStruct((total, D), LOW),
            far((total, FF), LOW),
            far((total, FF), LOW),
            far((total, D), LOW),
            far((total, D), LOW),
            far((total, 1), F32),
            near((total, D), LOW),
            near((total, 1), F32),
            jax.ShapeDtypeStruct((GROUP, D), LOW),
        ],
        scratch_shapes=[pltpu.VMEM((total, D), F32), pltpu.VMEM((GROUP, D), F32)],
        compiler_params=params(),
        cost_estimate=cost(20),
        name="feed",
    )(place, counts, tokens, attended, w_attn, w_in, w_out, rows, rows)


def norm_back(grad_out, unit_rows, inverse, gain):
    scaled = grad_out * gain
    along = jnp.mean(scaled * unit_rows, axis=-1, keepdims=True)
    return inverse * (scaled - jnp.mean(scaled, axis=-1, keepdims=True) - unit_rows * along)


def column_sums(*arrays):
    return [jnp.sum(a, axis=0, keepdims=True) for a in arrays]


def outer_kernel(place, counts, out_grad, grad_cls, unit_two, inverse_two, rows, two_out, low_out, vec_out):
    spot = lax.broadcasted_iota(jnp.int32, (SPAN, 1), 0) == 0
    sums = None
    for span in range(out_grad.shape[0] // SPAN):
        at = slice(span * SPAN, (span + 1) * SPAN)
        added = jnp.where(spot, grad_cls[span : span + 1], 0.0)
        live = live_rows(place, counts, span * SPAN, SPAN)
        grad_y = live * (out_grad[at].astype(F32) + added)
        unit_rows = unit_two[at].astype(F32)
        grad_two = norm_back(grad_y, unit_rows, inverse_two[at], row_of(rows, 1))
        two_out[at] = grad_two
        low_out[at] = grad_two.astype(LOW)
        here = column_sums(grad_y * unit_rows, grad_y, grad_two)
        sums = here if sums is None else [a + b for a, b in zip(sums, here)]
    for index, total in enumerate(sums):
        vec_out[index : index + 1] = total


def outer_grad(place, counts, out_grad, grad_cls, unit_two, inverse_two, rows):
    total = out_grad.shape[0]
    return pl.pallas_call(
        outer_kernel,
        in_specs=[SMEM, SMEM] + [pl.BlockSpec(memory_space=pltpu.VMEM)] * 5,
        out_shape=[
            jax.ShapeDtypeStruct((total, D), F32),
            jax.ShapeDtypeStruct((total, D), LOW),
            jax.ShapeDtypeStruct((3, D), F32),
        ],
        compiler_params=params(),
        cost_estimate=cost(5),
        name="outer",
    )(place, counts, out_grad, grad_cls, unit_two, inverse_two, rows)


def weight_kernel(panels, after, side, *refs):
    *sides, out = refs[after:]

    @pl.when(pl.program_id(0) < panels)
    def _():
        out[0] = dot(sides[0][...], sides[1][...], (0, 0)).astype(LOW)

    if len(sides) > 2:

        @pl.when(pl.program_id(0) == panels)
        def _():
            out[0] = dot(sides[2][...], sides[3][...], (0, 0)).astype(LOW)


def weight_half(hint, after, side, left_side, right_side, panels, banded, extra=()):
    total = left_side.shape[0]
    half = D // 2
    every = panels + len(extra) // 2
    tall = lambda width, at: pl.BlockSpec((total, width), at)
    last = lambda panel: jnp.minimum(panel, panels - 1)
    left_at = lambda panel, side: (0, last(panel) * 2 + side[0] if banded else side[0])
    right_at = lambda panel, side: (0, 0 if banded else last(panel))
    more = [tall(half, lambda p, s: (0, s[0])), tall(D, lambda p, s: (0, 0))]
    return pl.pallas_call(
        partial(weight_kernel, panels, len(after)),
        grid_spec=pltpu.PrefetchScalarGridSpec(
            num_scalar_prefetch=1,
            grid=(every,),
            in_specs=[ANY] * len(after)
            + [tall(half, left_at), tall(D, right_at)]
            + more[: len(extra)],
            out_specs=pl.BlockSpec((1, half, D), lambda p, s: (p, 0, 0)),
        ),
        out_shape=jax.ShapeDtypeStruct((every, half, D), LOW),
        compiler_params=params(),
        cost_estimate=cost(hint),
        name="weight",
    )(side.reshape(1), *after, left_side, right_side, *extra)


def inner_kernel(after, *refs):
    low, grad_two, slope, unit_one, inverse_one, w_attn, w_in, w_out, rows = refs[after:-6]
    pre_out, one_out, mixed_out, ga_out, vec_out, total = refs[-6:]
    band = pl.program_id(0)
    last = pl.num_programs(0) - 1
    step = 256
    for at in range(0, D, step):
        here = slice(at, at + step)
        grad_pre = dot(low[...], w_out[here], (1, 1)) * slope[:, here].astype(F32)
        pre_out[:, here] = grad_pre.astype(LOW)
        vec_out[pl.ds(3 + band, 1), here] = jnp.sum(grad_pre, axis=0, keepdims=True)

    @pl.when(band == 0)
    def _():
        total[...] = grad_two[...] + dot(pre_out[...], w_in[...], (1, 1))

    @pl.when((band > 0) & (band < last))
    def _():
        total[...] += dot(pre_out[...], w_in[...], (1, 1))

    @pl.when(band == last)
    def _():
        sums = None
        for first in range(0, low.shape[0], TALL):
            at = slice(first, first + TALL)
            grad_normed = total[at] + dot(pre_out[at], w_in[...], (1, 1))
            unit_rows = unit_one[at].astype(F32)
            grad_one = norm_back(grad_normed, unit_rows, inverse_one[at], row_of(rows, 0))
            one_out[at] = grad_one
            mixed = grad_one.astype(LOW)
            mixed_out[at] = mixed
            ga_out[at] = dot(mixed, w_attn[...], (1, 1)).astype(LOW)
            here = column_sums(grad_normed * unit_rows, grad_normed, grad_one)
            sums = here if sums is None else [a + b for a, b in zip(sums, here)]
        for index, value in enumerate(sums):
            vec_out[index : index + 1] = value


def inner_grad(after, low, grad_two, slope, unit_one, inverse_one, w_attn, w_in, w_out, rows):
    total = low.shape[0]
    bands = FF // D
    slope, w_attn, w_in, w_out, rows = streamed(slope, w_attn, w_in, w_out, rows)
    band = lambda height: pl.BlockSpec((height, D), lambda j: (0, j))
    return pl.pallas_call(
        partial(inner_kernel, len(after)),
        grid=(bands,),
        in_specs=[ANY] * len(after)
        + [
            whole(low.shape), whole(grad_two.shape), band(total), whole(unit_one.shape),
            whole(inverse_one.shape), whole(w_attn.shape), band(D),
            pl.BlockSpec((D, D), lambda j: (j, 0)), whole(rows.shape),
        ],
        out_specs=[band(total)] + [whole((total, D))] * 3 + [whole((3 + bands, D))],
        out_shape=[
            near((total, FF), LOW),
            far((total, D), F32),
            near((total, D), LOW),
            near((total, D), LOW),
            jax.ShapeDtypeStruct((3 + bands, D), F32),
        ],
        scratch_shapes=[pltpu.VMEM((total, D), F32)],
        compiler_params=params(),
        cost_estimate=cost(16),
        name="inner",
    )(*after, low, grad_two, slope, unit_one, inverse_one, w_attn, w_in, w_out, rows)


def unattend_kernel(after, sums, *refs):
    q, k, v, p, ga = refs[after : after + 5]
    vec_one, vec_two, vec_early = refs[after + 5 : -2] if sums else (None, None, None)
    stack_out, vec_out = refs[-2:]
    scaling = HEAD ** (-0.5)
    first = pl.program_id(0) == 0

    @pl.when(first)
    def _():
        if not sums:
            vec_out[...] = jnp.zeros_like(vec_out)
            return
        for index in range(2):
            vec_out[2 * index : 2 * index + 1] = vec_one[index : index + 1]
            vec_out[2 * index + 1 : 2 * index + 2] = vec_two[index : index + 1]
        vec_out[4:6] = vec_early[...]
        vec_out[6:7] = vec_one[2:3]
        vec_out[7:8] = vec_two[2:3]
        vec_out[8:] = vec_one[3:]

    place = 4 if sums else 0
    for span in range(p.shape[0]):
        at = slice(span * SPAN, (span + 1) * SPAN)
        for pair in range(HEADS // 2):
            lo = pair * 2 * HEAD
            lanes = slice(lo, lo + 2 * HEAD)
            weights = p[span, pair]
            grad = ga[at, lanes]
            spread_out = dot(grad, split_heads(v[at, lanes]), (1, 1))
            wide = weights.astype(F32)
            parts = []
            for half in range(2):
                cols = slice(half * SPAN, (half + 1) * SPAN)
                wgt, gw = wide[:, cols], spread_out[:, cols]
                parts.append((wgt * (gw - jnp.sum(gw * wgt, axis=-1, keepdims=True))).astype(LOW))
            grad_scores = jnp.concatenate(parts, axis=1)
            grad_q = dot(grad_scores, split_heads(k[at, lanes])) * scaling
            tall_scores = jnp.concatenate(parts, axis=0)
            tall_weights = jnp.concatenate([weights[:, :SPAN], weights[:, SPAN:]], axis=0)
            grad_k = dot(tall_scores, split_heads(q[at, lanes]), (0, 0))
            grad_v = dot(tall_weights, split_heads(grad), (0, 0))
            stack_out[at, lo : lo + 2 * HEAD] = grad_q.astype(LOW)
            stack_out[at, D + lo : D + lo + 2 * HEAD] = grad_k.astype(LOW)
            stack_out[at, 2 * D + lo : 2 * D + lo + 2 * HEAD] = grad_v.astype(LOW)
            vec_out[place : place + 1, lanes] += jnp.sum(grad_q, axis=0, keepdims=True)
            vec_out[place + 1 : place + 2, lanes] += jnp.sum(grad_v, axis=0, keepdims=True)


def unattend(after, part, parts, q, k, v, p, ga, stack=None, sums=()):
    total = q.shape[0]
    count = total // SPAN // parts
    first = part * count
    tall = lambda width: pl.BlockSpec((SPAN, width), lambda i: (first + i, 0))
    after = after if stack is None else [stack] + after
    vec_shape = (12, D) if sums else (2, D)
    return pl.pallas_call(
        partial(unattend_kernel, len(after), bool(sums)),
        grid=(count,),
        in_specs=[ANY] * len(after)
        + [tall(D)] * 3
        + [
            pl.BlockSpec((1, HEADS // 2, SPAN, 2 * SPAN), lambda i: (first + i, 0, 0, 0)),
            tall(D),
        ]
        + [whole(a.shape) for a in sums],
        out_specs=[tall(3 * D), whole(vec_shape)],
        out_shape=[far((total, 3 * D), LOW), jax.ShapeDtypeStruct(vec_shape, F32)],
        input_output_aliases={} if stack is None else {0: 0},
        compiler_params=params(),
        cost_estimate=cost(8),
        name="unattend",
    )(*after, q, k, v, p, ga, *sums)


def input_kernel(*refs):
    grad_one, stack, w_qkv, out = refs[-4:]
    total = grad_one[...]
    for index in range(3):
        total += dot(stack[:, index * D : (index + 1) * D], w_qkv[index], (1, 1))
    out[...] = total


def input_grad(after, grad_one, stack, w_qkv):
    total = grad_one.shape[0]
    tall = lambda width: pl.BlockSpec((TALL, width), lambda i: (i, 0))
    return pl.pallas_call(
        input_kernel,
        grid=(total // TALL,),
        in_specs=[ANY] * len(after) + [tall(D), tall(3 * D), whole(w_qkv.shape)],
        out_specs=tall(D),
        out_shape=jax.ShapeDtypeStruct((total, D), F32),
        compiler_params=params(),
        cost_estimate=cost(8),
        name="input",
    )(*after, grad_one, stack, w_qkv)


def contrast_kernel(slots, masks, place, rows, counts, partners, loss_out, grad_out):
    total, scale = rows.shape[0], 2.0 * D ** (-0.5)

    def number(shape, axis):
        at = lax.broadcasted_iota(jnp.int32, shape, axis)
        device, block = jnp.full(shape, place[0], jnp.int32), at // GROUP
        for bit, mask in enumerate(masks):
            device = device ^ (((block >> bit) & 1) * mask)
        return device, at % GROUP

    device, slot = number((counts.shape[1], total), 1)
    hit = lax.broadcasted_iota(jnp.int32, device.shape, 0) == device
    count = dot(counts[...].astype(LOW), jnp.where(hit, 1.0, 0.0).astype(LOW))
    live_across = (slot[:1].astype(F32) < count) & (slot[:1] < slots)
    device, slot = number((total, counts.shape[1]), 0)
    hit = lax.broadcasted_iota(jnp.int32, device.shape, 1) == device
    count = jnp.sum(jnp.where(hit, counts[...], 0.0), axis=1, keepdims=True)
    live_down = (slot[:, :1].astype(F32) < count) & (slot[:, :1] < slots)
    device, slot = number((total, partners.shape[1]), 0)
    own_id = device * slots + slot
    hit = lax.broadcasted_iota(jnp.int32, own_id.shape, 1) == own_id
    pair = jnp.sum(jnp.where(hit, partners[...], 0.0), axis=1, keepdims=True)
    device, slot = number((total, 128), 0)
    down = (device * slots + slot).astype(F32)[:, :1]
    device, slot = number((8, total), 1)
    across, slot = (device * slots + slot).astype(F32)[:1], slot[:1]
    valid = live_across & (down != across)
    matched = jnp.where((slot < slots) & (pair == across), 1.0, 0.0)
    anchor = jnp.where(live_down & (pair != down), 1.0, 0.0)
    similar = dot(rows[...], rows[...], (1, 1)) * scale
    masked = jnp.where(valid, similar, -1e30)
    peak = jnp.max(masked, axis=1, keepdims=True)
    summed = jnp.sum(jnp.where(valid, jnp.exp(masked - peak), 0.0), axis=1, keepdims=True)
    log_total = jnp.log(summed) + peak
    positive = jnp.sum(matched * similar, axis=1, keepdims=True)
    loss_out[...] = jnp.sum(anchor * (log_total - positive), axis=0, keepdims=True)
    grad = (anchor * (jnp.where(valid, jnp.exp(masked - log_total), 0.0) - matched)).astype(LOW)
    own = lax.broadcasted_iota(jnp.int32, (GROUP, total), 0)
    own = jnp.where(own == lax.broadcasted_iota(jnp.int32, (GROUP, total), 1), 1.0, 0.0)
    down_part = dot(dot(own.astype(LOW), grad, (1, 1)).astype(LOW), rows[...])
    grad_out[...] = (dot(grad[: 2 * GROUP], rows[...])[:GROUP] + down_part) * scale


def contrast(cls_rows, span_count, pair_index, device, slots):
    total = cls_rows.shape[0]
    scale = {"row": lax.axis_size("col"), "col": 1}
    masks = [scale[name] * bit for name, bit in gather_steps()]
    return pl.pallas_call(
        partial(contrast_kernel, slots, masks),
        in_specs=[pl.BlockSpec(memory_space=pltpu.SMEM)]
        + [pl.BlockSpec(memory_space=pltpu.VMEM)] * 3,
        out_shape=[
            jax.ShapeDtypeStruct((1, 1), F32),
            jax.ShapeDtypeStruct((GROUP, D), F32),
        ],
        compiler_params=params(),
        cost_estimate=cost(3),
        name="contrast",
    )(
        device,
        cls_rows,
        span_count.astype(F32).reshape(1, -1),
        pair_index.astype(F32).reshape(1, -1),
    )


def adam_kernel(
    packed, parts, position, *refs,
):
    gathered = refs[:parts]
    master, first, second, left, right, master_out, first_out, second_out, low_out, *scratch = refs[parts:]
    quarter = D // 4
    slot = pl.program_id(0)
    if packed:
        owned = scratch[0]
        shares, tall, _ = gathered[0].shape
        rows = D // (shares * parts)

        @pl.when(slot == 0)
        def _():
            for part in range(parts):
                for share in range(shares):
                    block = gathered[part][share].astype(F32)
                    number = part * shares + share
                    at = pl.multiple_of((number ^ position[0]) * rows, rows)
                    for index in range(owned.shape[0]):
                        lo = index * rows % tall
                        side = index * rows // tall
                        piece = block[lo : lo + rows, side * quarter : (side + 1) * quarter]
                        owned[index, pl.ds(at, rows), :] = piece

        gradient = owned[slot].astype(LOW)
    else:
        gradient = gathered[0][0]
    low_left, low_right = left[0], right[0].astype(LOW)
    turned = dot(gradient, low_left, (0, 0))
    turned = dot(low_right, turned.astype(LOW), (0, 0))
    new_first = 0.9 * first[0] + 0.1 * turned
    new_second = 0.999 * second[0] + 0.001 * turned * turned
    first_out[0] = new_first
    second_out[0] = new_second
    spread_by = jnp.sqrt(new_second * (1.0 / (1.0 - 0.999**STEP))) + 1e-08
    update = new_first * (1.0 / (1.0 - 0.9**STEP)) / spread_by
    update = dot(update.astype(LOW), low_left, (1, 1))
    update = dot(low_right, update.astype(LOW))
    new_master = master[0] - RATE * (update + DECAY * master[0])
    master_out[0] = new_master
    low_out[0] = new_master.astype(LOW)


def ready_kernel(*refs):
    source, out = refs[-2:]
    out[...] = source[...].astype(out.dtype)


def ready(after, array, kind):
    block = pl.BlockSpec((1,) + array.shape[1:], lambda s: (s, 0, 0))
    return pl.pallas_call(
        ready_kernel,
        grid=(array.shape[0],),
        in_specs=[ANY] * len(after) + [block],
        out_specs=block,
        out_shape=far(array.shape, kind),
        compiler_params=params(16),
        cost_estimate=cost(4),
        name="ready",
    )(*after, *streamed(array))


def to_owned(gathered, position, per_owner):
    quarter = D // 4
    gathered = jnp.take(gathered, jnp.arange(gathered.shape[0]) ^ position, axis=0)
    flat = jnp.concatenate([gathered[..., :quarter], gathered[..., quarter:]], axis=1)
    rows = flat.shape[1] // per_owner
    flat = flat.reshape(flat.shape[0], per_owner, rows, quarter).transpose(1, 0, 2, 3)
    return flat.reshape(per_owner, D, quarter)


def turn(array):
    return array.transpose(0, 2, 1)


def rotated_adam(position, gathered, master, first_moment, second_moment, left_basis, right_basis):
    per_owner, quarter, _ = master.shape
    rows = D // sum(part.shape[0] for part in gathered)
    packed = rows % 8 == 0 and per_owner % 2 == 0
    if not packed:
        gathered = [to_owned(jnp.concatenate(gathered), position, per_owner)]
    block = lambda a: pl.BlockSpec((1,) + a.shape[1:], lambda s, p: (s, 0, 0))
    operands = streamed(master, first_moment, second_moment, left_basis, right_basis)
    like = jax.ShapeDtypeStruct(operands[0].shape, F32)
    fixed = pl.BlockSpec(gathered[0].shape, lambda s, p: (0, 0, 0))
    outputs = pl.pallas_call(
        partial(adam_kernel, packed, len(gathered)),
        grid_spec=pltpu.PrefetchScalarGridSpec(
            num_scalar_prefetch=1,
            grid=(per_owner,),
            in_specs=[fixed if packed else block(part) for part in gathered]
            + [block(a) for a in operands],
            out_specs=[block(operands[0])] * 4,
            scratch_shapes=[pltpu.VMEM((per_owner, D, quarter), F32)] if packed else [],
        ),
        out_shape=[like, like, like, jax.ShapeDtypeStruct(like.shape, LOW)],
        compiler_params=params(28),
        cost_estimate=cost(20),
        name="adam",
    )(position.reshape(1), *gathered, *operands)
    return [turn(a) for a in outputs]


def axis_bits(name):
    size = lax.axis_size(name)
    return [(name, 1 << k) for k in range(size.bit_length() - 1)]


def bit_of(step):
    return jnp.where((lax.axis_index(step[0]) & step[1]) != 0, 1, 0)


def swap(send, step):
    size = lax.axis_size(step[0])
    return lax.ppermute(send, step[0], [(i, i ^ step[1]) for i in range(size)])


def gather_steps():
    core, across, y_bits, z_bits = row_steps()
    return z_bits[::-1] + y_bits + across + core


def gather_all(rows):
    for step in gather_steps():
        rows = jnp.concatenate([rows, swap(rows, step)])
    return rows


def row_steps():
    row_bits, col_bits = axis_bits("row"), axis_bits("col")
    core, across = row_bits[:1], row_bits[1:][::-1]
    y_bits, z_bits = col_bits[:-2][::-1], col_bits[-2:]
    return core, across, y_bits, z_bits


def pack_rider(rider, rows, width):
    parts = [rider[:, at : at + width] for at in range(0, D, width)]
    tall = rider.shape[0]
    if rows < tall:
        return [part[at : at + rows] for part in parts for at in range(0, tall, rows)]
    fold = rows // tall
    parts += parts[-1:] * (-len(parts) % fold)
    return [jnp.concatenate(parts[at : at + fold]) for at in range(0, len(parts), fold)]


def unpack_rider(blocks, tall):
    rows, width = blocks[0].shape
    if rows < tall:
        fold = tall // rows
        parts = [jnp.concatenate(blocks[at : at + fold]) for at in range(0, len(blocks), fold)]
    else:
        parts = [block[at : at + tall] for block in blocks for at in range(0, rows, tall)]
    parts = parts[: D // width]
    return parts[0] if len(parts) == 1 else jnp.concatenate(parts, axis=1)


def rider_blocks(rows, width, tall=12):
    return -(-tall * D // (rows * width))


def land_kernel(after, outs, rider, bits, *refs):
    refs = refs[after:]
    sides = len({source[0] for out in outs for source in out[3]})
    keeps, others = refs[0 : 2 * sides : 2], refs[1 : 2 * sides : 2]
    results = refs[2 * sides + (0 if rider is None else 1 + (rider == "array")) :]
    if rider is not None:
        total = refs[2 * sides][...]
        tall = total.shape[0]
        if rider == "array":
            total += refs[2 * sides + 1][...]
        else:
            blocks = [others[0][at].astype(F32) for at in range(keeps[0].shape[0], others[0].shape[0])]
            total += unpack_rider(blocks, tall)
        results[-1][...] = total
    for number, (at_bit, before, behind, sources) in enumerate(outs):
        bit = bits[at_bit]
        for which, target in enumerate(results[2 * number : 2 * number + 2]):
            half = bit if which else 1 - bit
            for at in range(before):
                here = pl.ds((2 * at + half) * behind, behind)
                there = slice(at * behind, (at + 1) * behind)
                for side, lanes, into in sources:
                    target[there, :, into] = keeps[side][here, :, lanes] + others[side][here, :, lanes]
        if rider is not None and number == 0:
            away = results[0]
            count, rows, width = away.shape
            blocks = pack_rider(total, rows, width)
            for index, block in enumerate(blocks):
                away[count - len(blocks) + index] = block.astype(LOW)


class Reduction:
    def __init__(self, bits, ways, send, keep, rider=None):
        core, across, y_bits, z_bits = row_steps()
        self.bits, self.order = bits, core + across + y_bits + z_bits
        left = across + y_bits + z_bits
        self.panels, height, _ = keep.shape
        self.rows = height >> len(left)
        other = swap(send, core[0])
        self.rider = None if rider is None else (rider, swap(rider, core[0]))
        split = lambda a: a.reshape(-1, self.rows, D)
        self.sides = [(split(keep), split(other), left)]
        cycle = [across, y_bits, z_bits[:1]][:ways]
        orders = [sum(cycle[at:] + cycle[:at], []) for at in range(ways)]
        self.stages = list(zip(*orders)) + [(step,) for step in z_bits[ways - 2 :]]
        self.ways = ways
        self.messages = []

    def sent(self):
        return self.messages

    def landing(self):
        return [side[1] for side in self.sides]

    def land(self, *after):
        stage = self.stages.pop(0)
        outs, shapes, lefts = [], [], []
        part = D // self.ways
        lanes = [slice(at, at + part) for at in range(0, D, part)]
        for index, step in enumerate(stage):
            if len(self.sides) == len(stage):
                width = self.sides[index][0].shape[2]
                sources = [(index, slice(0, width), slice(0, width))]
                left = self.sides[index][2]
            elif len(stage) > 1:
                width, left = part, self.sides[0][2]
                sources = [(0, lanes[index], slice(0, part))]
            else:
                width, left = D, self.sides[0][2]
                sources = [(side, slice(0, part), lanes[side]) for side in range(self.ways)]
            dim = left.index(step)
            behind = 1 << (len(left) - dim - 1)
            before = self.panels << dim
            outs.append((self.order.index(step), before, behind, sources))
            extra = rider_blocks(self.rows, width) if self.rider and index == 0 else 0
            shapes += [(before * behind + extra, self.rows, width), (before * behind, self.rows, width)]
            lefts.append([other for other in left if other != step])
        rider = None if self.rider is None else ("array" if len(self.rider) == 2 else "message")
        inputs = [a for keep, other, _ in self.sides for a in (keep, other)] + list(self.rider or ())
        out_shape = [jax.ShapeDtypeStruct(shape, LOW) for shape in shapes]
        if rider:
            out_shape.append(jax.ShapeDtypeStruct(self.rider[0].shape, F32))
        results = pl.pallas_call(
            partial(land_kernel, len(after), outs, rider),
            in_specs=[SMEM] + [ANY] * len(after) + [pl.BlockSpec(memory_space=pltpu.VMEM)] * len(inputs),
            out_shape=out_shape,
            compiler_params=params(24),
            cost_estimate=cost(2),
            name="land",
        )(self.bits, *after, *inputs)
        if rider:
            self.rider = (results[-1],)
        self.messages = list(results[0 : 2 * len(stage) : 2])
        keeps = results[1 : 2 * len(stage) : 2]
        self.sides = [
            (keep, swap(message, step), left)
            for keep, message, step, left in zip(keeps, self.messages, stage, lefts)
        ]

    def finish(self):
        while self.stages:
            self.land()


def slots_kernel(cols, panels, bits, owners, *refs):
    sums, rider = refs[:6], refs[6]
    away, here, rider_out, blocks, packed = refs[7:]
    quarter = D // 4
    found = [(sums[2 * run], sums[2 * run + 1], i) for run in range(3) for i in range(sums[2 * run].shape[0])]
    at = 0
    for panel in panels:
        keep, other, index = found[panel]
        value = keep[index].astype(F32) + other[index].astype(F32)
        for part in range(4):
            blocks[at] = value[:, part * quarter : (part + 1) * quarter]
            at += 1
    tail = [sums[1][index].astype(F32) for index in range(sums[0].shape[0], sums[1].shape[0])]
    rider_out[...] = rider[...] + unpack_rider(tail, rider.shape[0])
    rows, half = blocks.shape[1], packed.shape[1]
    for slot in range(at):
        col, place = divmod(slot, at // cols)
        value = blocks[owners[slot]]
        first = place * rows
        for side in range(2):
            lo, hi = max(first, side * half), min(first + rows, (side + 1) * half)
            if lo < hi:
                lanes = slice(side * quarter, (side + 1) * quarter)
                packed[col, lo - side * half : hi - side * half, lanes] = value[lo - first : hi - first]
    bit = bits[bits.shape[0] - 1]
    count = cols // 2
    away[...] = packed[pl.ds((1 - bit) * count, count)].astype(LOW)
    here[...] = packed[pl.ds(bit * count, count)].astype(LOW)


def to_slots(bits, runs, panels, owner_list):
    quarter, cols = D // 4, lax.axis_size("col")
    arrays = [a for run in runs for a in run.sides[0][:2]]
    rows = runs[0].rows
    shape = (cols, len(panels) * 4 // cols * rows // 2, 2 * quarter)
    like = jax.ShapeDtypeStruct((cols // 2,) + shape[1:], LOW)
    rider = runs[0].rider[0]
    return pl.pallas_call(
        partial(slots_kernel, cols, panels),
        in_specs=[SMEM, SMEM] + [pl.BlockSpec(memory_space=pltpu.VMEM)] * 7,
        out_shape=[like, like, jax.ShapeDtypeStruct(rider.shape, F32)],
        scratch_shapes=[pltpu.VMEM((len(panels) * 4, rows, quarter), F32), pltpu.VMEM(shape, F32)],
        compiler_params=params(24),
        cost_estimate=cost(4),
        name="slots",
    )(bits, owner_list, *arrays, rider)


def regroup_kernel(after, at_bit, before, behind, bits, *refs):
    parts, (away, here) = refs[after:-2], refs[-2:]
    bit = bits[at_bit]
    for which, target in ((1 - bit, away), (bit, here)):
        to = 0
        for part in parts:
            for at in range(before):
                target[to : to + behind] = part[pl.ds((2 * at + which) * behind, behind)]
                to += behind


def regroup(bits, at_bit, after, parts, before, behind):
    count, tall, width = parts[0].shape
    like = jax.ShapeDtypeStruct((count * len(parts) // 2, tall, width), LOW)
    return pl.pallas_call(
        partial(regroup_kernel, len(after), at_bit, before, behind),
        in_specs=[SMEM] + [ANY] * len(after) + [pl.BlockSpec(memory_space=pltpu.VMEM)] * len(parts),
        out_shape=[like, like],
        compiler_params=params(24),
        cost_estimate=cost(2),
        name="regroup",
    )(bits, *after, *parts)


def spread(bits, away, here, beside):
    core, across, y_bits, z_bits = row_steps()
    order = core + across + y_bits + z_bits
    left = axis_bits("col")[::-1]
    made, shares = [], 1
    for step in (y_bits + z_bits)[::-1]:
        dim = left.index(step)
        if shares > 1:
            after = streamed(*made[-1:]) if len(made) == shares.bit_length() - 1 else []
            behind = 1 << (len(left) - dim - 1)
            before = shares // 2 << dim
            away, here = regroup(bits, order.index(step), after, parts, before, behind)
        left.remove(step)
        parts = [here, swap(away, step)]
        if len(made) < len(beside):
            made.append(beside[len(made)]([away] + streamed(*made[-1:])))
        shares *= 2
    for step in (core + across)[::-1]:
        parts = parts + [swap(part, step) for part in parts]
    return parts, made


def row_place():
    place = 0
    for group in row_steps():
        for step in group:
            place = place * 2 + bit_of(step)
    return place


def shards(
    tokens,
    w_qkv,
    w_attn_out,
    w_in,
    w_out,
    vectors,
    out_grad,
    span_count,
    pair_index,
    owner_list,
    master,
    first_moment,
    second_moment,
    left_basis,
    right_basis,
    vec_first,
    vec_second,
):
    slots = tokens.shape[0] // SPAN
    device = (lax.axis_index("row") * lax.axis_size("col") + lax.axis_index("col")).reshape(1)
    core, across, y_bits, z_bits = row_steps()
    core_bit = bit_of(core[0])
    bits = jnp.stack([bit_of(step) for step in core + across + y_bits + z_bits])
    rows = vectors.reshape(1, -1)
    q, k, v, p, attended = attend(tokens, w_qkv, rows)
    encoded, hidden, slope, normed_low, unit_one, inverse_one, unit_two, inverse_two, cls_rows = (
        feed(device, span_count, tokens, attended, w_attn_out, w_in, w_out, rows)
    )
    loss, grad_cls = contrast(gather_all(cls_rows), span_count, pair_index, device, slots)
    grad_two, outer_low, vec_two = outer_grad(
        device, span_count, out_grad, grad_cls, unit_two, inverse_two, rows
    )
    outer_args = (hidden, outer_low, FF // D, True)
    outer_away = weight_half(8, [], 1 - core_bit, *outer_args)
    outer_here = weight_half(60, [outer_away], core_bit, *outer_args)
    outer_run = Reduction(bits, 2, outer_away, outer_here)
    outer_run.land()
    pre_low, grad_one, mixed_low, grad_attended, vec_one = inner_grad(
        outer_run.sent(), outer_low, grad_two, slope, unit_one, inverse_one,
        w_attn_out, w_in, w_out, rows,
    )
    outer_run.land(vec_one)
    inner_args = (normed_low, pre_low, FF // D, False, (attended, mixed_low))
    inner_away = weight_half(8, outer_run.sent(), 1 - core_bit, *inner_args)
    outer_run.land(inner_away)
    inner_here = weight_half(60, [inner_away] + outer_run.sent(), core_bit, *inner_args)
    outer_run.land(inner_here)
    inner_run = Reduction(bits, 3, inner_away, inner_here)
    inner_run.land()
    early, vec_early = unattend(
        outer_run.sent() + inner_run.sent(), 0, 2, q, k, v, p, grad_attended
    )
    stack_low, vec_grad = unattend(
        [], 1, 2, q, k, v, p, grad_attended, early, (vec_one, vec_two, vec_early)
    )
    inner_run.land(vec_grad)
    project_args = (tokens, stack_low, 3, False)
    project_away = weight_half(
        8, inner_run.sent() + outer_run.landing(), 1 - core_bit, *project_args
    )
    project_here = weight_half(60, [project_away], core_bit, *project_args)
    inner_run.land(project_here)
    project_run = Reduction(bits, 3, project_away, project_here, vec_grad)
    project_run.land()
    inner_run.land()
    project_run.land()
    for run in (outer_run, inner_run, project_run):
        run.finish()
    slots_away, slots_here, vec_grad = to_slots(
        bits, (project_run, inner_run, outer_run), (0, 1, 2, 7, 3, 4, 5, 6, 8, 9, 10, 11), owner_list
    )
    vec_grad = vec_grad.reshape(-1)
    gathered, (low_left, grad_tokens) = spread(
        bits,
        slots_away,
        slots_here,
        [
            lambda after: ready(after, left_basis, LOW),
            lambda after: input_grad(after, grad_one, stack_low, w_qkv),
        ],
    )
    new_master, new_first, new_second, master_copy = rotated_adam(
        row_place(), gathered, turn(master), turn(first_moment), turn(second_moment),
        low_left, right_basis,
    )
    vec_first_new = 0.9 * vec_first + 0.1 * vec_grad
    vec_second_new = 0.999 * vec_second + 0.001 * vec_grad * vec_grad
    vec_step = (
        vec_first_new / (1.0 - 0.9**STEP) / (jnp.sqrt(vec_second_new / (1.0 - 0.999**STEP)) + 1e-08)
    )
    vec_new = vectors - VECTOR_RATE * vec_step
    return (
        encoded,
        grad_tokens,
        loss[0, 0],
        new_master,
        new_first,
        new_second,
        master_copy,
        vec_new,
        vec_first_new,
        vec_second_new,
    )


def solution(mesh):
    in_specs = (
        P(("row", "col"), None),
        P(),
        P(),
        P(),
        P(),
        P(),
        P(("row", "col"), None),
        P(),
        P(),
        P(),
        P("col", None, None),
        P("col", None, None),
        P("col", None, None),
        P("col", None, None),
        P("col", None, None),
        P(),
        P(),
    )
    out_specs = (
        P(("row", "col"), None),
        P(("row", "col"), None),
        P(),
        P("col", None, None),
        P("col", None, None),
        P("col", None, None),
        P("col", None, None),
        P(),
        P(),
        P(),
    )
    return jax.shard_map(shards, mesh=mesh, in_specs=in_specs, out_specs=out_specs, check_vma=False)
```

```python
from functools import partial

import jax
import jax.numpy as jnp
from jax import lax
from jax.experimental import pallas as pl
from jax.experimental.pallas import tpu as pltpu
from jax.sharding import PartitionSpec as P

D = 768
HEADS = 12
HEAD = 64
FF = 3072
SPAN = 128
STEP = 10
GROUP = 8

RATE = 0.01
DECAY = 0.01
VECTOR_RATE = 0.3

LOW = jnp.bfloat16
F32 = jnp.float32
TALL = 2 * SPAN


def dot(left_side, right_side, contract=(1, 0)):
    dims = (((contract[0],), (contract[1],)), ((), ()))
    return lax.dot_general(left_side, right_side, dims, preferred_element_type=F32)


def whole(shape):
    return pl.BlockSpec(shape, lambda *ids: (0,) * len(shape))


def cost(microseconds, transcendentals=0):
    return pl.CostEstimate(
        flops=int(microseconds * 1.1e9), bytes_accessed=0, transcendentals=transcendentals
    )


def params(mebibytes=36):
    return pltpu.CompilerParams(vmem_limit_bytes=mebibytes * 1024 * 1024)


def row_of(rows, index):
    return rows[:, index * D : (index + 1) * D]


def live_rows(place, counts, first_row, height):
    at = first_row + lax.broadcasted_iota(jnp.int32, (height, 1), 0)
    return jnp.where(at < counts[place[0]] * SPAN, 1.0, 0.0)


near = pltpu.VMEM
far = pltpu.HBM


def streamed(*arrays):
    return [pltpu.with_memory_space_constraint(a, pltpu.HBM) for a in arrays]


ANY = pl.BlockSpec(memory_space=pl.ANY)
SMEM = pl.BlockSpec(memory_space=pltpu.SMEM)


def split_heads(pair):
    lane = lax.broadcasted_iota(jnp.int32, pair.shape, 1)
    zero = jnp.zeros_like(pair)
    return jnp.concatenate([jnp.where(lane < HEAD, pair, zero), jnp.where(lane < HEAD, zero, pair)])


def normalise(scores):
    peak = jnp.max(scores, axis=-1, keepdims=True)
    raised = jnp.exp(scores - peak)
    return raised * (1.0 / jnp.sum(raised, axis=-1, keepdims=True))


def attend_kernel(tokens, w_qkv, rows, q_out, k_out, v_out, p_out, a_out):
    block = tokens[...]
    scaling = HEAD ** (-0.5)
    q_out[...] = ((dot(block, w_qkv[0]) + row_of(rows, 4)).astype(LOW) * scaling).astype(LOW)
    k_out[...] = dot(block, w_qkv[1]).astype(LOW)
    v_out[...] = (dot(block, w_qkv[2]) + row_of(rows, 5)).astype(LOW)
    for span in range(TALL // SPAN):
        at = slice(span * SPAN, (span + 1) * SPAN)
        for pair in range(HEADS // 2):
            lanes = slice(pair * 2 * HEAD, (pair + 1) * 2 * HEAD)
            scores = dot(q_out[at, lanes], split_heads(k_out[at, lanes]), (1, 1))
            weights = jnp.concatenate(
                [normalise(scores[:, :SPAN]), normalise(scores[:, SPAN:])], axis=1
            ).astype(LOW)
            p_out[span, pair] = weights
            a_out[at, lanes] = dot(weights, split_heads(v_out[at, lanes])).astype(LOW)


def attend(tokens, w_qkv, rows):
    total = tokens.shape[0]
    tall = pl.BlockSpec((TALL, D), lambda i: (i, 0))
    like = far((total, D), LOW)
    tokens, w_qkv, rows = streamed(tokens, w_qkv, rows)
    spans = TALL // SPAN
    return pl.pallas_call(
        attend_kernel,
        grid=(total // TALL,),
        in_specs=[tall, whole(w_qkv.shape), whole(rows.shape)],
        out_specs=[
            tall,
            tall,
            tall,
            pl.BlockSpec((spans, HEADS // 2, SPAN, 2 * SPAN), lambda i: (i, 0, 0, 0)),
            tall,
        ],
        out_shape=[
            like,
            like,
            like,
            far((total // SPAN, HEADS // 2, SPAN, 2 * SPAN), LOW),
            near((total, D), LOW),
        ],
        compiler_params=params(),
        cost_estimate=cost(10),
        name="attend",
    )(tokens, w_qkv, rows)


def unit_norm(resid):
    centred = resid - jnp.mean(resid, axis=-1, keepdims=True)
    inverse = lax.rsqrt(jnp.mean(centred * centred, axis=-1, keepdims=True) + 1e-06)
    return centred * inverse, inverse


def gelu_pair(x):
    cdf = 0.5 + 0.5 * lax.erf(x * 0.7071067811865476)
    return x * cdf, cdf + x * jnp.exp(-0.5 * x * x) * 0.3989422804014327


def feed_kernel(
    place, counts, tokens, attended, w_attn, w_in, w_out, rows, bias,
    enc_out, hid_out, slope_out, norm_out, u1_out, i1_out, u2_out, i2_out, cls_out, total, firsts,
):
    band = pl.program_id(0)
    chunks = [slice(at, at + TALL) for at in range(0, tokens.shape[0], TALL)]

    @pl.when(band == 0)
    def _():
        for at in chunks:
            resid = tokens[at].astype(F32) + dot(attended[at], w_attn[...]) + row_of(rows, 6)
            unit_one, inverse_one = unit_norm(resid)
            value = unit_one * row_of(rows, 0) + row_of(rows, 2)
            u1_out[at] = unit_one.astype(LOW)
            i1_out[at] = inverse_one
            norm_out[at] = value.astype(LOW)
            total[at] = value + row_of(rows, 7)

    step = 256
    for at in range(0, hid_out.shape[1], step):
        here = slice(at, at + step)
        pre_act = dot(norm_out[...], w_in[:, here]) + bias[:, here]
        hidden, slope = gelu_pair(pre_act)
        hid_out[:, here] = hidden.astype(LOW)
        slope_out[:, here] = slope.astype(LOW)

    @pl.when(band < pl.num_programs(0) - 1)
    def _():
        total[...] += dot(hid_out[...], w_out[...])

    @pl.when(band == pl.num_programs(0) - 1)
    def _():
        for at in chunks:
            resid = total[at] + dot(hid_out[at], w_out[...])
            unit_two, inverse_two = unit_norm(resid)
            u2_out[at] = unit_two.astype(LOW)
            i2_out[at] = inverse_two
            live = live_rows(place, counts, at.start, TALL)
            value = live * (unit_two * row_of(rows, 1) + row_of(rows, 3))
            enc_out[at] = value.astype(LOW)
            for first in range(at.start, at.stop, SPAN):
                row = first - at.start
                firsts[first // SPAN : first // SPAN + 1] = value[row : row + 1]
        firsts[tokens.shape[0] // SPAN :] = jnp.zeros((GROUP - tokens.shape[0] // SPAN, D), F32)
        cls_out[...] = firsts[...].astype(LOW)


def feed(place, counts, tokens, attended, w_attn, w_in, w_out, rows):
    total = tokens.shape[0]
    tall = lambda width: pl.BlockSpec((total, width), lambda j: (0, 0))
    band = lambda height: pl.BlockSpec((height, D), lambda j: (0, j))
    tokens, w_attn, w_in, w_out, rows = streamed(tokens, w_attn, w_in, w_out, rows)
    return pl.pallas_call(
        feed_kernel,
        grid=(FF // D,),
        in_specs=[
            SMEM, SMEM, tall(D), tall(D), whole(w_attn.shape), band(D),
            pl.BlockSpec((D, D), lambda j: (j, 0)),
            pl.BlockSpec((1, 8 * D), lambda j: (0, 0)),
            pl.BlockSpec((1, D), lambda j: (0, 8 + j)),
        ],
        out_specs=[
            tall(D), band(total), band(total), tall(D), tall(D), tall(1), tall(D), tall(1),
            whole((GROUP, D)),
        ],
        out_shape=[
            jax.ShapeDtypeStruct((total, D), LOW),
            far((total, FF), LOW),
            far((total, FF), LOW),
            far((total, D), LOW),
            far((total, D), LOW),
            far((total, 1), F32),
            near((total, D), LOW),
            near((total, 1), F32),
            jax.ShapeDtypeStruct((GROUP, D), LOW),
        ],
        scratch_shapes=[pltpu.VMEM((total, D), F32), pltpu.VMEM((GROUP, D), F32)],
        compiler_params=params(),
        cost_estimate=cost(20),
        name="feed",
    )(place, counts, tokens, attended, w_attn, w_in, w_out, rows, rows)


def norm_back(grad_out, unit_rows, inverse, gain):
    scaled = grad_out * gain
    along = jnp.mean(scaled * unit_rows, axis=-1, keepdims=True)
    return inverse * (scaled - jnp.mean(scaled, axis=-1, keepdims=True) - unit_rows * along)


def column_sums(*arrays):
    return [jnp.sum(a, axis=0, keepdims=True) for a in arrays]


def outer_kernel(place, counts, out_grad, grad_cls, unit_two, inverse_two, rows, two_out, low_out, vec_out):
    spot = lax.broadcasted_iota(jnp.int32, (SPAN, 1), 0) == 0
    sums = None
    for span in range(out_grad.shape[0] // SPAN):
        at = slice(span * SPAN, (span + 1) * SPAN)
        added = jnp.where(spot, grad_cls[span : span + 1], 0.0)
        live = live_rows(place, counts, span * SPAN, SPAN)
        grad_y = live * (out_grad[at].astype(F32) + added)
        unit_rows = unit_two[at].astype(F32)
        grad_two = norm_back(grad_y, unit_rows, inverse_two[at], row_of(rows, 1))
        two_out[at] = grad_two
        low_out[at] = grad_two.astype(LOW)
        here = column_sums(grad_y * unit_rows, grad_y, grad_two)
        sums = here if sums is None else [a + b for a, b in zip(sums, here)]
    for index, total in enumerate(sums):
        vec_out[index : index + 1] = total


def outer_grad(place, counts, out_grad, grad_cls, unit_two, inverse_two, rows):
    total = out_grad.shape[0]
    return pl.pallas_call(
        outer_kernel,
        in_specs=[SMEM, SMEM] + [pl.BlockSpec(memory_space=pltpu.VMEM)] * 5,
        out_shape=[
            jax.ShapeDtypeStruct((total, D), F32),
            jax.ShapeDtypeStruct((total, D), LOW),
            jax.ShapeDtypeStruct((3, D), F32),
        ],
        compiler_params=params(),
        cost_estimate=cost(5),
        name="outer",
    )(place, counts, out_grad, grad_cls, unit_two, inverse_two, rows)


def weight_kernel(panels, after, side, *refs):
    *sides, out = refs[after:]

    @pl.when(pl.program_id(0) < panels)
    def _():
        out[0] = dot(sides[0][...], sides[1][...], (0, 0)).astype(LOW)

    if len(sides) > 2:

        @pl.when(pl.program_id(0) == panels)
        def _():
            out[0] = dot(sides[2][...], sides[3][...], (0, 0)).astype(LOW)


def weight_half(hint, after, side, left_side, right_side, panels, banded, extra=()):
    total = left_side.shape[0]
    half = D // 2
    every = panels + len(extra) // 2
    tall = lambda width, at: pl.BlockSpec((total, width), at)
    last = lambda panel: jnp.minimum(panel, panels - 1)
    left_at = lambda panel, side: (0, last(panel) * 2 + side[0] if banded else side[0])
    right_at = lambda panel, side: (0, 0 if banded else last(panel))
    more = [tall(half, lambda p, s: (0, s[0])), tall(D, lambda p, s: (0, 0))]
    return pl.pallas_call(
        partial(weight_kernel, panels, len(after)),
        grid_spec=pltpu.PrefetchScalarGridSpec(
            num_scalar_prefetch=1,
            grid=(every,),
            in_specs=[ANY] * len(after)
            + [tall(half, left_at), tall(D, right_at)]
            + more[: len(extra)],
            out_specs=pl.BlockSpec((1, half, D), lambda p, s: (p, 0, 0)),
        ),
        out_shape=jax.ShapeDtypeStruct((every, half, D), LOW),
        compiler_params=params(),
        cost_estimate=cost(hint),
        name="weight",
    )(side.reshape(1), *after, left_side, right_side, *extra)


def inner_kernel(after, *refs):
    low, grad_two, slope, unit_one, inverse_one, w_attn, w_in, w_out, rows = refs[after:-6]
    pre_out, one_out, mixed_out, ga_out, vec_out, total = refs[-6:]
    band = pl.program_id(0)
    last = pl.num_programs(0) - 1
    step = 256
    for at in range(0, D, step):
        here = slice(at, at + step)
        grad_pre = dot(low[...], w_out[here], (1, 1)) * slope[:, here].astype(F32)
        pre_out[:, here] = grad_pre.astype(LOW)
        vec_out[pl.ds(3 + band, 1), here] = jnp.sum(grad_pre, axis=0, keepdims=True)

    @pl.when(band == 0)
    def _():
        total[...] = grad_two[...] + dot(pre_out[...], w_in[...], (1, 1))

    @pl.when((band > 0) & (band < last))
    def _():
        total[...] += dot(pre_out[...], w_in[...], (1, 1))

    @pl.when(band == last)
    def _():
        sums = None
        for first in range(0, low.shape[0], TALL):
            at = slice(first, first + TALL)
            grad_normed = total[at] + dot(pre_out[at], w_in[...], (1, 1))
            unit_rows = unit_one[at].astype(F32)
            grad_one = norm_back(grad_normed, unit_rows, inverse_one[at], row_of(rows, 0))
            one_out[at] = grad_one
            mixed = grad_one.astype(LOW)
            mixed_out[at] = mixed
            ga_out[at] = dot(mixed, w_attn[...], (1, 1)).astype(LOW)
            here = column_sums(grad_normed * unit_rows, grad_normed, grad_one)
            sums = here if sums is None else [a + b for a, b in zip(sums, here)]
        for index, value in enumerate(sums):
            vec_out[index : index + 1] = value


def inner_grad(after, low, grad_two, slope, unit_one, inverse_one, w_attn, w_in, w_out, rows):
    total = low.shape[0]
    bands = FF // D
    slope, w_attn, w_in, w_out, rows = streamed(slope, w_attn, w_in, w_out, rows)
    band = lambda height: pl.BlockSpec((height, D), lambda j: (0, j))
    return pl.pallas_call(
        partial(inner_kernel, len(after)),
        grid=(bands,),
        in_specs=[ANY] * len(after)
        + [
            whole(low.shape), whole(grad_two.shape), band(total), whole(unit_one.shape),
            whole(inverse_one.shape), whole(w_attn.shape), band(D),
            pl.BlockSpec((D, D), lambda j: (j, 0)), whole(rows.shape),
        ],
        out_specs=[band(total)] + [whole((total, D))] * 3 + [whole((3 + bands, D))],
        out_shape=[
            near((total, FF), LOW),
            far((total, D), F32),
            near((total, D), LOW),
            near((total, D), LOW),
            jax.ShapeDtypeStruct((3 + bands, D), F32),
        ],
        scratch_shapes=[pltpu.VMEM((total, D), F32)],
        compiler_params=params(),
        cost_estimate=cost(16),
        name="inner",
    )(*after, low, grad_two, slope, unit_one, inverse_one, w_attn, w_in, w_out, rows)


def unattend_kernel(after, sums, *refs):
    q, k, v, p, ga, attended = refs[after : after + 6]
    vec_one, vec_two, vec_early = refs[after + 6 : -2] if sums else (None, None, None)
    stack_out, vec_out = refs[-2:]
    scaling = HEAD ** (-0.5)
    first = pl.program_id(0) == 0

    @pl.when(first)
    def _():
        if not sums:
            vec_out[...] = jnp.zeros_like(vec_out)
            return
        for index in range(2):
            vec_out[2 * index : 2 * index + 1] = vec_one[index : index + 1]
            vec_out[2 * index + 1 : 2 * index + 2] = vec_two[index : index + 1]
        vec_out[4:6] = vec_early[...]
        vec_out[6:7] = vec_one[2:3]
        vec_out[7:8] = vec_two[2:3]
        vec_out[8:] = vec_one[3:]

    place = 4 if sums else 0
    head_of_row = lax.broadcasted_iota(jnp.int32, (2 * HEAD, 2 * SPAN), 0) // HEAD
    head_of_lane = lax.broadcasted_iota(jnp.int32, (2 * HEAD, 2 * SPAN), 1) // SPAN
    by_head = jnp.where(head_of_row == head_of_lane, 1.0, 0.0).astype(LOW)
    for span in range(p.shape[0]):
        at = slice(span * SPAN, (span + 1) * SPAN)
        for pair in range(HEADS // 2):
            lo = pair * 2 * HEAD
            lanes = slice(lo, lo + 2 * HEAD)
            weights = p[span, pair]
            grad = ga[at, lanes]
            spread_out = dot(grad, split_heads(v[at, lanes]), (1, 1))
            along = (grad.astype(F32) * attended[at, lanes].astype(F32)).astype(LOW)
            grad_scores = (weights.astype(F32) * (spread_out - dot(along, by_head))).astype(LOW)
            parts = [grad_scores[:, :SPAN], grad_scores[:, SPAN:]]
            grad_q = dot(grad_scores, split_heads(k[at, lanes])) * scaling
            tall_scores = jnp.concatenate(parts, axis=0)
            tall_weights = jnp.concatenate([weights[:, :SPAN], weights[:, SPAN:]], axis=0)
            grad_k = dot(tall_scores, split_heads(q[at, lanes]), (0, 0))
            grad_v = dot(tall_weights, split_heads(grad), (0, 0))
            stack_out[at, lo : lo + 2 * HEAD] = grad_q.astype(LOW)
            stack_out[at, D + lo : D + lo + 2 * HEAD] = grad_k.astype(LOW)
            stack_out[at, 2 * D + lo : 2 * D + lo + 2 * HEAD] = grad_v.astype(LOW)
            vec_out[place : place + 1, lanes] += jnp.sum(grad_q, axis=0, keepdims=True)
            vec_out[place + 1 : place + 2, lanes] += jnp.sum(grad_v, axis=0, keepdims=True)


def unattend(after, part, parts, q, k, v, p, ga, attended, stack=None, sums=()):
    total = q.shape[0]
    count = total // SPAN // parts
    first = part * count
    tall = lambda width: pl.BlockSpec((SPAN, width), lambda i: (first + i, 0))
    after = after if stack is None else [stack] + after
    vec_shape = (12, D) if sums else (2, D)
    return pl.pallas_call(
        partial(unattend_kernel, len(after), bool(sums)),
        grid=(count,),
        in_specs=[ANY] * len(after)
        + [tall(D)] * 3
        + [
            pl.BlockSpec((1, HEADS // 2, SPAN, 2 * SPAN), lambda i: (first + i, 0, 0, 0)),
            tall(D),
            tall(D),
        ]
        + [whole(a.shape) for a in sums],
        out_specs=[tall(3 * D), whole(vec_shape)],
        out_shape=[far((total, 3 * D), LOW), jax.ShapeDtypeStruct(vec_shape, F32)],
        input_output_aliases={} if stack is None else {0: 0},
        compiler_params=params(),
        cost_estimate=cost(8),
        name="unattend",
    )(*after, q, k, v, p, ga, attended, *sums)


def input_kernel(*refs):
    grad_one, stack, w_qkv, out = refs[-4:]
    total = grad_one[...]
    for index in range(3):
        total += dot(stack[:, index * D : (index + 1) * D], w_qkv[index], (1, 1))
    out[...] = total


def input_grad(after, grad_one, stack, w_qkv):
    total = grad_one.shape[0]
    tall = lambda width: pl.BlockSpec((TALL, width), lambda i: (i, 0))
    return pl.pallas_call(
        input_kernel,
        grid=(total // TALL,),
        in_specs=[ANY] * len(after) + [tall(D), tall(3 * D), whole(w_qkv.shape)],
        out_specs=tall(D),
        out_shape=jax.ShapeDtypeStruct((total, D), F32),
        compiler_params=params(),
        cost_estimate=cost(8),
        name="input",
    )(*after, grad_one, stack, w_qkv)


def contrast_kernel(slots, masks, place, rows, counts, partners, loss_out, grad_out):
    total, scale = rows.shape[0], 2.0 * D ** (-0.5)

    def number(shape, axis):
        at = lax.broadcasted_iota(jnp.int32, shape, axis)
        device, block = jnp.full(shape, place[0], jnp.int32), at // GROUP
        for bit, mask in enumerate(masks):
            device = device ^ (((block >> bit) & 1) * mask)
        return device, at % GROUP

    device, slot = number((counts.shape[1], total), 1)
    hit = lax.broadcasted_iota(jnp.int32, device.shape, 0) == device
    count = dot(counts[...].astype(LOW), jnp.where(hit, 1.0, 0.0).astype(LOW))
    live_across = (slot[:1].astype(F32) < count) & (slot[:1] < slots)
    device, slot = number((total, counts.shape[1]), 0)
    hit = lax.broadcasted_iota(jnp.int32, device.shape, 1) == device
    count = jnp.sum(jnp.where(hit, counts[...], 0.0), axis=1, keepdims=True)
    live_down = (slot[:, :1].astype(F32) < count) & (slot[:, :1] < slots)
    device, slot = number((total, partners.shape[1]), 0)
    own_id = device * slots + slot
    hit = lax.broadcasted_iota(jnp.int32, own_id.shape, 1) == own_id
    pair = jnp.sum(jnp.where(hit, partners[...], 0.0), axis=1, keepdims=True)
    device, slot = number((total, 128), 0)
    down = (device * slots + slot).astype(F32)[:, :1]
    device, slot = number((8, total), 1)
    across, slot = (device * slots + slot).astype(F32)[:1], slot[:1]
    valid = live_across & (down != across)
    matched = jnp.where((slot < slots) & (pair == across), 1.0, 0.0)
    anchor = jnp.where(live_down & (pair != down), 1.0, 0.0)
    similar = dot(rows[...], rows[...], (1, 1)) * scale
    masked = jnp.where(valid, similar, -1e30)
    peak = jnp.max(masked, axis=1, keepdims=True)
    summed = jnp.sum(jnp.where(valid, jnp.exp(masked - peak), 0.0), axis=1, keepdims=True)
    log_total = jnp.log(summed) + peak
    positive = jnp.sum(matched * similar, axis=1, keepdims=True)
    loss_out[...] = jnp.sum(anchor * (log_total - positive), axis=0, keepdims=True)
    grad = (anchor * (jnp.where(valid, jnp.exp(masked - log_total), 0.0) - matched)).astype(LOW)
    own = lax.broadcasted_iota(jnp.int32, (GROUP, total), 0)
    own = jnp.where(own == lax.broadcasted_iota(jnp.int32, (GROUP, total), 1), 1.0, 0.0)
    down_part = dot(dot(own.astype(LOW), grad, (1, 1)).astype(LOW), rows[...])
    grad_out[...] = (dot(grad[: 2 * GROUP], rows[...])[:GROUP] + down_part) * scale


def contrast(cls_rows, span_count, pair_index, device, slots):
    total = cls_rows.shape[0]
    scale = {"row": lax.axis_size("col"), "col": 1}
    masks = [scale[name] * bit for phase in gather_steps() for name, bit in phase]
    return pl.pallas_call(
        partial(contrast_kernel, slots, masks),
        in_specs=[pl.BlockSpec(memory_space=pltpu.SMEM)]
        + [pl.BlockSpec(memory_space=pltpu.VMEM)] * 3,
        out_shape=[
            jax.ShapeDtypeStruct((1, 1), F32),
            jax.ShapeDtypeStruct((GROUP, D), F32),
        ],
        compiler_params=params(),
        cost_estimate=cost(3),
        name="contrast",
    )(
        device,
        cls_rows,
        span_count.astype(F32).reshape(1, -1),
        pair_index.astype(F32).reshape(1, -1),
    )


def adam_kernel(
    packed, parts, position, *refs,
):
    gathered = refs[:parts]
    master, first, second, left, right, master_out, first_out, second_out, low_out, *scratch = refs[parts:]
    quarter = D // 4
    slot = pl.program_id(0)
    if packed:
        owned = scratch[0]
        shares, tall, _ = gathered[0].shape
        rows = D // (shares * parts)

        @pl.when(slot == 0)
        def _():
            for part in range(parts):
                for share in range(shares):
                    block = gathered[part][share].astype(F32)
                    number = part * shares + share
                    at = pl.multiple_of((number ^ position[0]) * rows, rows)
                    for index in range(owned.shape[0]):
                        lo = index * rows % tall
                        side = index * rows // tall
                        piece = block[lo : lo + rows, side * quarter : (side + 1) * quarter]
                        owned[index, pl.ds(at, rows), :] = piece

    for here in range(master.shape[0]):
        if packed:
            gradient = owned[slot * master.shape[0] + here].astype(LOW)
        else:
            gradient = gathered[0][here]
        low_left, low_right = left[here], right[here].astype(LOW)
        turned = dot(gradient, low_left, (0, 0))
        turned = dot(low_right, turned.astype(LOW), (0, 0))
        new_first = 0.9 * first[here] + 0.1 * turned
        new_second = 0.999 * second[here] + 0.001 * turned * turned
        first_out[here] = new_first
        second_out[here] = new_second
        spread_by = jnp.sqrt(new_second * (1.0 / (1.0 - 0.999**STEP))) + 1e-08
        update = new_first * (1.0 / (1.0 - 0.9**STEP)) / spread_by
        update = dot(update.astype(LOW), low_left, (1, 1))
        update = dot(low_right, update.astype(LOW))
        new_master = master[here] - RATE * (update + DECAY * master[here])
        master_out[here] = new_master
        low_out[here] = new_master.astype(LOW)


def ready_kernel(*refs):
    source, out = refs[-2:]
    out[...] = source[...].astype(out.dtype)


def ready(after, array, kind):
    block = pl.BlockSpec((1,) + array.shape[1:], lambda s: (s, 0, 0))
    return pl.pallas_call(
        ready_kernel,
        grid=(array.shape[0],),
        in_specs=[ANY] * len(after) + [block],
        out_specs=block,
        out_shape=far(array.shape, kind),
        compiler_params=params(16),
        cost_estimate=cost(4),
        name="ready",
    )(*after, *streamed(array))


def to_owned(gathered, position, per_owner):
    quarter = D // 4
    gathered = jnp.take(gathered, jnp.arange(gathered.shape[0]) ^ position, axis=0)
    flat = jnp.concatenate([gathered[..., :quarter], gathered[..., quarter:]], axis=1)
    rows = flat.shape[1] // per_owner
    flat = flat.reshape(flat.shape[0], per_owner, rows, quarter).transpose(1, 0, 2, 3)
    return flat.reshape(per_owner, D, quarter)


def turn(array):
    return array.transpose(0, 2, 1)


def rotated_adam(position, gathered, master, first_moment, second_moment, left_basis, right_basis):
    per_owner, quarter, _ = master.shape
    rows = D // sum(part.shape[0] for part in gathered)
    packed = rows % 8 == 0 and per_owner % 2 == 0
    if not packed:
        gathered = [to_owned(jnp.concatenate(gathered), position, per_owner)]
    at_once = max(n for n in (1, 2, 3) if per_owner % n == 0)
    block = lambda a: pl.BlockSpec((at_once,) + a.shape[1:], lambda s, p: (s, 0, 0))
    operands = streamed(master, first_moment, second_moment, left_basis, right_basis)
    like = jax.ShapeDtypeStruct(operands[0].shape, F32)
    fixed = pl.BlockSpec(gathered[0].shape, lambda s, p: (0, 0, 0))
    outputs = pl.pallas_call(
        partial(adam_kernel, packed, len(gathered)),
        grid_spec=pltpu.PrefetchScalarGridSpec(
            num_scalar_prefetch=1,
            grid=(per_owner // at_once,),
            in_specs=[fixed if packed else block(part) for part in gathered]
            + [block(a) for a in operands],
            out_specs=[block(operands[0])] * 4,
            scratch_shapes=[pltpu.VMEM((per_owner, D, quarter), F32)] if packed else [],
        ),
        out_shape=[like, like, like, jax.ShapeDtypeStruct(like.shape, LOW)],
        compiler_params=params(48),
        cost_estimate=cost(20),
        name="adam",
    )(position.reshape(1), *gathered, *operands)
    return [turn(a) for a in outputs]


def axis_bits(name):
    size = lax.axis_size(name)
    return [(name, 1 << k) for k in range(size.bit_length() - 1)]


def bit_of(step):
    return jnp.where((lax.axis_index(step[0]) & step[1]) != 0, 1, 0)


def swap(send, step):
    size = lax.axis_size(step[0])
    return lax.ppermute(send, step[0], [(i, i ^ step[1]) for i in range(size)])


def gather_steps():
    core, across, y_bits, z_bits = row_steps()
    return [z_bits[::-1], y_bits + across, core]


def gather_all(rows):
    columns = lax.axis_size("col")
    every = lax.axis_size("row") * columns
    scale = {"row": columns, "col": 1}
    for phase in gather_steps():
        arrived = []
        for number in range(1, 1 << len(phase)):
            mask = sum(scale[name] * bit for j, (name, bit) in enumerate(phase) if number >> j & 1)
            pairs = [(i, i ^ mask) for i in range(every)]
            arrived.append(lax.ppermute(rows, ("row", "col"), pairs))
        rows = jnp.concatenate([rows] + arrived)
    return rows


def row_steps():
    row_bits, col_bits = axis_bits("row"), axis_bits("col")
    core, across = row_bits[:1], row_bits[1:][::-1]
    y_bits, z_bits = col_bits[:-2][::-1], col_bits[-2:]
    return core, across, y_bits, z_bits


def pack_rider(rider, rows, width):
    parts = [rider[:, at : at + width] for at in range(0, D, width)]
    tall = rider.shape[0]
    if rows < tall:
        return [part[at : at + rows] for part in parts for at in range(0, tall, rows)]
    fold = rows // tall
    parts += parts[-1:] * (-len(parts) % fold)
    return [jnp.concatenate(parts[at : at + fold]) for at in range(0, len(parts), fold)]


def unpack_rider(blocks, tall):
    rows, width = blocks[0].shape
    if rows < tall:
        fold = tall // rows
        parts = [jnp.concatenate(blocks[at : at + fold]) for at in range(0, len(blocks), fold)]
    else:
        parts = [block[at : at + tall] for block in blocks for at in range(0, rows, tall)]
    parts = parts[: D // width]
    return parts[0] if len(parts) == 1 else jnp.concatenate(parts, axis=1)


def rider_blocks(rows, width, tall=12):
    return -(-tall * D // (rows * width))


def land_kernel(after, outs, rider, bits, *refs):
    refs = refs[after:]
    sides = len({source[0] for out in outs for source in out[3]})
    keeps, others = refs[0 : 2 * sides : 2], refs[1 : 2 * sides : 2]
    results = refs[2 * sides + (0 if rider is None else 1 + (rider == "array")) :]
    if rider is not None:
        total = refs[2 * sides][...]
        tall = total.shape[0]
        if rider == "array":
            total += refs[2 * sides + 1][...]
        else:
            blocks = [others[0][at].astype(F32) for at in range(keeps[0].shape[0], others[0].shape[0])]
            total += unpack_rider(blocks, tall)
        results[-1][...] = total
    for number, (at_bit, before, behind, sources) in enumerate(outs):
        bit = bits[at_bit]
        for which, target in enumerate(results[2 * number : 2 * number + 2]):
            half = bit if which else 1 - bit
            for at in range(before):
                here = pl.ds((2 * at + half) * behind, behind)
                there = slice(at * behind, (at + 1) * behind)
                for side, lanes, into in sources:
                    target[there, :, into] = keeps[side][here, :, lanes] + others[side][here, :, lanes]
        if rider is not None and number == 0:
            away = results[0]
            count, rows, width = away.shape
            blocks = pack_rider(total, rows, width)
            for index, block in enumerate(blocks):
                away[count - len(blocks) + index] = block.astype(LOW)


class Reduction:
    def __init__(self, bits, ways, send, keep, rider=None):
        core, across, y_bits, z_bits = row_steps()
        self.bits, self.order = bits, core + across + y_bits + z_bits
        left = across + y_bits + z_bits
        self.panels, height, _ = keep.shape
        self.rows = height >> len(left)
        other = swap(send, core[0])
        self.rider = None if rider is None else (rider, swap(rider, core[0]))
        split = lambda a: a.reshape(-1, self.rows, D)
        self.sides = [(split(keep), split(other), left)]
        cycle = [across, y_bits, z_bits[:1]][:ways]
        orders = [sum(cycle[at:] + cycle[:at], []) for at in range(ways)]
        self.stages = list(zip(*orders)) + [(step,) for step in z_bits[ways - 2 :]]
        self.ways = ways
        self.messages = []

    def sent(self):
        return self.messages

    def landing(self):
        return [side[1] for side in self.sides]

    def land(self, *after):
        stage = self.stages.pop(0)
        outs, shapes, lefts = [], [], []
        part = D // self.ways
        lanes = [slice(at, at + part) for at in range(0, D, part)]
        for index, step in enumerate(stage):
            if len(self.sides) == len(stage):
                width = self.sides[index][0].shape[2]
                sources = [(index, slice(0, width), slice(0, width))]
                left = self.sides[index][2]
            elif len(stage) > 1:
                width, left = part, self.sides[0][2]
                sources = [(0, lanes[index], slice(0, part))]
            else:
                width, left = D, self.sides[0][2]
                sources = [(side, slice(0, part), lanes[side]) for side in range(self.ways)]
            dim = left.index(step)
            behind = 1 << (len(left) - dim - 1)
            before = self.panels << dim
            outs.append((self.order.index(step), before, behind, sources))
            extra = rider_blocks(self.rows, width) if self.rider and index == 0 else 0
            shapes += [(before * behind + extra, self.rows, width), (before * behind, self.rows, width)]
            lefts.append([other for other in left if other != step])
        rider = None if self.rider is None else ("array" if len(self.rider) == 2 else "message")
        inputs = [a for keep, other, _ in self.sides for a in (keep, other)] + list(self.rider or ())
        out_shape = [jax.ShapeDtypeStruct(shape, LOW) for shape in shapes]
        if rider:
            out_shape.append(jax.ShapeDtypeStruct(self.rider[0].shape, F32))
        results = pl.pallas_call(
            partial(land_kernel, len(after), outs, rider),
            in_specs=[SMEM] + [ANY] * len(after) + [pl.BlockSpec(memory_space=pltpu.VMEM)] * len(inputs),
            out_shape=out_shape,
            compiler_params=params(24),
            cost_estimate=cost(2),
            name="land",
        )(self.bits, *after, *inputs)
        if rider:
            self.rider = (results[-1],)
        self.messages = list(results[0 : 2 * len(stage) : 2])
        keeps = results[1 : 2 * len(stage) : 2]
        self.sides = [
            (keep, swap(message, step), left)
            for keep, message, step, left in zip(keeps, self.messages, stage, lefts)
        ]

    def finish(self):
        while self.stages:
            self.land()


def slots_kernel(cols, panels, bits, owners, *refs):
    sums, rider = refs[:6], refs[6]
    away, here, rider_out, blocks, packed = refs[7:]
    quarter = D // 4
    found = [(sums[2 * run], sums[2 * run + 1], i) for run in range(3) for i in range(sums[2 * run].shape[0])]
    at = 0
    for panel in panels:
        keep, other, index = found[panel]
        value = keep[index].astype(F32) + other[index].astype(F32)
        for part in range(4):
            blocks[at] = value[:, part * quarter : (part + 1) * quarter]
            at += 1
    tail = [sums[1][index].astype(F32) for index in range(sums[0].shape[0], sums[1].shape[0])]
    rider_out[...] = rider[...] + unpack_rider(tail, rider.shape[0])
    rows, half = blocks.shape[1], packed.shape[1]
    for slot in range(at):
        col, place = divmod(slot, at // cols)
        value = blocks[owners[slot]]
        first = place * rows
        for side in range(2):
            lo, hi = max(first, side * half), min(first + rows, (side + 1) * half)
            if lo < hi:
                lanes = slice(side * quarter, (side + 1) * quarter)
                packed[col, lo - side * half : hi - side * half, lanes] = value[lo - first : hi - first]
    bit = bits[bits.shape[0] - 1]
    count = cols // 2
    away[...] = packed[pl.ds((1 - bit) * count, count)].astype(LOW)
    here[...] = packed[pl.ds(bit * count, count)].astype(LOW)


def to_slots(bits, runs, panels, owner_list):
    quarter, cols = D // 4, lax.axis_size("col")
    arrays = [a for run in runs for a in run.sides[0][:2]]
    rows = runs[0].rows
    shape = (cols, len(panels) * 4 // cols * rows // 2, 2 * quarter)
    like = jax.ShapeDtypeStruct((cols // 2,) + shape[1:], LOW)
    rider = runs[0].rider[0]
    return pl.pallas_call(
        partial(slots_kernel, cols, panels),
        in_specs=[SMEM, SMEM] + [pl.BlockSpec(memory_space=pltpu.VMEM)] * 7,
        out_shape=[like, like, jax.ShapeDtypeStruct(rider.shape, F32)],
        scratch_shapes=[pltpu.VMEM((len(panels) * 4, rows, quarter), F32), pltpu.VMEM(shape, F32)],
        compiler_params=params(24),
        cost_estimate=cost(4),
        name="slots",
    )(bits, owner_list, *arrays, rider)


def regroup_kernel(after, at_bit, before, behind, bits, *refs):
    parts, (away, here) = refs[after:-2], refs[-2:]
    bit = bits[at_bit]
    for which, target in ((1 - bit, away), (bit, here)):
        to = 0
        for part in parts:
            for at in range(before):
                target[to : to + behind] = part[pl.ds((2 * at + which) * behind, behind)]
                to += behind


def regroup(bits, at_bit, after, parts, before, behind):
    count, tall, width = parts[0].shape
    like = jax.ShapeDtypeStruct((count * len(parts) // 2, tall, width), LOW)
    return pl.pallas_call(
        partial(regroup_kernel, len(after), at_bit, before, behind),
        in_specs=[SMEM] + [ANY] * len(after) + [pl.BlockSpec(memory_space=pltpu.VMEM)] * len(parts),
        out_shape=[like, like],
        compiler_params=params(24),
        cost_estimate=cost(2),
        name="regroup",
    )(bits, *after, *parts)


def spread(bits, away, here, beside):
    core, across, y_bits, z_bits = row_steps()
    order = core + across + y_bits + z_bits
    left = axis_bits("col")[::-1]
    made, shares = [], 1
    for step in (y_bits + z_bits)[::-1]:
        dim = left.index(step)
        if shares > 1:
            after = streamed(*made[-1:]) if len(made) == shares.bit_length() - 1 else []
            behind = 1 << (len(left) - dim - 1)
            before = shares // 2 << dim
            away, here = regroup(bits, order.index(step), after, parts, before, behind)
        left.remove(step)
        parts = [here, swap(away, step)]
        if len(made) < len(beside):
            made.append(beside[len(made)]([away] + streamed(*made[-1:])))
        shares *= 2
    for step in (core + across)[::-1]:
        parts = parts + [swap(part, step) for part in parts]
    return parts, made


def row_place():
    place = 0
    for group in row_steps():
        for step in group:
            place = place * 2 + bit_of(step)
    return place


def shards(
    tokens,
    w_qkv,
    w_attn_out,
    w_in,
    w_out,
    vectors,
    out_grad,
    span_count,
    pair_index,
    owner_list,
    master,
    first_moment,
    second_moment,
    left_basis,
    right_basis,
    vec_first,
    vec_second,
):
    slots = tokens.shape[0] // SPAN
    device = (lax.axis_index("row") * lax.axis_size("col") + lax.axis_index("col")).reshape(1)
    core, across, y_bits, z_bits = row_steps()
    core_bit = bit_of(core[0])
    bits = jnp.stack([bit_of(step) for step in core + across + y_bits + z_bits])
    rows = vectors.reshape(1, -1)
    q, k, v, p, attended = attend(tokens, w_qkv, rows)
    encoded, hidden, slope, normed_low, unit_one, inverse_one, unit_two, inverse_two, cls_rows = (
        feed(device, span_count, tokens, attended, w_attn_out, w_in, w_out, rows)
    )
    loss, grad_cls = contrast(gather_all(cls_rows), span_count, pair_index, device, slots)
    grad_two, outer_low, vec_two = outer_grad(
        device, span_count, out_grad, grad_cls, unit_two, inverse_two, rows
    )
    outer_args = (hidden, outer_low, FF // D, True)
    outer_away = weight_half(8, [], 1 - core_bit, *outer_args)
    outer_here = weight_half(60, [outer_away], core_bit, *outer_args)
    outer_run = Reduction(bits, 2, outer_away, outer_here)
    outer_run.land()
    pre_low, grad_one, mixed_low, grad_attended, vec_one = inner_grad(
        outer_run.sent(), outer_low, grad_two, slope, unit_one, inverse_one,
        w_attn_out, w_in, w_out, rows,
    )
    outer_run.land(vec_one)
    inner_args = (normed_low, pre_low, FF // D, False, (attended, mixed_low))
    inner_away = weight_half(8, outer_run.sent(), 1 - core_bit, *inner_args)
    outer_run.land(inner_away)
    inner_here = weight_half(60, [inner_away] + outer_run.sent(), core_bit, *inner_args)
    outer_run.land(inner_here)
    inner_run = Reduction(bits, 3, inner_away, inner_here)
    inner_run.land()
    early, vec_early = unattend(
        outer_run.sent() + inner_run.sent(), 0, 2, q, k, v, p, grad_attended, attended
    )
    stack_low, vec_grad = unattend(
        [], 1, 2, q, k, v, p, grad_attended, attended, early, (vec_one, vec_two, vec_early)
    )
    inner_run.land(vec_grad)
    project_args = (tokens, stack_low, 3, False)
    project_away = weight_half(
        8, inner_run.sent() + outer_run.landing(), 1 - core_bit, *project_args
    )
    project_here = weight_half(60, [project_away], core_bit, *project_args)
    project_run = Reduction(bits, 3, project_away, project_here, vec_grad)
    project_run.land(*inner_run.landing())
    inner_run.land()
    project_run.land()
    inner_run.land()
    project_run.land()
    for run in (outer_run, inner_run, project_run):
        run.finish()
    slots_away, slots_here, vec_grad = to_slots(
        bits, (project_run, inner_run, outer_run), (0, 1, 2, 7, 3, 4, 5, 6, 8, 9, 10, 11), owner_list
    )
    vec_grad = vec_grad.reshape(-1)
    gathered, (low_left, grad_tokens) = spread(
        bits,
        slots_away,
        slots_here,
        [
            lambda after: ready(after, left_basis, LOW),
            lambda after: input_grad(after, grad_one, stack_low, w_qkv),
        ],
    )
    new_master, new_first, new_second, master_copy = rotated_adam(
        row_place(), gathered, turn(master), turn(first_moment), turn(second_moment),
        low_left, right_basis,
    )
    vec_first_new = 0.9 * vec_first + 0.1 * vec_grad
    vec_second_new = 0.999 * vec_second + 0.001 * vec_grad * vec_grad
    vec_step = (
        vec_first_new / (1.0 - 0.9**STEP) / (jnp.sqrt(vec_second_new / (1.0 - 0.999**STEP)) + 1e-08)
    )
    vec_new = vectors - VECTOR_RATE * vec_step
    return (
        encoded,
        grad_tokens,
        loss[0, 0],
        new_master,
        new_first,
        new_second,
        master_copy,
        vec_new,
        vec_first_new,
        vec_second_new,
    )


def solution(mesh):
    in_specs = (
        P(("row", "col"), None),
        P(),
        P(),
        P(),
        P(),
        P(),
        P(("row", "col"), None),
        P(),
        P(),
        P(),
        P("col", None, None),
        P("col", None, None),
        P("col", None, None),
        P("col", None, None),
        P("col", None, None),
        P(),
        P(),
    )
    out_specs = (
        P(("row", "col"), None),
        P(("row", "col"), None),
        P(),
        P("col", None, None),
        P("col", None, None),
        P("col", None, None),
        P("col", None, None),
        P(),
        P(),
        P(),
    )
    return jax.shard_map(shards, mesh=mesh, in_specs=in_specs, out_specs=out_specs, check_vma=False)
```

```python
from functools import partial

import jax
import jax.numpy as jnp
from jax import lax
from jax.experimental import pallas as pl
from jax.experimental.pallas import tpu as pltpu
from jax.sharding import PartitionSpec as P

D = 768
HEADS = 12
HEAD = 64
FF = 3072
SPAN = 128
STEP = 10
GROUP = 8

RATE = 0.01
DECAY = 0.01
VECTOR_RATE = 0.3

LOW = jnp.bfloat16
F32 = jnp.float32
TALL = 2 * SPAN


def dot(left_side, right_side, contract=(1, 0)):
    dims = (((contract[0],), (contract[1],)), ((), ()))
    return lax.dot_general(left_side, right_side, dims, preferred_element_type=F32)


def whole(shape):
    return pl.BlockSpec(shape, lambda *ids: (0,) * len(shape))


def cost(microseconds, transcendentals=0):
    return pl.CostEstimate(
        flops=int(microseconds * 1.1e9), bytes_accessed=0, transcendentals=transcendentals
    )


def params(mebibytes=36):
    return pltpu.CompilerParams(vmem_limit_bytes=mebibytes * 1024 * 1024)


def row_of(rows, index):
    return rows[:, index * D : (index + 1) * D]


def live_rows(place, counts, first_row, height):
    at = first_row + lax.broadcasted_iota(jnp.int32, (height, 1), 0)
    return jnp.where(at < counts[place[0]] * SPAN, 1.0, 0.0)


near = pltpu.VMEM
far = pltpu.HBM


def streamed(*arrays):
    return [pltpu.with_memory_space_constraint(a, pltpu.HBM) for a in arrays]


ANY = pl.BlockSpec(memory_space=pl.ANY)
SMEM = pl.BlockSpec(memory_space=pltpu.SMEM)


def split_heads(pair):
    lane = lax.broadcasted_iota(jnp.int32, pair.shape, 1)
    zero = jnp.zeros_like(pair)
    return jnp.concatenate([jnp.where(lane < HEAD, pair, zero), jnp.where(lane < HEAD, zero, pair)])


def normalise(scores):
    peak = jnp.max(scores, axis=-1, keepdims=True)
    raised = jnp.exp(scores - peak)
    return raised * (1.0 / jnp.sum(raised, axis=-1, keepdims=True))


def attend_kernel(tokens, w_qkv, rows, q_out, k_out, v_out, p_out, a_out):
    block = tokens[...]
    scaling = HEAD ** (-0.5)
    q_out[...] = ((dot(block, w_qkv[0]) + row_of(rows, 4)).astype(LOW) * scaling).astype(LOW)
    k_out[...] = dot(block, w_qkv[1]).astype(LOW)
    v_out[...] = (dot(block, w_qkv[2]) + row_of(rows, 5)).astype(LOW)
    for span in range(TALL // SPAN):
        at = slice(span * SPAN, (span + 1) * SPAN)
        for pair in range(HEADS // 2):
            lanes = slice(pair * 2 * HEAD, (pair + 1) * 2 * HEAD)
            scores = dot(q_out[at, lanes], split_heads(k_out[at, lanes]), (1, 1))
            weights = jnp.concatenate(
                [normalise(scores[:, :SPAN]), normalise(scores[:, SPAN:])], axis=1
            ).astype(LOW)
            p_out[span, pair] = weights
            a_out[at, lanes] = dot(weights, split_heads(v_out[at, lanes])).astype(LOW)


def attend(tokens, w_qkv, rows):
    total = tokens.shape[0]
    tall = pl.BlockSpec((TALL, D), lambda i: (i, 0))
    like = far((total, D), LOW)
    tokens, w_qkv, rows = streamed(tokens, w_qkv, rows)
    spans = TALL // SPAN
    return pl.pallas_call(
        attend_kernel,
        grid=(total // TALL,),
        in_specs=[tall, whole(w_qkv.shape), whole(rows.shape)],
        out_specs=[
            tall,
            tall,
            tall,
            pl.BlockSpec((spans, HEADS // 2, SPAN, 2 * SPAN), lambda i: (i, 0, 0, 0)),
            tall,
        ],
        out_shape=[
            like,
            like,
            like,
            far((total // SPAN, HEADS // 2, SPAN, 2 * SPAN), LOW),
            near((total, D), LOW),
        ],
        compiler_params=params(),
        cost_estimate=cost(10),
        name="attend",
    )(tokens, w_qkv, rows)


def unit_norm(resid):
    centred = resid - jnp.mean(resid, axis=-1, keepdims=True)
    inverse = lax.rsqrt(jnp.mean(centred * centred, axis=-1, keepdims=True) + 1e-06)
    return centred * inverse, inverse


def gelu_pair(x):
    cdf = 0.5 + 0.5 * lax.erf(x * 0.7071067811865476)
    return x * cdf, cdf + x * jnp.exp(-0.5 * x * x) * 0.3989422804014327


def feed_kernel(
    place, counts, tokens, attended, w_attn, w_in, w_out, rows, bias,
    enc_out, hid_out, slope_out, norm_out, u1_out, i1_out, u2_out, i2_out, cls_out, total, firsts,
):
    band = pl.program_id(0)
    chunks = [slice(at, at + TALL) for at in range(0, tokens.shape[0], TALL)]

    @pl.when(band == 0)
    def _():
        for at in chunks:
            resid = tokens[at].astype(F32) + dot(attended[at], w_attn[...]) + row_of(rows, 6)
            unit_one, inverse_one = unit_norm(resid)
            value = unit_one * row_of(rows, 0) + row_of(rows, 2)
            u1_out[at] = unit_one.astype(LOW)
            i1_out[at] = inverse_one
            norm_out[at] = value.astype(LOW)
            total[at] = value + row_of(rows, 7)

    step = 256
    for at in range(0, hid_out.shape[1], step):
        here = slice(at, at + step)
        pre_act = dot(norm_out[...], w_in[:, here]) + bias[:, here]
        hidden, slope = gelu_pair(pre_act)
        hid_out[:, here] = hidden.astype(LOW)
        slope_out[:, here] = slope.astype(LOW)

    @pl.when(band < pl.num_programs(0) - 1)
    def _():
        total[...] += dot(hid_out[...], w_out[...])

    @pl.when(band == pl.num_programs(0) - 1)
    def _():
        for at in chunks:
            resid = total[at] + dot(hid_out[at], w_out[...])
            unit_two, inverse_two = unit_norm(resid)
            u2_out[at] = unit_two.astype(LOW)
            i2_out[at] = inverse_two
            live = live_rows(place, counts, at.start, TALL)
            value = live * (unit_two * row_of(rows, 1) + row_of(rows, 3))
            enc_out[at] = value.astype(LOW)
            for first in range(at.start, at.stop, SPAN):
                row = first - at.start
                firsts[first // SPAN : first // SPAN + 1] = value[row : row + 1]
        firsts[tokens.shape[0] // SPAN :] = jnp.zeros((GROUP - tokens.shape[0] // SPAN, D), F32)
        cls_out[...] = firsts[...].astype(LOW)


def feed(place, counts, tokens, attended, w_attn, w_in, w_out, rows):
    total = tokens.shape[0]
    tall = lambda width: pl.BlockSpec((total, width), lambda j: (0, 0))
    band = lambda height: pl.BlockSpec((height, D), lambda j: (0, j))
    tokens, w_attn, w_in, w_out, rows = streamed(tokens, w_attn, w_in, w_out, rows)
    return pl.pallas_call(
        feed_kernel,
        grid=(FF // D,),
        in_specs=[
            SMEM, SMEM, tall(D), tall(D), whole(w_attn.shape), band(D),
            pl.BlockSpec((D, D), lambda j: (j, 0)),
            pl.BlockSpec((1, 8 * D), lambda j: (0, 0)),
            pl.BlockSpec((1, D), lambda j: (0, 8 + j)),
        ],
        out_specs=[
            tall(D), band(total), band(total), tall(D), tall(D), tall(1), tall(D), tall(1),
            whole((GROUP, D)),
        ],
        out_shape=[
            jax.ShapeDtypeStruct((total, D), LOW),
            far((total, FF), LOW),
            far((total, FF), LOW),
            far((total, D), LOW),
            far((total, D), LOW),
            far((total, 1), F32),
            near((total, D), LOW),
            near((total, 1), F32),
            jax.ShapeDtypeStruct((GROUP, D), LOW),
        ],
        scratch_shapes=[pltpu.VMEM((total, D), F32), pltpu.VMEM((GROUP, D), F32)],
        compiler_params=params(),
        cost_estimate=cost(20),
        name="feed",
    )(place, counts, tokens, attended, w_attn, w_in, w_out, rows, rows)


def norm_back(grad_out, unit_rows, inverse, gain):
    scaled = grad_out * gain
    along = jnp.mean(scaled * unit_rows, axis=-1, keepdims=True)
    return inverse * (scaled - jnp.mean(scaled, axis=-1, keepdims=True) - unit_rows * along)


def column_sums(*arrays):
    return [jnp.sum(a, axis=0, keepdims=True) for a in arrays]


def outer_kernel(place, counts, out_grad, grad_cls, unit_two, inverse_two, rows, two_out, low_out, vec_out):
    spot = lax.broadcasted_iota(jnp.int32, (SPAN, 1), 0) == 0
    sums = None
    for span in range(out_grad.shape[0] // SPAN):
        at = slice(span * SPAN, (span + 1) * SPAN)
        added = jnp.where(spot, grad_cls[span : span + 1], 0.0)
        live = live_rows(place, counts, span * SPAN, SPAN)
        grad_y = live * (out_grad[at].astype(F32) + added)
        unit_rows = unit_two[at].astype(F32)
        grad_two = norm_back(grad_y, unit_rows, inverse_two[at], row_of(rows, 1))
        two_out[at] = grad_two
        low_out[at] = grad_two.astype(LOW)
        here = column_sums(grad_y * unit_rows, grad_y, grad_two)
        sums = here if sums is None else [a + b for a, b in zip(sums, here)]
    for index, total in enumerate(sums):
        vec_out[index : index + 1] = total


def outer_grad(place, counts, out_grad, grad_cls, unit_two, inverse_two, rows):
    total = out_grad.shape[0]
    return pl.pallas_call(
        outer_kernel,
        in_specs=[SMEM, SMEM] + [pl.BlockSpec(memory_space=pltpu.VMEM)] * 5,
        out_shape=[
            jax.ShapeDtypeStruct((total, D), F32),
            jax.ShapeDtypeStruct((total, D), LOW),
            jax.ShapeDtypeStruct((3, D), F32),
        ],
        compiler_params=params(),
        cost_estimate=cost(5),
        name="outer",
    )(place, counts, out_grad, grad_cls, unit_two, inverse_two, rows)


def weight_kernel(panels, after, side, *refs):
    *sides, out = refs[after:]

    @pl.when(pl.program_id(0) < panels)
    def _():
        out[0] = dot(sides[0][...], sides[1][...], (0, 0)).astype(LOW)

    if len(sides) > 2:

        @pl.when(pl.program_id(0) == panels)
        def _():
            out[0] = dot(sides[2][...], sides[3][...], (0, 0)).astype(LOW)


def weight_half(hint, after, side, left_side, right_side, panels, banded, extra=()):
    total = left_side.shape[0]
    half = D // 2
    every = panels + len(extra) // 2
    tall = lambda width, at: pl.BlockSpec((total, width), at)
    last = lambda panel: jnp.minimum(panel, panels - 1)
    left_at = lambda panel, side: (0, last(panel) * 2 + side[0] if banded else side[0])
    right_at = lambda panel, side: (0, 0 if banded else last(panel))
    more = [tall(half, lambda p, s: (0, s[0])), tall(D, lambda p, s: (0, 0))]
    return pl.pallas_call(
        partial(weight_kernel, panels, len(after)),
        grid_spec=pltpu.PrefetchScalarGridSpec(
            num_scalar_prefetch=1,
            grid=(every,),
            in_specs=[ANY] * len(after)
            + [tall(half, left_at), tall(D, right_at)]
            + more[: len(extra)],
            out_specs=pl.BlockSpec((1, half, D), lambda p, s: (p, 0, 0)),
        ),
        out_shape=jax.ShapeDtypeStruct((every, half, D), LOW),
        compiler_params=params(),
        cost_estimate=cost(hint),
        name="weight",
    )(side.reshape(1), *after, left_side, right_side, *extra)


def inner_kernel(after, *refs):
    low, grad_two, slope, unit_one, inverse_one, w_attn, w_in, w_out, rows = refs[after:-6]
    pre_out, one_out, mixed_out, ga_out, vec_out, total = refs[-6:]
    band = pl.program_id(0)
    last = pl.num_programs(0) - 1
    step = 256
    for at in range(0, D, step):
        here = slice(at, at + step)
        grad_pre = dot(low[...], w_out[here], (1, 1)) * slope[:, here].astype(F32)
        pre_out[:, here] = grad_pre.astype(LOW)
        vec_out[pl.ds(3 + band, 1), here] = jnp.sum(grad_pre, axis=0, keepdims=True)

    @pl.when(band == 0)
    def _():
        total[...] = grad_two[...] + dot(pre_out[...], w_in[...], (1, 1))

    @pl.when((band > 0) & (band < last))
    def _():
        total[...] += dot(pre_out[...], w_in[...], (1, 1))

    @pl.when(band == last)
    def _():
        sums = None
        for first in range(0, low.shape[0], TALL):
            at = slice(first, first + TALL)
            grad_normed = total[at] + dot(pre_out[at], w_in[...], (1, 1))
            unit_rows = unit_one[at].astype(F32)
            grad_one = norm_back(grad_normed, unit_rows, inverse_one[at], row_of(rows, 0))
            one_out[at] = grad_one
            mixed = grad_one.astype(LOW)
            mixed_out[at] = mixed
            ga_out[at] = dot(mixed, w_attn[...], (1, 1)).astype(LOW)
            here = column_sums(grad_normed * unit_rows, grad_normed, grad_one)
            sums = here if sums is None else [a + b for a, b in zip(sums, here)]
        for index, value in enumerate(sums):
            vec_out[index : index + 1] = value


def inner_grad(after, low, grad_two, slope, unit_one, inverse_one, w_attn, w_in, w_out, rows):
    total = low.shape[0]
    bands = FF // D
    slope, w_attn, w_in, w_out, rows = streamed(slope, w_attn, w_in, w_out, rows)
    band = lambda height: pl.BlockSpec((height, D), lambda j: (0, j))
    return pl.pallas_call(
        partial(inner_kernel, len(after)),
        grid=(bands,),
        in_specs=[ANY] * len(after)
        + [
            whole(low.shape), whole(grad_two.shape), band(total), whole(unit_one.shape),
            whole(inverse_one.shape), whole(w_attn.shape), band(D),
            pl.BlockSpec((D, D), lambda j: (j, 0)), whole(rows.shape),
        ],
        out_specs=[band(total)] + [whole((total, D))] * 3 + [whole((3 + bands, D))],
        out_shape=[
            near((total, FF), LOW),
            far((total, D), F32),
            near((total, D), LOW),
            near((total, D), LOW),
            jax.ShapeDtypeStruct((3 + bands, D), F32),
        ],
        scratch_shapes=[pltpu.VMEM((total, D), F32)],
        compiler_params=params(),
        cost_estimate=cost(16),
        name="inner",
    )(*after, low, grad_two, slope, unit_one, inverse_one, w_attn, w_in, w_out, rows)


def unattend_kernel(after, sums, *refs):
    q, k, v, p, ga, attended = refs[after : after + 6]
    vec_one, vec_two, vec_early = refs[after + 6 : -2] if sums else (None, None, None)
    stack_out, vec_out = refs[-2:]
    scaling = HEAD ** (-0.5)
    first = pl.program_id(0) == 0

    @pl.when(first)
    def _():
        if not sums:
            vec_out[...] = jnp.zeros_like(vec_out)
            return
        for index in range(2):
            vec_out[2 * index : 2 * index + 1] = vec_one[index : index + 1]
            vec_out[2 * index + 1 : 2 * index + 2] = vec_two[index : index + 1]
        vec_out[4:6] = vec_early[...]
        vec_out[6:7] = vec_one[2:3]
        vec_out[7:8] = vec_two[2:3]
        vec_out[8:] = vec_one[3:]

    place = 4 if sums else 0
    head_of_row = lax.broadcasted_iota(jnp.int32, (2 * HEAD, 2 * SPAN), 0) // HEAD
    head_of_lane = lax.broadcasted_iota(jnp.int32, (2 * HEAD, 2 * SPAN), 1) // SPAN
    by_head = jnp.where(head_of_row == head_of_lane, 1.0, 0.0).astype(LOW)
    for span in range(p.shape[0]):
        at = slice(span * SPAN, (span + 1) * SPAN)
        for pair in range(HEADS // 2):
            lo = pair * 2 * HEAD
            lanes = slice(lo, lo + 2 * HEAD)
            weights = p[span, pair]
            grad = ga[at, lanes]
            spread_out = dot(grad, split_heads(v[at, lanes]), (1, 1))
            along = (grad.astype(F32) * attended[at, lanes].astype(F32)).astype(LOW)
            grad_scores = (weights.astype(F32) * (spread_out - dot(along, by_head))).astype(LOW)
            parts = [grad_scores[:, :SPAN], grad_scores[:, SPAN:]]
            grad_q = dot(grad_scores, split_heads(k[at, lanes])) * scaling
            tall_scores = jnp.concatenate(parts, axis=0)
            tall_weights = jnp.concatenate([weights[:, :SPAN], weights[:, SPAN:]], axis=0)
            grad_k = dot(tall_scores, split_heads(q[at, lanes]), (0, 0))
            grad_v = dot(tall_weights, split_heads(grad), (0, 0))
            stack_out[at, lo : lo + 2 * HEAD] = grad_q.astype(LOW)
            stack_out[at, D + lo : D + lo + 2 * HEAD] = grad_k.astype(LOW)
            stack_out[at, 2 * D + lo : 2 * D + lo + 2 * HEAD] = grad_v.astype(LOW)
            vec_out[place : place + 1, lanes] += jnp.sum(grad_q, axis=0, keepdims=True)
            vec_out[place + 1 : place + 2, lanes] += jnp.sum(grad_v, axis=0, keepdims=True)


def unattend(after, part, parts, q, k, v, p, ga, attended, stack=None, sums=()):
    total = q.shape[0]
    count = total // SPAN // parts
    first = part * count
    tall = lambda width: pl.BlockSpec((SPAN, width), lambda i: (first + i, 0))
    after = after if stack is None else [stack] + after
    vec_shape = (12, D) if sums else (2, D)
    return pl.pallas_call(
        partial(unattend_kernel, len(after), bool(sums)),
        grid=(count,),
        in_specs=[ANY] * len(after)
        + [tall(D)] * 3
        + [
            pl.BlockSpec((1, HEADS // 2, SPAN, 2 * SPAN), lambda i: (first + i, 0, 0, 0)),
            tall(D),
            tall(D),
        ]
        + [whole(a.shape) for a in sums],
        out_specs=[tall(3 * D), whole(vec_shape)],
        out_shape=[far((total, 3 * D), LOW), jax.ShapeDtypeStruct(vec_shape, F32)],
        input_output_aliases={} if stack is None else {0: 0},
        compiler_params=params(),
        cost_estimate=cost(8),
        name="unattend",
    )(*after, q, k, v, p, ga, attended, *sums)


def input_kernel(*refs):
    grad_one, stack, w_qkv, out = refs[-4:]
    total = grad_one[...]
    for index in range(3):
        total += dot(stack[:, index * D : (index + 1) * D], w_qkv[index], (1, 1))
    out[...] = total


def input_grad(after, grad_one, stack, w_qkv):
    total = grad_one.shape[0]
    tall = lambda width: pl.BlockSpec((TALL, width), lambda i: (i, 0))
    return pl.pallas_call(
        input_kernel,
        grid=(total // TALL,),
        in_specs=[ANY] * len(after) + [tall(D), tall(3 * D), whole(w_qkv.shape)],
        out_specs=tall(D),
        out_shape=jax.ShapeDtypeStruct((total, D), F32),
        compiler_params=params(),
        cost_estimate=cost(8),
        name="input",
    )(*after, grad_one, stack, w_qkv)


def contrast_kernel(slots, masks, place, rows, counts, partners, loss_out, grad_out):
    total, scale = rows.shape[0], 2.0 * D ** (-0.5)

    def number(shape, axis):
        at = lax.broadcasted_iota(jnp.int32, shape, axis)
        device, block = jnp.full(shape, place[0], jnp.int32), at // GROUP
        for bit, mask in enumerate(masks):
            device = device ^ (((block >> bit) & 1) * mask)
        return device, at % GROUP

    device, slot = number((counts.shape[1], total), 1)
    hit = lax.broadcasted_iota(jnp.int32, device.shape, 0) == device
    count = dot(counts[...].astype(LOW), jnp.where(hit, 1.0, 0.0).astype(LOW))
    live_across = (slot[:1].astype(F32) < count) & (slot[:1] < slots)
    device, slot = number((total, counts.shape[1]), 0)
    hit = lax.broadcasted_iota(jnp.int32, device.shape, 1) == device
    count = jnp.sum(jnp.where(hit, counts[...], 0.0), axis=1, keepdims=True)
    live_down = (slot[:, :1].astype(F32) < count) & (slot[:, :1] < slots)
    device, slot = number((total, partners.shape[1]), 0)
    own_id = device * slots + slot
    hit = lax.broadcasted_iota(jnp.int32, own_id.shape, 1) == own_id
    pair = jnp.sum(jnp.where(hit, partners[...], 0.0), axis=1, keepdims=True)
    device, slot = number((total, 128), 0)
    down = (device * slots + slot).astype(F32)[:, :1]
    device, slot = number((8, total), 1)
    across, slot = (device * slots + slot).astype(F32)[:1], slot[:1]
    valid = live_across & (down != across)
    matched = jnp.where((slot < slots) & (pair == across), 1.0, 0.0)
    anchor = jnp.where(live_down & (pair != down), 1.0, 0.0)
    similar = dot(rows[...], rows[...], (1, 1)) * scale
    masked = jnp.where(valid, similar, -1e30)
    peak = jnp.max(masked, axis=1, keepdims=True)
    summed = jnp.sum(jnp.where(valid, jnp.exp(masked - peak), 0.0), axis=1, keepdims=True)
    log_total = jnp.log(summed) + peak
    positive = jnp.sum(matched * similar, axis=1, keepdims=True)
    loss_out[...] = jnp.sum(anchor * (log_total - positive), axis=0, keepdims=True)
    grad = (anchor * (jnp.where(valid, jnp.exp(masked - log_total), 0.0) - matched)).astype(LOW)
    own = lax.broadcasted_iota(jnp.int32, (GROUP, total), 0)
    own = jnp.where(own == lax.broadcasted_iota(jnp.int32, (GROUP, total), 1), 1.0, 0.0)
    down_part = dot(dot(own.astype(LOW), grad, (1, 1)).astype(LOW), rows[...])
    grad_out[...] = (dot(grad[: 2 * GROUP], rows[...])[:GROUP] + down_part) * scale


def contrast(cls_rows, span_count, pair_index, device, slots):
    total = cls_rows.shape[0]
    scale = {"row": lax.axis_size("col"), "col": 1}
    masks = [scale[name] * bit for phase in gather_steps() for name, bit in phase]
    return pl.pallas_call(
        partial(contrast_kernel, slots, masks),
        in_specs=[pl.BlockSpec(memory_space=pltpu.SMEM)]
        + [pl.BlockSpec(memory_space=pltpu.VMEM)] * 3,
        out_shape=[
            jax.ShapeDtypeStruct((1, 1), F32),
            jax.ShapeDtypeStruct((GROUP, D), F32),
        ],
        compiler_params=params(),
        cost_estimate=cost(3),
        name="contrast",
    )(
        device,
        cls_rows,
        span_count.astype(F32).reshape(1, -1),
        pair_index.astype(F32).reshape(1, -1),
    )


def adam_kernel(
    masks, parts, position, *refs,
):
    gathered = refs[:parts]
    master, first, second, left, right, master_out, first_out, second_out, low_out, *scratch = refs[parts:]
    quarter = D // 4
    slot = pl.program_id(0)
    if masks:
        owned = scratch[0]
        shares, tall, _ = gathered[0].shape
        rows = D // len(masks)

        @pl.when(slot == 0)
        def _():
            for number, mask in enumerate(masks):
                block = gathered[number // shares][number % shares].astype(F32)
                at = pl.multiple_of((mask ^ position[0]) * rows, rows)
                for index in range(owned.shape[0]):
                    lo = index * rows % tall
                    side = index * rows // tall
                    piece = block[lo : lo + rows, side * quarter : (side + 1) * quarter]
                    owned[index, pl.ds(at, rows), :] = piece

    for here in range(master.shape[0]):
        if masks:
            gradient = owned[slot * master.shape[0] + here].astype(LOW)
        else:
            gradient = gathered[0][here]
        low_left, low_right = left[here], right[here].astype(LOW)
        turned = dot(gradient, low_left, (0, 0))
        turned = dot(low_right, turned.astype(LOW), (0, 0))
        new_first = 0.9 * first[here] + 0.1 * turned
        new_second = 0.999 * second[here] + 0.001 * turned * turned
        first_out[here] = new_first
        second_out[here] = new_second
        spread_by = jnp.sqrt(new_second * (1.0 / (1.0 - 0.999**STEP))) + 1e-08
        update = new_first * (1.0 / (1.0 - 0.9**STEP)) / spread_by
        update = dot(update.astype(LOW), low_left, (1, 1))
        update = dot(low_right, update.astype(LOW))
        new_master = master[here] - RATE * (update + DECAY * master[here])
        master_out[here] = new_master
        low_out[here] = new_master.astype(LOW)


def ready_kernel(*refs):
    source, out = refs[-2:]
    out[...] = source[...].astype(out.dtype)


def ready(after, array, kind):
    block = pl.BlockSpec((1,) + array.shape[1:], lambda s: (s, 0, 0))
    return pl.pallas_call(
        ready_kernel,
        grid=(array.shape[0],),
        in_specs=[ANY] * len(after) + [block],
        out_specs=block,
        out_shape=far(array.shape, kind),
        compiler_params=params(16),
        cost_estimate=cost(4),
        name="ready",
    )(*after, *streamed(array))


def to_owned(gathered, masks, position, per_owner):
    quarter = D // 4
    places = jnp.array(masks, jnp.int32) ^ position
    gathered = jnp.zeros_like(gathered).at[places].set(gathered)
    flat = jnp.concatenate([gathered[..., :quarter], gathered[..., quarter:]], axis=1)
    rows = flat.shape[1] // per_owner
    flat = flat.reshape(flat.shape[0], per_owner, rows, quarter).transpose(1, 0, 2, 3)
    return flat.reshape(per_owner, D, quarter)


def turn(array):
    return array.transpose(0, 2, 1)


def rotated_adam(position, gathered, masks, master, first_moment, second_moment, left_basis, right_basis):
    per_owner, quarter, _ = master.shape
    if D // len(masks) % 8 or per_owner % 2:
        gathered = [to_owned(jnp.concatenate(gathered), masks, position, per_owner)]
        masks = []
    at_once = max(n for n in (1, 2, 3) if per_owner % n == 0)
    block = lambda a: pl.BlockSpec((at_once,) + a.shape[1:], lambda s, p: (s, 0, 0))
    operands = streamed(master, first_moment, second_moment, left_basis, right_basis)
    like = jax.ShapeDtypeStruct(operands[0].shape, F32)
    fixed = pl.BlockSpec(gathered[0].shape, lambda s, p: (0, 0, 0))
    outputs = pl.pallas_call(
        partial(adam_kernel, masks, len(gathered)),
        grid_spec=pltpu.PrefetchScalarGridSpec(
            num_scalar_prefetch=1,
            grid=(per_owner // at_once,),
            in_specs=[fixed if masks else block(part) for part in gathered]
            + [block(a) for a in operands],
            out_specs=[block(operands[0])] * 4,
            scratch_shapes=[pltpu.VMEM((per_owner, D, quarter), F32)] if masks else [],
        ),
        out_shape=[like, like, like, jax.ShapeDtypeStruct(like.shape, LOW)],
        compiler_params=params(48),
        cost_estimate=cost(20),
        name="adam",
    )(position.reshape(1), *gathered, *operands)
    return [turn(a) for a in outputs]


def axis_bits(name):
    size = lax.axis_size(name)
    return [(name, 1 << k) for k in range(size.bit_length() - 1)]


def bit_of(step):
    return jnp.where((lax.axis_index(step[0]) & step[1]) != 0, 1, 0)


def swap(send, step):
    size = lax.axis_size(step[0])
    return lax.ppermute(send, step[0], [(i, i ^ step[1]) for i in range(size)])


def gather_steps():
    core, across, y_bits, z_bits = row_steps()
    return [z_bits[::-1], y_bits + across, core]


def gather_all(rows):
    columns = lax.axis_size("col")
    every = lax.axis_size("row") * columns
    scale = {"row": columns, "col": 1}
    for phase in gather_steps():
        arrived = []
        for number in range(1, 1 << len(phase)):
            mask = sum(scale[name] * bit for j, (name, bit) in enumerate(phase) if number >> j & 1)
            pairs = [(i, i ^ mask) for i in range(every)]
            arrived.append(lax.ppermute(rows, ("row", "col"), pairs))
        rows = jnp.concatenate([rows] + arrived)
    return rows


def row_steps():
    row_bits, col_bits = axis_bits("row"), axis_bits("col")
    core, across = row_bits[:1], row_bits[1:][::-1]
    y_bits, z_bits = col_bits[:-2][::-1], col_bits[-2:]
    return core, across, y_bits, z_bits


def pack_rider(rider, rows, width):
    parts = [rider[:, at : at + width] for at in range(0, D, width)]
    tall = rider.shape[0]
    if rows < tall:
        return [part[at : at + rows] for part in parts for at in range(0, tall, rows)]
    fold = rows // tall
    parts += parts[-1:] * (-len(parts) % fold)
    return [jnp.concatenate(parts[at : at + fold]) for at in range(0, len(parts), fold)]


def unpack_rider(blocks, tall):
    rows, width = blocks[0].shape
    if rows < tall:
        fold = tall // rows
        parts = [jnp.concatenate(blocks[at : at + fold]) for at in range(0, len(blocks), fold)]
    else:
        parts = [block[at : at + tall] for block in blocks for at in range(0, rows, tall)]
    parts = parts[: D // width]
    return parts[0] if len(parts) == 1 else jnp.concatenate(parts, axis=1)


def rider_blocks(rows, width, tall=12):
    return -(-tall * D // (rows * width))


def land_kernel(after, outs, rider, bits, *refs):
    refs = refs[after:]
    sides = len({source[0] for out in outs for source in out[3]})
    keeps, others = refs[0 : 2 * sides : 2], refs[1 : 2 * sides : 2]
    results = refs[2 * sides + (0 if rider is None else 1 + (rider == "array")) :]
    if rider is not None:
        total = refs[2 * sides][...]
        tall = total.shape[0]
        if rider == "array":
            total += refs[2 * sides + 1][...]
        else:
            blocks = [others[0][at].astype(F32) for at in range(keeps[0].shape[0], others[0].shape[0])]
            total += unpack_rider(blocks, tall)
        results[-1][...] = total
    for number, (at_bit, before, behind, sources) in enumerate(outs):
        bit = bits[at_bit]
        for which, target in enumerate(results[2 * number : 2 * number + 2]):
            half = bit if which else 1 - bit
            for at in range(before):
                here = pl.ds((2 * at + half) * behind, behind)
                there = slice(at * behind, (at + 1) * behind)
                for side, lanes, into in sources:
                    target[there, :, into] = keeps[side][here, :, lanes] + others[side][here, :, lanes]
        if rider is not None and number == 0:
            away = results[0]
            count, rows, width = away.shape
            blocks = pack_rider(total, rows, width)
            for index, block in enumerate(blocks):
                away[count - len(blocks) + index] = block.astype(LOW)


class Reduction:
    def __init__(self, bits, ways, send, keep, rider=None):
        core, across, y_bits, z_bits = row_steps()
        self.bits, self.order = bits, core + across + y_bits + z_bits
        left = across + y_bits + z_bits
        self.panels, height, _ = keep.shape
        self.rows = height >> len(left)
        other = swap(send, core[0])
        self.rider = None if rider is None else (rider, swap(rider, core[0]))
        split = lambda a: a.reshape(-1, self.rows, D)
        self.sides = [(split(keep), split(other), left)]
        cycle = [across, y_bits, z_bits[:1]][:ways]
        orders = [sum(cycle[at:] + cycle[:at], []) for at in range(ways)]
        self.stages = list(zip(*orders)) + [(step,) for step in z_bits[ways - 2 :]]
        self.ways = ways
        self.messages = []

    def sent(self):
        return self.messages

    def landing(self):
        return [side[1] for side in self.sides]

    def land(self, *after):
        stage = self.stages.pop(0)
        outs, shapes, lefts = [], [], []
        part = D // self.ways
        lanes = [slice(at, at + part) for at in range(0, D, part)]
        for index, step in enumerate(stage):
            if len(self.sides) == len(stage):
                width = self.sides[index][0].shape[2]
                sources = [(index, slice(0, width), slice(0, width))]
                left = self.sides[index][2]
            elif len(stage) > 1:
                width, left = part, self.sides[0][2]
                sources = [(0, lanes[index], slice(0, part))]
            else:
                width, left = D, self.sides[0][2]
                sources = [(side, slice(0, part), lanes[side]) for side in range(self.ways)]
            dim = left.index(step)
            behind = 1 << (len(left) - dim - 1)
            before = self.panels << dim
            outs.append((self.order.index(step), before, behind, sources))
            extra = rider_blocks(self.rows, width) if self.rider and index == 0 else 0
            shapes += [(before * behind + extra, self.rows, width), (before * behind, self.rows, width)]
            lefts.append([other for other in left if other != step])
        rider = None if self.rider is None else ("array" if len(self.rider) == 2 else "message")
        inputs = [a for keep, other, _ in self.sides for a in (keep, other)] + list(self.rider or ())
        out_shape = [jax.ShapeDtypeStruct(shape, LOW) for shape in shapes]
        if rider:
            out_shape.append(jax.ShapeDtypeStruct(self.rider[0].shape, F32))
        results = pl.pallas_call(
            partial(land_kernel, len(after), outs, rider),
            in_specs=[SMEM] + [ANY] * len(after) + [pl.BlockSpec(memory_space=pltpu.VMEM)] * len(inputs),
            out_shape=out_shape,
            compiler_params=params(24),
            cost_estimate=cost(2),
            name="land",
        )(self.bits, *after, *inputs)
        if rider:
            self.rider = (results[-1],)
        self.messages = list(results[0 : 2 * len(stage) : 2])
        keeps = results[1 : 2 * len(stage) : 2]
        self.sides = [
            (keep, swap(message, step), left)
            for keep, message, step, left in zip(keeps, self.messages, stage, lefts)
        ]

    def finish(self):
        while self.stages:
            self.land()


def slots_kernel(after, cols, panels, column, owners, *refs):
    refs = refs[after:]
    sums, rider, rider_out = refs[:6], refs[6], refs[7]
    targets, blocks, packed = refs[8:-2], refs[-2], refs[-1]
    quarter = D // 4
    found = [(sums[2 * run], sums[2 * run + 1], i) for run in range(3) for i in range(sums[2 * run].shape[0])]
    at = 0
    for panel in panels:
        keep, other, index = found[panel]
        value = keep[index].astype(F32) + other[index].astype(F32)
        for part in range(4):
            blocks[at] = value[:, part * quarter : (part + 1) * quarter]
            at += 1
    tail = [sums[1][index].astype(F32) for index in range(sums[0].shape[0], sums[1].shape[0])]
    rider_out[...] = rider[...] + unpack_rider(tail, rider.shape[0])
    rows, half = blocks.shape[1], packed.shape[1]
    for slot in range(at):
        col, place = divmod(slot, at // cols)
        value = blocks[owners[slot]]
        first = place * rows
        for side in range(2):
            lo, hi = max(first, side * half), min(first + rows, (side + 1) * half)
            if lo < hi:
                lanes = slice(side * quarter, (side + 1) * quarter)
                packed[col, lo - side * half : hi - side * half, lanes] = value[lo - first : hi - first]
    for number, target in enumerate(targets):
        target[...] = packed[column[0] ^ number].astype(LOW)


def to_slots(after, runs, panels, owner_list):
    quarter, cols = D // 4, lax.axis_size("col")
    arrays = [a for run in runs for a in run.sides[0][:2]]
    rows = runs[0].rows
    shape = (len(panels) * 4 // cols * rows // 2, 2 * quarter)
    rider = runs[0].rider[0]
    return pl.pallas_call(
        partial(slots_kernel, len(after), cols, panels),
        in_specs=[SMEM, SMEM] + [ANY] * len(after) + [pl.BlockSpec(memory_space=pltpu.VMEM)] * 7,
        out_shape=[jax.ShapeDtypeStruct(rider.shape, F32)] + [jax.ShapeDtypeStruct(shape, LOW)] * cols,
        scratch_shapes=[
            pltpu.VMEM((len(panels) * 4, rows, quarter), F32),
            pltpu.VMEM((cols,) + shape, F32),
        ],
        compiler_params=params(24),
        cost_estimate=cost(4),
        name="slots",
    )(lax.axis_index("col").reshape(1), owner_list, *after, *arrays, rider)


def merge_kernel(after, *refs):
    *sources, target = refs[after:]
    for number, source in enumerate(sources):
        target[number] = source[...]


def merge(after, arrays):
    return pl.pallas_call(
        partial(merge_kernel, len(after)),
        in_specs=[ANY] * len(after) + [pl.BlockSpec(memory_space=pltpu.VMEM)] * len(arrays),
        out_shape=jax.ShapeDtypeStruct((len(arrays),) + arrays[0].shape, arrays[0].dtype),
        compiler_params=params(24),
        cost_estimate=cost(1),
        name="merge",
    )(*after, *arrays)


def spread(parts):
    core, across, y_bits, z_bits = row_steps()
    order = core + across + y_bits + z_bits
    weight = lambda step: 1 << (len(order) - 1 - order.index(step))
    cols, bits = len(parts), axis_bits("col")
    sent = lambda number: lax.ppermute(parts[number], "col", [(i, i ^ number) for i in range(cols)])
    arrived = [parts[0]] + [sent(number) for number in range(1, cols)]
    masks = [sum(weight(step) for step in bits if number & step[1]) for number in range(cols)]
    near = merge([], arrived[: cols // 2])
    first, *rest = (core + across)[::-1]
    moved = swap(near, first)
    far = merge([], arrived[cols // 2 :])
    shares = [near, far, moved, swap(far, first)]
    masks = masks + [mask ^ weight(first) for mask in masks]
    for step in rest:
        shares = shares + [swap(share, step) for share in shares]
        masks = masks + [mask ^ weight(step) for mask in masks]
    return shares, masks


def row_place():
    place = 0
    for group in row_steps():
        for step in group:
            place = place * 2 + bit_of(step)
    return place


def shards(
    tokens,
    w_qkv,
    w_attn_out,
    w_in,
    w_out,
    vectors,
    out_grad,
    span_count,
    pair_index,
    owner_list,
    master,
    first_moment,
    second_moment,
    left_basis,
    right_basis,
    vec_first,
    vec_second,
):
    slots = tokens.shape[0] // SPAN
    device = (lax.axis_index("row") * lax.axis_size("col") + lax.axis_index("col")).reshape(1)
    core, across, y_bits, z_bits = row_steps()
    core_bit = bit_of(core[0])
    bits = jnp.stack([bit_of(step) for step in core + across + y_bits + z_bits])
    rows = vectors.reshape(1, -1)
    q, k, v, p, attended = attend(tokens, w_qkv, rows)
    encoded, hidden, slope, normed_low, unit_one, inverse_one, unit_two, inverse_two, cls_rows = (
        feed(device, span_count, tokens, attended, w_attn_out, w_in, w_out, rows)
    )
    loss, grad_cls = contrast(gather_all(cls_rows), span_count, pair_index, device, slots)
    grad_two, outer_low, vec_two = outer_grad(
        device, span_count, out_grad, grad_cls, unit_two, inverse_two, rows
    )
    outer_args = (hidden, outer_low, FF // D, True)
    outer_away = weight_half(8, [], 1 - core_bit, *outer_args)
    outer_here = weight_half(60, [outer_away], core_bit, *outer_args)
    outer_run = Reduction(bits, 2, outer_away, outer_here)
    outer_run.land()
    pre_low, grad_one, mixed_low, grad_attended, vec_one = inner_grad(
        outer_run.sent(), outer_low, grad_two, slope, unit_one, inverse_one,
        w_attn_out, w_in, w_out, rows,
    )
    outer_run.land(vec_one)
    inner_args = (normed_low, pre_low, FF // D, False, (attended, mixed_low))
    inner_away = weight_half(8, outer_run.sent(), 1 - core_bit, *inner_args)
    outer_run.land(inner_away)
    inner_here = weight_half(60, [inner_away] + outer_run.sent(), core_bit, *inner_args)
    outer_run.land(inner_here)
    inner_run = Reduction(bits, 3, inner_away, inner_here)
    inner_run.land()
    early, vec_early = unattend(
        outer_run.sent() + inner_run.sent(), 0, 2, q, k, v, p, grad_attended, attended
    )
    stack_low, vec_grad = unattend(
        [], 1, 2, q, k, v, p, grad_attended, attended, early, (vec_one, vec_two, vec_early)
    )
    inner_run.land(vec_grad)
    project_args = (tokens, stack_low, 3, False)
    project_away = weight_half(
        8, inner_run.sent() + outer_run.landing(), 1 - core_bit, *project_args
    )
    project_here = weight_half(60, [project_away], core_bit, *project_args)
    project_run = Reduction(bits, 3, project_away, project_here, vec_grad)
    project_run.land(*inner_run.landing())
    grad_tokens = input_grad(project_run.sent(), grad_one, stack_low, w_qkv)
    inner_run.land()
    project_run.land(*streamed(grad_tokens))
    inner_run.land()
    project_run.land()
    for run in (outer_run, inner_run, project_run):
        run.finish()
    low_left = ready(project_run.sent(), left_basis, LOW)
    vec_grad, *parts = to_slots(
        streamed(low_left), (project_run, inner_run, outer_run),
        (0, 1, 2, 7, 3, 4, 5, 6, 8, 9, 10, 11), owner_list,
    )
    vec_grad = vec_grad.reshape(-1)
    gathered, masks = spread(parts)
    new_master, new_first, new_second, master_copy = rotated_adam(
        row_place(), gathered, masks, turn(master), turn(first_moment), turn(second_moment),
        low_left, right_basis,
    )
    vec_first_new = 0.9 * vec_first + 0.1 * vec_grad
    vec_second_new = 0.999 * vec_second + 0.001 * vec_grad * vec_grad
    vec_step = (
        vec_first_new / (1.0 - 0.9**STEP) / (jnp.sqrt(vec_second_new / (1.0 - 0.999**STEP)) + 1e-08)
    )
    vec_new = vectors - VECTOR_RATE * vec_step
    return (
        encoded,
        grad_tokens,
        loss[0, 0],
        new_master,
        new_first,
        new_second,
        master_copy,
        vec_new,
        vec_first_new,
        vec_second_new,
    )


def solution(mesh):
    in_specs = (
        P(("row", "col"), None),
        P(),
        P(),
        P(),
        P(),
        P(),
        P(("row", "col"), None),
        P(),
        P(),
        P(),
        P("col", None, None),
        P("col", None, None),
        P("col", None, None),
        P("col", None, None),
        P("col", None, None),
        P(),
        P(),
    )
    out_specs = (
        P(("row", "col"), None),
        P(("row", "col"), None),
        P(),
        P("col", None, None),
        P("col", None, None),
        P("col", None, None),
        P("col", None, None),
        P(),
        P(),
        P(),
    )
    return jax.shard_map(shards, mesh=mesh, in_specs=in_specs, out_specs=out_specs, check_vma=False)
```

```python
from functools import partial

import jax
import jax.numpy as jnp
from jax import lax
from jax.experimental import pallas as pl
from jax.experimental.pallas import tpu as pltpu
from jax.sharding import PartitionSpec as P

D = 768
HEADS = 12
HEAD = 64
FF = 3072
SPAN = 128
STEP = 10
GROUP = 8

RATE = 0.01
DECAY = 0.01
VECTOR_RATE = 0.3

LOW = jnp.bfloat16
F32 = jnp.float32
TALL = 2 * SPAN


def dot(left_side, right_side, contract=(1, 0)):
    dims = (((contract[0],), (contract[1],)), ((), ()))
    return lax.dot_general(left_side, right_side, dims, preferred_element_type=F32)


def whole(shape):
    return pl.BlockSpec(shape, lambda *ids: (0,) * len(shape))


def cost(microseconds, transcendentals=0):
    return pl.CostEstimate(
        flops=int(microseconds * 1.1e9), bytes_accessed=0, transcendentals=transcendentals
    )


def params(mebibytes=36):
    return pltpu.CompilerParams(vmem_limit_bytes=mebibytes * 1024 * 1024)


def row_of(rows, index):
    return rows[:, index * D : (index + 1) * D]


def live_rows(place, counts, first_row, height):
    at = first_row + lax.broadcasted_iota(jnp.int32, (height, 1), 0)
    return jnp.where(at < counts[place[0]] * SPAN, 1.0, 0.0)


near = pltpu.VMEM
far = pltpu.HBM


def streamed(*arrays):
    return [pltpu.with_memory_space_constraint(a, pltpu.HBM) for a in arrays]


ANY = pl.BlockSpec(memory_space=pl.ANY)
SMEM = pl.BlockSpec(memory_space=pltpu.SMEM)


def split_heads(pair):
    lane = lax.broadcasted_iota(jnp.int32, pair.shape, 1)
    zero = jnp.zeros_like(pair)
    return jnp.concatenate([jnp.where(lane < HEAD, pair, zero), jnp.where(lane < HEAD, zero, pair)])


def normalise(scores):
    peak = jnp.max(scores, axis=-1, keepdims=True)
    raised = jnp.exp(scores - peak)
    return raised * (1.0 / jnp.sum(raised, axis=-1, keepdims=True))


def attend_kernel(tokens, w_qkv, rows, q_out, k_out, v_out, p_out, a_out):
    block = tokens[...]
    scaling = HEAD ** (-0.5)
    q_out[...] = ((dot(block, w_qkv[0]) + row_of(rows, 4)).astype(LOW) * scaling).astype(LOW)
    k_out[...] = dot(block, w_qkv[1]).astype(LOW)
    v_out[...] = (dot(block, w_qkv[2]) + row_of(rows, 5)).astype(LOW)
    for span in range(TALL // SPAN):
        at = slice(span * SPAN, (span + 1) * SPAN)
        for pair in range(HEADS // 2):
            lanes = slice(pair * 2 * HEAD, (pair + 1) * 2 * HEAD)
            scores = dot(q_out[at, lanes], split_heads(k_out[at, lanes]), (1, 1))
            weights = jnp.concatenate(
                [normalise(scores[:, :SPAN]), normalise(scores[:, SPAN:])], axis=1
            ).astype(LOW)
            p_out[span, pair] = weights
            a_out[at, lanes] = dot(weights, split_heads(v_out[at, lanes])).astype(LOW)


def attend(tokens, w_qkv, rows):
    total = tokens.shape[0]
    tall = pl.BlockSpec((TALL, D), lambda i: (i, 0))
    like = far((total, D), LOW)
    tokens, w_qkv, rows = streamed(tokens, w_qkv, rows)
    spans = TALL // SPAN
    return pl.pallas_call(
        attend_kernel,
        grid=(total // TALL,),
        in_specs=[tall, whole(w_qkv.shape), whole(rows.shape)],
        out_specs=[
            tall,
            tall,
            tall,
            pl.BlockSpec((spans, HEADS // 2, SPAN, 2 * SPAN), lambda i: (i, 0, 0, 0)),
            tall,
        ],
        out_shape=[
            like,
            like,
            like,
            far((total // SPAN, HEADS // 2, SPAN, 2 * SPAN), LOW),
            near((total, D), LOW),
        ],
        compiler_params=params(),
        cost_estimate=cost(10),
        name="attend",
    )(tokens, w_qkv, rows)


def unit_norm(resid):
    centred = resid - jnp.mean(resid, axis=-1, keepdims=True)
    inverse = lax.rsqrt(jnp.mean(centred * centred, axis=-1, keepdims=True) + 1e-06)
    return centred * inverse, inverse


def gelu_pair(x):
    cdf = 0.5 + 0.5 * lax.erf(x * 0.7071067811865476)
    return x * cdf, cdf + x * jnp.exp(-0.5 * x * x) * 0.3989422804014327


def feed_kernel(
    place, counts, tokens, attended, w_attn, w_in, w_out, rows, bias,
    enc_out, hid_out, slope_out, norm_out, u1_out, i1_out, u2_out, i2_out, cls_out, total, firsts,
):
    band = pl.program_id(0)
    chunks = [slice(at, at + TALL) for at in range(0, tokens.shape[0], TALL)]

    @pl.when(band == 0)
    def _():
        for at in chunks:
            resid = tokens[at].astype(F32) + dot(attended[at], w_attn[...]) + row_of(rows, 6)
            unit_one, inverse_one = unit_norm(resid)
            value = unit_one * row_of(rows, 0) + row_of(rows, 2)
            u1_out[at] = unit_one.astype(LOW)
            i1_out[at] = inverse_one
            norm_out[at] = value.astype(LOW)
            total[at] = value + row_of(rows, 7)

    step = 256
    for at in range(0, hid_out.shape[1], step):
        here = slice(at, at + step)
        pre_act = dot(norm_out[...], w_in[:, here]) + bias[:, here]
        hidden, slope = gelu_pair(pre_act)
        hid_out[:, here] = hidden.astype(LOW)
        slope_out[:, here] = slope.astype(LOW)

    @pl.when(band < pl.num_programs(0) - 1)
    def _():
        total[...] += dot(hid_out[...], w_out[...])

    @pl.when(band == pl.num_programs(0) - 1)
    def _():
        for at in chunks:
            resid = total[at] + dot(hid_out[at], w_out[...])
            unit_two, inverse_two = unit_norm(resid)
            u2_out[at] = unit_two.astype(LOW)
            i2_out[at] = inverse_two
            live = live_rows(place, counts, at.start, TALL)
            value = live * (unit_two * row_of(rows, 1) + row_of(rows, 3))
            enc_out[at] = value.astype(LOW)
            for first in range(at.start, at.stop, SPAN):
                row = first - at.start
                firsts[first // SPAN : first // SPAN + 1] = value[row : row + 1]
        firsts[tokens.shape[0] // SPAN :] = jnp.zeros((GROUP - tokens.shape[0] // SPAN, D), F32)
        cls_out[...] = firsts[...].astype(LOW)


def feed(place, counts, tokens, attended, w_attn, w_in, w_out, rows):
    total = tokens.shape[0]
    tall = lambda width: pl.BlockSpec((total, width), lambda j: (0, 0))
    band = lambda height: pl.BlockSpec((height, D), lambda j: (0, j))
    tokens, w_attn, w_in, w_out, rows = streamed(tokens, w_attn, w_in, w_out, rows)
    return pl.pallas_call(
        feed_kernel,
        grid=(FF // D,),
        in_specs=[
            SMEM, SMEM, tall(D), tall(D), whole(w_attn.shape), band(D),
            pl.BlockSpec((D, D), lambda j: (j, 0)),
            pl.BlockSpec((1, 8 * D), lambda j: (0, 0)),
            pl.BlockSpec((1, D), lambda j: (0, 8 + j)),
        ],
        out_specs=[
            tall(D), band(total), band(total), tall(D), tall(D), tall(1), tall(D), tall(1),
            whole((GROUP, D)),
        ],
        out_shape=[
            jax.ShapeDtypeStruct((total, D), LOW),
            far((total, FF), LOW),
            far((total, FF), LOW),
            far((total, D), LOW),
            far((total, D), LOW),
            far((total, 1), F32),
            near((total, D), LOW),
            near((total, 1), F32),
            jax.ShapeDtypeStruct((GROUP, D), LOW),
        ],
        scratch_shapes=[pltpu.VMEM((total, D), F32), pltpu.VMEM((GROUP, D), F32)],
        compiler_params=params(),
        cost_estimate=cost(20),
        name="feed",
    )(place, counts, tokens, attended, w_attn, w_in, w_out, rows, rows)


def norm_back(grad_out, unit_rows, inverse, gain):
    scaled = grad_out * gain
    along = jnp.mean(scaled * unit_rows, axis=-1, keepdims=True)
    return inverse * (scaled - jnp.mean(scaled, axis=-1, keepdims=True) - unit_rows * along)


def column_sums(*arrays):
    return [jnp.sum(a, axis=0, keepdims=True) for a in arrays]


def outer_kernel(place, counts, out_grad, grad_cls, unit_two, inverse_two, rows, two_out, low_out, vec_out):
    spot = lax.broadcasted_iota(jnp.int32, (SPAN, 1), 0) == 0
    sums = None
    for span in range(out_grad.shape[0] // SPAN):
        at = slice(span * SPAN, (span + 1) * SPAN)
        added = jnp.where(spot, grad_cls[span : span + 1], 0.0)
        live = live_rows(place, counts, span * SPAN, SPAN)
        grad_y = live * (out_grad[at].astype(F32) + added)
        unit_rows = unit_two[at].astype(F32)
        grad_two = norm_back(grad_y, unit_rows, inverse_two[at], row_of(rows, 1))
        two_out[at] = grad_two
        low_out[at] = grad_two.astype(LOW)
        here = column_sums(grad_y * unit_rows, grad_y, grad_two)
        sums = here if sums is None else [a + b for a, b in zip(sums, here)]
    for index, total in enumerate(sums):
        vec_out[index : index + 1] = total


def outer_grad(place, counts, out_grad, grad_cls, unit_two, inverse_two, rows):
    total = out_grad.shape[0]
    return pl.pallas_call(
        outer_kernel,
        in_specs=[SMEM, SMEM] + [pl.BlockSpec(memory_space=pltpu.VMEM)] * 5,
        out_shape=[
            jax.ShapeDtypeStruct((total, D), F32),
            jax.ShapeDtypeStruct((total, D), LOW),
            jax.ShapeDtypeStruct((3, D), F32),
        ],
        compiler_params=params(),
        cost_estimate=cost(5),
        name="outer",
    )(place, counts, out_grad, grad_cls, unit_two, inverse_two, rows)


def weight_kernel(panels, after, side, *refs):
    *sides, out = refs[after:]

    @pl.when(pl.program_id(0) < panels)
    def _():
        out[0] = dot(sides[0][...], sides[1][...], (0, 0)).astype(LOW)

    if len(sides) > 2:

        @pl.when(pl.program_id(0) == panels)
        def _():
            out[0] = dot(sides[2][...], sides[3][...], (0, 0)).astype(LOW)


def weight_half(hint, after, side, left_side, right_side, panels, banded, extra=()):
    total = left_side.shape[0]
    half = D // 2
    every = panels + len(extra) // 2
    tall = lambda width, at: pl.BlockSpec((total, width), at)
    last = lambda panel: jnp.minimum(panel, panels - 1)
    left_at = lambda panel, side: (0, last(panel) * 2 + side[0] if banded else side[0])
    right_at = lambda panel, side: (0, 0 if banded else last(panel))
    more = [tall(half, lambda p, s: (0, s[0])), tall(D, lambda p, s: (0, 0))]
    return pl.pallas_call(
        partial(weight_kernel, panels, len(after)),
        grid_spec=pltpu.PrefetchScalarGridSpec(
            num_scalar_prefetch=1,
            grid=(every,),
            in_specs=[ANY] * len(after)
            + [tall(half, left_at), tall(D, right_at)]
            + more[: len(extra)],
            out_specs=pl.BlockSpec((1, half, D), lambda p, s: (p, 0, 0)),
        ),
        out_shape=jax.ShapeDtypeStruct((every, half, D), LOW),
        compiler_params=params(),
        cost_estimate=cost(hint),
        name="weight",
    )(side.reshape(1), *after, left_side, right_side, *extra)


def inner_kernel(after, *refs):
    low, grad_two, slope, unit_one, inverse_one, w_attn, w_in, w_out, rows = refs[after:-6]
    pre_out, one_out, mixed_out, ga_out, vec_out, total = refs[-6:]
    band = pl.program_id(0)
    last = pl.num_programs(0) - 1
    step = 256
    for at in range(0, D, step):
        here = slice(at, at + step)
        grad_pre = dot(low[...], w_out[here], (1, 1)) * slope[:, here].astype(F32)
        pre_out[:, here] = grad_pre.astype(LOW)
        vec_out[pl.ds(3 + band, 1), here] = jnp.sum(grad_pre, axis=0, keepdims=True)

    @pl.when(band == 0)
    def _():
        total[...] = grad_two[...] + dot(pre_out[...], w_in[...], (1, 1))

    @pl.when((band > 0) & (band < last))
    def _():
        total[...] += dot(pre_out[...], w_in[...], (1, 1))

    @pl.when(band == last)
    def _():
        sums = None
        for first in range(0, low.shape[0], TALL):
            at = slice(first, first + TALL)
            grad_normed = total[at] + dot(pre_out[at], w_in[...], (1, 1))
            unit_rows = unit_one[at].astype(F32)
            grad_one = norm_back(grad_normed, unit_rows, inverse_one[at], row_of(rows, 0))
            one_out[at] = grad_one
            mixed = grad_one.astype(LOW)
            mixed_out[at] = mixed
            ga_out[at] = dot(mixed, w_attn[...], (1, 1)).astype(LOW)
            here = column_sums(grad_normed * unit_rows, grad_normed, grad_one)
            sums = here if sums is None else [a + b for a, b in zip(sums, here)]
        for index, value in enumerate(sums):
            vec_out[index : index + 1] = value


def inner_grad(after, low, grad_two, slope, unit_one, inverse_one, w_attn, w_in, w_out, rows):
    total = low.shape[0]
    bands = FF // D
    slope, w_attn, w_in, w_out, rows = streamed(slope, w_attn, w_in, w_out, rows)
    band = lambda height: pl.BlockSpec((height, D), lambda j: (0, j))
    return pl.pallas_call(
        partial(inner_kernel, len(after)),
        grid=(bands,),
        in_specs=[ANY] * len(after)
        + [
            whole(low.shape), whole(grad_two.shape), band(total), whole(unit_one.shape),
            whole(inverse_one.shape), whole(w_attn.shape), band(D),
            pl.BlockSpec((D, D), lambda j: (j, 0)), whole(rows.shape),
        ],
        out_specs=[band(total)] + [whole((total, D))] * 3 + [whole((3 + bands, D))],
        out_shape=[
            near((total, FF), LOW),
            far((total, D), F32),
            near((total, D), LOW),
            near((total, D), LOW),
            jax.ShapeDtypeStruct((3 + bands, D), F32),
        ],
        scratch_shapes=[pltpu.VMEM((total, D), F32)],
        compiler_params=params(),
        cost_estimate=cost(16),
        name="inner",
    )(*after, low, grad_two, slope, unit_one, inverse_one, w_attn, w_in, w_out, rows)


def unattend_kernel(after, sums, *refs):
    q, k, v, p, ga, attended = refs[after : after + 6]
    vec_one, vec_two, vec_early = refs[after + 6 : -2] if sums else (None, None, None)
    stack_out, vec_out = refs[-2:]
    scaling = HEAD ** (-0.5)
    first = pl.program_id(0) == 0

    @pl.when(first)
    def _():
        if not sums:
            vec_out[...] = jnp.zeros_like(vec_out)
            return
        for index in range(2):
            vec_out[2 * index : 2 * index + 1] = vec_one[index : index + 1]
            vec_out[2 * index + 1 : 2 * index + 2] = vec_two[index : index + 1]
        vec_out[4:6] = vec_early[...]
        vec_out[6:7] = vec_one[2:3]
        vec_out[7:8] = vec_two[2:3]
        vec_out[8:] = vec_one[3:]

    place = 4 if sums else 0
    head_of_row = lax.broadcasted_iota(jnp.int32, (2 * HEAD, 2 * SPAN), 0) // HEAD
    head_of_lane = lax.broadcasted_iota(jnp.int32, (2 * HEAD, 2 * SPAN), 1) // SPAN
    by_head = jnp.where(head_of_row == head_of_lane, 1.0, 0.0).astype(LOW)
    for span in range(p.shape[0]):
        at = slice(span * SPAN, (span + 1) * SPAN)
        for pair in range(HEADS // 2):
            lo = pair * 2 * HEAD
            lanes = slice(lo, lo + 2 * HEAD)
            weights = p[span, pair]
            grad = ga[at, lanes]
            spread_out = dot(grad, split_heads(v[at, lanes]), (1, 1))
            along = (grad.astype(F32) * attended[at, lanes].astype(F32)).astype(LOW)
            grad_scores = (weights.astype(F32) * (spread_out - dot(along, by_head))).astype(LOW)
            parts = [grad_scores[:, :SPAN], grad_scores[:, SPAN:]]
            grad_q = dot(grad_scores, split_heads(k[at, lanes])) * scaling
            tall_scores = jnp.concatenate(parts, axis=0)
            tall_weights = jnp.concatenate([weights[:, :SPAN], weights[:, SPAN:]], axis=0)
            grad_k = dot(tall_scores, split_heads(q[at, lanes]), (0, 0))
            grad_v = dot(tall_weights, split_heads(grad), (0, 0))
            stack_out[at, lo : lo + 2 * HEAD] = grad_q.astype(LOW)
            stack_out[at, D + lo : D + lo + 2 * HEAD] = grad_k.astype(LOW)
            stack_out[at, 2 * D + lo : 2 * D + lo + 2 * HEAD] = grad_v.astype(LOW)
            vec_out[place : place + 1, lanes] += jnp.sum(grad_q, axis=0, keepdims=True)
            vec_out[place + 1 : place + 2, lanes] += jnp.sum(grad_v, axis=0, keepdims=True)


def unattend(after, part, parts, q, k, v, p, ga, attended, stack=None, sums=()):
    total = q.shape[0]
    count = total // SPAN // parts
    first = part * count
    tall = lambda width: pl.BlockSpec((SPAN, width), lambda i: (first + i, 0))
    after = after if stack is None else [stack] + after
    vec_shape = (12, D) if sums else (2, D)
    return pl.pallas_call(
        partial(unattend_kernel, len(after), bool(sums)),
        grid=(count,),
        in_specs=[ANY] * len(after)
        + [tall(D)] * 3
        + [
            pl.BlockSpec((1, HEADS // 2, SPAN, 2 * SPAN), lambda i: (first + i, 0, 0, 0)),
            tall(D),
            tall(D),
        ]
        + [whole(a.shape) for a in sums],
        out_specs=[tall(3 * D), whole(vec_shape)],
        out_shape=[far((total, 3 * D), LOW), jax.ShapeDtypeStruct(vec_shape, F32)],
        input_output_aliases={} if stack is None else {0: 0},
        compiler_params=params(),
        cost_estimate=cost(8),
        name="unattend",
    )(*after, q, k, v, p, ga, attended, *sums)


def input_kernel(*refs):
    grad_one, stack, w_qkv, out = refs[-4:]
    total = grad_one[...]
    for index in range(3):
        total += dot(stack[:, index * D : (index + 1) * D], w_qkv[index], (1, 1))
    out[...] = total


def input_grad(after, grad_one, stack, w_qkv):
    total = grad_one.shape[0]
    tall = lambda width: pl.BlockSpec((TALL, width), lambda i: (i, 0))
    return pl.pallas_call(
        input_kernel,
        grid=(total // TALL,),
        in_specs=[ANY] * len(after) + [tall(D), tall(3 * D), whole(w_qkv.shape)],
        out_specs=tall(D),
        out_shape=jax.ShapeDtypeStruct((total, D), F32),
        compiler_params=params(),
        cost_estimate=cost(8),
        name="input",
    )(*after, grad_one, stack, w_qkv)


def contrast_kernel(slots, masks, place, rows, counts, partners, loss_out, grad_out):
    total, scale = rows.shape[0], 2.0 * D ** (-0.5)

    def number(shape, axis):
        at = lax.broadcasted_iota(jnp.int32, shape, axis)
        device, block = jnp.full(shape, place[0], jnp.int32), at // GROUP
        for bit, mask in enumerate(masks):
            device = device ^ (((block >> bit) & 1) * mask)
        return device, at % GROUP

    device, slot = number((counts.shape[1], total), 1)
    hit = lax.broadcasted_iota(jnp.int32, device.shape, 0) == device
    count = dot(counts[...].astype(LOW), jnp.where(hit, 1.0, 0.0).astype(LOW))
    live_across = (slot[:1].astype(F32) < count) & (slot[:1] < slots)
    device, slot = number((total, counts.shape[1]), 0)
    hit = lax.broadcasted_iota(jnp.int32, device.shape, 1) == device
    count = jnp.sum(jnp.where(hit, counts[...], 0.0), axis=1, keepdims=True)
    live_down = (slot[:, :1].astype(F32) < count) & (slot[:, :1] < slots)
    device, slot = number((total, partners.shape[1]), 0)
    own_id = device * slots + slot
    hit = lax.broadcasted_iota(jnp.int32, own_id.shape, 1) == own_id
    pair = jnp.sum(jnp.where(hit, partners[...], 0.0), axis=1, keepdims=True)
    device, slot = number((total, 128), 0)
    down = (device * slots + slot).astype(F32)[:, :1]
    device, slot = number((8, total), 1)
    across, slot = (device * slots + slot).astype(F32)[:1], slot[:1]
    valid = live_across & (down != across)
    matched = jnp.where((slot < slots) & (pair == across), 1.0, 0.0)
    anchor = jnp.where(live_down & (pair != down), 1.0, 0.0)
    similar = dot(rows[...], rows[...], (1, 1)) * scale
    masked = jnp.where(valid, similar, -1e30)
    peak = jnp.max(masked, axis=1, keepdims=True)
    summed = jnp.sum(jnp.where(valid, jnp.exp(masked - peak), 0.0), axis=1, keepdims=True)
    log_total = jnp.log(summed) + peak
    positive = jnp.sum(matched * similar, axis=1, keepdims=True)
    loss_out[...] = jnp.sum(anchor * (log_total - positive), axis=0, keepdims=True)
    grad = (anchor * (jnp.where(valid, jnp.exp(masked - log_total), 0.0) - matched)).astype(LOW)
    own = lax.broadcasted_iota(jnp.int32, (GROUP, total), 0)
    own = jnp.where(own == lax.broadcasted_iota(jnp.int32, (GROUP, total), 1), 1.0, 0.0)
    down_part = dot(dot(own.astype(LOW), grad, (1, 1)).astype(LOW), rows[...])
    grad_out[...] = (dot(grad[: 2 * GROUP], rows[...])[:GROUP] + down_part) * scale


def contrast(cls_rows, span_count, pair_index, device, slots):
    total = cls_rows.shape[0]
    scale = {"row": lax.axis_size("col"), "col": 1}
    masks = [scale[name] * bit for phase in gather_steps() for name, bit in phase]
    return pl.pallas_call(
        partial(contrast_kernel, slots, masks),
        in_specs=[pl.BlockSpec(memory_space=pltpu.SMEM)]
        + [pl.BlockSpec(memory_space=pltpu.VMEM)] * 3,
        out_shape=[
            jax.ShapeDtypeStruct((1, 1), F32),
            jax.ShapeDtypeStruct((GROUP, D), F32),
        ],
        compiler_params=params(),
        cost_estimate=cost(3),
        name="contrast",
    )(
        device,
        cls_rows,
        span_count.astype(F32).reshape(1, -1),
        pair_index.astype(F32).reshape(1, -1),
    )


def adam_kernel(
    masks, parts, position, *refs,
):
    gathered = refs[:parts]
    master, first, second, left, right, master_out, first_out, second_out, low_out, *scratch = refs[parts:]
    quarter = D // 4
    slot = pl.program_id(0)
    if masks:
        owned = scratch[0]
        shares, tall, _ = gathered[0].shape
        rows = D // len(masks)

        @pl.when(slot == 0)
        def _():
            for number, mask in enumerate(masks):
                block = gathered[number // shares][number % shares].astype(F32)
                at = pl.multiple_of((mask ^ position[0]) * rows, rows)
                for index in range(owned.shape[0]):
                    lo = index * rows % tall
                    side = index * rows // tall
                    piece = block[lo : lo + rows, side * quarter : (side + 1) * quarter]
                    owned[index, pl.ds(at, rows), :] = piece

    for here in range(master.shape[0]):
        if masks:
            gradient = owned[slot * master.shape[0] + here].astype(LOW)
        else:
            gradient = gathered[0][here]
        low_left, low_right = left[here], right[here].astype(LOW)
        turned = dot(gradient, low_left, (0, 0))
        turned = dot(low_right, turned.astype(LOW), (0, 0))
        new_first = 0.9 * first[here] + 0.1 * turned
        new_second = 0.999 * second[here] + 0.001 * turned * turned
        first_out[here] = new_first
        second_out[here] = new_second
        spread_by = jnp.sqrt(new_second * (1.0 / (1.0 - 0.999**STEP))) + 1e-08
        update = new_first * (1.0 / (1.0 - 0.9**STEP)) / spread_by
        update = dot(update.astype(LOW), low_left, (1, 1))
        update = dot(low_right, update.astype(LOW))
        new_master = master[here] - RATE * (update + DECAY * master[here])
        master_out[here] = new_master
        low_out[here] = new_master.astype(LOW)


def ready_kernel(*refs):
    source, out = refs[-2:]
    out[...] = source[...].astype(out.dtype)


def ready(after, array, kind, first, count, before=()):
    block = pl.BlockSpec((1,) + array.shape[1:], lambda s: (first + s, 0, 0))
    first_in = list(before) + list(after)
    return pl.pallas_call(
        ready_kernel,
        grid=(count,),
        in_specs=[ANY] * len(first_in) + [block],
        out_specs=block,
        out_shape=far(array.shape, kind),
        input_output_aliases={0: 0} if before else {},
        compiler_params=params(16),
        cost_estimate=cost(1.5 * count),
        name="ready",
    )(*first_in, *streamed(array))


def to_owned(gathered, masks, position, per_owner):
    quarter = D // 4
    places = jnp.array(masks, jnp.int32) ^ position
    gathered = jnp.zeros_like(gathered).at[places].set(gathered)
    flat = jnp.concatenate([gathered[..., :quarter], gathered[..., quarter:]], axis=1)
    rows = flat.shape[1] // per_owner
    flat = flat.reshape(flat.shape[0], per_owner, rows, quarter).transpose(1, 0, 2, 3)
    return flat.reshape(per_owner, D, quarter)


def turn(array):
    return array.transpose(0, 2, 1)


def rotated_adam(position, gathered, masks, master, first_moment, second_moment, left_basis, right_basis):
    per_owner, quarter, _ = master.shape
    if D // len(masks) % 8 or per_owner % 2:
        gathered = [to_owned(jnp.concatenate(gathered), masks, position, per_owner)]
        masks = []
    at_once = max(n for n in (1, 2, 3) if per_owner % n == 0)
    block = lambda a: pl.BlockSpec((at_once,) + a.shape[1:], lambda s, p: (s, 0, 0))
    operands = streamed(master, first_moment, second_moment, left_basis, right_basis)
    like = jax.ShapeDtypeStruct(operands[0].shape, F32)
    fixed = pl.BlockSpec(gathered[0].shape, lambda s, p: (0, 0, 0))
    outputs = pl.pallas_call(
        partial(adam_kernel, masks, len(gathered)),
        grid_spec=pltpu.PrefetchScalarGridSpec(
            num_scalar_prefetch=1,
            grid=(per_owner // at_once,),
            in_specs=[fixed if masks else block(part) for part in gathered]
            + [block(a) for a in operands],
            out_specs=[block(operands[0])] * 4,
            scratch_shapes=[pltpu.VMEM((per_owner, D, quarter), F32)] if masks else [],
        ),
        out_shape=[like, like, like, jax.ShapeDtypeStruct(like.shape, LOW)],
        compiler_params=params(48),
        cost_estimate=cost(20),
        name="adam",
    )(position.reshape(1), *gathered, *operands)
    return [turn(a) for a in outputs]


def axis_bits(name):
    size = lax.axis_size(name)
    return [(name, 1 << k) for k in range(size.bit_length() - 1)]


def bit_of(step):
    return jnp.where((lax.axis_index(step[0]) & step[1]) != 0, 1, 0)


def swap(send, step):
    size = lax.axis_size(step[0])
    return lax.ppermute(send, step[0], [(i, i ^ step[1]) for i in range(size)])


def gather_steps():
    core, across, y_bits, z_bits = row_steps()
    return [z_bits[::-1], y_bits + across, core]


def gather_all(rows, beside):
    columns = lax.axis_size("col")
    every = lax.axis_size("row") * columns
    scale = {"row": columns, "col": 1}
    for phase in gather_steps():
        arrived = []
        for number in range(1, 1 << len(phase)):
            mask = sum(scale[name] * bit for j, (name, bit) in enumerate(phase) if number >> j & 1)
            pairs = [(i, i ^ mask) for i in range(every)]
            arrived.append(lax.ppermute(rows, ("row", "col"), pairs))
        if beside:
            rows = merge(beside, [rows] + arrived).reshape(-1, D)
            beside = []
        else:
            rows = jnp.concatenate([rows] + arrived)
    return rows


def row_steps():
    row_bits, col_bits = axis_bits("row"), axis_bits("col")
    core, across = row_bits[:1], row_bits[1:][::-1]
    y_bits, z_bits = col_bits[:-2][::-1], col_bits[-2:]
    return core, across, y_bits, z_bits


def pack_rider(rider, rows, width):
    parts = [rider[:, at : at + width] for at in range(0, D, width)]
    tall = rider.shape[0]
    if rows < tall:
        return [part[at : at + rows] for part in parts for at in range(0, tall, rows)]
    fold = rows // tall
    parts += parts[-1:] * (-len(parts) % fold)
    return [jnp.concatenate(parts[at : at + fold]) for at in range(0, len(parts), fold)]


def unpack_rider(blocks, tall):
    rows, width = blocks[0].shape
    if rows < tall:
        fold = tall // rows
        parts = [jnp.concatenate(blocks[at : at + fold]) for at in range(0, len(blocks), fold)]
    else:
        parts = [block[at : at + tall] for block in blocks for at in range(0, rows, tall)]
    parts = parts[: D // width]
    return parts[0] if len(parts) == 1 else jnp.concatenate(parts, axis=1)


def rider_blocks(rows, width, tall=12):
    return -(-tall * D // (rows * width))


def land_kernel(after, outs, rider, bits, *refs):
    refs = refs[after:]
    sides = len({source[0] for out in outs for source in out[3]})
    keeps, others = refs[0 : 2 * sides : 2], refs[1 : 2 * sides : 2]
    results = refs[2 * sides + (0 if rider is None else 1 + (rider == "array")) :]
    if rider is not None:
        total = refs[2 * sides][...]
        tall = total.shape[0]
        if rider == "array":
            total += refs[2 * sides + 1][...]
        else:
            blocks = [others[0][at].astype(F32) for at in range(keeps[0].shape[0], others[0].shape[0])]
            total += unpack_rider(blocks, tall)
        results[-1][...] = total
    for number, (at_bit, before, behind, sources) in enumerate(outs):
        bit = bits[at_bit]
        for which, target in enumerate(results[2 * number : 2 * number + 2]):
            half = bit if which else 1 - bit
            for at in range(before):
                here = pl.ds((2 * at + half) * behind, behind)
                there = slice(at * behind, (at + 1) * behind)
                for side, lanes, into in sources:
                    target[there, :, into] = keeps[side][here, :, lanes] + others[side][here, :, lanes]
        if rider is not None and number == 0:
            away = results[0]
            count, rows, width = away.shape
            blocks = pack_rider(total, rows, width)
            for index, block in enumerate(blocks):
                away[count - len(blocks) + index] = block.astype(LOW)


class Reduction:
    def __init__(self, bits, ways, send, keep, rider=None):
        core, across, y_bits, z_bits = row_steps()
        self.bits, self.order = bits, core + across + y_bits + z_bits
        left = across + y_bits + z_bits
        self.panels, height, _ = keep.shape
        self.rows = height >> len(left)
        other = swap(send, core[0])
        self.rider = None if rider is None else (rider, swap(rider, core[0]))
        split = lambda a: a.reshape(-1, self.rows, D)
        self.sides = [(split(keep), split(other), left)]
        cycle = [across, y_bits, z_bits[:1]][:ways]
        orders = [sum(cycle[at:] + cycle[:at], []) for at in range(ways)]
        self.stages = list(zip(*orders)) + [(step,) for step in z_bits[ways - 2 :]]
        self.ways = ways
        self.messages = []

    def sent(self):
        return self.messages

    def landing(self):
        return [side[1] for side in self.sides]

    def land(self, *after):
        stage = self.stages.pop(0)
        outs, shapes, lefts = [], [], []
        part = D // self.ways
        lanes = [slice(at, at + part) for at in range(0, D, part)]
        for index, step in enumerate(stage):
            if len(self.sides) == len(stage):
                width = self.sides[index][0].shape[2]
                sources = [(index, slice(0, width), slice(0, width))]
                left = self.sides[index][2]
            elif len(stage) > 1:
                width, left = part, self.sides[0][2]
                sources = [(0, lanes[index], slice(0, part))]
            else:
                width, left = D, self.sides[0][2]
                sources = [(side, slice(0, part), lanes[side]) for side in range(self.ways)]
            dim = left.index(step)
            behind = 1 << (len(left) - dim - 1)
            before = self.panels << dim
            outs.append((self.order.index(step), before, behind, sources))
            extra = rider_blocks(self.rows, width) if self.rider and index == 0 else 0
            shapes += [(before * behind + extra, self.rows, width), (before * behind, self.rows, width)]
            lefts.append([other for other in left if other != step])
        rider = None if self.rider is None else ("array" if len(self.rider) == 2 else "message")
        inputs = [a for keep, other, _ in self.sides for a in (keep, other)] + list(self.rider or ())
        out_shape = [jax.ShapeDtypeStruct(shape, LOW) for shape in shapes]
        if rider:
            out_shape.append(jax.ShapeDtypeStruct(self.rider[0].shape, F32))
        results = pl.pallas_call(
            partial(land_kernel, len(after), outs, rider),
            in_specs=[SMEM] + [ANY] * len(after) + [pl.BlockSpec(memory_space=pltpu.VMEM)] * len(inputs),
            out_shape=out_shape,
            compiler_params=params(24),
            cost_estimate=cost(2),
            name="land",
        )(self.bits, *after, *inputs)
        if rider:
            self.rider = (results[-1],)
        self.messages = list(results[0 : 2 * len(stage) : 2])
        keeps = results[1 : 2 * len(stage) : 2]
        self.sides = [
            (keep, swap(message, step), left)
            for keep, message, step, left in zip(keeps, self.messages, stage, lefts)
        ]

    def finish(self):
        while self.stages:
            self.land()


def slots_kernel(after, cols, panels, column, owners, *refs):
    refs = refs[after:]
    sums, rider, rider_out = refs[:6], refs[6], refs[7]
    targets, blocks, packed = refs[8:-2], refs[-2], refs[-1]
    quarter = D // 4
    found = [(sums[2 * run], sums[2 * run + 1], i) for run in range(3) for i in range(sums[2 * run].shape[0])]
    at = 0
    for panel in panels:
        keep, other, index = found[panel]
        value = keep[index].astype(F32) + other[index].astype(F32)
        for part in range(4):
            blocks[at] = value[:, part * quarter : (part + 1) * quarter]
            at += 1
    tail = [sums[1][index].astype(F32) for index in range(sums[0].shape[0], sums[1].shape[0])]
    rider_out[...] = rider[...] + unpack_rider(tail, rider.shape[0])
    rows, half = blocks.shape[1], packed.shape[1]
    for slot in range(at):
        col, place = divmod(slot, at // cols)
        value = blocks[owners[slot]]
        first = place * rows
        for side in range(2):
            lo, hi = max(first, side * half), min(first + rows, (side + 1) * half)
            if lo < hi:
                lanes = slice(side * quarter, (side + 1) * quarter)
                packed[col, lo - side * half : hi - side * half, lanes] = value[lo - first : hi - first]
    for number, target in enumerate(targets):
        target[...] = packed[column[0] ^ number].astype(LOW)


def to_slots(after, runs, panels, owner_list):
    quarter, cols = D // 4, lax.axis_size("col")
    arrays = [a for run in runs for a in run.sides[0][:2]]
    rows = runs[0].rows
    shape = (len(panels) * 4 // cols * rows // 2, 2 * quarter)
    rider = runs[0].rider[0]
    return pl.pallas_call(
        partial(slots_kernel, len(after), cols, panels),
        in_specs=[SMEM, SMEM] + [ANY] * len(after) + [pl.BlockSpec(memory_space=pltpu.VMEM)] * 7,
        out_shape=[jax.ShapeDtypeStruct(rider.shape, F32)] + [jax.ShapeDtypeStruct(shape, LOW)] * cols,
        scratch_shapes=[
            pltpu.VMEM((len(panels) * 4, rows, quarter), F32),
            pltpu.VMEM((cols,) + shape, F32),
        ],
        compiler_params=params(24),
        cost_estimate=cost(4),
        name="slots",
    )(lax.axis_index("col").reshape(1), owner_list, *after, *arrays, rider)


def merge_kernel(after, *refs):
    *sources, target = refs[after:]
    for number, source in enumerate(sources):
        target[number] = source[...]


def merge(after, arrays):
    return pl.pallas_call(
        partial(merge_kernel, len(after)),
        in_specs=[ANY] * len(after) + [pl.BlockSpec(memory_space=pltpu.VMEM)] * len(arrays),
        out_shape=jax.ShapeDtypeStruct((len(arrays),) + arrays[0].shape, arrays[0].dtype),
        compiler_params=params(24),
        cost_estimate=cost(1),
        name="merge",
    )(*after, *arrays)


def spread(parts):
    core, across, y_bits, z_bits = row_steps()
    order = core + across + y_bits + z_bits
    weight = lambda step: 1 << (len(order) - 1 - order.index(step))
    cols, bits = len(parts), axis_bits("col")
    sent = lambda number: lax.ppermute(parts[number], "col", [(i, i ^ number) for i in range(cols)])
    arrived = [parts[0]] + [sent(number) for number in range(1, cols)]
    masks = [sum(weight(step) for step in bits if number & step[1]) for number in range(cols)]
    near = merge([], arrived[: cols // 2])
    first, *rest = (core + across)[::-1]
    moved = swap(near, first)
    far = merge([], arrived[cols // 2 :])
    shares = [near, far, moved, swap(far, first)]
    masks = masks + [mask ^ weight(first) for mask in masks]
    for step in rest:
        shares = shares + [swap(share, step) for share in shares]
        masks = masks + [mask ^ weight(step) for mask in masks]
    return shares, masks


def row_place():
    place = 0
    for group in row_steps():
        for step in group:
            place = place * 2 + bit_of(step)
    return place


def shards(
    tokens,
    w_qkv,
    w_attn_out,
    w_in,
    w_out,
    vectors,
    out_grad,
    span_count,
    pair_index,
    owner_list,
    master,
    first_moment,
    second_moment,
    left_basis,
    right_basis,
    vec_first,
    vec_second,
):
    slots = tokens.shape[0] // SPAN
    device = (lax.axis_index("row") * lax.axis_size("col") + lax.axis_index("col")).reshape(1)
    core, across, y_bits, z_bits = row_steps()
    core_bit = bit_of(core[0])
    bits = jnp.stack([bit_of(step) for step in core + across + y_bits + z_bits])
    rows = vectors.reshape(1, -1)
    q, k, v, p, attended = attend(tokens, w_qkv, rows)
    encoded, hidden, slope, normed_low, unit_one, inverse_one, unit_two, inverse_two, cls_rows = (
        feed(device, span_count, tokens, attended, w_attn_out, w_in, w_out, rows)
    )
    per_owner = left_basis.shape[0]
    head = per_owner // 3
    low_left = ready([cls_rows], left_basis, LOW, 0, head)
    every_cls = gather_all(cls_rows, streamed(low_left))
    loss, grad_cls = contrast(every_cls, span_count, pair_index, device, slots)
    grad_two, outer_low, vec_two = outer_grad(
        device, span_count, out_grad, grad_cls, unit_two, inverse_two, rows
    )
    outer_args = (hidden, outer_low, FF // D, True)
    outer_away = weight_half(8, [], 1 - core_bit, *outer_args)
    outer_here = weight_half(60, [outer_away], core_bit, *outer_args)
    outer_run = Reduction(bits, 2, outer_away, outer_here)
    outer_run.land()
    pre_low, grad_one, mixed_low, grad_attended, vec_one = inner_grad(
        outer_run.sent(), outer_low, grad_two, slope, unit_one, inverse_one,
        w_attn_out, w_in, w_out, rows,
    )
    outer_run.land(vec_one)
    inner_args = (normed_low, pre_low, FF // D, False, (attended, mixed_low))
    inner_away = weight_half(8, outer_run.sent(), 1 - core_bit, *inner_args)
    outer_run.land(inner_away)
    inner_here = weight_half(60, [inner_away] + outer_run.sent(), core_bit, *inner_args)
    outer_run.land(inner_here)
    inner_run = Reduction(bits, 3, inner_away, inner_here)
    inner_run.land()
    early, vec_early = unattend(
        outer_run.sent() + inner_run.sent(), 0, 2, q, k, v, p, grad_attended, attended
    )
    stack_low, vec_grad = unattend(
        [], 1, 2, q, k, v, p, grad_attended, attended, early, (vec_one, vec_two, vec_early)
    )
    inner_run.land(vec_grad)
    project_args = (tokens, stack_low, 3, False)
    project_away = weight_half(
        8, inner_run.sent() + outer_run.landing(), 1 - core_bit, *project_args
    )
    project_here = weight_half(60, [project_away], core_bit, *project_args)
    project_run = Reduction(bits, 3, project_away, project_here, vec_grad)
    project_run.land(*inner_run.landing())
    grad_tokens = input_grad(project_run.sent(), grad_one, stack_low, w_qkv)
    inner_run.land(*streamed(grad_tokens))
    project_run.land(*streamed(grad_tokens))
    inner_run.land()
    project_run.land(*inner_run.sent())
    project_run.land(*inner_run.landing())
    for run in (outer_run, inner_run, project_run):
        run.finish()
    low_left = ready(
        project_run.sent(), left_basis, LOW, head, per_owner - head, [low_left]
    )
    vec_grad, *parts = to_slots(
        streamed(low_left), (project_run, inner_run, outer_run),
        (0, 1, 2, 7, 3, 4, 5, 6, 8, 9, 10, 11), owner_list,
    )
    vec_grad = vec_grad.reshape(-1)
    gathered, masks = spread(parts)
    new_master, new_first, new_second, master_copy = rotated_adam(
        row_place(), gathered, masks, turn(master), turn(first_moment), turn(second_moment),
        low_left, right_basis,
    )
    vec_first_new = 0.9 * vec_first + 0.1 * vec_grad
    vec_second_new = 0.999 * vec_second + 0.001 * vec_grad * vec_grad
    vec_step = (
        vec_first_new / (1.0 - 0.9**STEP) / (jnp.sqrt(vec_second_new / (1.0 - 0.999**STEP)) + 1e-08)
    )
    vec_new = vectors - VECTOR_RATE * vec_step
    return (
        encoded,
        grad_tokens,
        loss[0, 0],
        new_master,
        new_first,
        new_second,
        master_copy,
        vec_new,
        vec_first_new,
        vec_second_new,
    )


def solution(mesh):
    in_specs = (
        P(("row", "col"), None),
        P(),
        P(),
        P(),
        P(),
        P(),
        P(("row", "col"), None),
        P(),
        P(),
        P(),
        P("col", None, None),
        P("col", None, None),
        P("col", None, None),
        P("col", None, None),
        P("col", None, None),
        P(),
        P(),
    )
    out_specs = (
        P(("row", "col"), None),
        P(("row", "col"), None),
        P(),
        P("col", None, None),
        P("col", None, None),
        P("col", None, None),
        P("col", None, None),
        P(),
        P(),
        P(),
    )
    return jax.shard_map(shards, mesh=mesh, in_specs=in_specs, out_specs=out_specs, check_vma=False)
```

```python
from functools import partial

import jax
import jax.numpy as jnp
from jax import lax
from jax.experimental import pallas as pl
from jax.experimental.pallas import tpu as pltpu
from jax.sharding import PartitionSpec as P

D = 768
HEADS = 12
HEAD = 64
FF = 3072
SPAN = 128
STEP = 10
GROUP = 8

RATE = 0.01
DECAY = 0.01
VECTOR_RATE = 0.3

LOW = jnp.bfloat16
F32 = jnp.float32
TALL = 2 * SPAN


def dot(left_side, right_side, contract=(1, 0)):
    dims = (((contract[0],), (contract[1],)), ((), ()))
    return lax.dot_general(left_side, right_side, dims, preferred_element_type=F32)


def whole(shape):
    return pl.BlockSpec(shape, lambda *ids: (0,) * len(shape))


def cost(microseconds, transcendentals=0):
    return pl.CostEstimate(
        flops=int(microseconds * 1.1e9), bytes_accessed=0, transcendentals=transcendentals
    )


def params(mebibytes=36):
    return pltpu.CompilerParams(vmem_limit_bytes=mebibytes * 1024 * 1024)


def row_of(rows, index):
    return rows[:, index * D : (index + 1) * D]


def live_rows(place, counts, first_row, height):
    at = first_row + lax.broadcasted_iota(jnp.int32, (height, 1), 0)
    return jnp.where(at < counts[place[0]] * SPAN, 1.0, 0.0)


near = pltpu.VMEM
far = pltpu.HBM


def streamed(*arrays):
    return [pltpu.with_memory_space_constraint(a, pltpu.HBM) for a in arrays]


ANY = pl.BlockSpec(memory_space=pl.ANY)
SMEM = pl.BlockSpec(memory_space=pltpu.SMEM)


def split_heads(pair):
    lane = lax.broadcasted_iota(jnp.int32, pair.shape, 1)
    zero = jnp.zeros_like(pair)
    return jnp.concatenate([jnp.where(lane < HEAD, pair, zero), jnp.where(lane < HEAD, zero, pair)])


def normalise(scores):
    peak = jnp.max(scores, axis=-1, keepdims=True)
    raised = jnp.exp(scores - peak)
    return raised * (1.0 / jnp.sum(raised, axis=-1, keepdims=True))


def attend_kernel(tokens, w_qkv, rows, q_out, k_out, v_out, p_out, a_out):
    block = tokens[...]
    scaling = HEAD ** (-0.5)
    q_out[...] = ((dot(block, w_qkv[0]) + row_of(rows, 4)).astype(LOW) * scaling).astype(LOW)
    k_out[...] = dot(block, w_qkv[1]).astype(LOW)
    v_out[...] = (dot(block, w_qkv[2]) + row_of(rows, 5)).astype(LOW)
    for span in range(TALL // SPAN):
        at = slice(span * SPAN, (span + 1) * SPAN)
        for pair in range(HEADS // 2):
            lanes = slice(pair * 2 * HEAD, (pair + 1) * 2 * HEAD)
            scores = dot(q_out[at, lanes], split_heads(k_out[at, lanes]), (1, 1))
            weights = jnp.concatenate(
                [normalise(scores[:, :SPAN]), normalise(scores[:, SPAN:])], axis=1
            ).astype(LOW)
            p_out[span, pair] = weights
            a_out[at, lanes] = dot(weights, split_heads(v_out[at, lanes])).astype(LOW)


def attend(tokens, w_qkv, rows):
    total = tokens.shape[0]
    tall = pl.BlockSpec((TALL, D), lambda i: (i, 0))
    like = far((total, D), LOW)
    tokens, w_qkv, rows = streamed(tokens, w_qkv, rows)
    spans = TALL // SPAN
    return pl.pallas_call(
        attend_kernel,
        grid=(total // TALL,),
        in_specs=[tall, whole(w_qkv.shape), whole(rows.shape)],
        out_specs=[
            tall,
            tall,
            tall,
            pl.BlockSpec((spans, HEADS // 2, SPAN, 2 * SPAN), lambda i: (i, 0, 0, 0)),
            tall,
        ],
        out_shape=[
            like,
            like,
            like,
            far((total // SPAN, HEADS // 2, SPAN, 2 * SPAN), LOW),
            near((total, D), LOW),
        ],
        compiler_params=params(),
        cost_estimate=cost(10),
        name="attend",
    )(tokens, w_qkv, rows)


def unit_norm(resid):
    centred = resid - jnp.mean(resid, axis=-1, keepdims=True)
    inverse = lax.rsqrt(jnp.mean(centred * centred, axis=-1, keepdims=True) + 1e-06)
    return centred * inverse, inverse


def gelu_pair(x):
    cdf = 0.5 + 0.5 * lax.erf(x * 0.7071067811865476)
    gauss = jnp.exp2(x * x * -0.7213475204444817)
    return x * cdf, cdf + x * gauss * 0.3989422804014327


def feed_kernel(
    place, counts, tokens, attended, w_attn, w_in, w_out, rows, bias,
    enc_out, hid_out, slope_out, norm_out, u1_out, i1_out, u2_out, i2_out, cls_out, total, firsts,
):
    band = pl.program_id(0)
    chunks = [slice(at, at + TALL) for at in range(0, tokens.shape[0], TALL)]

    @pl.when(band == 0)
    def _():
        for at in chunks:
            resid = tokens[at].astype(F32) + dot(attended[at], w_attn[...]) + row_of(rows, 6)
            unit_one, inverse_one = unit_norm(resid)
            value = unit_one * row_of(rows, 0) + row_of(rows, 2)
            u1_out[at] = unit_one.astype(LOW)
            i1_out[at] = inverse_one
            norm_out[at] = value.astype(LOW)
            total[at] = value + row_of(rows, 7)

    step = 256
    for at in range(0, hid_out.shape[1], step):
        here = slice(at, at + step)
        for rows_at in chunks:
            pre_act = dot(norm_out[rows_at], w_in[:, here]) + bias[:, here]
            hidden, slope = gelu_pair(pre_act)
            hid_out[rows_at, here] = hidden.astype(LOW)
            slope_out[rows_at, here] = slope.astype(LOW)

    @pl.when(band < pl.num_programs(0) - 1)
    def _():
        total[...] += dot(hid_out[...], w_out[...])

    @pl.when(band == pl.num_programs(0) - 1)
    def _():
        for at in chunks:
            resid = total[at] + dot(hid_out[at], w_out[...])
            unit_two, inverse_two = unit_norm(resid)
            u2_out[at] = unit_two.astype(LOW)
            i2_out[at] = inverse_two
            live = live_rows(place, counts, at.start, TALL)
            value = live * (unit_two * row_of(rows, 1) + row_of(rows, 3))
            enc_out[at] = value.astype(LOW)
            for first in range(at.start, at.stop, SPAN):
                row = first - at.start
                firsts[first // SPAN : first // SPAN + 1] = value[row : row + 1]
        firsts[tokens.shape[0] // SPAN :] = jnp.zeros((GROUP - tokens.shape[0] // SPAN, D), F32)
        cls_out[...] = firsts[...].astype(LOW)


def feed(place, counts, tokens, attended, w_attn, w_in, w_out, rows):
    total = tokens.shape[0]
    tall = lambda width: pl.BlockSpec((total, width), lambda j: (0, 0))
    band = lambda height: pl.BlockSpec((height, D), lambda j: (0, j))
    tokens, w_attn, w_in, w_out, rows = streamed(tokens, w_attn, w_in, w_out, rows)
    return pl.pallas_call(
        feed_kernel,
        grid=(FF // D,),
        in_specs=[
            SMEM, SMEM, tall(D), tall(D), whole(w_attn.shape), band(D),
            pl.BlockSpec((D, D), lambda j: (j, 0)),
            pl.BlockSpec((1, 8 * D), lambda j: (0, 0)),
            pl.BlockSpec((1, D), lambda j: (0, 8 + j)),
        ],
        out_specs=[
            tall(D), band(total), band(total), tall(D), tall(D), tall(1), tall(D), tall(1),
            whole((GROUP, D)),
        ],
        out_shape=[
            jax.ShapeDtypeStruct((total, D), LOW),
            far((total, FF), LOW),
            far((total, FF), LOW),
            far((total, D), LOW),
            far((total, D), LOW),
            far((total, 1), F32),
            near((total, D), LOW),
            near((total, 1), F32),
            jax.ShapeDtypeStruct((GROUP, D), LOW),
        ],
        scratch_shapes=[pltpu.VMEM((total, D), F32), pltpu.VMEM((GROUP, D), F32)],
        compiler_params=params(),
        cost_estimate=cost(20),
        name="feed",
    )(place, counts, tokens, attended, w_attn, w_in, w_out, rows, rows)


def norm_back(grad_out, unit_rows, inverse, gain):
    scaled = grad_out * gain
    along = jnp.mean(scaled * unit_rows, axis=-1, keepdims=True)
    return inverse * (scaled - jnp.mean(scaled, axis=-1, keepdims=True) - unit_rows * along)


def column_sums(*arrays):
    return [jnp.sum(a, axis=0, keepdims=True) for a in arrays]


def outer_kernel(place, counts, out_grad, grad_cls, unit_two, inverse_two, rows, two_out, low_out, vec_out):
    spot = lax.broadcasted_iota(jnp.int32, (SPAN, 1), 0) == 0
    sums = None
    for span in range(out_grad.shape[0] // SPAN):
        at = slice(span * SPAN, (span + 1) * SPAN)
        added = jnp.where(spot, grad_cls[span : span + 1], 0.0)
        live = live_rows(place, counts, span * SPAN, SPAN)
        grad_y = live * (out_grad[at].astype(F32) + added)
        unit_rows = unit_two[at].astype(F32)
        grad_two = norm_back(grad_y, unit_rows, inverse_two[at], row_of(rows, 1))
        two_out[at] = grad_two
        low_out[at] = grad_two.astype(LOW)
        here = column_sums(grad_y * unit_rows, grad_y, grad_two)
        sums = here if sums is None else [a + b for a, b in zip(sums, here)]
    for index, total in enumerate(sums):
        vec_out[index : index + 1] = total


def outer_grad(place, counts, out_grad, grad_cls, unit_two, inverse_two, rows):
    total = out_grad.shape[0]
    return pl.pallas_call(
        outer_kernel,
        in_specs=[SMEM, SMEM] + [pl.BlockSpec(memory_space=pltpu.VMEM)] * 5,
        out_shape=[
            jax.ShapeDtypeStruct((total, D), F32),
            jax.ShapeDtypeStruct((total, D), LOW),
            jax.ShapeDtypeStruct((3, D), F32),
        ],
        compiler_params=params(),
        cost_estimate=cost(5),
        name="outer",
    )(place, counts, out_grad, grad_cls, unit_two, inverse_two, rows)


def weight_kernel(panels, group, after, side, *refs):
    *sides, out = refs[after:]
    lefts, right, extra = sides[: len(sides) - 1], sides[-1], ()
    if panels:
        lefts, right, extra = sides[:1], sides[1], sides[2:]

    def main():
        for index in range(group):
            here = right[:, index * D : (index + 1) * D] if right.shape[1] > D else right[...]
            left = lefts[index if len(lefts) > 1 else 0]
            out[index] = dot(left[...], here, (0, 0)).astype(LOW)

    if not extra:
        main()
        return
    pl.when(pl.program_id(0) < panels)(main)

    @pl.when(pl.program_id(0) == panels)
    def _():
        out[0] = dot(extra[0][...], extra[1][...], (0, 0)).astype(LOW)


def weight_half(hint, after, side, left_side, right_side, panels, banded, group=1, extra=()):
    total = left_side.shape[0]
    half = D // 2
    every = panels + len(extra) // 2
    tall = lambda width, at: pl.BlockSpec((total, width), at)
    last = lambda step: jnp.minimum(step, panels // group - 1)
    if banded:
        lefts = [
            tall(half, lambda i, s, j=j: (0, (i * group + j) * 2 + s[0])) for j in range(group)
        ]
        right = tall(D, lambda i, s: (0, 0))
    else:
        lefts = [tall(half, lambda i, s: (0, s[0]))]
        right = tall(group * D, lambda i, s: (0, last(i)))
    more = [tall(half, lambda i, s: (0, s[0])), tall(D, lambda i, s: (0, 0))]
    return pl.pallas_call(
        partial(weight_kernel, panels if extra else 0, group, len(after)),
        grid_spec=pltpu.PrefetchScalarGridSpec(
            num_scalar_prefetch=1,
            grid=(every // group,),
            in_specs=[ANY] * len(after) + lefts + [right] + more[: len(extra)],
            out_specs=pl.BlockSpec((group, half, D), lambda i, s: (i, 0, 0)),
        ),
        out_shape=jax.ShapeDtypeStruct((every, half, D), LOW),
        compiler_params=params(24),
        cost_estimate=cost(hint),
        name="weight",
    )(side.reshape(1), *after, *[left_side] * len(lefts), right_side, *extra)


def inner_kernel(after, *refs):
    low, grad_two, slope, unit_one, inverse_one, w_attn, w_in, w_out, rows = refs[after:-6]
    pre_out, one_out, mixed_out, ga_out, vec_out, total = refs[-6:]
    band = pl.program_id(0)
    last = pl.num_programs(0) - 1
    step = 256
    for at in range(0, D, step):
        here = slice(at, at + step)
        grad_pre = dot(low[...], w_out[here], (1, 1)) * slope[:, here].astype(F32)
        pre_out[:, here] = grad_pre.astype(LOW)
        vec_out[pl.ds(3 + band, 1), here] = jnp.sum(grad_pre, axis=0, keepdims=True)

    @pl.when(band == 0)
    def _():
        total[...] = grad_two[...] + dot(pre_out[...], w_in[...], (1, 1))

    @pl.when((band > 0) & (band < last))
    def _():
        total[...] += dot(pre_out[...], w_in[...], (1, 1))

    @pl.when(band == last)
    def _():
        sums = None
        for first in range(0, low.shape[0], TALL):
            at = slice(first, first + TALL)
            grad_normed = total[at] + dot(pre_out[at], w_in[...], (1, 1))
            unit_rows = unit_one[at].astype(F32)
            grad_one = norm_back(grad_normed, unit_rows, inverse_one[at], row_of(rows, 0))
            one_out[at] = grad_one
            mixed = grad_one.astype(LOW)
            mixed_out[at] = mixed
            ga_out[at] = dot(mixed, w_attn[...], (1, 1)).astype(LOW)
            here = column_sums(grad_normed * unit_rows, grad_normed, grad_one)
            sums = here if sums is None else [a + b for a, b in zip(sums, here)]
        for index, value in enumerate(sums):
            vec_out[index : index + 1] = value


def inner_grad(after, low, grad_two, slope, unit_one, inverse_one, w_attn, w_in, w_out, rows):
    total = low.shape[0]
    bands = FF // D
    slope, w_attn, w_in, w_out, rows = streamed(slope, w_attn, w_in, w_out, rows)
    band = lambda height: pl.BlockSpec((height, D), lambda j: (0, j))
    return pl.pallas_call(
        partial(inner_kernel, len(after)),
        grid=(bands,),
        in_specs=[ANY] * len(after)
        + [
            whole(low.shape), whole(grad_two.shape), band(total), whole(unit_one.shape),
            whole(inverse_one.shape), whole(w_attn.shape), band(D),
            pl.BlockSpec((D, D), lambda j: (j, 0)), whole(rows.shape),
        ],
        out_specs=[band(total)] + [whole((total, D))] * 3 + [whole((3 + bands, D))],
        out_shape=[
            near((total, FF), LOW),
            far((total, D), F32),
            near((total, D), LOW),
            near((total, D), LOW),
            jax.ShapeDtypeStruct((3 + bands, D), F32),
        ],
        scratch_shapes=[pltpu.VMEM((total, D), F32)],
        compiler_params=params(),
        cost_estimate=cost(16),
        name="inner",
    )(*after, low, grad_two, slope, unit_one, inverse_one, w_attn, w_in, w_out, rows)


def unattend_kernel(after, sums, *refs):
    q, k, v, p, ga, attended = refs[after : after + 6]
    vec_one, vec_two, vec_early = refs[after + 6 : -2] if sums else (None, None, None)
    stack_out, vec_out = refs[-2:]
    scaling = HEAD ** (-0.5)
    first = pl.program_id(0) == 0

    @pl.when(first)
    def _():
        if not sums:
            vec_out[...] = jnp.zeros_like(vec_out)
            return
        for index in range(2):
            vec_out[2 * index : 2 * index + 1] = vec_one[index : index + 1]
            vec_out[2 * index + 1 : 2 * index + 2] = vec_two[index : index + 1]
        vec_out[4:6] = vec_early[...]
        vec_out[6:7] = vec_one[2:3]
        vec_out[7:8] = vec_two[2:3]
        vec_out[8:] = vec_one[3:]

    place = 4 if sums else 0
    head_of_row = lax.broadcasted_iota(jnp.int32, (2 * HEAD, 2 * SPAN), 0) // HEAD
    head_of_lane = lax.broadcasted_iota(jnp.int32, (2 * HEAD, 2 * SPAN), 1) // SPAN
    by_head = jnp.where(head_of_row == head_of_lane, 1.0, 0.0).astype(LOW)
    for span in range(p.shape[0]):
        at = slice(span * SPAN, (span + 1) * SPAN)
        for pair in range(HEADS // 2):
            lo = pair * 2 * HEAD
            lanes = slice(lo, lo + 2 * HEAD)
            weights = p[span, pair]
            grad = ga[at, lanes]
            spread_out = dot(grad, split_heads(v[at, lanes]), (1, 1))
            along = (grad.astype(F32) * attended[at, lanes].astype(F32)).astype(LOW)
            grad_scores = (weights.astype(F32) * (spread_out - dot(along, by_head))).astype(LOW)
            parts = [grad_scores[:, :SPAN], grad_scores[:, SPAN:]]
            grad_q = dot(grad_scores, split_heads(k[at, lanes])) * scaling
            tall_scores = jnp.concatenate(parts, axis=0)
            tall_weights = jnp.concatenate([weights[:, :SPAN], weights[:, SPAN:]], axis=0)
            grad_k = dot(tall_scores, split_heads(q[at, lanes]), (0, 0))
            grad_v = dot(tall_weights, split_heads(grad), (0, 0))
            stack_out[at, lo : lo + 2 * HEAD] = grad_q.astype(LOW)
            stack_out[at, D + lo : D + lo + 2 * HEAD] = grad_k.astype(LOW)
            stack_out[at, 2 * D + lo : 2 * D + lo + 2 * HEAD] = grad_v.astype(LOW)
            vec_out[place : place + 1, lanes] += jnp.sum(grad_q, axis=0, keepdims=True)
            vec_out[place + 1 : place + 2, lanes] += jnp.sum(grad_v, axis=0, keepdims=True)


def unattend(after, part, parts, q, k, v, p, ga, attended, stack=None, sums=()):
    total = q.shape[0]
    count = total // SPAN // parts
    first = part * count
    tall = lambda width: pl.BlockSpec((SPAN, width), lambda i: (first + i, 0))
    after = after if stack is None else [stack] + after
    vec_shape = (12, D) if sums else (2, D)
    return pl.pallas_call(
        partial(unattend_kernel, len(after), bool(sums)),
        grid=(count,),
        in_specs=[ANY] * len(after)
        + [tall(D)] * 3
        + [
            pl.BlockSpec((1, HEADS // 2, SPAN, 2 * SPAN), lambda i: (first + i, 0, 0, 0)),
            tall(D),
            tall(D),
        ]
        + [whole(a.shape) for a in sums],
        out_specs=[tall(3 * D), whole(vec_shape)],
        out_shape=[far((total, 3 * D), LOW), jax.ShapeDtypeStruct(vec_shape, F32)],
        input_output_aliases={} if stack is None else {0: 0},
        compiler_params=params(),
        cost_estimate=cost(8),
        name="unattend",
    )(*after, q, k, v, p, ga, attended, *sums)


def input_kernel(*refs):
    grad_one, stack, w_qkv, out = refs[-4:]
    total = grad_one[...]
    for index in range(3):
        total += dot(stack[:, index * D : (index + 1) * D], w_qkv[index], (1, 1))
    out[...] = total


def input_grad(after, grad_one, stack, w_qkv):
    total = grad_one.shape[0]
    tall = lambda width: pl.BlockSpec((TALL, width), lambda i: (i, 0))
    return pl.pallas_call(
        input_kernel,
        grid=(total // TALL,),
        in_specs=[ANY] * len(after) + [tall(D), tall(3 * D), whole(w_qkv.shape)],
        out_specs=tall(D),
        out_shape=jax.ShapeDtypeStruct((total, D), F32),
        compiler_params=params(),
        cost_estimate=cost(8),
        name="input",
    )(*after, grad_one, stack, w_qkv)


def contrast_kernel(slots, masks, place, rows, counts, partners, loss_out, grad_out):
    total, scale = rows.shape[0], 2.0 * D ** (-0.5)

    def number(shape, axis):
        at = lax.broadcasted_iota(jnp.int32, shape, axis)
        device, block = jnp.full(shape, place[0], jnp.int32), at // GROUP
        for bit, mask in enumerate(masks):
            device = device ^ (((block >> bit) & 1) * mask)
        return device, at % GROUP

    device, slot = number((counts.shape[1], total), 1)
    hit = lax.broadcasted_iota(jnp.int32, device.shape, 0) == device
    count = dot(counts[...].astype(LOW), jnp.where(hit, 1.0, 0.0).astype(LOW))
    live_across = (slot[:1].astype(F32) < count) & (slot[:1] < slots)
    device, slot = number((total, counts.shape[1]), 0)
    hit = lax.broadcasted_iota(jnp.int32, device.shape, 1) == device
    count = jnp.sum(jnp.where(hit, counts[...], 0.0), axis=1, keepdims=True)
    live_down = (slot[:, :1].astype(F32) < count) & (slot[:, :1] < slots)
    device, slot = number((total, partners.shape[1]), 0)
    own_id = device * slots + slot
    hit = lax.broadcasted_iota(jnp.int32, own_id.shape, 1) == own_id
    pair = jnp.sum(jnp.where(hit, partners[...], 0.0), axis=1, keepdims=True)
    device, slot = number((total, 128), 0)
    down = (device * slots + slot).astype(F32)[:, :1]
    device, slot = number((8, total), 1)
    across, slot = (device * slots + slot).astype(F32)[:1], slot[:1]
    valid = live_across & (down != across)
    matched = jnp.where((slot < slots) & (pair == across), 1.0, 0.0)
    anchor = jnp.where(live_down & (pair != down), 1.0, 0.0)
    similar = dot(rows[...], rows[...], (1, 1)) * scale
    masked = jnp.where(valid, similar, -1e30)
    peak = jnp.max(masked, axis=1, keepdims=True)
    summed = jnp.sum(jnp.where(valid, jnp.exp(masked - peak), 0.0), axis=1, keepdims=True)
    log_total = jnp.log(summed) + peak
    positive = jnp.sum(matched * similar, axis=1, keepdims=True)
    loss_out[...] = jnp.sum(anchor * (log_total - positive), axis=0, keepdims=True)
    grad = (anchor * (jnp.where(valid, jnp.exp(masked - log_total), 0.0) - matched)).astype(LOW)
    own = lax.broadcasted_iota(jnp.int32, (GROUP, total), 0)
    own = jnp.where(own == lax.broadcasted_iota(jnp.int32, (GROUP, total), 1), 1.0, 0.0)
    down_part = dot(dot(own.astype(LOW), grad, (1, 1)).astype(LOW), rows[...])
    grad_out[...] = (dot(grad[: 2 * GROUP], rows[...])[:GROUP] + down_part) * scale


def contrast(cls_rows, span_count, pair_index, device, slots):
    total = cls_rows.shape[0]
    scale = {"row": lax.axis_size("col"), "col": 1}
    masks = [scale[name] * bit for phase in gather_steps() for name, bit in phase]
    return pl.pallas_call(
        partial(contrast_kernel, slots, masks),
        in_specs=[pl.BlockSpec(memory_space=pltpu.SMEM)]
        + [pl.BlockSpec(memory_space=pltpu.VMEM)] * 3,
        out_shape=[
            jax.ShapeDtypeStruct((1, 1), F32),
            jax.ShapeDtypeStruct((GROUP, D), F32),
        ],
        compiler_params=params(),
        cost_estimate=cost(3),
        name="contrast",
    )(
        device,
        cls_rows,
        span_count.astype(F32).reshape(1, -1),
        pair_index.astype(F32).reshape(1, -1),
    )


def adam_kernel(
    masks, parts, position, *refs,
):
    gathered = refs[:parts]
    master, first, second, left, right, master_out, first_out, second_out, low_out, *scratch = refs[parts:]
    quarter = D // 4
    slot = pl.program_id(0)
    if masks:
        owned = scratch[0]
        shares, tall, _ = gathered[0].shape
        rows = D // len(masks)

        @pl.when(slot == 0)
        def _():
            for number, mask in enumerate(masks):
                block = gathered[number // shares][number % shares].astype(F32)
                at = pl.multiple_of((mask ^ position[0]) * rows, rows)
                for index in range(owned.shape[0]):
                    lo = index * rows % tall
                    side = index * rows // tall
                    piece = block[lo : lo + rows, side * quarter : (side + 1) * quarter]
                    owned[index, pl.ds(at, rows), :] = piece

    for here in range(master.shape[0]):
        if masks:
            gradient = owned[slot * master.shape[0] + here].astype(LOW)
        else:
            gradient = gathered[0][here]
        low_left, low_right = left[here], right[here].astype(LOW)
        turned = dot(gradient, low_left, (0, 0))
        turned = dot(low_right, turned.astype(LOW), (0, 0))
        new_first = 0.9 * first[here] + 0.1 * turned
        new_second = 0.999 * second[here] + 0.001 * turned * turned
        first_out[here] = new_first
        second_out[here] = new_second
        spread_by = jnp.sqrt(new_second * (1.0 / (1.0 - 0.999**STEP))) + 1e-08
        update = new_first * (1.0 / (1.0 - 0.9**STEP)) / spread_by
        update = dot(update.astype(LOW), low_left, (1, 1))
        update = dot(low_right, update.astype(LOW))
        new_master = master[here] - RATE * (update + DECAY * master[here])
        master_out[here] = new_master
        low_out[here] = new_master.astype(LOW)


def ready_kernel(*refs):
    source, out = refs[-2:]
    out[...] = source[...].astype(out.dtype)


def ready(after, array, kind, first, count, before=()):
    block = pl.BlockSpec((1,) + array.shape[1:], lambda s: (first + s, 0, 0))
    first_in = list(before) + list(after)
    return pl.pallas_call(
        ready_kernel,
        grid=(count,),
        in_specs=[ANY] * len(first_in) + [block],
        out_specs=block,
        out_shape=far(array.shape, kind),
        input_output_aliases={0: 0} if before else {},
        compiler_params=params(16),
        cost_estimate=cost(1.5 * count),
        name="ready",
    )(*first_in, *streamed(array))


def to_owned(gathered, masks, position, per_owner):
    quarter = D // 4
    places = jnp.array(masks, jnp.int32) ^ position
    gathered = jnp.zeros_like(gathered).at[places].set(gathered)
    flat = jnp.concatenate([gathered[..., :quarter], gathered[..., quarter:]], axis=1)
    rows = flat.shape[1] // per_owner
    flat = flat.reshape(flat.shape[0], per_owner, rows, quarter).transpose(1, 0, 2, 3)
    return flat.reshape(per_owner, D, quarter)


def turn(array):
    return array.transpose(0, 2, 1)


def rotated_adam(position, gathered, masks, master, first_moment, second_moment, left_basis, right_basis):
    per_owner, quarter, _ = master.shape
    if D // len(masks) % 8 or per_owner % 2:
        gathered = [to_owned(jnp.concatenate(gathered), masks, position, per_owner)]
        masks = []
    at_once = max(n for n in (1, 2, 3) if per_owner % n == 0)
    block = lambda a: pl.BlockSpec((at_once,) + a.shape[1:], lambda s, p: (s, 0, 0))
    operands = streamed(master, first_moment, second_moment, left_basis, right_basis)
    like = jax.ShapeDtypeStruct(operands[0].shape, F32)
    fixed = pl.BlockSpec(gathered[0].shape, lambda s, p: (0, 0, 0))
    outputs = pl.pallas_call(
        partial(adam_kernel, masks, len(gathered)),
        grid_spec=pltpu.PrefetchScalarGridSpec(
            num_scalar_prefetch=1,
            grid=(per_owner // at_once,),
            in_specs=[fixed if masks else block(part) for part in gathered]
            + [block(a) for a in operands],
            out_specs=[block(operands[0])] * 4,
            scratch_shapes=[pltpu.VMEM((per_owner, D, quarter), F32)] if masks else [],
        ),
        out_shape=[like, like, like, jax.ShapeDtypeStruct(like.shape, LOW)],
        compiler_params=params(48),
        cost_estimate=cost(20),
        name="adam",
    )(position.reshape(1), *gathered, *operands)
    return [turn(a) for a in outputs]


def axis_bits(name):
    size = lax.axis_size(name)
    return [(name, 1 << k) for k in range(size.bit_length() - 1)]


def bit_of(step):
    return jnp.where((lax.axis_index(step[0]) & step[1]) != 0, 1, 0)


def swap(send, step):
    size = lax.axis_size(step[0])
    return lax.ppermute(send, step[0], [(i, i ^ step[1]) for i in range(size)])


def gather_steps():
    core, across, y_bits, z_bits = row_steps()
    return [z_bits[::-1], y_bits + across, core]


def gather_all(rows, beside):
    columns = lax.axis_size("col")
    every = lax.axis_size("row") * columns
    scale = {"row": columns, "col": 1}
    for phase in gather_steps():
        arrived = []
        for number in range(1, 1 << len(phase)):
            mask = sum(scale[name] * bit for j, (name, bit) in enumerate(phase) if number >> j & 1)
            pairs = [(i, i ^ mask) for i in range(every)]
            arrived.append(lax.ppermute(rows, ("row", "col"), pairs))
        if beside:
            rows = merge(beside, [rows] + arrived).reshape(-1, D)
            beside = []
        else:
            rows = jnp.concatenate([rows] + arrived)
    return rows


def row_steps():
    row_bits, col_bits = axis_bits("row"), axis_bits("col")
    core, across = row_bits[:1], row_bits[1:][::-1]
    y_bits, z_bits = col_bits[:-2][::-1], col_bits[-2:]
    return core, across, y_bits, z_bits


def pack_rider(rider, rows, width):
    parts = [rider[:, at : at + width] for at in range(0, D, width)]
    tall = rider.shape[0]
    if rows < tall:
        return [part[at : at + rows] for part in parts for at in range(0, tall, rows)]
    fold = rows // tall
    parts += parts[-1:] * (-len(parts) % fold)
    return [jnp.concatenate(parts[at : at + fold]) for at in range(0, len(parts), fold)]


def unpack_rider(blocks, tall):
    rows, width = blocks[0].shape
    if rows < tall:
        fold = tall // rows
        parts = [jnp.concatenate(blocks[at : at + fold]) for at in range(0, len(blocks), fold)]
    else:
        parts = [block[at : at + tall] for block in blocks for at in range(0, rows, tall)]
    parts = parts[: D // width]
    return parts[0] if len(parts) == 1 else jnp.concatenate(parts, axis=1)


def rider_blocks(rows, width, tall=12):
    return -(-tall * D // (rows * width))


def land_kernel(after, outs, rider, bits, *refs):
    refs = refs[after:]
    sides = len({source[0] for out in outs for source in out[3]})
    keeps, others = refs[0 : 2 * sides : 2], refs[1 : 2 * sides : 2]
    results = refs[2 * sides + (0 if rider is None else 1 + (rider == "array")) :]
    if rider is not None:
        total = refs[2 * sides][...]
        tall = total.shape[0]
        if rider == "array":
            total += refs[2 * sides + 1][...]
        else:
            blocks = [others[0][at].astype(F32) for at in range(keeps[0].shape[0], others[0].shape[0])]
            total += unpack_rider(blocks, tall)
        results[-1][...] = total
    for number, (at_bit, before, behind, sources) in enumerate(outs):
        bit = bits[at_bit]
        for which, target in enumerate(results[2 * number : 2 * number + 2]):
            half = bit if which else 1 - bit
            for at in range(before):
                here = pl.ds((2 * at + half) * behind, behind)
                there = slice(at * behind, (at + 1) * behind)
                for side, lanes, into in sources:
                    target[there, :, into] = keeps[side][here, :, lanes] + others[side][here, :, lanes]
        if rider is not None and number == 0:
            away = results[0]
            count, rows, width = away.shape
            blocks = pack_rider(total, rows, width)
            for index, block in enumerate(blocks):
                away[count - len(blocks) + index] = block.astype(LOW)


class Reduction:
    def __init__(self, bits, ways, send, keep, rider=None):
        core, across, y_bits, z_bits = row_steps()
        self.bits, self.order = bits, core + across + y_bits + z_bits
        left = across + y_bits + z_bits
        self.panels, height, _ = keep.shape
        self.rows = height >> len(left)
        other = swap(send, core[0])
        self.rider = None if rider is None else (rider, swap(rider, core[0]))
        split = lambda a: a.reshape(-1, self.rows, D)
        self.sides = [(split(keep), split(other), left)]
        cycle = [across, y_bits, z_bits[:1]][:ways]
        orders = [sum(cycle[at:] + cycle[:at], []) for at in range(ways)]
        self.stages = list(zip(*orders)) + [(step,) for step in z_bits[ways - 2 :]]
        self.ways = ways
        self.messages = []

    def sent(self):
        return self.messages

    def landing(self):
        return [side[1] for side in self.sides]

    def land(self, *after):
        stage = self.stages.pop(0)
        outs, shapes, lefts = [], [], []
        part = D // self.ways
        lanes = [slice(at, at + part) for at in range(0, D, part)]
        for index, step in enumerate(stage):
            if len(self.sides) == len(stage):
                width = self.sides[index][0].shape[2]
                sources = [(index, slice(0, width), slice(0, width))]
                left = self.sides[index][2]
            elif len(stage) > 1:
                width, left = part, self.sides[0][2]
                sources = [(0, lanes[index], slice(0, part))]
            else:
                width, left = D, self.sides[0][2]
                sources = [(side, slice(0, part), lanes[side]) for side in range(self.ways)]
            dim = left.index(step)
            behind = 1 << (len(left) - dim - 1)
            before = self.panels << dim
            outs.append((self.order.index(step), before, behind, sources))
            extra = rider_blocks(self.rows, width) if self.rider and index == 0 else 0
            shapes += [(before * behind + extra, self.rows, width), (before * behind, self.rows, width)]
            lefts.append([other for other in left if other != step])
        rider = None if self.rider is None else ("array" if len(self.rider) == 2 else "message")
        inputs = [a for keep, other, _ in self.sides for a in (keep, other)] + list(self.rider or ())
        out_shape = [jax.ShapeDtypeStruct(shape, LOW) for shape in shapes]
        if rider:
            out_shape.append(jax.ShapeDtypeStruct(self.rider[0].shape, F32))
        results = pl.pallas_call(
            partial(land_kernel, len(after), outs, rider),
            in_specs=[SMEM] + [ANY] * len(after) + [pl.BlockSpec(memory_space=pltpu.VMEM)] * len(inputs),
            out_shape=out_shape,
            compiler_params=params(24),
            cost_estimate=cost(2),
            name="land",
        )(self.bits, *after, *inputs)
        if rider:
            self.rider = (results[-1],)
        self.messages = list(results[0 : 2 * len(stage) : 2])
        keeps = results[1 : 2 * len(stage) : 2]
        self.sides = [
            (keep, swap(message, step), left)
            for keep, message, step, left in zip(keeps, self.messages, stage, lefts)
        ]

    def finish(self):
        while self.stages:
            self.land()


def slots_kernel(after, cols, panels, column, owners, *refs):
    refs = refs[after:]
    sums, rider, rider_out = refs[:6], refs[6], refs[7]
    targets, blocks, packed = refs[8:-2], refs[-2], refs[-1]
    quarter = D // 4
    found = [(sums[2 * run], sums[2 * run + 1], i) for run in range(3) for i in range(sums[2 * run].shape[0])]
    at = 0
    for panel in panels:
        keep, other, index = found[panel]
        value = keep[index].astype(F32) + other[index].astype(F32)
        for part in range(4):
            blocks[at] = value[:, part * quarter : (part + 1) * quarter]
            at += 1
    tail = [sums[1][index].astype(F32) for index in range(sums[0].shape[0], sums[1].shape[0])]
    rider_out[...] = rider[...] + unpack_rider(tail, rider.shape[0])
    rows, half = blocks.shape[1], packed.shape[1]
    for slot in range(at):
        col, place = divmod(slot, at // cols)
        value = blocks[owners[slot]]
        first = place * rows
        for side in range(2):
            lo, hi = max(first, side * half), min(first + rows, (side + 1) * half)
            if lo < hi:
                lanes = slice(side * quarter, (side + 1) * quarter)
                packed[col, lo - side * half : hi - side * half, lanes] = value[lo - first : hi - first]
    for number, target in enumerate(targets):
        target[...] = packed[column[0] ^ number].astype(LOW)


def to_slots(after, runs, panels, owner_list):
    quarter, cols = D // 4, lax.axis_size("col")
    arrays = [a for run in runs for a in run.sides[0][:2]]
    rows = runs[0].rows
    shape = (len(panels) * 4 // cols * rows // 2, 2 * quarter)
    rider = runs[0].rider[0]
    return pl.pallas_call(
        partial(slots_kernel, len(after), cols, panels),
        in_specs=[SMEM, SMEM] + [ANY] * len(after) + [pl.BlockSpec(memory_space=pltpu.VMEM)] * 7,
        out_shape=[jax.ShapeDtypeStruct(rider.shape, F32)] + [jax.ShapeDtypeStruct(shape, LOW)] * cols,
        scratch_shapes=[
            pltpu.VMEM((len(panels) * 4, rows, quarter), F32),
            pltpu.VMEM((cols,) + shape, F32),
        ],
        compiler_params=params(24),
        cost_estimate=cost(4),
        name="slots",
    )(lax.axis_index("col").reshape(1), owner_list, *after, *arrays, rider)


def merge_kernel(after, *refs):
    *sources, target = refs[after:]
    for number, source in enumerate(sources):
        target[number] = source[...]


def merge(after, arrays):
    return pl.pallas_call(
        partial(merge_kernel, len(after)),
        in_specs=[ANY] * len(after) + [pl.BlockSpec(memory_space=pltpu.VMEM)] * len(arrays),
        out_shape=jax.ShapeDtypeStruct((len(arrays),) + arrays[0].shape, arrays[0].dtype),
        compiler_params=params(24),
        cost_estimate=cost(1),
        name="merge",
    )(*after, *arrays)


def spread(parts):
    core, across, y_bits, z_bits = row_steps()
    order = core + across + y_bits + z_bits
    weight = lambda step: 1 << (len(order) - 1 - order.index(step))
    cols, bits = len(parts), axis_bits("col")
    sent = lambda number: lax.ppermute(parts[number], "col", [(i, i ^ number) for i in range(cols)])
    arrived = [parts[0]] + [sent(number) for number in range(1, cols)]
    masks = [sum(weight(step) for step in bits if number & step[1]) for number in range(cols)]
    near = merge([], arrived[: cols // 2])
    first, *rest = (core + across)[::-1]
    moved = swap(near, first)
    far = merge([], arrived[cols // 2 :])
    shares = [near, far, moved, swap(far, first)]
    masks = masks + [mask ^ weight(first) for mask in masks]
    for step in rest:
        shares = shares + [swap(share, step) for share in shares]
        masks = masks + [mask ^ weight(step) for mask in masks]
    return shares, masks


def row_place():
    place = 0
    for group in row_steps():
        for step in group:
            place = place * 2 + bit_of(step)
    return place


def shards(
    tokens,
    w_qkv,
    w_attn_out,
    w_in,
    w_out,
    vectors,
    out_grad,
    span_count,
    pair_index,
    owner_list,
    master,
    first_moment,
    second_moment,
    left_basis,
    right_basis,
    vec_first,
    vec_second,
):
    slots = tokens.shape[0] // SPAN
    device = (lax.axis_index("row") * lax.axis_size("col") + lax.axis_index("col")).reshape(1)
    core, across, y_bits, z_bits = row_steps()
    core_bit = bit_of(core[0])
    bits = jnp.stack([bit_of(step) for step in core + across + y_bits + z_bits])
    rows = vectors.reshape(1, -1)
    q, k, v, p, attended = attend(tokens, w_qkv, rows)
    encoded, hidden, slope, normed_low, unit_one, inverse_one, unit_two, inverse_two, cls_rows = (
        feed(device, span_count, tokens, attended, w_attn_out, w_in, w_out, rows)
    )
    per_owner = left_basis.shape[0]
    head = per_owner // 3
    low_left = ready([cls_rows], left_basis, LOW, 0, head)
    every_cls = gather_all(cls_rows, streamed(low_left))
    loss, grad_cls = contrast(every_cls, span_count, pair_index, device, slots)
    grad_two, outer_low, vec_two = outer_grad(
        device, span_count, out_grad, grad_cls, unit_two, inverse_two, rows
    )
    outer_args = (hidden, outer_low, FF // D, True, 4)
    outer_away = weight_half(8, [], 1 - core_bit, *outer_args)
    outer_here = weight_half(60, [outer_away], core_bit, *outer_args)
    outer_run = Reduction(bits, 2, outer_away, outer_here)
    outer_run.land()
    pre_low, grad_one, mixed_low, grad_attended, vec_one = inner_grad(
        outer_run.sent(), outer_low, grad_two, slope, unit_one, inverse_one,
        w_attn_out, w_in, w_out, rows,
    )
    outer_run.land(vec_one)
    inner_args = (normed_low, pre_low, FF // D, False, 1, (attended, mixed_low))
    inner_away = weight_half(8, outer_run.sent(), 1 - core_bit, *inner_args)
    outer_run.land(inner_away)
    inner_here = weight_half(60, [inner_away] + outer_run.sent(), core_bit, *inner_args)
    outer_run.land(inner_here)
    inner_run = Reduction(bits, 3, inner_away, inner_here)
    inner_run.land()
    early, vec_early = unattend(
        outer_run.sent() + inner_run.sent(), 0, 2, q, k, v, p, grad_attended, attended
    )
    stack_low, vec_grad = unattend(
        [], 1, 2, q, k, v, p, grad_attended, attended, early, (vec_one, vec_two, vec_early)
    )
    inner_run.land(vec_grad)
    project_args = (tokens, stack_low, 3, False, 3)
    project_away = weight_half(
        8, inner_run.sent() + outer_run.landing(), 1 - core_bit, *project_args
    )
    project_here = weight_half(60, [project_away], core_bit, *project_args)
    project_run = Reduction(bits, 3, project_away, project_here, vec_grad)
    project_run.land(*inner_run.landing())
    grad_tokens = input_grad(project_run.sent(), grad_one, stack_low, w_qkv)
    inner_run.land(*streamed(grad_tokens))
    project_run.land(*streamed(grad_tokens))
    inner_run.land()
    project_run.land(*inner_run.sent())
    project_run.land(*inner_run.landing())
    for run in (outer_run, inner_run, project_run):
        run.finish()
    low_left = ready(
        project_run.sent(), left_basis, LOW, head, per_owner - head, [low_left]
    )
    vec_grad, *parts = to_slots(
        streamed(low_left), (project_run, inner_run, outer_run),
        (0, 1, 2, 7, 3, 4, 5, 6, 8, 9, 10, 11), owner_list,
    )
    vec_grad = vec_grad.reshape(-1)
    gathered, masks = spread(parts)
    new_master, new_first, new_second, master_copy = rotated_adam(
        row_place(), gathered, masks, turn(master), turn(first_moment), turn(second_moment),
        low_left, right_basis,
    )
    vec_first_new = 0.9 * vec_first + 0.1 * vec_grad
    vec_second_new = 0.999 * vec_second + 0.001 * vec_grad * vec_grad
    vec_step = (
        vec_first_new / (1.0 - 0.9**STEP) / (jnp.sqrt(vec_second_new / (1.0 - 0.999**STEP)) + 1e-08)
    )
    vec_new = vectors - VECTOR_RATE * vec_step
    return (
        encoded,
        grad_tokens,
        loss[0, 0],
        new_master,
        new_first,
        new_second,
        master_copy,
        vec_new,
        vec_first_new,
        vec_second_new,
    )


def solution(mesh):
    in_specs = (
        P(("row", "col"), None),
        P(),
        P(),
        P(),
        P(),
        P(),
        P(("row", "col"), None),
        P(),
        P(),
        P(),
        P("col", None, None),
        P("col", None, None),
        P("col", None, None),
        P("col", None, None),
        P("col", None, None),
        P(),
        P(),
    )
    out_specs = (
        P(("row", "col"), None),
        P(("row", "col"), None),
        P(),
        P("col", None, None),
        P("col", None, None),
        P("col", None, None),
        P("col", None, None),
        P(),
        P(),
        P(),
    )
    return jax.shard_map(shards, mesh=mesh, in_specs=in_specs, out_specs=out_specs, check_vma=False)
```

```python
from functools import partial

import jax
import jax.numpy as jnp
from jax import lax
from jax.experimental import pallas as pl
from jax.experimental.pallas import tpu as pltpu
from jax.sharding import PartitionSpec as P

D = 768
HEADS = 12
HEAD = 64
FF = 3072
SPAN = 128
STEP = 10
GROUP = 8

RATE = 0.01
DECAY = 0.01
VECTOR_RATE = 0.3

LOW = jnp.bfloat16
F32 = jnp.float32
TALL = 2 * SPAN


def dot(left_side, right_side, contract=(1, 0)):
    dims = (((contract[0],), (contract[1],)), ((), ()))
    return lax.dot_general(left_side, right_side, dims, preferred_element_type=F32)


def whole(shape):
    return pl.BlockSpec(shape, lambda *ids: (0,) * len(shape))


def cost(microseconds, transcendentals=0):
    return pl.CostEstimate(
        flops=int(microseconds * 1.1e9), bytes_accessed=0, transcendentals=transcendentals
    )


def params(mebibytes=36):
    return pltpu.CompilerParams(vmem_limit_bytes=mebibytes * 1024 * 1024)


def row_of(rows, index):
    return rows[:, index * D : (index + 1) * D]


def live_rows(place, counts, first_row, height):
    at = first_row + lax.broadcasted_iota(jnp.int32, (height, 1), 0)
    return jnp.where(at < counts[place[0]] * SPAN, 1.0, 0.0)


near = pltpu.VMEM
far = pltpu.HBM


def streamed(*arrays):
    return [pltpu.with_memory_space_constraint(a, pltpu.HBM) for a in arrays]


ANY = pl.BlockSpec(memory_space=pl.ANY)
SMEM = pl.BlockSpec(memory_space=pltpu.SMEM)


def split_heads(pair):
    lane = lax.broadcasted_iota(jnp.int32, pair.shape, 1)
    zero = jnp.zeros_like(pair)
    return jnp.concatenate([jnp.where(lane < HEAD, pair, zero), jnp.where(lane < HEAD, zero, pair)])


def normalise(scores):
    peak = jnp.max(scores, axis=-1, keepdims=True)
    raised = jnp.exp(scores - peak)
    return raised * (1.0 / jnp.sum(raised, axis=-1, keepdims=True))


def attend_kernel(tokens, w_qkv, rows, q_out, k_out, v_out, p_out, a_out):
    block = tokens[...]
    scaling = HEAD ** (-0.5)
    q_out[...] = ((dot(block, w_qkv[0]) + row_of(rows, 4)).astype(LOW) * scaling).astype(LOW)
    k_out[...] = dot(block, w_qkv[1]).astype(LOW)
    v_out[...] = (dot(block, w_qkv[2]) + row_of(rows, 5)).astype(LOW)
    for span in range(TALL // SPAN):
        at = slice(span * SPAN, (span + 1) * SPAN)
        for pair in range(HEADS // 2):
            lanes = slice(pair * 2 * HEAD, (pair + 1) * 2 * HEAD)
            scores = dot(q_out[at, lanes], split_heads(k_out[at, lanes]), (1, 1))
            weights = jnp.concatenate(
                [normalise(scores[:, :SPAN]), normalise(scores[:, SPAN:])], axis=1
            ).astype(LOW)
            p_out[span, pair] = weights
            a_out[at, lanes] = dot(weights, split_heads(v_out[at, lanes])).astype(LOW)


def attend(tokens, w_qkv, rows):
    total = tokens.shape[0]
    tall = pl.BlockSpec((TALL, D), lambda i: (i, 0))
    like = far((total, D), LOW)
    tokens, w_qkv, rows = streamed(tokens, w_qkv, rows)
    spans = TALL // SPAN
    return pl.pallas_call(
        attend_kernel,
        grid=(total // TALL,),
        in_specs=[tall, whole(w_qkv.shape), whole(rows.shape)],
        out_specs=[
            tall,
            tall,
            tall,
            pl.BlockSpec((spans, HEADS // 2, SPAN, 2 * SPAN), lambda i: (i, 0, 0, 0)),
            tall,
        ],
        out_shape=[
            like,
            like,
            like,
            far((total // SPAN, HEADS // 2, SPAN, 2 * SPAN), LOW),
            near((total, D), LOW),
        ],
        compiler_params=params(),
        cost_estimate=cost(10),
        name="attend",
    )(tokens, w_qkv, rows)


def unit_norm(resid):
    centred = resid - jnp.mean(resid, axis=-1, keepdims=True)
    inverse = lax.rsqrt(jnp.mean(centred * centred, axis=-1, keepdims=True) + 1e-06)
    return centred * inverse, inverse


def gelu_pair(x):
    cdf = 0.5 + 0.5 * lax.erf(x * 0.7071067811865476)
    gauss = jnp.exp2(x * x * -0.7213475204444817)
    return x * cdf, cdf + x * gauss * 0.3989422804014327


def feed_kernel(
    place, counts, tokens, attended, w_attn, w_in, w_out, rows, bias,
    enc_out, hid_out, slope_out, norm_out, u1_out, i1_out, u2_out, i2_out, cls_out, total, firsts,
):
    band = pl.program_id(0)
    chunks = [slice(at, at + TALL) for at in range(0, tokens.shape[0], TALL)]

    @pl.when(band == 0)
    def _():
        for at in chunks:
            resid = tokens[at].astype(F32) + dot(attended[at], w_attn[...]) + row_of(rows, 6)
            unit_one, inverse_one = unit_norm(resid)
            value = unit_one * row_of(rows, 0) + row_of(rows, 2)
            u1_out[at] = unit_one.astype(LOW)
            i1_out[at] = inverse_one
            norm_out[at] = value.astype(LOW)
            total[at] = value + row_of(rows, 7)

    step = 256
    for at in range(0, hid_out.shape[1], step):
        here = slice(at, at + step)
        pre_act = dot(norm_out[...], w_in[:, here]) + bias[:, here]
        hidden, slope = gelu_pair(pre_act)
        hid_out[:, here] = hidden.astype(LOW)
        slope_out[:, here] = slope.astype(LOW)

    @pl.when(band < pl.num_programs(0) - 1)
    def _():
        total[...] += dot(hid_out[...], w_out[...])

    @pl.when(band == pl.num_programs(0) - 1)
    def _():
        for at in chunks:
            resid = total[at] + dot(hid_out[at], w_out[...])
            unit_two, inverse_two = unit_norm(resid)
            u2_out[at] = unit_two.astype(LOW)
            i2_out[at] = inverse_two
            live = live_rows(place, counts, at.start, TALL)
            value = live * (unit_two * row_of(rows, 1) + row_of(rows, 3))
            enc_out[at] = value.astype(LOW)
            for first in range(at.start, at.stop, SPAN):
                row = first - at.start
                firsts[first // SPAN : first // SPAN + 1] = value[row : row + 1]
        firsts[tokens.shape[0] // SPAN :] = jnp.zeros((GROUP - tokens.shape[0] // SPAN, D), F32)
        cls_out[...] = firsts[...].astype(LOW)


def feed(place, counts, tokens, attended, w_attn, w_in, w_out, rows):
    total = tokens.shape[0]
    tall = lambda width: pl.BlockSpec((total, width), lambda j: (0, 0))
    band = lambda height: pl.BlockSpec((height, D), lambda j: (0, j))
    tokens, w_attn, w_in, w_out, rows = streamed(tokens, w_attn, w_in, w_out, rows)
    return pl.pallas_call(
        feed_kernel,
        grid=(FF // D,),
        in_specs=[
            SMEM, SMEM, tall(D), tall(D), whole(w_attn.shape), band(D),
            pl.BlockSpec((D, D), lambda j: (j, 0)),
            pl.BlockSpec((1, 8 * D), lambda j: (0, 0)),
            pl.BlockSpec((1, D), lambda j: (0, 8 + j)),
        ],
        out_specs=[
            tall(D), band(total), band(total), tall(D), tall(D), tall(1), tall(D), tall(1),
            whole((GROUP, D)),
        ],
        out_shape=[
            jax.ShapeDtypeStruct((total, D), LOW),
            far((total, FF), LOW),
            far((total, FF), LOW),
            far((total, D), LOW),
            far((total, D), LOW),
            far((total, 1), F32),
            near((total, D), LOW),
            near((total, 1), F32),
            jax.ShapeDtypeStruct((GROUP, D), LOW),
        ],
        scratch_shapes=[pltpu.VMEM((total, D), F32), pltpu.VMEM((GROUP, D), F32)],
        compiler_params=params(),
        cost_estimate=cost(20),
        name="feed",
    )(place, counts, tokens, attended, w_attn, w_in, w_out, rows, rows)


def norm_back(grad_out, unit_rows, inverse, gain):
    scaled = grad_out * gain
    along = jnp.mean(scaled * unit_rows, axis=-1, keepdims=True)
    return inverse * (scaled - jnp.mean(scaled, axis=-1, keepdims=True) - unit_rows * along)


def column_sums(*arrays):
    return [jnp.sum(a, axis=0, keepdims=True) for a in arrays]


def outer_kernel(place, counts, out_grad, grad_cls, unit_two, inverse_two, rows, two_out, low_out, vec_out):
    spot = lax.broadcasted_iota(jnp.int32, (SPAN, 1), 0) == 0
    sums = None
    for span in range(out_grad.shape[0] // SPAN):
        at = slice(span * SPAN, (span + 1) * SPAN)
        added = jnp.where(spot, grad_cls[span : span + 1], 0.0)
        live = live_rows(place, counts, span * SPAN, SPAN)
        grad_y = live * (out_grad[at].astype(F32) + added)
        unit_rows = unit_two[at].astype(F32)
        grad_two = norm_back(grad_y, unit_rows, inverse_two[at], row_of(rows, 1))
        two_out[at] = grad_two
        low_out[at] = grad_two.astype(LOW)
        here = column_sums(grad_y * unit_rows, grad_y, grad_two)
        sums = here if sums is None else [a + b for a, b in zip(sums, here)]
    for index, total in enumerate(sums):
        vec_out[index : index + 1] = total


def outer_grad(place, counts, out_grad, grad_cls, unit_two, inverse_two, rows):
    total = out_grad.shape[0]
    return pl.pallas_call(
        outer_kernel,
        in_specs=[SMEM, SMEM] + [pl.BlockSpec(memory_space=pltpu.VMEM)] * 5,
        out_shape=[
            jax.ShapeDtypeStruct((total, D), F32),
            jax.ShapeDtypeStruct((total, D), LOW),
            jax.ShapeDtypeStruct((3, D), F32),
        ],
        compiler_params=params(),
        cost_estimate=cost(5),
        name="outer",
    )(place, counts, out_grad, grad_cls, unit_two, inverse_two, rows)


def weight_kernel(panels, after, side, *refs):
    *sides, out = refs[after:]

    @pl.when(pl.program_id(0) < panels)
    def _():
        out[0] = dot(sides[0][...], sides[1][...], (0, 0)).astype(LOW)

    if len(sides) > 2:

        @pl.when(pl.program_id(0) == panels)
        def _():
            out[0] = dot(sides[2][...], sides[3][...], (0, 0)).astype(LOW)


def weight_half(hint, after, side, left_side, right_side, panels, banded, extra=()):
    total = left_side.shape[0]
    half = D // 2
    every = panels + len(extra) // 2
    tall = lambda width, at: pl.BlockSpec((total, width), at)
    last = lambda panel: jnp.minimum(panel, panels - 1)
    left_at = lambda panel, side: (0, last(panel) * 2 + side[0] if banded else side[0])
    right_at = lambda panel, side: (0, 0 if banded else last(panel))
    more = [tall(half, lambda p, s: (0, s[0])), tall(D, lambda p, s: (0, 0))]
    return pl.pallas_call(
        partial(weight_kernel, panels, len(after)),
        grid_spec=pltpu.PrefetchScalarGridSpec(
            num_scalar_prefetch=1,
            grid=(every,),
            in_specs=[ANY] * len(after)
            + [tall(half, left_at), tall(D, right_at)]
            + more[: len(extra)],
            out_specs=pl.BlockSpec((1, half, D), lambda p, s: (p, 0, 0)),
        ),
        out_shape=jax.ShapeDtypeStruct((every, half, D), LOW),
        compiler_params=params(),
        cost_estimate=cost(hint),
        name="weight",
    )(side.reshape(1), *after, left_side, right_side, *extra)


def inner_kernel(after, *refs):
    low, grad_two, slope, unit_one, inverse_one, w_attn, w_in, w_out, rows = refs[after:-6]
    pre_out, one_out, mixed_out, ga_out, vec_out, total = refs[-6:]
    band = pl.program_id(0)
    last = pl.num_programs(0) - 1
    step = 256
    for at in range(0, D, step):
        here = slice(at, at + step)
        grad_pre = dot(low[...], w_out[here], (1, 1)) * slope[:, here].astype(F32)
        pre_out[:, here] = grad_pre.astype(LOW)
        vec_out[pl.ds(3 + band, 1), here] = jnp.sum(grad_pre, axis=0, keepdims=True)

    @pl.when(band == 0)
    def _():
        total[...] = grad_two[...] + dot(pre_out[...], w_in[...], (1, 1))

    @pl.when((band > 0) & (band < last))
    def _():
        total[...] += dot(pre_out[...], w_in[...], (1, 1))

    @pl.when(band == last)
    def _():
        sums = None
        for first in range(0, low.shape[0], TALL):
            at = slice(first, first + TALL)
            grad_normed = total[at] + dot(pre_out[at], w_in[...], (1, 1))
            unit_rows = unit_one[at].astype(F32)
            grad_one = norm_back(grad_normed, unit_rows, inverse_one[at], row_of(rows, 0))
            one_out[at] = grad_one
            mixed = grad_one.astype(LOW)
            mixed_out[at] = mixed
            ga_out[at] = dot(mixed, w_attn[...], (1, 1)).astype(LOW)
            here = column_sums(grad_normed * unit_rows, grad_normed, grad_one)
            sums = here if sums is None else [a + b for a, b in zip(sums, here)]
        for index, value in enumerate(sums):
            vec_out[index : index + 1] = value


def inner_grad(after, low, grad_two, slope, unit_one, inverse_one, w_attn, w_in, w_out, rows):
    total = low.shape[0]
    bands = FF // D
    slope, w_attn, w_in, w_out, rows = streamed(slope, w_attn, w_in, w_out, rows)
    band = lambda height: pl.BlockSpec((height, D), lambda j: (0, j))
    return pl.pallas_call(
        partial(inner_kernel, len(after)),
        grid=(bands,),
        in_specs=[ANY] * len(after)
        + [
            whole(low.shape), whole(grad_two.shape), band(total), whole(unit_one.shape),
            whole(inverse_one.shape), whole(w_attn.shape), band(D),
            pl.BlockSpec((D, D), lambda j: (j, 0)), whole(rows.shape),
        ],
        out_specs=[band(total)] + [whole((total, D))] * 3 + [whole((3 + bands, D))],
        out_shape=[
            near((total, FF), LOW),
            far((total, D), F32),
            near((total, D), LOW),
            near((total, D), LOW),
            jax.ShapeDtypeStruct((3 + bands, D), F32),
        ],
        scratch_shapes=[pltpu.VMEM((total, D), F32)],
        compiler_params=params(),
        cost_estimate=cost(16),
        name="inner",
    )(*after, low, grad_two, slope, unit_one, inverse_one, w_attn, w_in, w_out, rows)


def unattend_kernel(after, sums, *refs):
    q, k, v, p, ga, attended = refs[after : after + 6]
    vec_one, vec_two, vec_early = refs[after + 6 : -2] if sums else (None, None, None)
    stack_out, vec_out = refs[-2:]
    scaling = HEAD ** (-0.5)
    first = pl.program_id(0) == 0

    @pl.when(first)
    def _():
        if not sums:
            vec_out[...] = jnp.zeros_like(vec_out)
            return
        for index in range(2):
            vec_out[2 * index : 2 * index + 1] = vec_one[index : index + 1]
            vec_out[2 * index + 1 : 2 * index + 2] = vec_two[index : index + 1]
        vec_out[4:6] = vec_early[...]
        vec_out[6:7] = vec_one[2:3]
        vec_out[7:8] = vec_two[2:3]
        vec_out[8:] = vec_one[3:]

    place = 4 if sums else 0
    head_of_row = lax.broadcasted_iota(jnp.int32, (2 * HEAD, 2 * SPAN), 0) // HEAD
    head_of_lane = lax.broadcasted_iota(jnp.int32, (2 * HEAD, 2 * SPAN), 1) // SPAN
    by_head = jnp.where(head_of_row == head_of_lane, 1.0, 0.0).astype(LOW)
    for span in range(p.shape[0]):
        at = slice(span * SPAN, (span + 1) * SPAN)
        for pair in range(HEADS // 2):
            lo = pair * 2 * HEAD
            lanes = slice(lo, lo + 2 * HEAD)
            weights = p[span, pair]
            grad = ga[at, lanes]
            spread_out = dot(grad, split_heads(v[at, lanes]), (1, 1))
            along = (grad.astype(F32) * attended[at, lanes].astype(F32)).astype(LOW)
            grad_scores = (weights.astype(F32) * (spread_out - dot(along, by_head))).astype(LOW)
            parts = [grad_scores[:, :SPAN], grad_scores[:, SPAN:]]
            grad_q = dot(grad_scores, split_heads(k[at, lanes])) * scaling
            tall_scores = jnp.concatenate(parts, axis=0)
            tall_weights = jnp.concatenate([weights[:, :SPAN], weights[:, SPAN:]], axis=0)
            grad_k = dot(tall_scores, split_heads(q[at, lanes]), (0, 0))
            grad_v = dot(tall_weights, split_heads(grad), (0, 0))
            stack_out[at, lo : lo + 2 * HEAD] = grad_q.astype(LOW)
            stack_out[at, D + lo : D + lo + 2 * HEAD] = grad_k.astype(LOW)
            stack_out[at, 2 * D + lo : 2 * D + lo + 2 * HEAD] = grad_v.astype(LOW)
            vec_out[place : place + 1, lanes] += jnp.sum(grad_q, axis=0, keepdims=True)
            vec_out[place + 1 : place + 2, lanes] += jnp.sum(grad_v, axis=0, keepdims=True)


def unattend(after, part, parts, q, k, v, p, ga, attended, stack=None, sums=()):
    total = q.shape[0]
    count = total // SPAN // parts
    first = part * count
    tall = lambda width: pl.BlockSpec((SPAN, width), lambda i: (first + i, 0))
    after = after if stack is None else [stack] + after
    vec_shape = (12, D) if sums else (2, D)
    return pl.pallas_call(
        partial(unattend_kernel, len(after), bool(sums)),
        grid=(count,),
        in_specs=[ANY] * len(after)
        + [tall(D)] * 3
        + [
            pl.BlockSpec((1, HEADS // 2, SPAN, 2 * SPAN), lambda i: (first + i, 0, 0, 0)),
            tall(D),
            tall(D),
        ]
        + [whole(a.shape) for a in sums],
        out_specs=[tall(3 * D), whole(vec_shape)],
        out_shape=[far((total, 3 * D), LOW), jax.ShapeDtypeStruct(vec_shape, F32)],
        input_output_aliases={} if stack is None else {0: 0},
        compiler_params=params(),
        cost_estimate=cost(8),
        name="unattend",
    )(*after, q, k, v, p, ga, attended, *sums)


def input_kernel(*refs):
    grad_one, stack, w_qkv, out = refs[-4:]
    total = grad_one[...]
    for index in range(3):
        total += dot(stack[:, index * D : (index + 1) * D], w_qkv[index], (1, 1))
    out[...] = total


def input_grad(after, grad_one, stack, w_qkv):
    total = grad_one.shape[0]
    tall = lambda width: pl.BlockSpec((TALL, width), lambda i: (i, 0))
    return pl.pallas_call(
        input_kernel,
        grid=(total // TALL,),
        in_specs=[ANY] * len(after) + [tall(D), tall(3 * D), whole(w_qkv.shape)],
        out_specs=tall(D),
        out_shape=jax.ShapeDtypeStruct((total, D), F32),
        compiler_params=params(),
        cost_estimate=cost(8),
        name="input",
    )(*after, grad_one, stack, w_qkv)


def contrast_kernel(slots, masks, place, rows, counts, partners, loss_out, grad_out):
    total, scale = rows.shape[0], 2.0 * D ** (-0.5)

    def number(shape, axis):
        at = lax.broadcasted_iota(jnp.int32, shape, axis)
        device, block = jnp.full(shape, place[0], jnp.int32), at // GROUP
        for bit, mask in enumerate(masks):
            device = device ^ (((block >> bit) & 1) * mask)
        return device, at % GROUP

    device, slot = number((counts.shape[1], total), 1)
    hit = lax.broadcasted_iota(jnp.int32, device.shape, 0) == device
    count = dot(counts[...].astype(LOW), jnp.where(hit, 1.0, 0.0).astype(LOW))
    live_across = (slot[:1].astype(F32) < count) & (slot[:1] < slots)
    device, slot = number((total, counts.shape[1]), 0)
    hit = lax.broadcasted_iota(jnp.int32, device.shape, 1) == device
    count = jnp.sum(jnp.where(hit, counts[...], 0.0), axis=1, keepdims=True)
    live_down = (slot[:, :1].astype(F32) < count) & (slot[:, :1] < slots)
    device, slot = number((total, partners.shape[1]), 0)
    own_id = device * slots + slot
    hit = lax.broadcasted_iota(jnp.int32, own_id.shape, 1) == own_id
    pair = jnp.sum(jnp.where(hit, partners[...], 0.0), axis=1, keepdims=True)
    device, slot = number((total, 128), 0)
    down = (device * slots + slot).astype(F32)[:, :1]
    device, slot = number((8, total), 1)
    across, slot = (device * slots + slot).astype(F32)[:1], slot[:1]
    valid = live_across & (down != across)
    matched = jnp.where((slot < slots) & (pair == across), 1.0, 0.0)
    anchor = jnp.where(live_down & (pair != down), 1.0, 0.0)
    similar = dot(rows[...], rows[...], (1, 1)) * scale
    masked = jnp.where(valid, similar, -1e30)
    peak = jnp.max(masked, axis=1, keepdims=True)
    summed = jnp.sum(jnp.where(valid, jnp.exp(masked - peak), 0.0), axis=1, keepdims=True)
    log_total = jnp.log(summed) + peak
    positive = jnp.sum(matched * similar, axis=1, keepdims=True)
    loss_out[...] = jnp.sum(anchor * (log_total - positive), axis=0, keepdims=True)
    grad = (anchor * (jnp.where(valid, jnp.exp(masked - log_total), 0.0) - matched)).astype(LOW)
    own = lax.broadcasted_iota(jnp.int32, (GROUP, total), 0)
    own = jnp.where(own == lax.broadcasted_iota(jnp.int32, (GROUP, total), 1), 1.0, 0.0)
    down_part = dot(dot(own.astype(LOW), grad, (1, 1)).astype(LOW), rows[...])
    grad_out[...] = (dot(grad[: 2 * GROUP], rows[...])[:GROUP] + down_part) * scale


def contrast(cls_rows, span_count, pair_index, device, slots):
    total = cls_rows.shape[0]
    scale = {"row": lax.axis_size("col"), "col": 1}
    masks = [scale[name] * bit for phase in gather_steps() for name, bit in phase]
    return pl.pallas_call(
        partial(contrast_kernel, slots, masks),
        in_specs=[pl.BlockSpec(memory_space=pltpu.SMEM)]
        + [pl.BlockSpec(memory_space=pltpu.VMEM)] * 3,
        out_shape=[
            jax.ShapeDtypeStruct((1, 1), F32),
            jax.ShapeDtypeStruct((GROUP, D), F32),
        ],
        compiler_params=params(),
        cost_estimate=cost(3),
        name="contrast",
    )(
        device,
        cls_rows,
        span_count.astype(F32).reshape(1, -1),
        pair_index.astype(F32).reshape(1, -1),
    )


def adam_kernel(
    masks, parts, position, *refs,
):
    gathered = refs[:parts]
    master, first, second, left, right, master_out, first_out, second_out, low_out, *scratch = refs[parts:]
    quarter = D // 4
    slot = pl.program_id(0)
    if masks:
        owned = scratch[0]
        shares, tall, _ = gathered[0].shape
        rows = D // len(masks)

        @pl.when(slot == 0)
        def _():
            for number, mask in enumerate(masks):
                block = gathered[number // shares][number % shares].astype(F32)
                at = pl.multiple_of((mask ^ position[0]) * rows, rows)
                for index in range(owned.shape[0]):
                    lo = index * rows % tall
                    side = index * rows // tall
                    piece = block[lo : lo + rows, side * quarter : (side + 1) * quarter]
                    owned[index, pl.ds(at, rows), :] = piece

    for here in range(master.shape[0]):
        if masks:
            gradient = owned[slot * master.shape[0] + here].astype(LOW)
        else:
            gradient = gathered[0][here]
        low_left, low_right = left[here], right[here].astype(LOW)
        turned = dot(gradient, low_left, (0, 0))
        turned = dot(low_right, turned.astype(LOW), (0, 0))
        new_first = 0.9 * first[here] + 0.1 * turned
        new_second = 0.999 * second[here] + 0.001 * turned * turned
        first_out[here] = new_first
        second_out[here] = new_second
        spread_by = jnp.sqrt(new_second * (1.0 / (1.0 - 0.999**STEP))) + 1e-08
        update = new_first * (1.0 / (1.0 - 0.9**STEP)) / spread_by
        update = dot(update.astype(LOW), low_left, (1, 1))
        update = dot(low_right, update.astype(LOW))
        new_master = master[here] - RATE * (update + DECAY * master[here])
        master_out[here] = new_master
        low_out[here] = new_master.astype(LOW)


def ready_kernel(*refs):
    source, out = refs[-2:]
    out[...] = source[...].astype(out.dtype)


def ready(after, array, kind, first, count, before=()):
    block = pl.BlockSpec((1,) + array.shape[1:], lambda s: (first + s, 0, 0))
    first_in = list(before) + list(after)
    return pl.pallas_call(
        ready_kernel,
        grid=(count,),
        in_specs=[ANY] * len(first_in) + [block],
        out_specs=block,
        out_shape=far(array.shape, kind),
        input_output_aliases={0: 0} if before else {},
        compiler_params=params(16),
        cost_estimate=cost(1.5 * count),
        name="ready",
    )(*first_in, *streamed(array))


def to_owned(gathered, masks, position, per_owner):
    quarter = D // 4
    places = jnp.array(masks, jnp.int32) ^ position
    gathered = jnp.zeros_like(gathered).at[places].set(gathered)
    flat = jnp.concatenate([gathered[..., :quarter], gathered[..., quarter:]], axis=1)
    rows = flat.shape[1] // per_owner
    flat = flat.reshape(flat.shape[0], per_owner, rows, quarter).transpose(1, 0, 2, 3)
    return flat.reshape(per_owner, D, quarter)


def turn(array):
    return array.transpose(0, 2, 1)


def rotated_adam(position, gathered, masks, master, first_moment, second_moment, left_basis, right_basis):
    per_owner, quarter, _ = master.shape
    if D // len(masks) % 8 or per_owner % 2:
        gathered = [to_owned(jnp.concatenate(gathered), masks, position, per_owner)]
        masks = []
    at_once = max(n for n in (1, 2, 3) if per_owner % n == 0)
    block = lambda a: pl.BlockSpec((at_once,) + a.shape[1:], lambda s, p: (s, 0, 0))
    operands = streamed(master, first_moment, second_moment, left_basis, right_basis)
    like = jax.ShapeDtypeStruct(operands[0].shape, F32)
    fixed = pl.BlockSpec(gathered[0].shape, lambda s, p: (0, 0, 0))
    outputs = pl.pallas_call(
        partial(adam_kernel, masks, len(gathered)),
        grid_spec=pltpu.PrefetchScalarGridSpec(
            num_scalar_prefetch=1,
            grid=(per_owner // at_once,),
            in_specs=[fixed if masks else block(part) for part in gathered]
            + [block(a) for a in operands],
            out_specs=[block(operands[0])] * 4,
            scratch_shapes=[pltpu.VMEM((per_owner, D, quarter), F32)] if masks else [],
        ),
        out_shape=[like, like, like, jax.ShapeDtypeStruct(like.shape, LOW)],
        compiler_params=params(48),
        cost_estimate=cost(20),
        name="adam",
    )(position.reshape(1), *gathered, *operands)
    return [turn(a) for a in outputs]


def axis_bits(name):
    size = lax.axis_size(name)
    return [(name, 1 << k) for k in range(size.bit_length() - 1)]


def bit_of(step):
    return jnp.where((lax.axis_index(step[0]) & step[1]) != 0, 1, 0)


def swap(send, step):
    size = lax.axis_size(step[0])
    return lax.ppermute(send, step[0], [(i, i ^ step[1]) for i in range(size)])


def gather_steps():
    core, across, y_bits, z_bits = row_steps()
    return [z_bits[::-1], y_bits + across, core]


def gather_all(rows, beside):
    columns = lax.axis_size("col")
    every = lax.axis_size("row") * columns
    scale = {"row": columns, "col": 1}
    for phase in gather_steps():
        arrived = []
        for number in range(1, 1 << len(phase)):
            mask = sum(scale[name] * bit for j, (name, bit) in enumerate(phase) if number >> j & 1)
            pairs = [(i, i ^ mask) for i in range(every)]
            arrived.append(lax.ppermute(rows, ("row", "col"), pairs))
        if beside:
            rows = merge(beside, [rows] + arrived).reshape(-1, D)
            beside = []
        else:
            rows = jnp.concatenate([rows] + arrived)
    return rows


def row_steps():
    row_bits, col_bits = axis_bits("row"), axis_bits("col")
    core, across = row_bits[:1], row_bits[1:][::-1]
    y_bits, z_bits = col_bits[:-2][::-1], col_bits[-2:]
    return core, across, y_bits, z_bits


def pack_rider(rider, rows, width):
    parts = [rider[:, at : at + width] for at in range(0, D, width)]
    tall = rider.shape[0]
    if rows < tall:
        return [part[at : at + rows] for part in parts for at in range(0, tall, rows)]
    fold = rows // tall
    parts += parts[-1:] * (-len(parts) % fold)
    return [jnp.concatenate(parts[at : at + fold]) for at in range(0, len(parts), fold)]


def unpack_rider(blocks, tall):
    rows, width = blocks[0].shape
    if rows < tall:
        fold = tall // rows
        parts = [jnp.concatenate(blocks[at : at + fold]) for at in range(0, len(blocks), fold)]
    else:
        parts = [block[at : at + tall] for block in blocks for at in range(0, rows, tall)]
    parts = parts[: D // width]
    return parts[0] if len(parts) == 1 else jnp.concatenate(parts, axis=1)


def rider_blocks(rows, width, tall=12):
    return -(-tall * D // (rows * width))


def land_kernel(after, outs, rider, bits, *refs):
    refs = refs[after:]
    sides = len({source[0] for out in outs for source in out[3]})
    keeps, others = refs[0 : 2 * sides : 2], refs[1 : 2 * sides : 2]
    results = refs[2 * sides + (0 if rider is None else 1 + (rider == "array")) :]
    if rider is not None:
        total = refs[2 * sides][...]
        tall = total.shape[0]
        if rider == "array":
            total += refs[2 * sides + 1][...]
        else:
            blocks = [others[0][at].astype(F32) for at in range(keeps[0].shape[0], others[0].shape[0])]
            total += unpack_rider(blocks, tall)
        results[-1][...] = total
    for number, (at_bit, before, behind, sources) in enumerate(outs):
        bit = bits[at_bit]
        for which, target in enumerate(results[2 * number : 2 * number + 2]):
            half = bit if which else 1 - bit
            for at in range(before):
                here = pl.ds((2 * at + half) * behind, behind)
                there = slice(at * behind, (at + 1) * behind)
                for side, lanes, into in sources:
                    target[there, :, into] = keeps[side][here, :, lanes] + others[side][here, :, lanes]
        if rider is not None and number == 0:
            away = results[0]
            count, rows, width = away.shape
            blocks = pack_rider(total, rows, width)
            for index, block in enumerate(blocks):
                away[count - len(blocks) + index] = block.astype(LOW)


class Reduction:
    def __init__(self, bits, ways, send, keep, rider=None):
        core, across, y_bits, z_bits = row_steps()
        self.bits, self.order = bits, core + across + y_bits + z_bits
        left = across + y_bits + z_bits
        self.panels, height, _ = keep.shape
        self.rows = height >> len(left)
        other = swap(send, core[0])
        self.rider = None if rider is None else (rider, swap(rider, core[0]))
        split = lambda a: a.reshape(-1, self.rows, D)
        self.sides = [(split(keep), split(other), left)]
        cycle = [across, y_bits, z_bits[:1]][:ways]
        orders = [sum(cycle[at:] + cycle[:at], []) for at in range(ways)]
        self.stages = list(zip(*orders)) + [(step,) for step in z_bits[ways - 2 :]]
        self.ways = ways
        self.messages = []

    def sent(self):
        return self.messages

    def landing(self):
        return [side[1] for side in self.sides]

    def land(self, *after):
        stage = self.stages.pop(0)
        outs, shapes, lefts = [], [], []
        part = D // self.ways
        lanes = [slice(at, at + part) for at in range(0, D, part)]
        for index, step in enumerate(stage):
            if len(self.sides) == len(stage):
                width = self.sides[index][0].shape[2]
                sources = [(index, slice(0, width), slice(0, width))]
                left = self.sides[index][2]
            elif len(stage) > 1:
                width, left = part, self.sides[0][2]
                sources = [(0, lanes[index], slice(0, part))]
            else:
                width, left = D, self.sides[0][2]
                sources = [(side, slice(0, part), lanes[side]) for side in range(self.ways)]
            dim = left.index(step)
            behind = 1 << (len(left) - dim - 1)
            before = self.panels << dim
            outs.append((self.order.index(step), before, behind, sources))
            extra = rider_blocks(self.rows, width) if self.rider and index == 0 else 0
            shapes += [(before * behind + extra, self.rows, width), (before * behind, self.rows, width)]
            lefts.append([other for other in left if other != step])
        rider = None if self.rider is None else ("array" if len(self.rider) == 2 else "message")
        inputs = [a for keep, other, _ in self.sides for a in (keep, other)] + list(self.rider or ())
        out_shape = [jax.ShapeDtypeStruct(shape, LOW) for shape in shapes]
        if rider:
            out_shape.append(jax.ShapeDtypeStruct(self.rider[0].shape, F32))
        results = pl.pallas_call(
            partial(land_kernel, len(after), outs, rider),
            in_specs=[SMEM] + [ANY] * len(after) + [pl.BlockSpec(memory_space=pltpu.VMEM)] * len(inputs),
            out_shape=out_shape,
            compiler_params=params(24),
            cost_estimate=cost(2),
            name="land",
        )(self.bits, *after, *inputs)
        if rider:
            self.rider = (results[-1],)
        self.messages = list(results[0 : 2 * len(stage) : 2])
        keeps = results[1 : 2 * len(stage) : 2]
        self.sides = [
            (keep, swap(message, step), left)
            for keep, message, step, left in zip(keeps, self.messages, stage, lefts)
        ]

    def finish(self):
        while self.stages:
            self.land()


def slots_kernel(after, cols, panels, column, owners, *refs):
    refs = refs[after:]
    sums, rider, rider_out = refs[:6], refs[6], refs[7]
    targets, blocks, packed = refs[8:-2], refs[-2], refs[-1]
    quarter = D // 4
    found = [(sums[2 * run], sums[2 * run + 1], i) for run in range(3) for i in range(sums[2 * run].shape[0])]
    at = 0
    for panel in panels:
        keep, other, index = found[panel]
        value = keep[index].astype(F32) + other[index].astype(F32)
        for part in range(4):
            blocks[at] = value[:, part * quarter : (part + 1) * quarter]
            at += 1
    tail = [sums[1][index].astype(F32) for index in range(sums[0].shape[0], sums[1].shape[0])]
    rider_out[...] = rider[...] + unpack_rider(tail, rider.shape[0])
    rows, half = blocks.shape[1], packed.shape[1]
    for slot in range(at):
        col, place = divmod(slot, at // cols)
        value = blocks[owners[slot]]
        first = place * rows
        for side in range(2):
            lo, hi = max(first, side * half), min(first + rows, (side + 1) * half)
            if lo < hi:
                lanes = slice(side * quarter, (side + 1) * quarter)
                packed[col, lo - side * half : hi - side * half, lanes] = value[lo - first : hi - first]
    for number, target in enumerate(targets):
        target[...] = packed[column[0] ^ number].astype(LOW)


def to_slots(after, runs, panels, owner_list):
    quarter, cols = D // 4, lax.axis_size("col")
    arrays = [a for run in runs for a in run.sides[0][:2]]
    rows = runs[0].rows
    shape = (len(panels) * 4 // cols * rows // 2, 2 * quarter)
    rider = runs[0].rider[0]
    return pl.pallas_call(
        partial(slots_kernel, len(after), cols, panels),
        in_specs=[SMEM, SMEM] + [ANY] * len(after) + [pl.BlockSpec(memory_space=pltpu.VMEM)] * 7,
        out_shape=[jax.ShapeDtypeStruct(rider.shape, F32)] + [jax.ShapeDtypeStruct(shape, LOW)] * cols,
        scratch_shapes=[
            pltpu.VMEM((len(panels) * 4, rows, quarter), F32),
            pltpu.VMEM((cols,) + shape, F32),
        ],
        compiler_params=params(24),
        cost_estimate=cost(4),
        name="slots",
    )(lax.axis_index("col").reshape(1), owner_list, *after, *arrays, rider)


def merge_kernel(after, *refs):
    *sources, target = refs[after:]
    for number, source in enumerate(sources):
        target[number] = source[...]


def merge(after, arrays):
    return pl.pallas_call(
        partial(merge_kernel, len(after)),
        in_specs=[ANY] * len(after) + [pl.BlockSpec(memory_space=pltpu.VMEM)] * len(arrays),
        out_shape=jax.ShapeDtypeStruct((len(arrays),) + arrays[0].shape, arrays[0].dtype),
        compiler_params=params(24),
        cost_estimate=cost(1),
        name="merge",
    )(*after, *arrays)


def spread(parts):
    core, across, y_bits, z_bits = row_steps()
    order = core + across + y_bits + z_bits
    weight = lambda step: 1 << (len(order) - 1 - order.index(step))
    cols, bits = len(parts), axis_bits("col")
    sent = lambda number: lax.ppermute(parts[number], "col", [(i, i ^ number) for i in range(cols)])
    arrived = [parts[0]] + [sent(number) for number in range(1, cols)]
    masks = [sum(weight(step) for step in bits if number & step[1]) for number in range(cols)]
    near = merge([], arrived[: cols // 2])
    first, *rest = (core + across)[::-1]
    moved = swap(near, first)
    far = merge([], arrived[cols // 2 :])
    shares = [near, far, moved, swap(far, first)]
    masks = masks + [mask ^ weight(first) for mask in masks]
    for step in rest:
        shares = shares + [swap(share, step) for share in shares]
        masks = masks + [mask ^ weight(step) for mask in masks]
    return shares, masks


def row_place():
    place = 0
    for group in row_steps():
        for step in group:
            place = place * 2 + bit_of(step)
    return place


def shards(
    tokens,
    w_qkv,
    w_attn_out,
    w_in,
    w_out,
    vectors,
    out_grad,
    span_count,
    pair_index,
    owner_list,
    master,
    first_moment,
    second_moment,
    left_basis,
    right_basis,
    vec_first,
    vec_second,
):
    slots = tokens.shape[0] // SPAN
    device = (lax.axis_index("row") * lax.axis_size("col") + lax.axis_index("col")).reshape(1)
    core, across, y_bits, z_bits = row_steps()
    core_bit = bit_of(core[0])
    bits = jnp.stack([bit_of(step) for step in core + across + y_bits + z_bits])
    rows = vectors.reshape(1, -1)
    q, k, v, p, attended = attend(tokens, w_qkv, rows)
    encoded, hidden, slope, normed_low, unit_one, inverse_one, unit_two, inverse_two, cls_rows = (
        feed(device, span_count, tokens, attended, w_attn_out, w_in, w_out, rows)
    )
    per_owner = left_basis.shape[0]
    head = per_owner // 3
    low_left = ready([cls_rows], left_basis, LOW, 0, head)
    every_cls = gather_all(cls_rows, streamed(low_left))
    loss, grad_cls = contrast(every_cls, span_count, pair_index, device, slots)
    grad_two, outer_low, vec_two = outer_grad(
        device, span_count, out_grad, grad_cls, unit_two, inverse_two, rows
    )
    outer_args = (hidden, outer_low, FF // D, True)
    outer_away = weight_half(8, [], 1 - core_bit, *outer_args)
    outer_here = weight_half(60, [outer_away], core_bit, *outer_args)
    outer_run = Reduction(bits, 2, outer_away, outer_here)
    outer_run.land()
    pre_low, grad_one, mixed_low, grad_attended, vec_one = inner_grad(
        outer_run.sent(), outer_low, grad_two, slope, unit_one, inverse_one,
        w_attn_out, w_in, w_out, rows,
    )
    outer_run.land(vec_one)
    inner_args = (normed_low, pre_low, FF // D, False, (attended, mixed_low))
    inner_away = weight_half(8, outer_run.sent(), 1 - core_bit, *inner_args)
    outer_run.land(inner_away)
    inner_here = weight_half(60, [inner_away] + outer_run.sent(), core_bit, *inner_args)
    outer_run.land(inner_here)
    inner_run = Reduction(bits, 3, inner_away, inner_here)
    inner_run.land()
    early, vec_early = unattend(
        outer_run.sent() + inner_run.sent(), 0, 2, q, k, v, p, grad_attended, attended
    )
    stack_low, vec_grad = unattend(
        [], 1, 2, q, k, v, p, grad_attended, attended, early, (vec_one, vec_two, vec_early)
    )
    inner_run.land(vec_grad)
    project_args = (tokens, stack_low, 3, False)
    project_away = weight_half(
        8, inner_run.sent() + outer_run.landing(), 1 - core_bit, *project_args
    )
    project_here = weight_half(60, [project_away], core_bit, *project_args)
    project_run = Reduction(bits, 3, project_away, project_here, vec_grad)
    project_run.land(*inner_run.landing())
    grad_tokens = input_grad(project_run.sent(), grad_one, stack_low, w_qkv)
    inner_run.land(*streamed(grad_tokens))
    project_run.land(*streamed(grad_tokens))
    inner_run.land()
    project_run.land(*inner_run.sent())
    project_run.land(*inner_run.landing())
    for run in (outer_run, inner_run, project_run):
        run.finish()
    low_left = ready(
        project_run.sent(), left_basis, LOW, head, per_owner - head, [low_left]
    )
    vec_grad, *parts = to_slots(
        streamed(low_left), (project_run, inner_run, outer_run),
        (0, 1, 2, 7, 3, 4, 5, 6, 8, 9, 10, 11), owner_list,
    )
    vec_grad = vec_grad.reshape(-1)
    gathered, masks = spread(parts)
    new_master, new_first, new_second, master_copy = rotated_adam(
        row_place(), gathered, masks, turn(master), turn(first_moment), turn(second_moment),
        low_left, right_basis,
    )
    vec_first_new = 0.9 * vec_first + 0.1 * vec_grad
    vec_second_new = 0.999 * vec_second + 0.001 * vec_grad * vec_grad
    vec_step = (
        vec_first_new / (1.0 - 0.9**STEP) / (jnp.sqrt(vec_second_new / (1.0 - 0.999**STEP)) + 1e-08)
    )
    vec_new = vectors - VECTOR_RATE * vec_step
    return (
        encoded,
        grad_tokens,
        loss[0, 0],
        new_master,
        new_first,
        new_second,
        master_copy,
        vec_new,
        vec_first_new,
        vec_second_new,
    )


def solution(mesh):
    in_specs = (
        P(("row", "col"), None),
        P(),
        P(),
        P(),
        P(),
        P(),
        P(("row", "col"), None),
        P(),
        P(),
        P(),
        P("col", None, None),
        P("col", None, None),
        P("col", None, None),
        P("col", None, None),
        P("col", None, None),
        P(),
        P(),
    )
    out_specs = (
        P(("row", "col"), None),
        P(("row", "col"), None),
        P(),
        P("col", None, None),
        P("col", None, None),
        P("col", None, None),
        P("col", None, None),
        P(),
        P(),
        P(),
    )
    return jax.shard_map(shards, mesh=mesh, in_specs=in_specs, out_specs=out_specs, check_vma=False)
```

```python
from functools import partial

import jax
import jax.numpy as jnp
from jax import lax
from jax.experimental import pallas as pl
from jax.experimental.pallas import tpu as pltpu
from jax.sharding import PartitionSpec as P

D = 768
HEADS = 12
HEAD = 64
FF = 3072
SPAN = 128
STEP = 10
GROUP = 8

RATE = 0.01
DECAY = 0.01
VECTOR_RATE = 0.3

LOW = jnp.bfloat16
F32 = jnp.float32
TALL = 2 * SPAN


def dot(left_side, right_side, contract=(1, 0)):
    dims = (((contract[0],), (contract[1],)), ((), ()))
    return lax.dot_general(left_side, right_side, dims, preferred_element_type=F32)


def whole(shape):
    return pl.BlockSpec(shape, lambda *ids: (0,) * len(shape))


def cost(microseconds, transcendentals=0):
    return pl.CostEstimate(
        flops=int(microseconds * 1.1e9), bytes_accessed=0, transcendentals=transcendentals
    )


def params(mebibytes=36):
    return pltpu.CompilerParams(vmem_limit_bytes=mebibytes * 1024 * 1024)


def row_of(rows, index):
    return rows[:, index * D : (index + 1) * D]


def live_rows(place, counts, first_row, height):
    at = first_row + lax.broadcasted_iota(jnp.int32, (height, 1), 0)
    return jnp.where(at < counts[place[0]] * SPAN, 1.0, 0.0)


near = pltpu.VMEM
far = pltpu.HBM


def streamed(*arrays):
    return [pltpu.with_memory_space_constraint(a, pltpu.HBM) for a in arrays]


ANY = pl.BlockSpec(memory_space=pl.ANY)
SMEM = pl.BlockSpec(memory_space=pltpu.SMEM)


def split_heads(pair):
    lane = lax.broadcasted_iota(jnp.int32, pair.shape, 1)
    zero = jnp.zeros_like(pair)
    return jnp.concatenate([jnp.where(lane < HEAD, pair, zero), jnp.where(lane < HEAD, zero, pair)])


def normalise(scores):
    peak = jnp.max(scores, axis=-1, keepdims=True)
    raised = jnp.exp(scores - peak)
    return raised * (1.0 / jnp.sum(raised, axis=-1, keepdims=True))


def attend_kernel(tokens, w_qkv, rows, q_out, k_out, v_out, p_out, a_out):
    block = tokens[...]
    scaling = HEAD ** (-0.5)
    q_out[...] = ((dot(block, w_qkv[0]) + row_of(rows, 4)).astype(LOW) * scaling).astype(LOW)
    k_out[...] = dot(block, w_qkv[1]).astype(LOW)
    v_out[...] = (dot(block, w_qkv[2]) + row_of(rows, 5)).astype(LOW)
    for span in range(TALL // SPAN):
        at = slice(span * SPAN, (span + 1) * SPAN)
        for pair in range(HEADS // 2):
            lanes = slice(pair * 2 * HEAD, (pair + 1) * 2 * HEAD)
            scores = dot(q_out[at, lanes], split_heads(k_out[at, lanes]), (1, 1))
            weights = jnp.concatenate(
                [normalise(scores[:, :SPAN]), normalise(scores[:, SPAN:])], axis=1
            ).astype(LOW)
            p_out[span, pair] = weights
            a_out[at, lanes] = dot(weights, split_heads(v_out[at, lanes])).astype(LOW)


def attend(tokens, w_qkv, rows):
    total = tokens.shape[0]
    tall = pl.BlockSpec((TALL, D), lambda i: (i, 0))
    like = far((total, D), LOW)
    tokens, w_qkv, rows = streamed(tokens, w_qkv, rows)
    spans = TALL // SPAN
    return pl.pallas_call(
        attend_kernel,
        grid=(total // TALL,),
        in_specs=[tall, whole(w_qkv.shape), whole(rows.shape)],
        out_specs=[
            tall,
            tall,
            tall,
            pl.BlockSpec((spans, HEADS // 2, SPAN, 2 * SPAN), lambda i: (i, 0, 0, 0)),
            tall,
        ],
        out_shape=[
            like,
            like,
            like,
            far((total // SPAN, HEADS // 2, SPAN, 2 * SPAN), LOW),
            near((total, D), LOW),
        ],
        compiler_params=params(),
        cost_estimate=cost(10),
        name="attend",
    )(tokens, w_qkv, rows)


def unit_norm(resid):
    centred = resid - jnp.mean(resid, axis=-1, keepdims=True)
    inverse = lax.rsqrt(jnp.mean(centred * centred, axis=-1, keepdims=True) + 1e-06)
    return centred * inverse, inverse


def gelu_pair(x):
    cdf = 0.5 + 0.5 * lax.erf(x * 0.7071067811865476)
    gauss = jnp.exp2(x * x * -0.7213475204444817)
    return x * cdf, cdf + x * gauss * 0.3989422804014327


def feed_kernel(
    place, counts, tokens, attended, w_attn, w_in, w_out, rows, bias,
    enc_out, hid_out, slope_out, norm_out, u1_out, i1_out, u2_out, i2_out, cls_out, total, firsts,
):
    band = pl.program_id(0)
    chunks = [slice(at, at + TALL) for at in range(0, tokens.shape[0], TALL)]

    @pl.when(band == 0)
    def _():
        for at in chunks:
            resid = tokens[at].astype(F32) + dot(attended[at], w_attn[...]) + row_of(rows, 6)
            unit_one, inverse_one = unit_norm(resid)
            value = unit_one * row_of(rows, 0) + row_of(rows, 2)
            u1_out[at] = unit_one.astype(LOW)
            i1_out[at] = inverse_one
            norm_out[at] = value.astype(LOW)
            total[at] = value + row_of(rows, 7)

    step = 256
    for at in range(0, hid_out.shape[1], step):
        here = slice(at, at + step)
        pre_act = dot(norm_out[...], w_in[:, here]) + bias[:, here]
        hidden, slope = gelu_pair(pre_act)
        hid_out[:, here] = hidden.astype(LOW)
        slope_out[:, here] = slope.astype(LOW)

    @pl.when(band < pl.num_programs(0) - 1)
    def _():
        total[...] += dot(hid_out[...], w_out[...])

    @pl.when(band == pl.num_programs(0) - 1)
    def _():
        for at in chunks:
            resid = total[at] + dot(hid_out[at], w_out[...])
            unit_two, inverse_two = unit_norm(resid)
            u2_out[at] = unit_two.astype(LOW)
            i2_out[at] = inverse_two
            live = live_rows(place, counts, at.start, TALL)
            value = live * (unit_two * row_of(rows, 1) + row_of(rows, 3))
            enc_out[at] = value.astype(LOW)
            for first in range(at.start, at.stop, SPAN):
                row = first - at.start
                firsts[first // SPAN : first // SPAN + 1] = value[row : row + 1]
        firsts[tokens.shape[0] // SPAN :] = jnp.zeros((GROUP - tokens.shape[0] // SPAN, D), F32)
        cls_out[...] = firsts[...].astype(LOW)


def feed(place, counts, tokens, attended, w_attn, w_in, w_out, rows):
    total = tokens.shape[0]
    tall = lambda width: pl.BlockSpec((total, width), lambda j: (0, 0))
    band = lambda height: pl.BlockSpec((height, D), lambda j: (0, j))
    tokens, w_attn, w_in, w_out, rows = streamed(tokens, w_attn, w_in, w_out, rows)
    return pl.pallas_call(
        feed_kernel,
        grid=(FF // D,),
        in_specs=[
            SMEM, SMEM, tall(D), tall(D), whole(w_attn.shape), band(D),
            pl.BlockSpec((D, D), lambda j: (j, 0)),
            pl.BlockSpec((1, 8 * D), lambda j: (0, 0)),
            pl.BlockSpec((1, D), lambda j: (0, 8 + j)),
        ],
        out_specs=[
            tall(D), band(total), band(total), tall(D), tall(D), tall(1), tall(D), tall(1),
            whole((GROUP, D)),
        ],
        out_shape=[
            jax.ShapeDtypeStruct((total, D), LOW),
            far((total, FF), LOW),
            far((total, FF), LOW),
            far((total, D), LOW),
            far((total, D), LOW),
            far((total, 1), F32),
            near((total, D), LOW),
            near((total, 1), F32),
            jax.ShapeDtypeStruct((GROUP, D), LOW),
        ],
        scratch_shapes=[pltpu.VMEM((total, D), F32), pltpu.VMEM((GROUP, D), F32)],
        compiler_params=params(),
        cost_estimate=cost(20),
        name="feed",
    )(place, counts, tokens, attended, w_attn, w_in, w_out, rows, rows)


def norm_back(grad_out, unit_rows, inverse, gain):
    scaled = grad_out * gain
    along = jnp.mean(scaled * unit_rows, axis=-1, keepdims=True)
    return inverse * (scaled - jnp.mean(scaled, axis=-1, keepdims=True) - unit_rows * along)


def column_sums(*arrays):
    return [jnp.sum(a, axis=0, keepdims=True) for a in arrays]


def outer_kernel(place, counts, out_grad, grad_cls, unit_two, inverse_two, rows, two_out, low_out, vec_out):
    spot = lax.broadcasted_iota(jnp.int32, (SPAN, 1), 0) == 0
    sums = None
    for span in range(out_grad.shape[0] // SPAN):
        at = slice(span * SPAN, (span + 1) * SPAN)
        added = jnp.where(spot, grad_cls[span : span + 1], 0.0)
        live = live_rows(place, counts, span * SPAN, SPAN)
        grad_y = live * (out_grad[at].astype(F32) + added)
        unit_rows = unit_two[at].astype(F32)
        grad_two = norm_back(grad_y, unit_rows, inverse_two[at], row_of(rows, 1))
        two_out[at] = grad_two
        low_out[at] = grad_two.astype(LOW)
        here = column_sums(grad_y * unit_rows, grad_y, grad_two)
        sums = here if sums is None else [a + b for a, b in zip(sums, here)]
    for index, total in enumerate(sums):
        vec_out[index : index + 1] = total


def outer_grad(place, counts, out_grad, grad_cls, unit_two, inverse_two, rows):
    total = out_grad.shape[0]
    return pl.pallas_call(
        outer_kernel,
        in_specs=[SMEM, SMEM] + [pl.BlockSpec(memory_space=pltpu.VMEM)] * 5,
        out_shape=[
            jax.ShapeDtypeStruct((total, D), F32),
            jax.ShapeDtypeStruct((total, D), LOW),
            jax.ShapeDtypeStruct((3, D), F32),
        ],
        compiler_params=params(),
        cost_estimate=cost(5),
        name="outer",
    )(place, counts, out_grad, grad_cls, unit_two, inverse_two, rows)


def weight_kernel(panels, group, after, side, *refs):
    *sides, out = refs[after:]
    lefts, right, extra = sides[: len(sides) - 1], sides[-1], ()
    if panels:
        lefts, right, extra = sides[:1], sides[1], sides[2:]

    def main():
        for index in range(group):
            here = right[:, index * D : (index + 1) * D] if right.shape[1] > D else right[...]
            left = lefts[index if len(lefts) > 1 else 0]
            out[index] = dot(left[...], here, (0, 0)).astype(LOW)

    if not extra:
        main()
        return
    pl.when(pl.program_id(0) < panels)(main)

    @pl.when(pl.program_id(0) == panels)
    def _():
        out[0] = dot(extra[0][...], extra[1][...], (0, 0)).astype(LOW)


def weight_half(hint, after, side, left_side, right_side, panels, banded, group=1, extra=()):
    total = left_side.shape[0]
    half = D // 2
    every = panels + len(extra) // 2
    tall = lambda width, at: pl.BlockSpec((total, width), at)
    last = lambda step: jnp.minimum(step, panels // group - 1)
    if banded:
        lefts = [
            tall(half, lambda i, s, j=j: (0, (i * group + j) * 2 + s[0])) for j in range(group)
        ]
        right = tall(D, lambda i, s: (0, 0))
    else:
        lefts = [tall(half, lambda i, s: (0, s[0]))]
        right = tall(group * D, lambda i, s: (0, last(i)))
    more = [tall(half, lambda i, s: (0, s[0])), tall(D, lambda i, s: (0, 0))]
    return pl.pallas_call(
        partial(weight_kernel, panels if extra else 0, group, len(after)),
        grid_spec=pltpu.PrefetchScalarGridSpec(
            num_scalar_prefetch=1,
            grid=(every // group,),
            in_specs=[ANY] * len(after) + lefts + [right] + more[: len(extra)],
            out_specs=pl.BlockSpec((group, half, D), lambda i, s: (i, 0, 0)),
        ),
        out_shape=jax.ShapeDtypeStruct((every, half, D), LOW),
        compiler_params=params(),
        cost_estimate=cost(hint),
        name="weight",
    )(side.reshape(1), *after, *[left_side] * len(lefts), right_side, *extra)


def inner_kernel(after, *refs):
    low, grad_two, slope, unit_one, inverse_one, w_attn, w_in, w_out, rows = refs[after:-6]
    pre_out, one_out, mixed_out, ga_out, vec_out, total = refs[-6:]
    band = pl.program_id(0)
    last = pl.num_programs(0) - 1
    step = 256
    for at in range(0, D, step):
        here = slice(at, at + step)
        grad_pre = dot(low[...], w_out[here], (1, 1)) * slope[:, here].astype(F32)
        pre_out[:, here] = grad_pre.astype(LOW)
        vec_out[pl.ds(3 + band, 1), here] = jnp.sum(grad_pre, axis=0, keepdims=True)

    @pl.when(band == 0)
    def _():
        total[...] = grad_two[...] + dot(pre_out[...], w_in[...], (1, 1))

    @pl.when((band > 0) & (band < last))
    def _():
        total[...] += dot(pre_out[...], w_in[...], (1, 1))

    @pl.when(band == last)
    def _():
        sums = None
        for first in range(0, low.shape[0], TALL):
            at = slice(first, first + TALL)
            grad_normed = total[at] + dot(pre_out[at], w_in[...], (1, 1))
            unit_rows = unit_one[at].astype(F32)
            grad_one = norm_back(grad_normed, unit_rows, inverse_one[at], row_of(rows, 0))
            one_out[at] = grad_one
            mixed = grad_one.astype(LOW)
            mixed_out[at] = mixed
            ga_out[at] = dot(mixed, w_attn[...], (1, 1)).astype(LOW)
            here = column_sums(grad_normed * unit_rows, grad_normed, grad_one)
            sums = here if sums is None else [a + b for a, b in zip(sums, here)]
        for index, value in enumerate(sums):
            vec_out[index : index + 1] = value


def inner_grad(after, low, grad_two, slope, unit_one, inverse_one, w_attn, w_in, w_out, rows):
    total = low.shape[0]
    bands = FF // D
    slope, w_attn, w_in, w_out, rows = streamed(slope, w_attn, w_in, w_out, rows)
    band = lambda height: pl.BlockSpec((height, D), lambda j: (0, j))
    return pl.pallas_call(
        partial(inner_kernel, len(after)),
        grid=(bands,),
        in_specs=[ANY] * len(after)
        + [
            whole(low.shape), whole(grad_two.shape), band(total), whole(unit_one.shape),
            whole(inverse_one.shape), whole(w_attn.shape), band(D),
            pl.BlockSpec((D, D), lambda j: (j, 0)), whole(rows.shape),
        ],
        out_specs=[band(total)] + [whole((total, D))] * 3 + [whole((3 + bands, D))],
        out_shape=[
            near((total, FF), LOW),
            far((total, D), F32),
            near((total, D), LOW),
            near((total, D), LOW),
            jax.ShapeDtypeStruct((3 + bands, D), F32),
        ],
        scratch_shapes=[pltpu.VMEM((total, D), F32)],
        compiler_params=params(),
        cost_estimate=cost(16),
        name="inner",
    )(*after, low, grad_two, slope, unit_one, inverse_one, w_attn, w_in, w_out, rows)


def unattend_kernel(after, sums, *refs):
    q, k, v, p, ga, attended = refs[after : after + 6]
    vec_one, vec_two, vec_early = refs[after + 6 : -2] if sums else (None, None, None)
    stack_out, vec_out = refs[-2:]
    scaling = HEAD ** (-0.5)
    first = pl.program_id(0) == 0

    @pl.when(first)
    def _():
        if not sums:
            vec_out[...] = jnp.zeros_like(vec_out)
            return
        for index in range(2):
            vec_out[2 * index : 2 * index + 1] = vec_one[index : index + 1]
            vec_out[2 * index + 1 : 2 * index + 2] = vec_two[index : index + 1]
        vec_out[4:6] = vec_early[...]
        vec_out[6:7] = vec_one[2:3]
        vec_out[7:8] = vec_two[2:3]
        vec_out[8:] = vec_one[3:]

    place = 4 if sums else 0
    head_of_row = lax.broadcasted_iota(jnp.int32, (2 * HEAD, 2 * SPAN), 0) // HEAD
    head_of_lane = lax.broadcasted_iota(jnp.int32, (2 * HEAD, 2 * SPAN), 1) // SPAN
    by_head = jnp.where(head_of_row == head_of_lane, 1.0, 0.0).astype(LOW)
    for span in range(p.shape[0]):
        at = slice(span * SPAN, (span + 1) * SPAN)
        for pair in range(HEADS // 2):
            lo = pair * 2 * HEAD
            lanes = slice(lo, lo + 2 * HEAD)
            weights = p[span, pair]
            grad = ga[at, lanes]
            spread_out = dot(grad, split_heads(v[at, lanes]), (1, 1))
            along = (grad.astype(F32) * attended[at, lanes].astype(F32)).astype(LOW)
            grad_scores = (weights.astype(F32) * (spread_out - dot(along, by_head))).astype(LOW)
            parts = [grad_scores[:, :SPAN], grad_scores[:, SPAN:]]
            grad_q = dot(grad_scores, split_heads(k[at, lanes])) * scaling
            tall_scores = jnp.concatenate(parts, axis=0)
            tall_weights = jnp.concatenate([weights[:, :SPAN], weights[:, SPAN:]], axis=0)
            grad_k = dot(tall_scores, split_heads(q[at, lanes]), (0, 0))
            grad_v = dot(tall_weights, split_heads(grad), (0, 0))
            stack_out[at, lo : lo + 2 * HEAD] = grad_q.astype(LOW)
            stack_out[at, D + lo : D + lo + 2 * HEAD] = grad_k.astype(LOW)
            stack_out[at, 2 * D + lo : 2 * D + lo + 2 * HEAD] = grad_v.astype(LOW)
            vec_out[place : place + 1, lanes] += jnp.sum(grad_q, axis=0, keepdims=True)
            vec_out[place + 1 : place + 2, lanes] += jnp.sum(grad_v, axis=0, keepdims=True)


def unattend(after, part, parts, q, k, v, p, ga, attended, stack=None, sums=()):
    total = q.shape[0]
    count = total // SPAN // parts
    first = part * count
    tall = lambda width: pl.BlockSpec((SPAN, width), lambda i: (first + i, 0))
    after = after if stack is None else [stack] + after
    vec_shape = (12, D) if sums else (2, D)
    return pl.pallas_call(
        partial(unattend_kernel, len(after), bool(sums)),
        grid=(count,),
        in_specs=[ANY] * len(after)
        + [tall(D)] * 3
        + [
            pl.BlockSpec((1, HEADS // 2, SPAN, 2 * SPAN), lambda i: (first + i, 0, 0, 0)),
            tall(D),
            tall(D),
        ]
        + [whole(a.shape) for a in sums],
        out_specs=[tall(3 * D), whole(vec_shape)],
        out_shape=[far((total, 3 * D), LOW), jax.ShapeDtypeStruct(vec_shape, F32)],
        input_output_aliases={} if stack is None else {0: 0},
        compiler_params=params(),
        cost_estimate=cost(8),
        name="unattend",
    )(*after, q, k, v, p, ga, attended, *sums)


def input_kernel(*refs):
    grad_one, stack, w_qkv, out = refs[-4:]
    total = grad_one[...]
    for index in range(3):
        total += dot(stack[:, index * D : (index + 1) * D], w_qkv[index], (1, 1))
    out[...] = total


def input_grad(after, grad_one, stack, w_qkv):
    total = grad_one.shape[0]
    tall = lambda width: pl.BlockSpec((TALL, width), lambda i: (i, 0))
    return pl.pallas_call(
        input_kernel,
        grid=(total // TALL,),
        in_specs=[ANY] * len(after) + [tall(D), tall(3 * D), whole(w_qkv.shape)],
        out_specs=tall(D),
        out_shape=jax.ShapeDtypeStruct((total, D), F32),
        compiler_params=params(),
        cost_estimate=cost(8),
        name="input",
    )(*after, grad_one, stack, w_qkv)


def contrast_kernel(slots, masks, place, rows, counts, partners, loss_out, grad_out):
    total, scale = rows.shape[0], 2.0 * D ** (-0.5)

    def number(shape, axis):
        at = lax.broadcasted_iota(jnp.int32, shape, axis)
        device, block = jnp.full(shape, place[0], jnp.int32), at // GROUP
        for bit, mask in enumerate(masks):
            device = device ^ (((block >> bit) & 1) * mask)
        return device, at % GROUP

    device, slot = number((counts.shape[1], total), 1)
    hit = lax.broadcasted_iota(jnp.int32, device.shape, 0) == device
    count = dot(counts[...].astype(LOW), jnp.where(hit, 1.0, 0.0).astype(LOW))
    live_across = (slot[:1].astype(F32) < count) & (slot[:1] < slots)
    device, slot = number((total, counts.shape[1]), 0)
    hit = lax.broadcasted_iota(jnp.int32, device.shape, 1) == device
    count = jnp.sum(jnp.where(hit, counts[...], 0.0), axis=1, keepdims=True)
    live_down = (slot[:, :1].astype(F32) < count) & (slot[:, :1] < slots)
    device, slot = number((total, partners.shape[1]), 0)
    own_id = device * slots + slot
    hit = lax.broadcasted_iota(jnp.int32, own_id.shape, 1) == own_id
    pair = jnp.sum(jnp.where(hit, partners[...], 0.0), axis=1, keepdims=True)
    device, slot = number((total, 128), 0)
    down = (device * slots + slot).astype(F32)[:, :1]
    device, slot = number((8, total), 1)
    across, slot = (device * slots + slot).astype(F32)[:1], slot[:1]
    valid = live_across & (down != across)
    matched = jnp.where((slot < slots) & (pair == across), 1.0, 0.0)
    anchor = jnp.where(live_down & (pair != down), 1.0, 0.0)
    similar = dot(rows[...], rows[...], (1, 1)) * scale
    masked = jnp.where(valid, similar, -1e30)
    peak = jnp.max(masked, axis=1, keepdims=True)
    summed = jnp.sum(jnp.where(valid, jnp.exp(masked - peak), 0.0), axis=1, keepdims=True)
    log_total = jnp.log(summed) + peak
    positive = jnp.sum(matched * similar, axis=1, keepdims=True)
    loss_out[...] = jnp.sum(anchor * (log_total - positive), axis=0, keepdims=True)
    grad = (anchor * (jnp.where(valid, jnp.exp(masked - log_total), 0.0) - matched)).astype(LOW)
    own = lax.broadcasted_iota(jnp.int32, (GROUP, total), 0)
    own = jnp.where(own == lax.broadcasted_iota(jnp.int32, (GROUP, total), 1), 1.0, 0.0)
    down_part = dot(dot(own.astype(LOW), grad, (1, 1)).astype(LOW), rows[...])
    grad_out[...] = (dot(grad[: 2 * GROUP], rows[...])[:GROUP] + down_part) * scale


def contrast(cls_rows, span_count, pair_index, device, slots):
    total = cls_rows.shape[0]
    scale = {"row": lax.axis_size("col"), "col": 1}
    masks = [scale[name] * bit for phase in gather_steps() for name, bit in phase]
    return pl.pallas_call(
        partial(contrast_kernel, slots, masks),
        in_specs=[pl.BlockSpec(memory_space=pltpu.SMEM)]
        + [pl.BlockSpec(memory_space=pltpu.VMEM)] * 3,
        out_shape=[
            jax.ShapeDtypeStruct((1, 1), F32),
            jax.ShapeDtypeStruct((GROUP, D), F32),
        ],
        compiler_params=params(),
        cost_estimate=cost(3),
        name="contrast",
    )(
        device,
        cls_rows,
        span_count.astype(F32).reshape(1, -1),
        pair_index.astype(F32).reshape(1, -1),
    )


def adam_kernel(
    masks, parts, position, *refs,
):
    gathered = refs[:parts]
    master, first, second, left, right, master_out, first_out, second_out, low_out, *scratch = refs[parts:]
    quarter = D // 4
    slot = pl.program_id(0)
    if masks:
        owned = scratch[0]
        shares, tall, _ = gathered[0].shape
        rows = D // len(masks)

        @pl.when(slot == 0)
        def _():
            for number, mask in enumerate(masks):
                block = gathered[number // shares][number % shares].astype(F32)
                at = pl.multiple_of((mask ^ position[0]) * rows, rows)
                for index in range(owned.shape[0]):
                    lo = index * rows % tall
                    side = index * rows // tall
                    piece = block[lo : lo + rows, side * quarter : (side + 1) * quarter]
                    owned[index, pl.ds(at, rows), :] = piece

    for here in range(master.shape[0]):
        if masks:
            gradient = owned[slot * master.shape[0] + here].astype(LOW)
        else:
            gradient = gathered[0][here]
        low_left, low_right = left[here], right[here].astype(LOW)
        turned = dot(gradient, low_left, (0, 0))
        turned = dot(low_right, turned.astype(LOW), (0, 0))
        new_first = 0.9 * first[here] + 0.1 * turned
        new_second = 0.999 * second[here] + 0.001 * turned * turned
        first_out[here] = new_first
        second_out[here] = new_second
        spread_by = jnp.sqrt(new_second * (1.0 / (1.0 - 0.999**STEP))) + 1e-08
        update = new_first * (1.0 / (1.0 - 0.9**STEP)) / spread_by
        update = dot(update.astype(LOW), low_left, (1, 1))
        update = dot(low_right, update.astype(LOW))
        new_master = master[here] - RATE * (update + DECAY * master[here])
        master_out[here] = new_master
        low_out[here] = new_master.astype(LOW)


def ready_kernel(*refs):
    source, out = refs[-2:]
    out[...] = source[...].astype(out.dtype)


def ready(after, array, kind, first, count, before=()):
    block = pl.BlockSpec((1,) + array.shape[1:], lambda s: (first + s, 0, 0))
    first_in = list(before) + list(after)
    return pl.pallas_call(
        ready_kernel,
        grid=(count,),
        in_specs=[ANY] * len(first_in) + [block],
        out_specs=block,
        out_shape=far(array.shape, kind),
        input_output_aliases={0: 0} if before else {},
        compiler_params=params(16),
        cost_estimate=cost(1.5 * count),
        name="ready",
    )(*first_in, *streamed(array))


def to_owned(gathered, masks, position, per_owner):
    quarter = D // 4
    places = jnp.array(masks, jnp.int32) ^ position
    gathered = jnp.zeros_like(gathered).at[places].set(gathered)
    flat = jnp.concatenate([gathered[..., :quarter], gathered[..., quarter:]], axis=1)
    rows = flat.shape[1] // per_owner
    flat = flat.reshape(flat.shape[0], per_owner, rows, quarter).transpose(1, 0, 2, 3)
    return flat.reshape(per_owner, D, quarter)


def turn(array):
    return array.transpose(0, 2, 1)


def rotated_adam(position, gathered, masks, master, first_moment, second_moment, left_basis, right_basis):
    per_owner, quarter, _ = master.shape
    if D // len(masks) % 8 or per_owner % 2:
        gathered = [to_owned(jnp.concatenate(gathered), masks, position, per_owner)]
        masks = []
    at_once = max(n for n in (1, 2, 3) if per_owner % n == 0)
    block = lambda a: pl.BlockSpec((at_once,) + a.shape[1:], lambda s, p: (s, 0, 0))
    operands = streamed(master, first_moment, second_moment, left_basis, right_basis)
    like = jax.ShapeDtypeStruct(operands[0].shape, F32)
    fixed = pl.BlockSpec(gathered[0].shape, lambda s, p: (0, 0, 0))
    outputs = pl.pallas_call(
        partial(adam_kernel, masks, len(gathered)),
        grid_spec=pltpu.PrefetchScalarGridSpec(
            num_scalar_prefetch=1,
            grid=(per_owner // at_once,),
            in_specs=[fixed if masks else block(part) for part in gathered]
            + [block(a) for a in operands],
            out_specs=[block(operands[0])] * 4,
            scratch_shapes=[pltpu.VMEM((per_owner, D, quarter), F32)] if masks else [],
        ),
        out_shape=[like, like, like, jax.ShapeDtypeStruct(like.shape, LOW)],
        compiler_params=params(48),
        cost_estimate=cost(20),
        name="adam",
    )(position.reshape(1), *gathered, *operands)
    return [turn(a) for a in outputs]


def axis_bits(name):
    size = lax.axis_size(name)
    return [(name, 1 << k) for k in range(size.bit_length() - 1)]


def bit_of(step):
    return jnp.where((lax.axis_index(step[0]) & step[1]) != 0, 1, 0)


def swap(send, step):
    size = lax.axis_size(step[0])
    return lax.ppermute(send, step[0], [(i, i ^ step[1]) for i in range(size)])


def gather_steps():
    core, across, y_bits, z_bits = row_steps()
    return [z_bits[::-1], y_bits + across, core]


def gather_all(rows, beside):
    columns = lax.axis_size("col")
    every = lax.axis_size("row") * columns
    scale = {"row": columns, "col": 1}
    for phase in gather_steps():
        arrived = []
        for number in range(1, 1 << len(phase)):
            mask = sum(scale[name] * bit for j, (name, bit) in enumerate(phase) if number >> j & 1)
            pairs = [(i, i ^ mask) for i in range(every)]
            arrived.append(lax.ppermute(rows, ("row", "col"), pairs))
        if beside:
            rows = merge(beside, [rows] + arrived).reshape(-1, D)
            beside = []
        else:
            rows = jnp.concatenate([rows] + arrived)
    return rows


def row_steps():
    row_bits, col_bits = axis_bits("row"), axis_bits("col")
    core, across = row_bits[:1], row_bits[1:][::-1]
    y_bits, z_bits = col_bits[:-2][::-1], col_bits[-2:]
    return core, across, y_bits, z_bits


def pack_rider(rider, rows, width):
    parts = [rider[:, at : at + width] for at in range(0, D, width)]
    tall = rider.shape[0]
    if rows < tall:
        return [part[at : at + rows] for part in parts for at in range(0, tall, rows)]
    fold = rows // tall
    parts += parts[-1:] * (-len(parts) % fold)
    return [jnp.concatenate(parts[at : at + fold]) for at in range(0, len(parts), fold)]


def unpack_rider(blocks, tall):
    rows, width = blocks[0].shape
    if rows < tall:
        fold = tall // rows
        parts = [jnp.concatenate(blocks[at : at + fold]) for at in range(0, len(blocks), fold)]
    else:
        parts = [block[at : at + tall] for block in blocks for at in range(0, rows, tall)]
    parts = parts[: D // width]
    return parts[0] if len(parts) == 1 else jnp.concatenate(parts, axis=1)


def rider_blocks(rows, width, tall=12):
    return -(-tall * D // (rows * width))


def land_kernel(after, outs, rider, bits, *refs):
    refs = refs[after:]
    sides = len({source[0] for out in outs for source in out[3]})
    keeps, others = refs[0 : 2 * sides : 2], refs[1 : 2 * sides : 2]
    results = refs[2 * sides + (0 if rider is None else 1 + (rider == "array")) :]
    if rider is not None:
        total = refs[2 * sides][...]
        tall = total.shape[0]
        if rider == "array":
            total += refs[2 * sides + 1][...]
        else:
            blocks = [others[0][at].astype(F32) for at in range(keeps[0].shape[0], others[0].shape[0])]
            total += unpack_rider(blocks, tall)
        results[-1][...] = total
    for number, (at_bit, before, behind, sources) in enumerate(outs):
        bit = bits[at_bit]
        for which, target in enumerate(results[2 * number : 2 * number + 2]):
            half = bit if which else 1 - bit
            for at in range(before):
                here = pl.ds((2 * at + half) * behind, behind)
                there = slice(at * behind, (at + 1) * behind)
                for side, lanes, into in sources:
                    target[there, :, into] = keeps[side][here, :, lanes] + others[side][here, :, lanes]
        if rider is not None and number == 0:
            away = results[0]
            count, rows, width = away.shape
            blocks = pack_rider(total, rows, width)
            for index, block in enumerate(blocks):
                away[count - len(blocks) + index] = block.astype(LOW)


class Reduction:
    def __init__(self, bits, ways, send, keep, rider=None):
        core, across, y_bits, z_bits = row_steps()
        self.bits, self.order = bits, core + across + y_bits + z_bits
        left = across + y_bits + z_bits
        self.panels, height, _ = keep.shape
        self.rows = height >> len(left)
        other = swap(send, core[0])
        self.rider = None if rider is None else (rider, swap(rider, core[0]))
        split = lambda a: a.reshape(-1, self.rows, D)
        self.sides = [(split(keep), split(other), left)]
        cycle = [across, y_bits, z_bits[:1]][:ways]
        orders = [sum(cycle[at:] + cycle[:at], []) for at in range(ways)]
        self.stages = list(zip(*orders)) + [(step,) for step in z_bits[ways - 2 :]]
        self.ways = ways
        self.messages = []

    def sent(self):
        return self.messages

    def landing(self):
        return [side[1] for side in self.sides]

    def land(self, *after):
        stage = self.stages.pop(0)
        outs, shapes, lefts = [], [], []
        part = D // self.ways
        lanes = [slice(at, at + part) for at in range(0, D, part)]
        for index, step in enumerate(stage):
            if len(self.sides) == len(stage):
                width = self.sides[index][0].shape[2]
                sources = [(index, slice(0, width), slice(0, width))]
                left = self.sides[index][2]
            elif len(stage) > 1:
                width, left = part, self.sides[0][2]
                sources = [(0, lanes[index], slice(0, part))]
            else:
                width, left = D, self.sides[0][2]
                sources = [(side, slice(0, part), lanes[side]) for side in range(self.ways)]
            dim = left.index(step)
            behind = 1 << (len(left) - dim - 1)
            before = self.panels << dim
            outs.append((self.order.index(step), before, behind, sources))
            extra = rider_blocks(self.rows, width) if self.rider and index == 0 else 0
            shapes += [(before * behind + extra, self.rows, width), (before * behind, self.rows, width)]
            lefts.append([other for other in left if other != step])
        rider = None if self.rider is None else ("array" if len(self.rider) == 2 else "message")
        inputs = [a for keep, other, _ in self.sides for a in (keep, other)] + list(self.rider or ())
        out_shape = [jax.ShapeDtypeStruct(shape, LOW) for shape in shapes]
        if rider:
            out_shape.append(jax.ShapeDtypeStruct(self.rider[0].shape, F32))
        results = pl.pallas_call(
            partial(land_kernel, len(after), outs, rider),
            in_specs=[SMEM] + [ANY] * len(after) + [pl.BlockSpec(memory_space=pltpu.VMEM)] * len(inputs),
            out_shape=out_shape,
            compiler_params=params(24),
            cost_estimate=cost(2),
            name="land",
        )(self.bits, *after, *inputs)
        if rider:
            self.rider = (results[-1],)
        self.messages = list(results[0 : 2 * len(stage) : 2])
        keeps = results[1 : 2 * len(stage) : 2]
        self.sides = [
            (keep, swap(message, step), left)
            for keep, message, step, left in zip(keeps, self.messages, stage, lefts)
        ]

    def finish(self):
        while self.stages:
            self.land()


def slots_kernel(after, cols, panels, column, owners, *refs):
    refs = refs[after:]
    sums, rider, rider_out = refs[:6], refs[6], refs[7]
    targets, blocks, packed = refs[8:-2], refs[-2], refs[-1]
    quarter = D // 4
    found = [(sums[2 * run], sums[2 * run + 1], i) for run in range(3) for i in range(sums[2 * run].shape[0])]
    at = 0
    for panel in panels:
        keep, other, index = found[panel]
        value = keep[index].astype(F32) + other[index].astype(F32)
        for part in range(4):
            blocks[at] = value[:, part * quarter : (part + 1) * quarter]
            at += 1
    tail = [sums[1][index].astype(F32) for index in range(sums[0].shape[0], sums[1].shape[0])]
    rider_out[...] = rider[...] + unpack_rider(tail, rider.shape[0])
    rows, half = blocks.shape[1], packed.shape[1]
    for slot in range(at):
        col, place = divmod(slot, at // cols)
        value = blocks[owners[slot]]
        first = place * rows
        for side in range(2):
            lo, hi = max(first, side * half), min(first + rows, (side + 1) * half)
            if lo < hi:
                lanes = slice(side * quarter, (side + 1) * quarter)
                packed[col, lo - side * half : hi - side * half, lanes] = value[lo - first : hi - first]
    for number, target in enumerate(targets):
        target[...] = packed[column[0] ^ number].astype(LOW)


def to_slots(after, runs, panels, owner_list):
    quarter, cols = D // 4, lax.axis_size("col")
    arrays = [a for run in runs for a in run.sides[0][:2]]
    rows = runs[0].rows
    shape = (len(panels) * 4 // cols * rows // 2, 2 * quarter)
    rider = runs[0].rider[0]
    return pl.pallas_call(
        partial(slots_kernel, len(after), cols, panels),
        in_specs=[SMEM, SMEM] + [ANY] * len(after) + [pl.BlockSpec(memory_space=pltpu.VMEM)] * 7,
        out_shape=[jax.ShapeDtypeStruct(rider.shape, F32)] + [jax.ShapeDtypeStruct(shape, LOW)] * cols,
        scratch_shapes=[
            pltpu.VMEM((len(panels) * 4, rows, quarter), F32),
            pltpu.VMEM((cols,) + shape, F32),
        ],
        compiler_params=params(24),
        cost_estimate=cost(4),
        name="slots",
    )(lax.axis_index("col").reshape(1), owner_list, *after, *arrays, rider)


def merge_kernel(after, *refs):
    *sources, target = refs[after:]
    for number, source in enumerate(sources):
        target[number] = source[...]


def merge(after, arrays):
    return pl.pallas_call(
        partial(merge_kernel, len(after)),
        in_specs=[ANY] * len(after) + [pl.BlockSpec(memory_space=pltpu.VMEM)] * len(arrays),
        out_shape=jax.ShapeDtypeStruct((len(arrays),) + arrays[0].shape, arrays[0].dtype),
        compiler_params=params(24),
        cost_estimate=cost(1),
        name="merge",
    )(*after, *arrays)


def spread(parts):
    core, across, y_bits, z_bits = row_steps()
    order = core + across + y_bits + z_bits
    weight = lambda step: 1 << (len(order) - 1 - order.index(step))
    cols, bits = len(parts), axis_bits("col")
    sent = lambda number: lax.ppermute(parts[number], "col", [(i, i ^ number) for i in range(cols)])
    arrived = [parts[0]] + [sent(number) for number in range(1, cols)]
    masks = [sum(weight(step) for step in bits if number & step[1]) for number in range(cols)]
    near = merge([], arrived[: cols // 2])
    first, *rest = (core + across)[::-1]
    moved = swap(near, first)
    far = merge([], arrived[cols // 2 :])
    shares = [near, far, moved, swap(far, first)]
    masks = masks + [mask ^ weight(first) for mask in masks]
    for step in rest:
        shares = shares + [swap(share, step) for share in shares]
        masks = masks + [mask ^ weight(step) for mask in masks]
    return shares, masks


def row_place():
    place = 0
    for group in row_steps():
        for step in group:
            place = place * 2 + bit_of(step)
    return place


def shards(
    tokens,
    w_qkv,
    w_attn_out,
    w_in,
    w_out,
    vectors,
    out_grad,
    span_count,
    pair_index,
    owner_list,
    master,
    first_moment,
    second_moment,
    left_basis,
    right_basis,
    vec_first,
    vec_second,
):
    slots = tokens.shape[0] // SPAN
    device = (lax.axis_index("row") * lax.axis_size("col") + lax.axis_index("col")).reshape(1)
    core, across, y_bits, z_bits = row_steps()
    core_bit = bit_of(core[0])
    bits = jnp.stack([bit_of(step) for step in core + across + y_bits + z_bits])
    rows = vectors.reshape(1, -1)
    q, k, v, p, attended = attend(tokens, w_qkv, rows)
    encoded, hidden, slope, normed_low, unit_one, inverse_one, unit_two, inverse_two, cls_rows = (
        feed(device, span_count, tokens, attended, w_attn_out, w_in, w_out, rows)
    )
    per_owner = left_basis.shape[0]
    head = per_owner // 3
    low_left = ready([cls_rows], left_basis, LOW, 0, head)
    every_cls = gather_all(cls_rows, streamed(low_left))
    loss, grad_cls = contrast(every_cls, span_count, pair_index, device, slots)
    grad_two, outer_low, vec_two = outer_grad(
        device, span_count, out_grad, grad_cls, unit_two, inverse_two, rows
    )
    outer_args = (hidden, outer_low, FF // D, True, 1)
    outer_away = weight_half(8, [], 1 - core_bit, *outer_args)
    outer_here = weight_half(60, [outer_away], core_bit, *outer_args)
    outer_run = Reduction(bits, 2, outer_away, outer_here)
    outer_run.land()
    pre_low, grad_one, mixed_low, grad_attended, vec_one = inner_grad(
        outer_run.sent(), outer_low, grad_two, slope, unit_one, inverse_one,
        w_attn_out, w_in, w_out, rows,
    )
    outer_run.land(vec_one)
    inner_args = (normed_low, pre_low, FF // D, False, 1, (attended, mixed_low))
    inner_away = weight_half(8, outer_run.sent(), 1 - core_bit, *inner_args)
    outer_run.land(inner_away)
    inner_here = weight_half(60, [inner_away] + outer_run.sent(), core_bit, *inner_args)
    outer_run.land(inner_here)
    inner_run = Reduction(bits, 3, inner_away, inner_here)
    inner_run.land()
    early, vec_early = unattend(
        outer_run.sent() + inner_run.sent(), 0, 2, q, k, v, p, grad_attended, attended
    )
    stack_low, vec_grad = unattend(
        [], 1, 2, q, k, v, p, grad_attended, attended, early, (vec_one, vec_two, vec_early)
    )
    inner_run.land(vec_grad)
    project_args = (tokens, stack_low, 3, False, 3)
    project_away = weight_half(
        8, inner_run.sent() + outer_run.landing(), 1 - core_bit, *project_args
    )
    project_here = weight_half(60, [project_away], core_bit, *project_args)
    project_run = Reduction(bits, 3, project_away, project_here, vec_grad)
    project_run.land(*inner_run.landing())
    grad_tokens = input_grad(project_run.sent(), grad_one, stack_low, w_qkv)
    inner_run.land(*streamed(grad_tokens))
    project_run.land(*streamed(grad_tokens))
    inner_run.land()
    project_run.land(*inner_run.sent())
    project_run.land(*inner_run.landing())
    for run in (outer_run, inner_run, project_run):
        run.finish()
    low_left = ready(
        project_run.sent(), left_basis, LOW, head, per_owner - head, [low_left]
    )
    vec_grad, *parts = to_slots(
        streamed(low_left), (project_run, inner_run, outer_run),
        (0, 1, 2, 7, 3, 4, 5, 6, 8, 9, 10, 11), owner_list,
    )
    vec_grad = vec_grad.reshape(-1)
    gathered, masks = spread(parts)
    new_master, new_first, new_second, master_copy = rotated_adam(
        row_place(), gathered, masks, turn(master), turn(first_moment), turn(second_moment),
        low_left, right_basis,
    )
    vec_first_new = 0.9 * vec_first + 0.1 * vec_grad
    vec_second_new = 0.999 * vec_second + 0.001 * vec_grad * vec_grad
    vec_step = (
        vec_first_new / (1.0 - 0.9**STEP) / (jnp.sqrt(vec_second_new / (1.0 - 0.999**STEP)) + 1e-08)
    )
    vec_new = vectors - VECTOR_RATE * vec_step
    return (
        encoded,
        grad_tokens,
        loss[0, 0],
        new_master,
        new_first,
        new_second,
        master_copy,
        vec_new,
        vec_first_new,
        vec_second_new,
    )


def solution(mesh):
    in_specs = (
        P(("row", "col"), None),
        P(),
        P(),
        P(),
        P(),
        P(),
        P(("row", "col"), None),
        P(),
        P(),
        P(),
        P("col", None, None),
        P("col", None, None),
        P("col", None, None),
        P("col", None, None),
        P("col", None, None),
        P(),
        P(),
    )
    out_specs = (
        P(("row", "col"), None),
        P(("row", "col"), None),
        P(),
        P("col", None, None),
        P("col", None, None),
        P("col", None, None),
        P("col", None, None),
        P(),
        P(),
        P(),
    )
    return jax.shard_map(shards, mesh=mesh, in_specs=in_specs, out_specs=out_specs, check_vma=False)
```
